32 devices in a mesh: req: 32 (over z, y, x, core), seq: 1.
Axes of the slice: x: 2, y: 2, z: 4, core: 2. Of those that a mesh axis runs over, the one named last changes fastest.
Arguments:
- hidden_in: bfloat16 [32, 256, 1792], P('req', 'seq'), may hold values from -6 to 6
- lengths: int32 [32], P('req'), may hold values from 1 to 256, 4096 in all
- log_decay: float32 [32, 256, 8], P('req', 'seq'), may hold values from -1 to 0
- mix_gain: float32 [1792], replicated, may hold values from 0.1 to 1.9
- conv_weight: float32 [3, 1792], replicated, may hold values from -3 to 3
- query_weight: bfloat16 [1792, 128], replicated, may hold values from -0.375 to 0.375
- key_weight: bfloat16 [1792, 128], replicated, may hold values from -0.375 to 0.375
- value_weight: bfloat16 [1792, 896], replicated, may hold values from -0.125 to 0.125
- out_weight: bfloat16 [896, 1792], replicated, may hold values from -0.1875 to 0.1875
- mlp_gain: float32 [1792], replicated, may hold values from 0.1 to 1.9
- gate_weight: bfloat16 [1792, 1792], P(None, 'req'), may hold values from -0.125 to 0.125
- up_weight: bfloat16 [1792, 1792], P(None, 'req'), may hold values from -0.125 to 0.125
- down_weight: bfloat16 [1792, 1792], P(None, 'req'), may hold values from -0.125 to 0.125
Outputs:
- layer_out: bfloat16 [32, 256, 1792], P('req', 'seq')
- end_states: float32 [32, 1, 273, 896], P('req', 'seq')
- end_norms: float32 [32, 1, 273, 8], P('req', 'seq')
The draws below stay inside these ranges and needn't reach their ends.
Inputs may be any that keep to these rules, and one draw needn't show every extreme that they name: Each prompt has at least one token; the lengths sum to 4096 and the longest fills all 256 slots.
All inputs are finite; a program needn't handle non-finite values. No bound on the sum of `lengths` on one device may be relied on, other than what follows from the above.
Results may differ from the reference program's by a relative error of at most 0.0085.
Values may be sent and summed in bfloat16 or wider, within the bound.
No kernel may reach another device: no remote copies, remote signals or barrier semaphores. Data moves between devices by JAX's collectives and lax.ppermute only.
A program may use at most 128 MiB of HBM per device.

```python
import math
import jax
import jax.numpy as jnp
import numpy as np
from jax import lax

D = 1792
HALF_HEADS = 8
DV = 112
FEAT_IN = 16
FF = 1792
KCONV = 3
LOCAL_LEN = 256
REQUEST_COUNT = 32
PROMPT_SLOTS = 256
TOTAL = 4096
N_SEQ = 1


def draw_log_decay(key, part):
    base_key = jax.random.fold_in(key, 11)
    key_vectors = jax.random.split(base_key, 7)
    share = 0.5
    fast_heads = jax.random.uniform(key_vectors[0], (REQUEST_COUNT, 1, HALF_HEADS)) < share
    fast_rate = jnp.exp(jax.random.uniform(key_vectors[1], (REQUEST_COUNT, 1, HALF_HEADS), jnp.float32, math.log(1.0 / 50.0), math.log(1.0 / 30.0)))
    slow_rate = jnp.exp(jax.random.uniform(key_vectors[2], (REQUEST_COUNT, 1, HALF_HEADS), jnp.float32, math.log(0.1 / PROMPT_SLOTS), math.log(0.6 / PROMPT_SLOTS)))
    base_rate = jnp.where(fast_heads, fast_rate, slow_rate)
    span_factor = jnp.exp(jax.random.uniform(key_vectors[3], (REQUEST_COUNT, PROMPT_SLOTS // LOCAL_LEN, 1, HALF_HEADS), jnp.float32, -0.7, 0.7))
    span_factor = jnp.broadcast_to(span_factor, (REQUEST_COUNT, PROMPT_SLOTS // LOCAL_LEN, LOCAL_LEN, HALF_HEADS)).reshape(REQUEST_COUNT, PROMPT_SLOTS, HALF_HEADS)
    jitter = jnp.exp(jax.random.uniform(key_vectors[4], (REQUEST_COUNT, PROMPT_SLOTS, HALF_HEADS), jnp.float32, -0.7, 0.7))
    spike_position = jax.random.randint(key_vectors[5], (REQUEST_COUNT, 2), 0, PROMPT_SLOTS)
    token_positions = jnp.arange(PROMPT_SLOTS, dtype=jnp.int32)
    spike_flag = jnp.any(token_positions[None, :, None] == spike_position[:, None, :], axis=-1)
    spike_penalty = jax.random.uniform(key_vectors[6], (REQUEST_COUNT, PROMPT_SLOTS, HALF_HEADS), jnp.float32, math.log(0.5), math.log(0.8))
    decay_rates = base_rate * span_factor * jitter
    return (jnp.where(spike_flag[:, :, None], spike_penalty, 0.0) - decay_rates).astype(jnp.float32)


def block_levels(rng, dims, cuts, smallest, high):
    def one(axis_at, shards_of):
        heights = jax.random.uniform(jax.random.fold_in(jax.random.fold_in(rng, 6), axis_at), (shards_of,), jnp.float32, smallest / len(cuts), high / len(cuts))
        return jnp.repeat(jnp.exp(heights), dims[axis_at] // shards_of).reshape((-1,) + (1,) * (len(dims) - axis_at - 1))

    level = one(*cuts[0])
    for cut in cuts[1:]:
        level = level * one(*cut)
    return level


def split_up(count, total, bound, slope):
    loads = [(1 << 20) // math.isqrt(standing ** slope) + 1 for standing in range(2, count + 1)]
    surplus, given = total - bound - (count - 1), [1] * (count - 1)
    while surplus > 0:
        movable = [i for i in range(count - 1) if given[i] < bound]
        pool, left = sum([loads[i] for i in movable]), surplus
        for i in movable:
            extra = min(bound - given[i], max(1, left * loads[i] // pool), surplus)
            given[i] = given[i] + extra
            surplus = surplus - extra
    return np.array([bound] + given)


def ragged_sizes(own_key, amount, total, most, lean):
    if amount == 2:
        one = jax.random.randint(own_key, (), max(1, total - most), min(most, total - 1) + 1)
        return jnp.stack([one, total - one])
    sizes = jnp.asarray(split_up(amount, total, most, lean), jnp.int32)
    couples = (amount - 1) // 2
    source_of, sink = sizes[1:1 + 2 * couples:2], sizes[2:2 + 2 * couples:2]
    margin = jnp.minimum(source_of - 1, most - sink)
    moved = jax.random.randint(jax.random.fold_in(own_key, 1), (couples,), 0, 1 << 20) % (margin + 1)
    sizes = sizes.at[1:1 + 2 * couples:2].set(source_of - moved).at[2:2 + 2 * couples:2].set(sink + moved)
    return sizes[jax.random.permutation(jax.random.fold_in(own_key, 2), amount)]


def noise(key, dims, spread, reach, cuts=(), kind=jnp.bfloat16):
    level = block_levels(key, dims, cuts, -0.22, 0.18) if cuts else 1.0
    entries = jax.random.normal(key, dims, jnp.float32) * spread * level
    return jnp.minimum(jnp.maximum(entries, -reach), reach).astype(kind)


def setup_inputs(seed: int = 0) -> dict:
    keys = jax.random.split(jax.random.key(seed), 14)
    hidden_in = noise(keys[0], (REQUEST_COUNT, PROMPT_SLOTS, D), 1.0, 6.0, ((0, 32),))
    lengths = ragged_sizes(keys[1], REQUEST_COUNT, TOTAL, PROMPT_SLOTS, 2).astype(jnp.int32)
    log_decay = draw_log_decay(jax.random.fold_in(keys[13], 71), 0)
    mix_gain = jnp.clip(1.0 + 0.18 * jax.random.normal(keys[3], (D,), jnp.float32), 0.1, 1.9)
    conv_weight = noise(keys[4], (KCONV, D), 0.6, 3.0, (), jnp.float32)
    query_weight = noise(keys[5], (D, HALF_HEADS * FEAT_IN), (D // 8) ** -0.5, 0.375)
    key_weight = noise(keys[6], (D, HALF_HEADS * FEAT_IN), (D // 8) ** -0.5, 0.375)
    value_weight = noise(keys[7], (D, HALF_HEADS * DV), D ** -0.5, 0.125)
    out_weight = noise(keys[8], (HALF_HEADS * DV, D), (HALF_HEADS * DV) ** -0.5, 0.1875)
    mlp_gain = jnp.clip(1.0 + 0.18 * jax.random.normal(keys[9], (D,), jnp.float32), 0.1, 1.9)
    gate_weight = noise(keys[10], (D, FF), D ** -0.5, 0.125, ((1, 32),))
    up_weight = noise(keys[11], (D, FF), D ** -0.5, 0.125, ((1, 32),))
    down_weight = noise(keys[12], (D, FF), FF ** -0.5, 0.125, ((1, 32),))
    return dict(hidden_in=hidden_in, lengths=lengths, log_decay=log_decay, mix_gain=mix_gain, conv_weight=conv_weight, query_weight=query_weight, key_weight=key_weight, value_weight=value_weight, out_weight=out_weight, mlp_gain=mlp_gain, gate_weight=gate_weight, up_weight=up_weight, down_weight=down_weight)


def features(vectors):
    constant = jnp.ones(vectors.shape[:-1] + (1,), jnp.float32)
    width = vectors.shape[-1]
    squares = (vectors[..., :, None] * vectors[..., None, :]).reshape(vectors.shape[:-1] + (width * width,))
    return jnp.concatenate([constant, vectors, squares * 0.5 ** 0.5], axis=-1)

def block_step(carry, inputs):
    memory, key_sum = carry
    query_blk, key_blk, value_blk, decay_rate, valid_mask = inputs
    highest = lax.Precision.HIGHEST
    cumulative = jnp.cumsum(decay_rate, axis=0)
    scores = jnp.einsum('thi,uhi->htu', query_blk, key_blk, precision=highest)
    kernel = 1.0 + scores + 0.5 * scores * scores
    gap_log = cumulative.T[:, :, None] - cumulative.T[:, None, :]
    block_len = decay_rate.shape[0]
    causal = jnp.arange(block_len)[:, None] >= jnp.arange(block_len)[None, :]
    weights = jnp.where(causal[None], jnp.exp(jnp.minimum(gap_log, 0.0)), 0.0) * kernel * valid_mask[None, None, :]
    rounded = lax.optimization_barrier(weights.astype(jnp.bfloat16))
    numerator = jnp.einsum('htu,uhv->thv', rounded.astype(jnp.float32), value_blk, precision=highest)
    denominator = lax.optimization_barrier(jnp.sum(weights, axis=2)).T
    query_feat = features(query_blk)
    key_feat = features(key_blk) * valid_mask[:, None, None]
    growth = jnp.exp(cumulative)
    numerator = numerator + jnp.einsum('thf,fhv->thv', query_feat, memory, precision=highest) * growth[:, :, None]
    denominator = denominator + jnp.einsum('thf,fh->th', query_feat, key_sum, precision=highest) * growth
    closing = cumulative[-1]
    fading = jnp.exp(closing[None, :] - cumulative)
    faded_keys = key_feat * fading[:, :, None]
    memory = memory * jnp.exp(closing)[None, :, None] + jnp.einsum('uhf,uhv->fhv', faded_keys, value_blk, precision=highest)
    key_sum = key_sum * jnp.exp(closing)[None, :] + lax.optimization_barrier(jnp.sum(faded_keys, axis=0)).T
    return ((memory, key_sum), (numerator, denominator))

def span_attention(query_f32, key_f32, value_f32, decay_rate, valid_mask, memory, key_sum, block_len):
    span = query_f32.shape[0]
    blocks = span // block_len

    def split(array):
        return array.reshape((blocks, block_len) + array.shape[1:])
    carry, outputs = lax.scan(block_step, (memory, key_sum), (split(query_f32), split(key_f32), split(value_f32), split(decay_rate), split(valid_mask)))
    numerator = outputs[0].reshape((span,) + outputs[0].shape[2:])
    denominator = outputs[1].reshape((span,) + outputs[1].shape[2:])
    return (carry[0], carry[1], numerator, denominator)

def rms_scale(rows, gain):
    rows_f32 = rows.astype(jnp.float32)
    factor = lax.rsqrt(lax.optimization_barrier(jnp.mean(rows_f32 * rows_f32, axis=-1, keepdims=True)) + 1e-05)
    return (rows_f32 * factor * gain).astype(jnp.bfloat16)

def reference(hidden_in, lengths, log_decay, mix_gain, conv_weight, query_weight, key_weight, value_weight, out_weight, mlp_gain, gate_weight, up_weight, down_weight):
    head_count = log_decay.shape[2]
    value_len = value_weight.shape[1] // head_count
    feat_in = query_weight.shape[1] // head_count
    feat_len = 1 + feat_in + feat_in * feat_in
    tap_count = conv_weight.shape[0]
    block_len = min(256, LOCAL_LEN)
    feature_scale = feat_in ** (-0.25)

    def one_request(inputs):
        rows_in, length, decays = inputs
        total_len = rows_in.shape[0]
        token_positions = jnp.arange(total_len, dtype=jnp.int32)
        valid_mask = (token_positions < length).astype(jnp.float32)
        normed = rms_scale(rows_in, mix_gain)
        extended = jnp.concatenate([jnp.zeros((tap_count - 1, normed.shape[1]), jnp.bfloat16), normed], axis=0)
        convolved = jnp.zeros(normed.shape, jnp.float32)
        for tap in range(tap_count):
            convolved = convolved + conv_weight[tap][None, :] * extended[tap_count - 1 - tap:tap_count - 1 - tap + total_len].astype(jnp.float32)
        gated_rows = (convolved * jax.nn.sigmoid(normed.astype(jnp.float32))).astype(jnp.bfloat16)
        queries = (jnp.dot(gated_rows, query_weight, preferred_element_type=jnp.float32) * feature_scale).astype(jnp.bfloat16)
        key_rows = (jnp.dot(gated_rows, key_weight, preferred_element_type=jnp.float32) * feature_scale).astype(jnp.bfloat16)
        values = jnp.dot(gated_rows, value_weight, preferred_element_type=jnp.float32).astype(jnp.bfloat16)
        query_f32 = queries.astype(jnp.float32).reshape(total_len, head_count, feat_in)
        key_f32 = key_rows.astype(jnp.float32).reshape(total_len, head_count, feat_in)
        value_f32 = values.astype(jnp.float32).reshape(total_len, head_count, value_len)
        decay_rate = jnp.where(valid_mask[:, None] > 0, decays, 0.0)
        memory = jnp.zeros((feat_len, head_count, value_len), jnp.float32)
        key_sum = jnp.zeros((feat_len, head_count), jnp.float32)
        numer_parts = []
        denom_parts = []
        state_list = []
        norm_list = []
        for segment in range(N_SEQ):
            low = segment * LOCAL_LEN
            high = low + LOCAL_LEN
            memory, key_sum, numerator, denominator = span_attention(query_f32[low:high], key_f32[low:high], value_f32[low:high], decay_rate[low:high], valid_mask[low:high], memory, key_sum, block_len)
            numer_parts.append(numerator)
            denom_parts.append(denominator)
            state_list.append(memory.reshape(feat_len, head_count * value_len))
            norm_list.append(key_sum)
        numerator = jnp.concatenate(numer_parts, axis=0)
        denominator = jnp.concatenate(denom_parts, axis=0)
        attended = (numerator / denominator[:, :, None]).reshape(total_len, head_count * value_len).astype(jnp.bfloat16)
        mixed_rows = (rows_in.astype(jnp.float32) + jnp.dot(attended, out_weight, preferred_element_type=jnp.float32)).astype(jnp.bfloat16)
        mlp_in = rms_scale(mixed_rows, mlp_gain)
        gate_act = jnp.dot(mlp_in, gate_weight, preferred_element_type=jnp.float32)
        up_act = jnp.dot(mlp_in, up_weight, preferred_element_type=jnp.float32)
        hidden_units = (jax.nn.silu(gate_act) * up_act).astype(jnp.bfloat16)
        ffn_out = lax.dot_general(hidden_units, down_weight, (((1,), (1,)), ((), ())), preferred_element_type=jnp.float32)
        result = ((mixed_rows.astype(jnp.float32) + ffn_out) * valid_mask[:, None]).astype(jnp.bfloat16)
        return (result, jnp.stack(state_list), jnp.stack(norm_list))
    layer_out, end_states, end_norms = lax.map(one_request, (hidden_in, lengths, log_decay))
    return (layer_out, end_states, end_norms)
```

```python
import functools

import jax
import jax.numpy as jnp
from jax import lax
from jax.experimental import pallas as pl
from jax.experimental.pallas import tpu as pltpu
from jax.sharding import PartitionSpec as P


def from_behind(array, axis, by):
    count = lax.axis_size(axis)
    pairs = [(i, i + by) for i in range(count) if 0 <= i + by < count]
    return lax.ppermute(array, axis, pairs)


def entering(array, axis, combine, identity):
    count, here = (lax.axis_size(axis), lax.axis_index(axis))
    everything = jax.tree.map(
        lambda part, kind: lax.all_gather(part.astype(kind), axis),
        array,
        (jnp.bfloat16, jnp.bfloat16, jnp.bfloat16),
    )
    start = jax.tree.map(
        lambda part, zero: jnp.broadcast_to(jnp.asarray(zero, part.dtype), part.shape),
        array,
        identity,
    )

    def hop(k, before):
        reached = k < here
        new = combine(
            before, jax.tree.map(lambda part, own: part[k].astype(own.dtype), everything, array)
        )
        return jax.tree.map(lambda a, b: jnp.where(reached, a, b), new, before)

    return lax.fori_loop(0, count, hop, start)


def features(vectors):
    constant = jnp.ones(vectors.shape[:-1] + (1,), jnp.float32)
    width = vectors.shape[-1]
    squares = (vectors[..., :, None] * vectors[..., None, :]).reshape(
        vectors.shape[:-1] + (width * width,)
    )
    return jnp.concatenate([constant, vectors, squares * 0.5**0.5], axis=-1)


def block_step(carry, inputs):
    memory, key_sum = carry
    query_blk, key_blk, value_blk, value_half, decay_rate, valid_mask = inputs
    highest = lax.Precision.HIGHEST
    cumulative = jnp.cumsum(decay_rate, axis=0)
    scores = jnp.einsum("thi,uhi->htu", query_blk, key_blk, precision=highest)
    kernel = 1.0 + scores + 0.5 * scores * scores
    gap_log = cumulative.T[:, :, None] - cumulative.T[:, None, :]
    block_len = decay_rate.shape[0]
    causal = jnp.arange(block_len)[:, None] >= jnp.arange(block_len)[None, :]
    weights = (
        jnp.where(causal[None], jnp.exp(jnp.minimum(gap_log, 0.0)), 0.0)
        * kernel
        * valid_mask[None, None, :]
    )
    numerator = jnp.einsum(
        "htu,uhv->thv", weights.astype(jnp.bfloat16), value_half, preferred_element_type=jnp.float32
    )
    denominator = jnp.sum(weights, axis=2).T
    query_feat = features(query_blk)
    key_feat = features(key_blk) * valid_mask[:, None, None]
    growth = jnp.exp(cumulative)
    numerator = (
        numerator
        + jnp.einsum("thf,fhv->thv", query_feat, memory, precision=highest) * growth[:, :, None]
    )
    denominator = (
        denominator + jnp.einsum("thf,fh->th", query_feat, key_sum, precision=highest) * growth
    )
    closing = cumulative[-1]
    fading = jnp.exp(closing[None, :] - cumulative)
    faded_keys = key_feat * fading[:, :, None]
    memory = memory * jnp.exp(closing)[None, :, None] + jnp.einsum(
        "uhf,uhv->fhv", faded_keys, value_blk, precision=highest
    )
    key_sum = key_sum * jnp.exp(closing)[None, :] + jnp.sum(faded_keys, axis=0).T
    return ((memory, key_sum), (numerator, denominator))


def span_attention(
    query_f32, key_f32, value_f32, value_half, decay_rate, valid_mask, memory, key_sum, block_len
):
    span = query_f32.shape[0]
    blocks = span // block_len

    def split(array):
        return array.reshape((blocks, block_len) + array.shape[1:])

    carry, outputs = lax.scan(
        block_step,
        (memory, key_sum),
        (
            split(query_f32),
            split(key_f32),
            split(value_f32),
            split(value_half),
            split(decay_rate),
            split(valid_mask),
        ),
    )
    numerator = outputs[0].reshape((span,) + outputs[0].shape[2:])
    denominator = outputs[1].reshape((span,) + outputs[1].shape[2:])
    return (carry[0], carry[1], numerator, denominator)


def rms_scale(rows, gain):
    rows_f32 = rows.astype(jnp.float32)
    factor = lax.rsqrt(jnp.mean(rows_f32 * rows_f32, axis=-1, keepdims=True) + 1e-05)
    return (rows_f32 * factor * gain).astype(jnp.bfloat16)


def permute(array, target):
    count = lax.axis_size("req")
    return lax.ppermute(array, "req", [(i, target(i)) for i in range(count)])


def flip_core(array):
    return permute(array, lambda i: i ^ 1)


def flip_near(array):
    return permute(array, lambda i: i ^ 2)


def flip_far(array):
    return permute(array, lambda i: i ^ 4)


def next_plane(array):
    count = lax.axis_size("req")
    return permute(array, lambda i: (i + 8) % count)


def together(*arrays):
    return lax.optimization_barrier(arrays)


def slot(*sends):
    operands = together(*[array for _, array in sends])
    return together(*[send(array) for (send, _), array in zip(sends, operands)])


def swiglu_terms(rows, gate_rows, up_rows, down_rows):
    nt = (((1,), (1,)), ((), ()))
    gate_act = lax.dot_general(rows, gate_rows, nt, preferred_element_type=jnp.float32)
    up_act = lax.dot_general(rows, up_rows, nt, preferred_element_type=jnp.float32)
    hidden_units = (gate_act * jax.nn.sigmoid(gate_act) * up_act).astype(jnp.bfloat16)
    return jnp.dot(hidden_units, down_rows, preferred_element_type=jnp.float32)


def piece_rows(refs, main):
    if len(refs) == 1:
        (ref,) = refs
        return ref[:main], ref[main : 2 * main], ref[2 * main : 3 * main]
    first, second = refs
    cut = first.shape[0]
    up_rows = jnp.concatenate([first[main:cut], second[: 2 * main - cut]], axis=0)
    return first[:main], up_rows, second[2 * main - cut : 3 * main - cut]


def accumulate_body(main, sizes, has_acc, *refs):
    own_ref, other_ref = refs[:2]
    at = 2
    parts = ([], [], [])
    for size in sizes:
        for part, rows in zip(parts, piece_rows(refs[at : at + size], main)):
            part.append(rows)
        at += size
    gate_rows, up_rows, down_rows = (jnp.concatenate(part, axis=0) for part in parts)
    outs = refs[-2:]
    for k, rows_ref in enumerate((own_ref, other_ref)):
        terms = swiglu_terms(rows_ref[...], gate_rows, up_rows, down_rows)
        if has_acc:
            terms = terms + refs[at + k][...]
        outs[k][...] = terms


def accumulate(rows, pieces, main, acc):
    sizes = tuple(len(piece) for piece in pieces)
    flat = [array for piece in pieces for array in piece]
    shape = jax.ShapeDtypeStruct(rows[0].shape, jnp.float32)
    start = 2 + len(flat)
    return pl.pallas_call(
        functools.partial(accumulate_body, main, sizes, acc is not None),
        out_shape=(shape, shape),
        in_specs=[pl.BlockSpec(memory_space=pltpu.VMEM)] * (start + (2 if acc else 0)),
        out_specs=(pl.BlockSpec(memory_space=pltpu.VMEM),) * 2,
        input_output_aliases={start: 0, start + 1: 1} if acc else {},
        compiler_params=pltpu.CompilerParams(vmem_limit_bytes=40 * 1024 * 1024),
        cost_estimate=pl.CostEstimate(flops=1000, bytes_accessed=1000, transcendentals=0),
        name="accumulate",
    )(*rows, *flat, *(acc or ()))


def edge_rows(refs, edge):
    parts = ([], [], [])
    for ref, low in refs:
        array = ref[...].astype(jnp.float32)
        for base in range(low, array.shape[0], 3 * edge):
            for k in range(3):
                parts[k].append(array[base + k * edge : base + (k + 1) * edge])
    return [jnp.concatenate(part, axis=0).astype(jnp.bfloat16) for part in parts]


def finish_body(main, edge, n_edges, lows, rows_ref, first_ref, second_ref, *refs):
    edges = edge_rows(list(zip(refs[:n_edges], lows)), edge)
    whole = piece_rows((first_ref, second_ref), main)
    parts = [jnp.concatenate(pair, axis=0) for pair in zip(edges, whole)]
    terms = swiglu_terms(rows_ref[...], *parts) + refs[n_edges][...]
    refs[-1][...] = terms.astype(refs[-1].dtype)


def finish(rows, last, edges, main, edge, acc, dtype):
    lows = tuple(low for _, low in edges)
    return pl.pallas_call(
        functools.partial(finish_body, main, edge, len(edges), lows),
        out_shape=jax.ShapeDtypeStruct(rows.shape, dtype),
        in_specs=[pl.BlockSpec(memory_space=pltpu.VMEM)] * (4 + len(edges)),
        out_specs=pl.BlockSpec(memory_space=pltpu.VMEM),
        compiler_params=pltpu.CompilerParams(vmem_limit_bytes=40 * 1024 * 1024),
        cost_estimate=pl.CostEstimate(flops=1000, bytes_accessed=1000, transcendentals=0),
        name="finish",
    )(rows, *last, *[array for array, _ in edges], acc)


def weight_slots(gate_weight, up_weight, down_weight):
    units = gate_weight.shape[1]
    edge = units // 7
    main = units - edge
    width = 3 * main
    cut = main + 2 * main // 3
    turned = [weight.T for weight in (gate_weight, up_weight, down_weight)]
    shard = jnp.concatenate([w[:main] for w in turned] + [w[main:] for w in turned], axis=0)
    near, far, deep1 = slot((flip_near, shard), (flip_far, shard), (next_plane, shard[:width]))
    yield [(shard,), (near,), (far,), (deep1,)], []
    edges = jnp.concatenate([shard[width:], near[width:], far[width:]], axis=0)
    near1, far1, deep2, edges1, first, second = slot(
        (flip_near, deep1),
        (flip_far, deep1),
        (next_plane, deep1),
        (next_plane, edges),
        (flip_near, far[:cut]),
        (flip_far, near[cut:]),
    )
    corner = second[width - cut :]
    yield (
        [(first, second), (near1,), (far1,), (deep2,)],
        [(shard, width), (near, width), (far, width), (second, width - cut), (edges1, 0)],
    )
    near2, far2, deep3, edges2, first1, second1, corner1 = slot(
        (flip_near, deep2),
        (flip_far, deep2),
        (next_plane, deep2),
        (next_plane, edges1),
        (flip_near, far1[:cut]),
        (flip_far, near1[cut:]),
        (next_plane, corner),
    )
    yield [(first1, second1), (near2,), (far2,), (deep3,)], [(edges2, 0), (corner1, 0)]
    near3, far3, edges3, first2, second2, corner2 = slot(
        (flip_near, deep3),
        (flip_far, deep3),
        (next_plane, edges2),
        (flip_near, far2[:cut]),
        (flip_far, near2[cut:]),
        (next_plane, corner1),
    )
    yield [(first2, second2), (near3,), (far3,)], [(edges3, 0), (corner2, 0)]
    first3, second3, corner3 = slot(
        (flip_near, far3[:cut]), (flip_far, near3[cut:]), (next_plane, corner2)
    )
    yield [(first3, second3)], [(corner3, 0)]


def finish_rows(mixed_rows, valid_mask, mlp_gain, gate_weight, up_weight, down_weight):
    units = gate_weight.shape[1]
    edge = units // 7
    main = units - edge
    mlp_in = rms_scale(mixed_rows, mlp_gain)
    rows = (mlp_in, flip_core(mlp_in))
    slots = list(weight_slots(gate_weight, up_weight, down_weight))
    edges = [part for _, parts in slots for part in parts]
    acc = accumulate(rows, slots[0][0] + slots[1][0], main, None)
    acc = accumulate(rows, slots[2][0], main, acc)
    acc = accumulate(rows, slots[3][0], main, acc)
    last = slots[4][0][0]
    given = finish(rows[1], last, edges, main, edge, acc[1], jnp.bfloat16)
    kept = finish(rows[0], last, edges, main, edge, acc[0], jnp.float32)
    ffn_out = kept + flip_core(given).astype(jnp.float32)
    return ((mixed_rows.astype(jnp.float32) + ffn_out) * valid_mask[:, None]).astype(jnp.bfloat16)


def local(
    hidden_in,
    lengths,
    log_decay,
    mix_gain,
    conv_weight,
    query_weight,
    key_weight,
    value_weight,
    out_weight,
    mlp_gain,
    gate_weight,
    up_weight,
    down_weight,
):
    local_len = hidden_in.shape[1]
    rows_in = hidden_in[0]
    decays = log_decay[0]
    head_count = log_decay.shape[2]
    value_len = value_weight.shape[1] // head_count
    feat_in = query_weight.shape[1] // head_count
    feat_len = 1 + feat_in + feat_in * feat_in
    tap_count = conv_weight.shape[0]
    block_len = min(256, local_len)
    feature_scale = feat_in ** (-0.25)
    token_positions = lax.axis_index("seq") * local_len + jnp.arange(local_len, dtype=jnp.int32)
    valid_mask = (token_positions < lengths[0]).astype(jnp.float32)
    normed = rms_scale(rows_in, mix_gain)
    edge_rows = from_behind(normed[local_len - (tap_count - 1) :], "seq", 1)
    extended = jnp.concatenate([edge_rows, normed], axis=0)
    convolved = jnp.zeros(normed.shape, jnp.float32)
    for tap in range(tap_count):
        convolved = convolved + conv_weight[tap][None, :] * extended[
            tap_count - 1 - tap : tap_count - 1 - tap + local_len
        ].astype(jnp.float32)
    gated_rows = (convolved * jax.nn.sigmoid(normed.astype(jnp.float32))).astype(jnp.bfloat16)
    queries = (
        jnp.dot(gated_rows, query_weight, preferred_element_type=jnp.float32) * feature_scale
    ).astype(jnp.bfloat16)
    key_rows = (
        jnp.dot(gated_rows, key_weight, preferred_element_type=jnp.float32) * feature_scale
    ).astype(jnp.bfloat16)
    values = jnp.dot(gated_rows, value_weight, preferred_element_type=jnp.float32).astype(
        jnp.bfloat16
    )
    query_f32 = queries.astype(jnp.float32).reshape(local_len, head_count, feat_in)
    key_f32 = key_rows.astype(jnp.float32).reshape(local_len, head_count, feat_in)
    value_half = values.reshape(local_len, head_count, value_len)
    value_f32 = value_half.astype(jnp.float32)
    decay_rate = jnp.where(valid_mask[:, None] > 0, decays, 0.0)
    empty_memory = jnp.zeros((feat_len, head_count, value_len), jnp.float32)
    empty_keys = jnp.zeros((feat_len, head_count), jnp.float32)
    memory, key_sum, numerator, denominator = span_attention(
        query_f32,
        key_f32,
        value_f32,
        value_half,
        decay_rate,
        valid_mask,
        empty_memory,
        empty_keys,
        block_len,
    )
    span_decay = jnp.sum(decay_rate, axis=0)
    flat_memory = memory.reshape(feat_len, head_count * value_len)

    end_state, end_norm = (flat_memory, key_sum)
    if lax.axis_size("seq") > 1:

        def merge_states(earlier, later):
            factor = jnp.exp(later[0])
            return (
                earlier[0] + later[0],
                earlier[1] * jnp.repeat(factor, value_len)[None, :] + later[1],
                earlier[2] * factor[None, :] + later[2],
            )

        neutral = (jnp.zeros_like(span_decay), jnp.zeros_like(flat_memory), jnp.zeros_like(key_sum))
        carried = entering((span_decay, flat_memory, key_sum), "seq", merge_states, neutral)
        prior_memory = carried[1]
        prior_keys = carried[2]
        highest = lax.Precision.HIGHEST
        growth = jnp.exp(jnp.cumsum(decay_rate, axis=0))
        query_feat = features(query_f32)
        numerator = (
            numerator
            + jnp.einsum(
                "thf,fhv->thv",
                query_feat,
                prior_memory.reshape(feat_len, head_count, value_len),
                precision=highest,
            )
            * growth[:, :, None]
        )
        denominator = (
            denominator + jnp.einsum("thf,fh->th", query_feat, prior_keys, precision=highest) * growth
        )
        span_factor = jnp.exp(span_decay)
        end_state = prior_memory * jnp.repeat(span_factor, value_len)[None, :] + flat_memory
        end_norm = prior_keys * span_factor[None, :] + key_sum
    attended = (
        (numerator / denominator[:, :, None])
        .reshape(local_len, head_count * value_len)
        .astype(jnp.bfloat16)
    )
    mixed_rows = (
        rows_in.astype(jnp.float32)
        + jnp.dot(attended, out_weight, preferred_element_type=jnp.float32)
    ).astype(jnp.bfloat16)
    result = finish_rows(mixed_rows, valid_mask, mlp_gain, gate_weight, up_weight, down_weight)
    return (result[None], end_state[None, None], end_norm[None, None])


def solution(mesh):
    return jax.shard_map(
        local,
        mesh=mesh,
        in_specs=(
            P("req", "seq", None),
            P("req"),
            P("req", "seq", None),
            P(),
            P(),
            P(),
            P(),
            P(),
            P(),
            P(),
            P(None, "req"),
            P(None, "req"),
            P(None, "req"),
        ),
        out_specs=(P("req", "seq", None), P("req", "seq", None, None), P("req", "seq", None, None)),
        check_vma=False,
    )
```

```python
import functools

import jax
import jax.numpy as jnp
from jax import lax
from jax.experimental import pallas as pl
from jax.experimental.pallas import tpu as pltpu
from jax.sharding import PartitionSpec as P


def from_behind(array, axis, by):
    count = lax.axis_size(axis)
    pairs = [(i, i + by) for i in range(count) if 0 <= i + by < count]
    return lax.ppermute(array, axis, pairs)


def entering(array, axis, combine, identity):
    count, here = (lax.axis_size(axis), lax.axis_index(axis))
    everything = jax.tree.map(
        lambda part, kind: lax.all_gather(part.astype(kind), axis),
        array,
        (jnp.bfloat16, jnp.bfloat16, jnp.bfloat16),
    )
    start = jax.tree.map(
        lambda part, zero: jnp.broadcast_to(jnp.asarray(zero, part.dtype), part.shape),
        array,
        identity,
    )

    def hop(k, before):
        reached = k < here
        new = combine(
            before, jax.tree.map(lambda part, own: part[k].astype(own.dtype), everything, array)
        )
        return jax.tree.map(lambda a, b: jnp.where(reached, a, b), new, before)

    return lax.fori_loop(0, count, hop, start)


def features(vectors):
    constant = jnp.ones(vectors.shape[:-1] + (1,), jnp.float32)
    width = vectors.shape[-1]
    squares = (vectors[..., :, None] * vectors[..., None, :]).reshape(
        vectors.shape[:-1] + (width * width,)
    )
    return jnp.concatenate([constant, vectors, squares * 0.5**0.5], axis=-1)


def carry_in(valid_mask, decays, queries, numerator, denominator, flat_memory, key_sum):
    local_len = numerator.shape[0]
    feat_len, head_count = key_sum.shape
    value_len = flat_memory.shape[1] // head_count
    feat_in = queries.shape[1] // head_count
    decay_rate = jnp.where(valid_mask[:, None] > 0, decays, 0.0)
    span_decay = jnp.sum(decay_rate, axis=0)

    def merge_states(earlier, later):
        factor = jnp.exp(later[0])
        return (
            earlier[0] + later[0],
            earlier[1] * jnp.repeat(factor, value_len)[None, :] + later[1],
            earlier[2] * factor[None, :] + later[2],
        )

    neutral = (jnp.zeros_like(span_decay), jnp.zeros_like(flat_memory), jnp.zeros_like(key_sum))
    carried = entering((span_decay, flat_memory, key_sum), "seq", merge_states, neutral)
    prior_memory = carried[1]
    prior_keys = carried[2]
    highest = lax.Precision.HIGHEST
    growth = jnp.exp(jnp.cumsum(decay_rate, axis=0))
    query_feat = features(queries.astype(jnp.float32).reshape(local_len, head_count, feat_in))
    added = jnp.einsum(
        "thf,fhv->thv",
        query_feat,
        prior_memory.reshape(feat_len, head_count, value_len),
        precision=highest,
    )
    numerator = numerator + (added * growth[:, :, None]).reshape(local_len, -1)
    denominator = (
        denominator + jnp.einsum("thf,fh->th", query_feat, prior_keys, precision=highest) * growth
    )
    span_factor = jnp.exp(span_decay)
    end_state = prior_memory * jnp.repeat(span_factor, value_len)[None, :] + flat_memory
    end_norm = prior_keys * span_factor[None, :] + key_sum
    return numerator, denominator, end_state, end_norm


def permute(array, target):
    count = lax.axis_size("req")
    return lax.ppermute(array, "req", [(i, target(i)) for i in range(count)])


def flip_core(array):
    return permute(array, lambda i: i ^ 1)


def flip_near(array):
    return permute(array, lambda i: i ^ 2)


def flip_far(array):
    return permute(array, lambda i: i ^ 4)


def next_plane(array):
    count = lax.axis_size("req")
    return permute(array, lambda i: (i + 8) % count)


def together(*arrays):
    return lax.optimization_barrier(arrays)


def slot(*sends):
    operands = together(*[array for _, array in sends])
    return together(*[send(array) for (send, _), array in zip(sends, operands)])


def vmem(count):
    return [pl.BlockSpec(memory_space=pltpu.VMEM)] * count


def kernel_call(body, name, out_shape, *operands, scratch=(), aliases=None, specs=None):
    many = isinstance(out_shape, tuple)
    return pl.pallas_call(
        body,
        out_shape=out_shape,
        in_specs=specs or vmem(len(operands)),
        out_specs=tuple(vmem(len(out_shape))) if many else vmem(1)[0],
        scratch_shapes=list(scratch),
        input_output_aliases=aliases or {},
        compiler_params=pltpu.CompilerParams(vmem_limit_bytes=48 * 1024 * 1024),
        cost_estimate=pl.CostEstimate(flops=1000, bytes_accessed=1000, transcendentals=0),
        name=name,
    )(*operands)


def like(rows, columns, dtype):
    return jax.ShapeDtypeStruct((rows, columns), dtype)


NT = (((1,), (1,)), ((), ()))


def unit_rows(rows, gain):
    factor = lax.rsqrt(jnp.mean(rows * rows, axis=-1, keepdims=True) + 1e-05)
    return (rows * factor * gain).astype(jnp.bfloat16).astype(jnp.float32)


def project_body(
    step,
    scale,
    rows_ref,
    edge_ref,
    gain_ref,
    conv_ref,
    query_ref,
    key_ref,
    value_ref,
    queries_ref,
    keys_ref,
    values_ref,
    normed,
    gated,
):
    gain = gain_ref[...]
    count = rows_ref.shape[0]
    lead = edge_ref.shape[0]
    taps = conv_ref.shape[0]
    normed[:lead] = unit_rows(edge_ref[...].astype(jnp.float32), gain)

    @pl.loop(0, count // step)
    def _(block):
        at = pl.multiple_of(block * step, step)
        rows = rows_ref[pl.ds(at, step), :].astype(jnp.float32)
        normed[pl.ds(lead + at, step), :] = unit_rows(rows, gain)

    @pl.loop(0, count // step)
    def _(block):
        at = pl.multiple_of(block * step, step)
        window = normed[pl.ds(at, step + lead), :]
        here = window[lead:]
        total = conv_ref[0:1] * here
        for tap in range(1, taps):
            total = total + conv_ref[tap : tap + 1] * window[lead - tap : lead - tap + step]
        gated[pl.ds(at, step), :] = (total * jax.nn.sigmoid(here)).astype(jnp.bfloat16)

    rows = gated[...]
    for weight_ref, out_ref, factor in (
        (query_ref, queries_ref, scale),
        (key_ref, keys_ref, scale),
        (value_ref, values_ref, None),
    ):
        product = jnp.dot(rows, weight_ref[...], preferred_element_type=jnp.float32)
        if factor is not None:
            product = product * factor
        out_ref[...] = product.astype(jnp.bfloat16)


def project(rows, edge, mix_gain, conv_weight, query_weight, key_weight, value_weight, scale):
    count, width = rows.shape
    step = 32
    return kernel_call(
        functools.partial(project_body, step, scale),
        "project",
        tuple(like(count, w.shape[1], jnp.bfloat16) for w in (query_weight, key_weight, value_weight)),
        rows,
        edge,
        mix_gain[None],
        conv_weight,
        query_weight,
        key_weight,
        value_weight,
        scratch=(
            pltpu.VMEM((count + edge.shape[0], width), jnp.float32),
            pltpu.VMEM((count, width), jnp.bfloat16),
        ),
    )


def attend_body(
    feat_in,
    value_len,
    valid_ref,
    rate_ref,
    queries_ref,
    keys_ref,
    values_ref,
    numer_ref,
    denom_ref,
    state_ref,
    norm_ref,
    turned,
    total,
    norms,
):
    heads, count = rate_ref.shape
    columns = values_ref.shape[1]
    lane = lax.broadcasted_iota(jnp.int32, (count, count), 1)
    row = lax.broadcasted_iota(jnp.int32, (count, count), 0)
    valid = valid_ref[...]
    rate = jnp.where(valid > 0, rate_ref[...], 0.0)
    upto = (row <= lane).astype(jnp.float32)
    across = jnp.dot(
        rate, upto, precision=lax.Precision.HIGHEST, preferred_element_type=jnp.float32
    )
    down = across.T
    closing = across[:, count - 1 : count]
    fading = jnp.exp(closing - across) * valid
    causal = row >= lane
    keys = keys_ref[...]
    turned[...] = keys.astype(jnp.float32).T
    owner = lax.broadcasted_iota(jnp.int32, queries_ref.shape, 1)
    spare = lax.broadcasted_iota(jnp.int32, (8, count), 0) == 0
    head_lane = lax.broadcasted_iota(jnp.int32, (count, 128), 1)
    numer_ref[...] = jnp.zeros(numer_ref.shape, jnp.float32)
    total[...] = jnp.zeros(total.shape, jnp.float32)
    norm_total = jnp.zeros(norms.shape, jnp.float32)
    denominators = jnp.zeros((count, 128), jnp.float32)
    for h in range(heads):
        low = min(h * value_len // 128 * 128, max(columns - 256, 0))
        high = min(low + 256, columns)
        mine = lax.broadcasted_iota(jnp.int32, (count, high - low), 1) + low
        mine = (mine >= h * value_len) & (mine < (h + 1) * value_len)
        values = jnp.where(mine, values_ref[:, low:high].astype(jnp.float32), 0.0)
        values = values.astype(jnp.bfloat16)
        asks = (owner >= h * feat_in) & (owner < (h + 1) * feat_in)
        queries = jnp.where(asks, queries_ref[...].astype(jnp.float32), 0.0)
        scores = lax.dot_general(
            queries.astype(jnp.bfloat16), keys, NT, preferred_element_type=jnp.float32
        )
        gap = down[:, h : h + 1] - across[h : h + 1]
        weights = jnp.where(causal, jnp.exp(jnp.minimum(gap, 0.0)) * valid, 0.0)
        weights = weights * (1.0 + scores + 0.5 * scores * scores)
        numer_ref[:, low:high] += jnp.dot(
            weights.astype(jnp.bfloat16), values, preferred_element_type=jnp.float32
        )
        sums = jnp.sum(weights, axis=1, keepdims=True)
        denominators = jnp.where(head_lane == h, sums, denominators)
        own = turned[h * feat_in : (h + 1) * feat_in]
        fade = fading[h : h + 1]
        faded = own * fade
        scaled = faded * 0.5**0.5
        parts = [own[i : i + 1] * scaled for i in range(feat_in)]
        parts += [faded, jnp.where(spare, fade, 0.0)]
        feats = jnp.concatenate(parts, axis=0).astype(jnp.bfloat16)
        total[:, low:high] += jnp.dot(feats, values, preferred_element_type=jnp.float32)
        mark = (head_lane == h).astype(jnp.bfloat16)
        norm_total = norm_total + jnp.dot(feats, mark, preferred_element_type=jnp.float32)
    denom_ref[...] = denominators[:, :heads]
    norms[...] = norm_total
    pairs = feat_in * feat_in
    for out_ref, source, width in ((state_ref, total, columns), (norm_ref, norms, heads)):
        out_ref[0:1, :] = source[pairs + feat_in : pairs + feat_in + 1, :width]
        out_ref[1 : 1 + feat_in, :] = source[pairs : pairs + feat_in, :width]
        out_ref[1 + feat_in :, :] = source[:pairs, :width]


def attend(valid, rate, queries, keys, values, feat_in, value_len):
    heads, count = rate.shape
    columns = values.shape[1]
    feat_len = 1 + feat_in + feat_in * feat_in
    padded = feat_in * feat_in + feat_in + 8
    return kernel_call(
        functools.partial(attend_body, feat_in, value_len),
        "attend",
        (
            like(count, columns, jnp.float32),
            like(count, heads, jnp.float32),
            like(feat_len, columns, jnp.float32),
            like(feat_len, heads, jnp.float32),
        ),
        valid,
        rate,
        queries,
        keys,
        values,
        scratch=(
            pltpu.VMEM((queries.shape[1], count), jnp.float32),
            pltpu.VMEM((padded, columns), jnp.float32),
            pltpu.VMEM((padded, 128), jnp.float32),
        ),
    )


def mix_body(
    value_len, step, numer_ref, denom_ref, rows_ref, out_ref, gain_ref, mixed_ref, mlp_ref, sums
):
    count, columns = numer_ref.shape
    heads = denom_ref.shape[1]
    column = lax.broadcasted_iota(jnp.int32, (1, columns), 1)
    inverse = 1.0 / denom_ref[...]
    spread = jnp.zeros((count, columns), jnp.float32)
    for h in range(heads):
        here = (column >= h * value_len) & (column < (h + 1) * value_len)
        spread = jnp.where(here, inverse[:, h : h + 1], spread)
    attended = (numer_ref[...] * spread).astype(jnp.bfloat16)
    sums[...] = jnp.dot(attended, out_ref[...], preferred_element_type=jnp.float32)
    gain = gain_ref[...]

    @pl.loop(0, count // step)
    def _(block):
        at = pl.ds(pl.multiple_of(block * step, step), step)
        mixed = (rows_ref[at, :].astype(jnp.float32) + sums[at, :]).astype(jnp.bfloat16)
        mixed_ref[at, :] = mixed
        mlp_ref[at, :] = unit_rows(mixed.astype(jnp.float32), gain).astype(jnp.bfloat16)


def mix(numer, denom, rows, out_weight, mlp_gain, value_len):
    count, width = rows.shape
    shape = like(count, width, jnp.bfloat16)
    return kernel_call(
        functools.partial(mix_body, value_len, 32),
        "mix",
        (shape, shape),
        numer,
        denom,
        rows,
        out_weight,
        mlp_gain[None],
        scratch=(pltpu.VMEM((count, width), jnp.float32),),
    )


def swiglu_terms(rows, gate_rows, up_rows, down_rows):
    gate_act = lax.dot_general(rows, gate_rows, NT, preferred_element_type=jnp.float32)
    up_act = lax.dot_general(rows, up_rows, NT, preferred_element_type=jnp.float32)
    hidden_units = (gate_act * jax.nn.sigmoid(gate_act) * up_act).astype(jnp.bfloat16)
    return jnp.dot(hidden_units, down_rows, preferred_element_type=jnp.float32)


def main_rows(refs, main):
    if len(refs) == 1:
        (ref,) = refs
        return [ref[:main]], [ref[main : 2 * main]], [ref[2 * main : 3 * main]]
    first, second = refs
    cut = main + 2 * main // 3
    rest = 2 * main - cut
    return [first[:main]], [first[main:cut], second[:rest]], [second[rest : rest + main]]


def edge_rows(array, edge):
    parts = ([], [], [])
    for base in range(0, array.shape[0], 3 * edge):
        for k in range(3):
            parts[k].append(array[base + k * edge : base + (k + 1) * edge])
    return parts


def gather_units(refs, pieces, edges, main, edge):
    parts = ([], [], [])
    for piece in pieces:
        for part, rows in zip(parts, main_rows([refs[i] for i in piece], main)):
            part.extend(rows)
    edge_parts = ([], [], [])
    for i, low in edges:
        for part, rows in zip(edge_parts, edge_rows(refs[i][...].astype(jnp.float32)[low:], edge)):
            part.extend(rows)
    for part, rows in zip(parts, edge_parts):
        if rows:
            part.append(jnp.concatenate(rows, axis=0).astype(jnp.bfloat16))
    return [jnp.concatenate(part, axis=0) for part in parts]


def accumulate_body(main, edge, n_weights, pieces, edges, n_acc, n_rows, *refs):
    weights = refs[:n_weights]
    rows = refs[n_weights : n_weights + n_rows]
    acc = refs[n_weights + n_rows : n_weights + n_rows + n_acc]
    parts = gather_units(weights, pieces, edges, main, edge)
    for k, rows_ref in enumerate(rows):
        out_ref = refs[len(refs) - n_rows + k]
        terms = swiglu_terms(rows_ref[...], *parts)
        if n_acc:
            terms = terms + acc[k][...]
        out_ref[...] = terms.astype(out_ref.dtype)


def accumulate(rows, weights, pieces, edges, main, edge, acc, dtype, name):
    shapes = tuple(like(*array.shape, dtype) for array in rows)
    start = len(weights) + len(rows)
    in_place = acc and dtype == jnp.float32
    body = functools.partial(
        accumulate_body, main, edge, len(weights), pieces, edges, len(acc), len(rows)
    )
    aliases = {start + k: k for k in range(len(acc))} if in_place else {}
    return kernel_call(body, name, shapes, *weights, *rows, *acc, aliases=aliases)


def shard_body(main, gate_ref, up_ref, down_ref, shard_ref, main_ref):
    arrays = [ref[...].astype(jnp.float32) for ref in (gate_ref, up_ref, down_ref)]
    tops = [array[:main] for array in arrays]
    ends = [array[main:] for array in arrays]
    shard_ref[...] = jnp.concatenate(tops + ends, axis=0).astype(jnp.bfloat16)
    main_ref[...] = jnp.concatenate(tops, axis=0).astype(jnp.bfloat16)


def second_slot_body(width, cut, shard_ref, near_ref, far_ref, deep_ref, line_ref, first, second):
    shard, near, far, deep = [
        ref[...].astype(jnp.float32) for ref in (shard_ref, near_ref, far_ref, deep_ref)
    ]
    line = [deep, shard[width:], near[width:], far[width:]]
    line_ref[...] = jnp.concatenate(line, axis=0).astype(jnp.bfloat16)
    first[...] = far[:cut].astype(jnp.bfloat16)
    second[...] = near[cut:].astype(jnp.bfloat16)


def third_slot_body(low, line_ref, corner_ref, out_ref):
    line, corner = [ref[...].astype(jnp.float32) for ref in (line_ref, corner_ref)]
    out_ref[...] = jnp.concatenate([line, corner[low:]], axis=0).astype(jnp.bfloat16)


def local(
    hidden_in,
    lengths,
    log_decay,
    mix_gain,
    conv_weight,
    query_weight,
    key_weight,
    value_weight,
    out_weight,
    mlp_gain,
    gate_weight,
    up_weight,
    down_weight,
):
    local_len = hidden_in.shape[1]
    rows_in = hidden_in[0]
    decays = log_decay[0]
    head_count = log_decay.shape[2]
    value_len = value_weight.shape[1] // head_count
    feat_in = query_weight.shape[1] // head_count
    feature_scale = feat_in ** (-0.25)
    token_positions = lax.axis_index("seq") * local_len + jnp.arange(local_len, dtype=jnp.int32)
    valid_mask = (token_positions < lengths[0]).astype(jnp.float32)
    spans = lax.axis_size("seq")
    units, model = gate_weight.shape[1], gate_weight.shape[0]
    edge = units // 7
    main = units - edge
    width = 3 * main
    cut = main + 2 * main // 3
    low = width - cut

    shard, shard_main = kernel_call(
        functools.partial(shard_body, main),
        "shard",
        (like(3 * units, model, jnp.bfloat16), like(width, model, jnp.bfloat16)),
        gate_weight.T,
        up_weight.T,
        down_weight.T,
    )
    near, far, deep1 = slot((flip_near, shard), (flip_far, shard), (next_plane, shard_main))

    lead = 16
    if spans > 1:
        edge_in = from_behind(rows_in[local_len - lead :], "seq", 1)
    else:
        edge_in = jnp.zeros((lead, model), jnp.bfloat16)
    queries, key_rows, values = project(
        rows_in, edge_in, mix_gain, conv_weight, query_weight, key_weight, value_weight, feature_scale
    )

    near, far, deep1, queries, key_rows, values = together(
        near, far, deep1, queries, key_rows, values
    )
    line, first, second = kernel_call(
        functools.partial(second_slot_body, width, cut),
        "second_slot",
        (
            like(width + 9 * edge, model, jnp.bfloat16),
            like(cut, model, jnp.bfloat16),
            like(3 * units - cut, model, jnp.bfloat16),
        ),
        shard,
        near,
        far,
        deep1,
    )
    near1, far1, line1, first, second = slot(
        (flip_near, deep1), (flip_far, deep1), (next_plane, line), (flip_near, first), (flip_far, second)
    )

    rate = log_decay[0].T
    numerator, denominator, end_state, end_norm = attend(
        valid_mask[None], rate, queries, key_rows, values, feat_in, value_len
    )
    if spans > 1:
        numerator, denominator, end_state, end_norm = carry_in(
            valid_mask, decays, queries, numerator, denominator, end_state, end_norm
        )
    mixed_rows, mlp_in = mix(numerator, denominator, rows_in, out_weight, mlp_gain, value_len)

    near1, far1, line1, first, second, mixed_rows, mlp_in = together(
        near1, far1, line1, first, second, mixed_rows, mlp_in
    )
    line = kernel_call(
        functools.partial(third_slot_body, low),
        "third_slot",
        like(width + 12 * edge, model, jnp.bfloat16),
        line1,
        second,
    )
    near2, far2, line2, first1, second1 = slot(
        (flip_near, line1[:width]),
        (flip_far, line1[:width]),
        (next_plane, line),
        (flip_near, far1[:cut]),
        (flip_far, near1[cut:]),
    )
    other_in, near3, far3, line3 = slot(
        (flip_core, mlp_in),
        (flip_near, line2[:width]),
        (flip_far, line2[:width]),
        (next_plane, line2[width:]),
    )
    rows = (mlp_in, other_in)
    weights = (shard, near, far, first, second, deep1, near1, far1, line1, near2, far2, line2, first1, second1)
    pieces = ((0,), (1,), (2,), (3, 4), (5,), (6,), (7,), (8,), (9,), (10,), (11,), (12, 13))
    acc = accumulate(rows, weights, pieces, (), main, edge, (), jnp.float32, "accumulate_most")
    near3, far3, line3, *acc = together(near3, far3, line3, *acc)
    first2, second2, first3, second3, corner = slot(
        (flip_near, far2[:cut]),
        (flip_far, near2[cut:]),
        (flip_near, far3[:cut]),
        (flip_far, near3[cut:]),
        (next_plane, line3[9 * edge :]),
    )
    weights = (near3, far3, shard, near, far, second, line1, line2, line3)
    edges = ((2, width), (3, width), (4, width), (5, low), (6, width), (7, width), (8, 0))
    acc = accumulate(
        rows, weights, ((0,), (1,)), edges, main, edge, tuple(acc), jnp.float32, "accumulate_edges"
    )
    weights = (first2, second2, first3, second3, corner)
    pieces = ((0, 1), (2, 3))
    edges = ((4, 0),)
    (given,) = accumulate(
        rows[1:], weights, pieces, edges, main, edge, acc[1:], jnp.bfloat16, "finish_other"
    )
    (kept,) = accumulate(
        rows[:1], weights, pieces, edges, main, edge, acc[:1], jnp.float32, "finish_own"
    )
    ffn_out = kept + flip_core(given).astype(jnp.float32)
    result = ((mixed_rows.astype(jnp.float32) + ffn_out) * valid_mask[:, None]).astype(jnp.bfloat16)
    return (result[None], end_state[None, None], end_norm[None, None])


def solution(mesh):
    return jax.shard_map(
        local,
        mesh=mesh,
        in_specs=(
            P("req", "seq", None),
            P("req"),
            P("req", "seq", None),
            P(),
            P(),
            P(),
            P(),
            P(),
            P(),
            P(),
            P(None, "req"),
            P(None, "req"),
            P(None, "req"),
        ),
        out_specs=(P("req", "seq", None), P("req", "seq", None, None), P("req", "seq", None, None)),
        check_vma=False,
    )
```

```python
import functools

import jax
import jax.numpy as jnp
from jax import lax
from jax.experimental import pallas as pl
from jax.experimental.pallas import tpu as pltpu
from jax.sharding import PartitionSpec as P


def from_behind(array, axis, by):
    count = lax.axis_size(axis)
    pairs = [(i, i + by) for i in range(count) if 0 <= i + by < count]
    return lax.ppermute(array, axis, pairs)


def entering(array, axis, combine, identity):
    count, here = (lax.axis_size(axis), lax.axis_index(axis))
    everything = jax.tree.map(
        lambda part, kind: lax.all_gather(part.astype(kind), axis),
        array,
        (jnp.bfloat16, jnp.bfloat16, jnp.bfloat16),
    )
    start = jax.tree.map(
        lambda part, zero: jnp.broadcast_to(jnp.asarray(zero, part.dtype), part.shape),
        array,
        identity,
    )

    def hop(k, before):
        reached = k < here
        new = combine(
            before, jax.tree.map(lambda part, own: part[k].astype(own.dtype), everything, array)
        )
        return jax.tree.map(lambda a, b: jnp.where(reached, a, b), new, before)

    return lax.fori_loop(0, count, hop, start)


def features(vectors):
    constant = jnp.ones(vectors.shape[:-1] + (1,), jnp.float32)
    width = vectors.shape[-1]
    squares = (vectors[..., :, None] * vectors[..., None, :]).reshape(
        vectors.shape[:-1] + (width * width,)
    )
    return jnp.concatenate([constant, vectors, squares * 0.5**0.5], axis=-1)


def carry_in(valid_mask, decays, queries, numerator, denominator, flat_memory, key_sum):
    local_len = numerator.shape[0]
    feat_len, head_count = key_sum.shape
    value_len = flat_memory.shape[1] // head_count
    feat_in = queries.shape[1] // head_count
    decay_rate = jnp.where(valid_mask[:, None] > 0, decays, 0.0)
    span_decay = jnp.sum(decay_rate, axis=0)

    def merge_states(earlier, later):
        factor = jnp.exp(later[0])
        return (
            earlier[0] + later[0],
            earlier[1] * jnp.repeat(factor, value_len)[None, :] + later[1],
            earlier[2] * factor[None, :] + later[2],
        )

    neutral = (jnp.zeros_like(span_decay), jnp.zeros_like(flat_memory), jnp.zeros_like(key_sum))
    carried = entering((span_decay, flat_memory, key_sum), "seq", merge_states, neutral)
    prior_memory = carried[1]
    prior_keys = carried[2]
    highest = lax.Precision.HIGHEST
    growth = jnp.exp(jnp.cumsum(decay_rate, axis=0))
    query_feat = features(queries.astype(jnp.float32).reshape(local_len, head_count, feat_in))
    added = jnp.einsum(
        "thf,fhv->thv",
        query_feat,
        prior_memory.reshape(feat_len, head_count, value_len),
        precision=highest,
    )
    numerator = numerator + (added * growth[:, :, None]).reshape(local_len, -1)
    denominator = (
        denominator + jnp.einsum("thf,fh->th", query_feat, prior_keys, precision=highest) * growth
    )
    span_factor = jnp.exp(span_decay)
    end_state = prior_memory * jnp.repeat(span_factor, value_len)[None, :] + flat_memory
    end_norm = prior_keys * span_factor[None, :] + key_sum
    return numerator, denominator, end_state, end_norm


def permute(array, target):
    count = lax.axis_size("req")
    return lax.ppermute(array, "req", [(i, target(i)) for i in range(count)])


def flip_core(array):
    return permute(array, lambda i: i ^ 1)


def flip_near(array):
    return permute(array, lambda i: i ^ 2)


def flip_far(array):
    return permute(array, lambda i: i ^ 4)


def next_plane(array):
    count = lax.axis_size("req")
    return permute(array, lambda i: (i + 8) % count)


def together(*arrays):
    return lax.optimization_barrier(arrays)


def slot(*sends):
    operands = together(*[array for _, array in sends])
    return together(*[send(array) for (send, _), array in zip(sends, operands)])


def vmem(count):
    return [pl.BlockSpec(memory_space=pltpu.VMEM)] * count


def kernel_call(body, name, out_shape, *operands, scratch=(), aliases=None, specs=None, mib=24):
    many = isinstance(out_shape, tuple)
    return pl.pallas_call(
        body,
        out_shape=out_shape,
        in_specs=specs or vmem(len(operands)),
        out_specs=tuple(vmem(len(out_shape))) if many else vmem(1)[0],
        scratch_shapes=list(scratch),
        input_output_aliases=aliases or {},
        compiler_params=pltpu.CompilerParams(vmem_limit_bytes=mib * 1024 * 1024),
        cost_estimate=pl.CostEstimate(flops=1000, bytes_accessed=1000, transcendentals=0),
        name=name,
    )(*operands)


def like(rows, columns, dtype):
    return jax.ShapeDtypeStruct((rows, columns), dtype)


NT = (((1,), (1,)), ((), ()))


def unit_rows(rows, gain):
    factor = lax.rsqrt(jnp.mean(rows * rows, axis=-1, keepdims=True) + 1e-05)
    return (rows * factor * gain).astype(jnp.bfloat16).astype(jnp.float32)


def project_body(
    step,
    scale,
    rows_ref,
    edge_ref,
    gain_ref,
    conv_ref,
    query_ref,
    key_ref,
    value_ref,
    queries_ref,
    keys_ref,
    values_ref,
    normed,
    gated,
):
    gain = gain_ref[...]
    count = rows_ref.shape[0]
    lead = edge_ref.shape[0]
    taps = conv_ref.shape[0]
    normed[:lead] = unit_rows(edge_ref[...].astype(jnp.float32), gain)

    @pl.loop(0, count // step)
    def _(block):
        at = pl.multiple_of(block * step, step)
        rows = rows_ref[pl.ds(at, step), :].astype(jnp.float32)
        normed[pl.ds(lead + at, step), :] = unit_rows(rows, gain)

    @pl.loop(0, count // step)
    def _(block):
        at = pl.multiple_of(block * step, step)
        window = normed[pl.ds(at, step + lead), :]
        here = window[lead:]
        total = conv_ref[0:1] * here
        for tap in range(1, taps):
            total = total + conv_ref[tap : tap + 1] * window[lead - tap : lead - tap + step]
        gated[pl.ds(at, step), :] = (total * jax.nn.sigmoid(here)).astype(jnp.bfloat16)

    rows = gated[...]
    for weight_ref, out_ref, factor in (
        (query_ref, queries_ref, scale),
        (key_ref, keys_ref, scale),
        (value_ref, values_ref, None),
    ):
        product = jnp.dot(rows, weight_ref[...], preferred_element_type=jnp.float32)
        if factor is not None:
            product = product * factor
        out_ref[...] = product.astype(jnp.bfloat16)


def project(rows, edge, mix_gain, conv_weight, query_weight, key_weight, value_weight, scale):
    count, width = rows.shape
    step = 32
    return kernel_call(
        functools.partial(project_body, step, scale),
        "project",
        tuple(like(count, w.shape[1], jnp.bfloat16) for w in (query_weight, key_weight, value_weight)),
        rows,
        edge,
        mix_gain[None],
        conv_weight,
        query_weight,
        key_weight,
        value_weight,
        scratch=(
            pltpu.VMEM((count + edge.shape[0], width), jnp.float32),
            pltpu.VMEM((count, width), jnp.bfloat16),
        ),
    )


def attend_body(
    feat_in,
    value_len,
    count_ref,
    rate_ref,
    queries_ref,
    keys_ref,
    values_ref,
    numer_ref,
    denom_ref,
    state_ref,
    norm_ref,
    turned,
    total,
    norms,
):
    heads, count = rate_ref.shape
    columns = values_ref.shape[1]
    lane = lax.broadcasted_iota(jnp.int32, (count, count), 1)
    row = lax.broadcasted_iota(jnp.int32, (count, count), 0)
    valid = (lane[:1] < count_ref[0]).astype(jnp.float32)
    rate = jnp.where(valid > 0, rate_ref[...], 0.0)
    upto = (row <= lane).astype(jnp.float32)
    across = jnp.dot(
        rate, upto, precision=lax.Precision.HIGHEST, preferred_element_type=jnp.float32
    )
    down = across.T
    closing = across[:, count - 1 : count]
    fading = jnp.exp(closing - across) * valid
    causal = row >= lane
    keys = keys_ref[...]
    turned[...] = keys.astype(jnp.float32).T
    owner = lax.broadcasted_iota(jnp.int32, queries_ref.shape, 1)
    spare = lax.broadcasted_iota(jnp.int32, (8, count), 0) == 0
    head_lane = lax.broadcasted_iota(jnp.int32, (count, 128), 1)
    numer_ref[...] = jnp.zeros(numer_ref.shape, jnp.float32)
    total[...] = jnp.zeros(total.shape, jnp.float32)
    norm_total = jnp.zeros(norms.shape, jnp.float32)
    denominators = jnp.zeros((count, 128), jnp.float32)
    for h in range(heads):
        low = min(h * value_len // 128 * 128, max(columns - 256, 0))
        high = min(low + 256, columns)
        mine = lax.broadcasted_iota(jnp.int32, (count, high - low), 1) + low
        mine = (mine >= h * value_len) & (mine < (h + 1) * value_len)
        values = jnp.where(mine, values_ref[:, low:high].astype(jnp.float32), 0.0)
        values = values.astype(jnp.bfloat16)
        asks = (owner >= h * feat_in) & (owner < (h + 1) * feat_in)
        queries = jnp.where(asks, queries_ref[...].astype(jnp.float32), 0.0)
        scores = lax.dot_general(
            queries.astype(jnp.bfloat16), keys, NT, preferred_element_type=jnp.float32
        )
        gap = down[:, h : h + 1] - across[h : h + 1]
        weights = jnp.where(causal, jnp.exp(jnp.minimum(gap, 0.0)) * valid, 0.0)
        weights = weights * (1.0 + scores + 0.5 * scores * scores)
        numer_ref[:, low:high] += jnp.dot(
            weights.astype(jnp.bfloat16), values, preferred_element_type=jnp.float32
        )
        sums = jnp.sum(weights, axis=1, keepdims=True)
        denominators = jnp.where(head_lane == h, sums, denominators)
        own = turned[h * feat_in : (h + 1) * feat_in]
        fade = fading[h : h + 1]
        faded = own * fade
        scaled = faded * 0.5**0.5
        parts = [own[i : i + 1] * scaled for i in range(feat_in)]
        parts += [faded, jnp.where(spare, fade, 0.0)]
        feats = jnp.concatenate(parts, axis=0).astype(jnp.bfloat16)
        total[:, low:high] += jnp.dot(feats, values, preferred_element_type=jnp.float32)
        mark = (head_lane == h).astype(jnp.bfloat16)
        norm_total = norm_total + jnp.dot(feats, mark, preferred_element_type=jnp.float32)
    denom_ref[...] = denominators[:, :heads]
    norms[...] = norm_total
    pairs = feat_in * feat_in
    for out_ref, source, width in ((state_ref, total, columns), (norm_ref, norms, heads)):
        out_ref[0:1, :] = source[pairs + feat_in : pairs + feat_in + 1, :width]
        out_ref[1 : 1 + feat_in, :] = source[pairs : pairs + feat_in, :width]
        out_ref[1 + feat_in :, :] = source[:pairs, :width]


def attend(valid_count, rate, queries, keys, values, feat_in, value_len):
    heads, count = rate.shape
    columns = values.shape[1]
    feat_len = 1 + feat_in + feat_in * feat_in
    padded = feat_in * feat_in + feat_in + 8
    return kernel_call(
        functools.partial(attend_body, feat_in, value_len),
        "attend",
        (
            like(count, columns, jnp.float32),
            like(count, heads, jnp.float32),
            like(feat_len, columns, jnp.float32),
            like(feat_len, heads, jnp.float32),
        ),
        valid_count,
        rate,
        queries,
        keys,
        values,
        specs=[pl.BlockSpec(memory_space=pltpu.SMEM)] + vmem(4),
        scratch=(
            pltpu.VMEM((queries.shape[1], count), jnp.float32),
            pltpu.VMEM((padded, columns), jnp.float32),
            pltpu.VMEM((padded, 128), jnp.float32),
        ),
    )


def mix_body(
    value_len, step, numer_ref, denom_ref, rows_ref, out_ref, gain_ref, mixed_ref, mlp_ref, sums
):
    count, columns = numer_ref.shape
    heads = denom_ref.shape[1]
    column = lax.broadcasted_iota(jnp.int32, (1, columns), 1)
    inverse = 1.0 / denom_ref[...]
    spread = jnp.zeros((count, columns), jnp.float32)
    for h in range(heads):
        here = (column >= h * value_len) & (column < (h + 1) * value_len)
        spread = jnp.where(here, inverse[:, h : h + 1], spread)
    attended = (numer_ref[...] * spread).astype(jnp.bfloat16)
    sums[...] = jnp.dot(attended, out_ref[...], preferred_element_type=jnp.float32)
    gain = gain_ref[...]

    @pl.loop(0, count // step)
    def _(block):
        at = pl.ds(pl.multiple_of(block * step, step), step)
        mixed = (rows_ref[at, :].astype(jnp.float32) + sums[at, :]).astype(jnp.bfloat16)
        mixed_ref[at, :] = mixed
        mlp_ref[at, :] = unit_rows(mixed.astype(jnp.float32), gain).astype(jnp.bfloat16)


def mix(numer, denom, rows, out_weight, mlp_gain, value_len):
    count, width = rows.shape
    shape = like(count, width, jnp.bfloat16)
    return kernel_call(
        functools.partial(mix_body, value_len, 32),
        "mix",
        (shape, shape),
        numer,
        denom,
        rows,
        out_weight,
        mlp_gain[None],
        scratch=(pltpu.VMEM((count, width), jnp.float32),),
    )


def swiglu_terms(rows, gate_rows, up_rows, down_rows):
    gate_act = lax.dot_general(rows, gate_rows, NT, preferred_element_type=jnp.float32)
    up_act = lax.dot_general(rows, up_rows, NT, preferred_element_type=jnp.float32)
    hidden_units = (gate_act * jax.nn.sigmoid(gate_act) * up_act).astype(jnp.bfloat16)
    return jnp.dot(hidden_units, down_rows, preferred_element_type=jnp.float32)


def on_grid(run):
    return all(low % 16 == 0 and high % 16 == 0 for _, low, high in run)


def read_units(refs, units):
    parts = []
    for k in range(3):
        rows = [refs[run[k][0]][run[k][1] : run[k][2]] for run in units if on_grid(run)]
        rest = [
            refs[run[k][0]][...].astype(jnp.float32)[run[k][1] : run[k][2]]
            for run in units
            if not on_grid(run)
        ]
        if rest:
            rows.append(jnp.concatenate(rest, axis=0).astype(jnp.bfloat16))
        parts.append(jnp.concatenate(rows, axis=0))
    return parts


def accumulate_body(units, n_weights, n_rows, n_acc, residual, *refs):
    weights = refs[:n_weights]
    rows = refs[n_weights : n_weights + n_rows]
    acc = refs[n_weights + n_rows : n_weights + n_rows + n_acc]
    parts = read_units(weights, units)
    for k, rows_ref in enumerate(rows):
        out_ref = refs[len(refs) - n_rows + k]
        terms = swiglu_terms(rows_ref[...], *parts)
        if n_acc:
            terms = terms + acc[k][...]
        if residual:
            terms = terms + refs[n_weights + n_rows + n_acc][...].astype(jnp.float32)
        out_ref[...] = terms.astype(out_ref.dtype)


def accumulate(rows, weights, units, acc, dtype, name, residual=None):
    shapes = tuple(like(*array.shape, dtype) for array in rows)
    start = len(weights) + len(rows)
    aliases = {start + k: k for k in range(len(acc))} if dtype == jnp.float32 else {}
    extra = () if residual is None else (residual,)
    body = functools.partial(
        accumulate_body, tuple(units), len(weights), len(rows), len(acc), bool(extra)
    )
    return kernel_call(body, name, shapes, *weights, *rows, *acc, *extra, aliases=aliases)


def runs(which, low, size):
    return tuple((which, low + k * size, low + (k + 1) * size) for k in range(3))


def split_runs(first, second, main):
    (i, at), (j, then) = first, second
    held = 2 * main // 3
    rest = main - held
    return (
        ((i, at, at + held), (i, at + main, at + main + held), (j, then + rest, then + main)),
        ((i, at + held, at + main), (j, then, then + rest), (j, then + main, then + rest + main)),
    )


def collect_body(plans, *refs):
    outs = refs[len(refs) - len(plans) :]
    for out_ref, plan in zip(outs, plans):
        rows = [refs[i][...].astype(jnp.float32)[low:high] for i, low, high in plan]
        out_ref[...] = jnp.concatenate(rows, axis=0).astype(jnp.bfloat16)


def collect(arrays, plans, name):
    columns = arrays[0].shape[1]
    shapes = tuple(like(sum(h - l for _, l, h in plan), columns, jnp.bfloat16) for plan in plans)
    return kernel_call(functools.partial(collect_body, plans), name, shapes, *arrays)


def shard_body(main, gate_ref, up_ref, down_ref, shard_ref, main_ref, *rest):
    buffers, sems = rest[:3], rest[3]
    copies = [
        pltpu.make_async_copy(source, buffer, sems.at[k])
        for k, (source, buffer) in enumerate(zip((gate_ref, up_ref, down_ref), buffers))
    ]
    for copy in copies:
        copy.start()
    for copy in copies:
        copy.wait()
    arrays = [buffer[...].astype(jnp.float32) for buffer in buffers]
    tops = [array[:main] for array in arrays]
    ends = [array[main:] for array in arrays]
    shard_ref[...] = jnp.concatenate(tops + ends, axis=0).astype(jnp.bfloat16)
    main_ref[...] = jnp.concatenate(tops, axis=0).astype(jnp.bfloat16)


def final_body(step, count_ref, kept_ref, given_ref, out_ref):
    count = kept_ref.shape[0]

    @pl.loop(0, count // step)
    def _(block):
        first = pl.multiple_of(block * step, step)
        at = pl.ds(first, step)
        total = kept_ref[at, :] + given_ref[at, :].astype(jnp.float32)
        row = lax.broadcasted_iota(jnp.int32, total.shape, 0) + first
        out_ref[at, :] = jnp.where(row < count_ref[0], total, 0.0).astype(out_ref.dtype)


def local(
    hidden_in,
    lengths,
    log_decay,
    mix_gain,
    conv_weight,
    query_weight,
    key_weight,
    value_weight,
    out_weight,
    mlp_gain,
    gate_weight,
    up_weight,
    down_weight,
):
    local_len = hidden_in.shape[1]
    rows_in = hidden_in[0]
    decays = log_decay[0]
    head_count = log_decay.shape[2]
    value_len = value_weight.shape[1] // head_count
    feat_in = query_weight.shape[1] // head_count
    feature_scale = feat_in ** (-0.25)
    valid_count = lengths - lax.axis_index("seq") * local_len
    spans = lax.axis_size("seq")
    units, model = gate_weight.shape[1], gate_weight.shape[0]
    edge = units // 7
    main = units - edge
    wide = 3 * main
    full = 3 * units
    narrow = full - wide
    cut = main + 2 * main // 3

    shard, shard_main = kernel_call(
        functools.partial(shard_body, main),
        "shard",
        (like(full, model, jnp.bfloat16), like(wide, model, jnp.bfloat16)),
        gate_weight.T,
        up_weight.T,
        down_weight.T,
        specs=[pl.BlockSpec(memory_space=pl.ANY)] * 3,
        scratch=[pltpu.VMEM((units, model), jnp.bfloat16)] * 3 + [pltpu.SemaphoreType.DMA((3,))],
        mib=56,
    )
    near, far, deep = slot((flip_near, shard), (flip_far, shard), (next_plane, shard_main))

    lead = 16
    if spans > 1:
        edge_in = from_behind(rows_in[local_len - lead :], "seq", 1)
    else:
        edge_in = jnp.zeros((lead, model), jnp.bfloat16)
    queries, key_rows, values = project(
        rows_in, edge_in, mix_gain, conv_weight, query_weight, key_weight, value_weight, feature_scale
    )
    near, far, deep, queries, key_rows, values = together(
        near, far, deep, queries, key_rows, values
    )

    sends = collect(
        (shard, near, far, deep),
        (
            ((3, 0, wide), (2, 0, cut)),
            ((3, 0, wide), (1, cut, full)),
            ((3, 0, wide), (0, wide, full), (1, wide, full), (2, wide, full)),
        ),
        "collect_second",
    )
    near1, far1, deep1 = slot(*zip((flip_near, flip_far, next_plane), sends))

    numerator, denominator, end_state, end_norm = attend(
        valid_count, log_decay[0].T, queries, key_rows, values, feat_in, value_len
    )
    if spans > 1:
        positions = jnp.arange(local_len, dtype=jnp.int32)
        numerator, denominator, end_state, end_norm = carry_in(
            (positions < valid_count).astype(jnp.float32),
            decays,
            queries,
            numerator,
            denominator,
            end_state,
            end_norm,
        )
    mixed_rows, mlp_in = mix(numerator, denominator, rows_in, out_weight, mlp_gain, value_len)
    near1, far1, deep1, mixed_rows, mlp_in, end_state, end_norm = together(
        near1, far1, deep1, mixed_rows, mlp_in, end_state[None, None], end_norm[None, None]
    )

    sends = collect(
        (near1, far1, deep1),
        (
            ((2, 0, wide), (1, 0, cut)),
            ((2, 0, wide), (0, cut, wide)),
            ((2, 0, wide + 3 * narrow), (1, wide + wide - cut, wide + full - cut)),
        ),
        "collect_third",
    )
    near2, far2, deep2 = slot(*zip((flip_near, flip_far, next_plane), sends))
    rows = (mlp_in, flip_core(mlp_in))
    acc = accumulate(
        rows,
        (shard, near, far, deep, near1, far1, deep1),
        [runs(i, 0, main) for i in range(7)] + list(split_runs((4, wide), (5, wide), main)),
        (),
        jnp.float32,
        "accumulate_second",
    )
    near2, far2, deep2, *acc = together(near2, far2, deep2, *acc)

    deep3_main, line = collect(
        (far2, deep2),
        (
            ((1, 0, wide),),
            ((1, wide, wide + 4 * narrow), (0, wide + wide - cut - main, wide + wide - cut)),
        ),
        "collect_fourth",
    )
    near3, far3, deep3 = slot((flip_near, deep3_main), (flip_far, deep3_main), (next_plane, line))
    acc = accumulate(
        rows,
        (shard, near, far, far1, deep1, near2, far2, deep2),
        [runs(i, 0, main) for i in (5, 6, 7)]
        + list(split_runs((5, wide), (6, wide), main))
        + [runs(i, wide, edge) for i in (0, 1, 2)]
        + [runs(3, wide + wide - cut, edge)]
        + [runs(4, wide + k * narrow, edge) for k in range(3)]
        + [runs(7, wide + k * narrow, edge) for k in range(4)],
        tuple(acc),
        jnp.float32,
        "accumulate_third",
    )
    near3, far3, deep3, *acc = together(near3, far3, deep3, *acc)

    sends = collect(
        (near2, far2, near3, far3, deep3),
        (
            ((1, 0, main), (3, 0, main)),
            ((0, main, 2 * main), (2, main, 2 * main)),
            ((4, 3 * narrow, 4 * narrow + main),),
        ),
        "collect_fifth",
    )
    near4, far4, deep4 = slot(*zip((flip_near, flip_far, next_plane), sends))
    acc = accumulate(
        rows,
        (near3, far3, deep3),
        [runs(0, 0, main), runs(1, 0, main)] + [runs(2, k * narrow, edge) for k in range(4)],
        tuple(acc),
        jnp.float32,
        "accumulate_fourth",
    )
    weights = (near4, far4, deep3, deep4)
    last = [
        ((0, 0, main), (1, 0, main), (2, 4 * narrow, 4 * narrow + main)),
        ((0, main, 2 * main), (1, main, 2 * main), (3, narrow, narrow + main)),
        runs(3, 0, edge),
    ]
    (given,) = accumulate(rows[1:], weights, last, acc[1:], jnp.bfloat16, "finish_other")
    (kept,) = accumulate(
        rows[:1], weights, last, acc[:1], jnp.float32, "finish_own", residual=mixed_rows
    )
    result = kernel_call(
        functools.partial(final_body, 64),
        "final",
        like(local_len, model, jnp.bfloat16),
        valid_count,
        kept,
        flip_core(given),
        specs=[pl.BlockSpec(memory_space=pltpu.SMEM)] + vmem(2),
    )
    return (result[None], end_state, end_norm)


def solution(mesh):
    return jax.shard_map(
        local,
        mesh=mesh,
        in_specs=(
            P("req", "seq", None),
            P("req"),
            P("req", "seq", None),
            P(),
            P(),
            P(),
            P(),
            P(),
            P(),
            P(),
            P(None, "req"),
            P(None, "req"),
            P(None, "req"),
        ),
        out_specs=(P("req", "seq", None), P("req", "seq", None, None), P("req", "seq", None, None)),
        check_vma=False,
    )
```

```python
import functools

import jax
import jax.numpy as jnp
from jax import lax
from jax.experimental import pallas as pl
from jax.experimental.pallas import tpu as pltpu
from jax.sharding import PartitionSpec as P


def from_behind(array, axis, by):
    count = lax.axis_size(axis)
    pairs = [(i, i + by) for i in range(count) if 0 <= i + by < count]
    return lax.ppermute(array, axis, pairs)


def entering(array, axis, combine, identity):
    count, here = (lax.axis_size(axis), lax.axis_index(axis))
    everything = jax.tree.map(
        lambda part, kind: lax.all_gather(part.astype(kind), axis),
        array,
        (jnp.bfloat16, jnp.bfloat16, jnp.bfloat16),
    )
    start = jax.tree.map(
        lambda part, zero: jnp.broadcast_to(jnp.asarray(zero, part.dtype), part.shape),
        array,
        identity,
    )

    def hop(k, before):
        reached = k < here
        new = combine(
            before, jax.tree.map(lambda part, own: part[k].astype(own.dtype), everything, array)
        )
        return jax.tree.map(lambda a, b: jnp.where(reached, a, b), new, before)

    return lax.fori_loop(0, count, hop, start)


def features(vectors):
    constant = jnp.ones(vectors.shape[:-1] + (1,), jnp.float32)
    width = vectors.shape[-1]
    squares = (vectors[..., :, None] * vectors[..., None, :]).reshape(
        vectors.shape[:-1] + (width * width,)
    )
    return jnp.concatenate([constant, vectors, squares * 0.5**0.5], axis=-1)


def carry_in(valid_mask, decays, queries, numerator, denominator, flat_memory, key_sum):
    local_len = numerator.shape[0]
    feat_len, head_count = key_sum.shape
    value_len = flat_memory.shape[1] // head_count
    feat_in = queries.shape[1] // head_count
    decay_rate = jnp.where(valid_mask[:, None] > 0, decays, 0.0)
    span_decay = jnp.sum(decay_rate, axis=0)

    def merge_states(earlier, later):
        factor = jnp.exp(later[0])
        return (
            earlier[0] + later[0],
            earlier[1] * jnp.repeat(factor, value_len)[None, :] + later[1],
            earlier[2] * factor[None, :] + later[2],
        )

    neutral = (jnp.zeros_like(span_decay), jnp.zeros_like(flat_memory), jnp.zeros_like(key_sum))
    carried = entering((span_decay, flat_memory, key_sum), "seq", merge_states, neutral)
    prior_memory = carried[1]
    prior_keys = carried[2]
    highest = lax.Precision.HIGHEST
    growth = jnp.exp(jnp.cumsum(decay_rate, axis=0))
    query_feat = features(queries.astype(jnp.float32).reshape(local_len, head_count, feat_in))
    added = jnp.einsum(
        "thf,fhv->thv",
        query_feat,
        prior_memory.reshape(feat_len, head_count, value_len),
        precision=highest,
    )
    numerator = numerator + (added * growth[:, :, None]).reshape(local_len, -1)
    denominator = (
        denominator + jnp.einsum("thf,fh->th", query_feat, prior_keys, precision=highest) * growth
    )
    span_factor = jnp.exp(span_decay)
    end_state = prior_memory * jnp.repeat(span_factor, value_len)[None, :] + flat_memory
    end_norm = prior_keys * span_factor[None, :] + key_sum
    return numerator, denominator, end_state, end_norm


def permute(array, target):
    count = lax.axis_size("req")
    return lax.ppermute(array, "req", [(i, target(i)) for i in range(count)])


def flip_core(array):
    return permute(array, lambda i: i ^ 1)


def flip_near(array):
    return permute(array, lambda i: i ^ 2)


def flip_far(array):
    return permute(array, lambda i: i ^ 4)


def next_plane(array):
    count = lax.axis_size("req")
    return permute(array, lambda i: (i + 8) % count)


def together(*arrays):
    return lax.optimization_barrier(arrays)


def slot(*sends):
    operands = together(*[array for _, array in sends])
    return together(*[send(array) for (send, _), array in zip(sends, operands)])


def vmem(count):
    return [pl.BlockSpec(memory_space=pltpu.VMEM)] * count


def kernel_call(body, name, out_shape, *operands, scratch=(), aliases=None, specs=None, mib=24):
    many = isinstance(out_shape, tuple)
    return pl.pallas_call(
        body,
        out_shape=out_shape,
        in_specs=specs or vmem(len(operands)),
        out_specs=tuple(vmem(len(out_shape))) if many else vmem(1)[0],
        scratch_shapes=list(scratch),
        input_output_aliases=aliases or {},
        compiler_params=pltpu.CompilerParams(vmem_limit_bytes=mib * 1024 * 1024),
        cost_estimate=pl.CostEstimate(flops=1000, bytes_accessed=1000, transcendentals=0),
        name=name,
    )(*operands)


def like(rows, columns, dtype):
    return jax.ShapeDtypeStruct((rows, columns), dtype)


NT = (((1,), (1,)), ((), ()))


def unit_rows(rows, gain):
    factor = lax.rsqrt(jnp.mean(rows * rows, axis=-1, keepdims=True) + 1e-05)
    return (rows * factor * gain).astype(jnp.bfloat16).astype(jnp.float32)


def project_body(
    step,
    scale,
    rows_ref,
    edge_ref,
    gain_ref,
    conv_ref,
    query_ref,
    key_ref,
    value_ref,
    queries_ref,
    keys_ref,
    values_ref,
    normed,
    gated,
):
    gain = gain_ref[...]
    count = rows_ref.shape[0]
    lead = edge_ref.shape[0]
    taps = conv_ref.shape[0]
    normed[:lead] = unit_rows(edge_ref[...].astype(jnp.float32), gain)

    @pl.loop(0, count // step)
    def _(block):
        at = pl.multiple_of(block * step, step)
        rows = rows_ref[pl.ds(at, step), :].astype(jnp.float32)
        normed[pl.ds(lead + at, step), :] = unit_rows(rows, gain)

    @pl.loop(0, count // step)
    def _(block):
        at = pl.multiple_of(block * step, step)
        window = normed[pl.ds(at, step + lead), :]
        here = window[lead:]
        total = conv_ref[0:1] * here
        for tap in range(1, taps):
            total = total + conv_ref[tap : tap + 1] * window[lead - tap : lead - tap + step]
        gated[pl.ds(at, step), :] = (total * jax.nn.sigmoid(here)).astype(jnp.bfloat16)

    rows = gated[...]
    for weight_ref, out_ref, factor in (
        (query_ref, queries_ref, scale),
        (key_ref, keys_ref, scale),
        (value_ref, values_ref, None),
    ):
        product = jnp.dot(rows, weight_ref[...], preferred_element_type=jnp.float32)
        if factor is not None:
            product = product * factor
        out_ref[...] = product.astype(jnp.bfloat16)


def project(rows, edge, mix_gain, conv_weight, query_weight, key_weight, value_weight, scale):
    count, width = rows.shape
    step = 32
    return kernel_call(
        functools.partial(project_body, step, scale),
        "project",
        tuple(like(count, w.shape[1], jnp.bfloat16) for w in (query_weight, key_weight, value_weight)),
        rows,
        edge,
        mix_gain[None],
        conv_weight,
        query_weight,
        key_weight,
        value_weight,
        scratch=(
            pltpu.VMEM((count + edge.shape[0], width), jnp.float32),
            pltpu.VMEM((count, width), jnp.bfloat16),
        ),
    )


def attend_body(
    feat_in,
    value_len,
    count_ref,
    rate_ref,
    queries_ref,
    keys_ref,
    values_ref,
    numer_ref,
    denom_ref,
    state_ref,
    norm_ref,
    turned,
    total,
    norms,
):
    heads, count = rate_ref.shape
    columns = values_ref.shape[1]
    lane = lax.broadcasted_iota(jnp.int32, (count, count), 1)
    row = lax.broadcasted_iota(jnp.int32, (count, count), 0)
    valid = (lane[:1] < count_ref[0]).astype(jnp.float32)
    rate = jnp.where(valid > 0, rate_ref[...], 0.0)
    upto = (row <= lane).astype(jnp.float32)
    across = jnp.dot(
        rate, upto, precision=lax.Precision.HIGHEST, preferred_element_type=jnp.float32
    )
    down = across.T
    closing = across[:, count - 1 : count]
    fading = jnp.exp(closing - across) * valid
    causal = row >= lane
    keys = keys_ref[...]
    turned[...] = keys.astype(jnp.float32).T
    owner = lax.broadcasted_iota(jnp.int32, queries_ref.shape, 1)
    spare = lax.broadcasted_iota(jnp.int32, (8, count), 0) == 0
    head_lane = lax.broadcasted_iota(jnp.int32, (count, 128), 1)
    numer_ref[...] = jnp.zeros(numer_ref.shape, jnp.float32)
    total[...] = jnp.zeros(total.shape, jnp.float32)
    norms[...] = jnp.zeros(norms.shape, jnp.float32)
    norm_total = jnp.zeros((total.shape[0], 128), jnp.float32)
    denominators = jnp.zeros((count, 128), jnp.float32)
    for h in range(heads):
        low = min(h * value_len // 128 * 128, max(columns - 256, 0))
        high = min(low + 256, columns)
        mine = lax.broadcasted_iota(jnp.int32, (count, high - low), 1) + low
        mine = (mine >= h * value_len) & (mine < (h + 1) * value_len)
        values = jnp.where(mine, values_ref[:, low:high].astype(jnp.float32), 0.0)
        values = values.astype(jnp.bfloat16)
        asks = (owner >= h * feat_in) & (owner < (h + 1) * feat_in)
        queries = jnp.where(asks, queries_ref[...].astype(jnp.float32), 0.0)
        scores = lax.dot_general(
            queries.astype(jnp.bfloat16), keys, NT, preferred_element_type=jnp.float32
        )
        gap = down[:, h : h + 1] - across[h : h + 1]
        weights = jnp.where(causal, jnp.exp(jnp.minimum(gap, 0.0)) * valid, 0.0)
        weights = weights * (1.0 + scores + 0.5 * scores * scores)
        numer_ref[:, low:high] += jnp.dot(
            weights.astype(jnp.bfloat16), values, preferred_element_type=jnp.float32
        )
        sums = jnp.sum(weights, axis=1, keepdims=True)
        denominators = jnp.where(head_lane == h, sums, denominators)
        own = turned[h * feat_in : (h + 1) * feat_in]
        fade = fading[h : h + 1]
        faded = own * fade
        scaled = faded * 0.5**0.5
        parts = [own[i : i + 1] * scaled for i in range(feat_in)]
        parts += [faded, jnp.where(spare, fade, 0.0)]
        feats = jnp.concatenate(parts, axis=0).astype(jnp.bfloat16)
        total[:, low:high] += jnp.dot(feats, values, preferred_element_type=jnp.float32)
        mark = (head_lane == h).astype(jnp.bfloat16)
        norm_total = norm_total + jnp.dot(feats, mark, preferred_element_type=jnp.float32)
    denom_ref[...] = denominators[:, :heads]
    pairs = feat_in * feat_in
    state_ref[0] = total[pairs + feat_in : pairs + feat_in + 1, :]
    for f in range(feat_in):
        state_ref[1 + f] = total[pairs + f : pairs + f + 1, :]

    @pl.loop(0, pairs // 8)
    def _(block):
        for k in range(8):
            f = block * 8 + k
            state_ref[1 + feat_in + f] = total[pl.ds(f, 1), :]

    norms[0:1, :] = norm_total[pairs + feat_in : pairs + feat_in + 1]
    norms[1 : 1 + feat_in, :] = norm_total[pairs : pairs + feat_in]
    norms[1 + feat_in : 1 + feat_in + pairs, :] = norm_total[:pairs]
    norm_ref[...] = norms[...].T[:heads, : 1 + feat_in + pairs]


def attend(valid_count, rate, queries, keys, values, feat_in, value_len):
    heads, count = rate.shape
    columns = values.shape[1]
    feat_len = 1 + feat_in + feat_in * feat_in
    padded = feat_in * feat_in + feat_in + 8
    return kernel_call(
        functools.partial(attend_body, feat_in, value_len),
        "attend",
        (
            like(count, columns, jnp.float32),
            like(count, heads, jnp.float32),
            jax.ShapeDtypeStruct((feat_len, 1, columns), jnp.float32),
            like(heads, feat_len, jnp.float32),
        ),
        valid_count,
        rate,
        queries,
        keys,
        values,
        specs=[pl.BlockSpec(memory_space=pltpu.SMEM)] + vmem(4),
        scratch=(
            pltpu.VMEM((queries.shape[1], count), jnp.float32),
            pltpu.VMEM((padded, columns), jnp.float32),
            pltpu.VMEM(((feat_len + 127) // 128 * 128, 128), jnp.float32),
        ),
    )


def mix_body(
    value_len, step, numer_ref, denom_ref, rows_ref, out_ref, gain_ref, mixed_ref, mlp_ref, sums
):
    count, columns = numer_ref.shape
    heads = denom_ref.shape[1]
    column = lax.broadcasted_iota(jnp.int32, (1, columns), 1)
    inverse = 1.0 / denom_ref[...]
    spread = jnp.zeros((count, columns), jnp.float32)
    for h in range(heads):
        here = (column >= h * value_len) & (column < (h + 1) * value_len)
        spread = jnp.where(here, inverse[:, h : h + 1], spread)
    attended = (numer_ref[...] * spread).astype(jnp.bfloat16)
    sums[...] = jnp.dot(attended, out_ref[...], preferred_element_type=jnp.float32)
    gain = gain_ref[...]

    @pl.loop(0, count // step)
    def _(block):
        at = pl.ds(pl.multiple_of(block * step, step), step)
        mixed = (rows_ref[at, :].astype(jnp.float32) + sums[at, :]).astype(jnp.bfloat16)
        mixed_ref[at, :] = mixed
        mlp_ref[at, :] = unit_rows(mixed.astype(jnp.float32), gain).astype(jnp.bfloat16)


def mix(numer, denom, rows, out_weight, mlp_gain, value_len):
    count, width = rows.shape
    shape = like(count, width, jnp.bfloat16)
    return kernel_call(
        functools.partial(mix_body, value_len, 32),
        "mix",
        (shape, shape),
        numer,
        denom,
        rows,
        out_weight,
        mlp_gain[None],
        scratch=(pltpu.VMEM((count, width), jnp.float32),),
    )


def swiglu_terms(rows, gate_rows, up_rows, down_rows):
    gate_act = lax.dot_general(rows, gate_rows, NT, preferred_element_type=jnp.float32)
    up_act = lax.dot_general(rows, up_rows, NT, preferred_element_type=jnp.float32)
    hidden_units = (gate_act * jax.nn.sigmoid(gate_act) * up_act).astype(jnp.bfloat16)
    return jnp.dot(hidden_units, down_rows, preferred_element_type=jnp.float32)


def on_grid(run):
    return all(low % 16 == 0 and high % 16 == 0 for _, low, high in run)


def read_units(refs, units):
    parts = []
    for k in range(3):
        rows = [refs[run[k][0]][run[k][1] : run[k][2]] for run in units if on_grid(run)]
        rest = [
            refs[run[k][0]][...].astype(jnp.float32)[run[k][1] : run[k][2]]
            for run in units
            if not on_grid(run)
        ]
        if rest:
            rows.append(jnp.concatenate(rest, axis=0).astype(jnp.bfloat16))
        parts.append(jnp.concatenate(rows, axis=0))
    return parts


def accumulate_body(units, n_weights, n_rows, n_acc, residual, *refs):
    weights = refs[:n_weights]
    rows = refs[n_weights : n_weights + n_rows]
    acc = refs[n_weights + n_rows : n_weights + n_rows + n_acc]
    parts = read_units(weights, units)
    for k, rows_ref in enumerate(rows):
        out_ref = refs[len(refs) - n_rows + k]
        terms = swiglu_terms(rows_ref[...], *parts)
        if n_acc:
            terms = terms + acc[k][...]
        if residual:
            terms = terms + refs[n_weights + n_rows + n_acc][...].astype(jnp.float32)
        out_ref[...] = terms.astype(out_ref.dtype)


def accumulate(rows, weights, units, acc, dtype, name, residual=None):
    shapes = tuple(like(*array.shape, dtype) for array in rows)
    start = len(weights) + len(rows)
    aliases = {start + k: k for k in range(len(acc))} if dtype == jnp.float32 else {}
    extra = () if residual is None else (residual,)
    body = functools.partial(
        accumulate_body, tuple(units), len(weights), len(rows), len(acc), bool(extra)
    )
    return kernel_call(body, name, shapes, *weights, *rows, *acc, *extra, aliases=aliases)


def runs(which, low, size):
    return tuple((which, low + k * size, low + (k + 1) * size) for k in range(3))


def split_runs(first, second, main):
    (i, at), (j, then) = first, second
    held = 2 * main // 3
    rest = main - held
    return (
        ((i, at, at + held), (i, at + main, at + main + held), (j, then + rest, then + main)),
        ((i, at + held, at + main), (j, then, then + rest), (j, then + main, then + rest + main)),
    )


def collect_body(plans, *refs):
    outs = refs[len(refs) - len(plans) :]
    for out_ref, plan in zip(outs, plans):
        rows = [refs[i][...].astype(jnp.float32)[low:high] for i, low, high in plan]
        out_ref[...] = jnp.concatenate(rows, axis=0).astype(jnp.bfloat16)


def collect(arrays, plans, name):
    columns = arrays[0].shape[1]
    shapes = tuple(like(sum(h - l for _, l, h in plan), columns, jnp.bfloat16) for plan in plans)
    return kernel_call(functools.partial(collect_body, plans), name, shapes, *arrays)


def shard_body(main, gate_ref, up_ref, down_ref, shard_ref, main_ref, *rest):
    buffers, sems = rest[:3], rest[3]
    copies = [
        pltpu.make_async_copy(source, buffer, sems.at[k])
        for k, (source, buffer) in enumerate(zip((gate_ref, up_ref, down_ref), buffers))
    ]
    for copy in copies:
        copy.start()
    for copy in copies:
        copy.wait()
    arrays = [buffer[...].astype(jnp.float32) for buffer in buffers]
    tops = [array[:main] for array in arrays]
    ends = [array[main:] for array in arrays]
    shard_ref[...] = jnp.concatenate(tops + ends, axis=0).astype(jnp.bfloat16)
    main_ref[...] = jnp.concatenate(tops, axis=0).astype(jnp.bfloat16)


def final_body(step, count_ref, kept_ref, given_ref, out_ref):
    count = kept_ref.shape[0]

    @pl.loop(0, count // step)
    def _(block):
        first = pl.multiple_of(block * step, step)
        at = pl.ds(first, step)
        total = kept_ref[at, :] + given_ref[at, :].astype(jnp.float32)
        row = lax.broadcasted_iota(jnp.int32, total.shape, 0) + first
        out_ref[at, :] = jnp.where(row < count_ref[0], total, 0.0).astype(out_ref.dtype)


def local(
    hidden_in,
    lengths,
    log_decay,
    mix_gain,
    conv_weight,
    query_weight,
    key_weight,
    value_weight,
    out_weight,
    mlp_gain,
    gate_weight,
    up_weight,
    down_weight,
):
    local_len = hidden_in.shape[1]
    rows_in = hidden_in[0]
    decays = log_decay[0]
    head_count = log_decay.shape[2]
    value_len = value_weight.shape[1] // head_count
    feat_in = query_weight.shape[1] // head_count
    feature_scale = feat_in ** (-0.25)
    valid_count = lengths - lax.axis_index("seq") * local_len
    spans = lax.axis_size("seq")
    units, model = gate_weight.shape[1], gate_weight.shape[0]
    edge = units // 7
    main = units - edge
    wide = 3 * main
    full = 3 * units
    narrow = full - wide
    cut = main + 2 * main // 3

    shard, shard_main = kernel_call(
        functools.partial(shard_body, main),
        "shard",
        (like(full, model, jnp.bfloat16), like(wide, model, jnp.bfloat16)),
        gate_weight.T,
        up_weight.T,
        down_weight.T,
        specs=[pl.BlockSpec(memory_space=pl.ANY)] * 3,
        scratch=[pltpu.VMEM((units, model), jnp.bfloat16)] * 3 + [pltpu.SemaphoreType.DMA((3,))],
        mib=56,
    )
    near, far, deep = slot((flip_near, shard), (flip_far, shard), (next_plane, shard_main))

    lead = 16
    if spans > 1:
        edge_in = from_behind(rows_in[local_len - lead :], "seq", 1)
    else:
        edge_in = jnp.zeros((lead, model), jnp.bfloat16)
    queries, key_rows, values = project(
        rows_in, edge_in, mix_gain, conv_weight, query_weight, key_weight, value_weight, feature_scale
    )
    near, far, deep, queries, key_rows, values = together(
        near, far, deep, queries, key_rows, values
    )

    sends = collect(
        (shard, near, far, deep),
        (
            ((3, 0, wide), (2, 0, cut)),
            ((3, 0, wide), (1, cut, full)),
            ((3, 0, wide), (0, wide, full), (1, wide, full), (2, wide, full)),
        ),
        "collect_second",
    )
    near1, far1, deep1 = slot(*zip((flip_near, flip_far, next_plane), sends))

    numerator, denominator, end_state, end_norm = attend(
        valid_count, log_decay[0].T, queries, key_rows, values, feat_in, value_len
    )
    if spans > 1:
        positions = jnp.arange(local_len, dtype=jnp.int32)
        numerator, denominator, end_state, end_norm = carry_in(
            (positions < valid_count).astype(jnp.float32),
            decays,
            queries,
            numerator,
            denominator,
            end_state[:, 0],
            end_norm.T,
        )
    else:
        end_norm = end_norm.T
    mixed_rows, mlp_in = mix(numerator, denominator, rows_in, out_weight, mlp_gain, value_len)
    near1, far1, deep1, mixed_rows, mlp_in, end_state, end_norm = together(
        near1, far1, deep1, mixed_rows, mlp_in, end_state, end_norm
    )

    sends = collect(
        (near1, far1, deep1),
        (
            ((2, 0, wide), (1, 0, cut)),
            ((2, 0, wide), (0, cut, wide)),
            ((2, 0, wide + 3 * narrow), (1, wide + wide - cut, wide + full - cut)),
        ),
        "collect_third",
    )
    near2, far2, deep2 = slot(*zip((flip_near, flip_far, next_plane), sends))
    rows = (mlp_in, flip_core(mlp_in))
    acc = accumulate(
        rows,
        (shard, near, far, deep, near1, far1, deep1),
        [runs(i, 0, main) for i in range(7)] + list(split_runs((4, wide), (5, wide), main)),
        (),
        jnp.float32,
        "accumulate_second",
    )
    near2, far2, deep2 = together(near2, far2, deep2)

    deep3_main, line = collect(
        (far2, deep2),
        (
            ((1, 0, wide),),
            ((1, wide, wide + 4 * narrow), (0, wide + wide - cut - main, wide + wide - cut)),
        ),
        "collect_fourth",
    )
    near3, far3, deep3 = slot((flip_near, deep3_main), (flip_far, deep3_main), (next_plane, line))
    acc = accumulate(
        rows,
        (shard, near, far, far1, deep1, near2, far2, deep2),
        [runs(i, 0, main) for i in (5, 6, 7)]
        + list(split_runs((5, wide), (6, wide), main))
        + [runs(i, wide, edge) for i in (0, 1, 2)]
        + [runs(3, wide + wide - cut, edge)]
        + [runs(4, wide + k * narrow, edge) for k in range(3)]
        + [runs(7, wide + k * narrow, edge) for k in range(4)],
        tuple(acc),
        jnp.float32,
        "accumulate_third",
    )
    near3, far3, deep3, *acc = together(near3, far3, deep3, *acc)

    sends = collect(
        (near2, far2, near3, far3, deep3),
        (
            ((1, 0, main), (3, 0, main)),
            ((0, main, 2 * main), (2, main, 2 * main)),
            ((4, 3 * narrow, 4 * narrow + main),),
        ),
        "collect_fifth",
    )
    near4, far4, deep4 = slot(*zip((flip_near, flip_far, next_plane), sends))
    acc = accumulate(
        rows,
        (near3, far3, deep3),
        [runs(0, 0, main), runs(1, 0, main)] + [runs(2, k * narrow, edge) for k in range(4)],
        tuple(acc),
        jnp.float32,
        "accumulate_fourth",
    )
    weights = (near4, far4, deep3, deep4)
    last = [
        ((0, 0, main), (1, 0, main), (2, 4 * narrow, 4 * narrow + main)),
        ((0, main, 2 * main), (1, main, 2 * main), (3, narrow, narrow + main)),
        runs(3, 0, edge),
    ]
    (given,) = accumulate(rows[1:], weights, last, acc[1:], jnp.bfloat16, "finish_other")
    (kept,) = accumulate(
        rows[:1], weights, last, acc[:1], jnp.float32, "finish_own", residual=mixed_rows
    )
    result = kernel_call(
        functools.partial(final_body, 64),
        "final",
        like(local_len, model, jnp.bfloat16),
        valid_count,
        kept,
        flip_core(given),
        specs=[pl.BlockSpec(memory_space=pltpu.SMEM)] + vmem(2),
    )
    return (
        result[None],
        end_state.reshape((1, 1) + end_state.shape[:1] + end_state.shape[-1:]),
        end_norm[None, None],
    )


def solution(mesh):
    return jax.shard_map(
        local,
        mesh=mesh,
        in_specs=(
            P("req", "seq", None),
            P("req"),
            P("req", "seq", None),
            P(),
            P(),
            P(),
            P(),
            P(),
            P(),
            P(),
            P(None, "req"),
            P(None, "req"),
            P(None, "req"),
        ),
        out_specs=(P("req", "seq", None), P("req", "seq", None, None), P("req", "seq", None, None)),
        check_vma=False,
    )
```

```python
import functools

import jax
import jax.numpy as jnp
from jax import lax
from jax.experimental import pallas as pl
from jax.experimental.pallas import tpu as pltpu
from jax.sharding import PartitionSpec as P


def from_behind(array, axis, by):
    count = lax.axis_size(axis)
    pairs = [(i, i + by) for i in range(count) if 0 <= i + by < count]
    return lax.ppermute(array, axis, pairs)


def entering(array, axis, combine, identity):
    count, here = (lax.axis_size(axis), lax.axis_index(axis))
    everything = jax.tree.map(
        lambda part, kind: lax.all_gather(part.astype(kind), axis),
        array,
        (jnp.bfloat16, jnp.bfloat16, jnp.bfloat16),
    )
    start = jax.tree.map(
        lambda part, zero: jnp.broadcast_to(jnp.asarray(zero, part.dtype), part.shape),
        array,
        identity,
    )

    def hop(k, before):
        reached = k < here
        new = combine(
            before, jax.tree.map(lambda part, own: part[k].astype(own.dtype), everything, array)
        )
        return jax.tree.map(lambda a, b: jnp.where(reached, a, b), new, before)

    return lax.fori_loop(0, count, hop, start)


def features(vectors):
    constant = jnp.ones(vectors.shape[:-1] + (1,), jnp.float32)
    width = vectors.shape[-1]
    squares = (vectors[..., :, None] * vectors[..., None, :]).reshape(
        vectors.shape[:-1] + (width * width,)
    )
    return jnp.concatenate([constant, vectors, squares * 0.5**0.5], axis=-1)


def carry_in(valid_mask, decays, queries, numerator, denominator, flat_memory, key_sum):
    local_len = numerator.shape[0]
    feat_len, head_count = key_sum.shape
    value_len = flat_memory.shape[1] // head_count
    feat_in = queries.shape[1] // head_count
    decay_rate = jnp.where(valid_mask[:, None] > 0, decays, 0.0)
    span_decay = jnp.sum(decay_rate, axis=0)

    def merge_states(earlier, later):
        factor = jnp.exp(later[0])
        return (
            earlier[0] + later[0],
            earlier[1] * jnp.repeat(factor, value_len)[None, :] + later[1],
            earlier[2] * factor[None, :] + later[2],
        )

    neutral = (jnp.zeros_like(span_decay), jnp.zeros_like(flat_memory), jnp.zeros_like(key_sum))
    carried = entering((span_decay, flat_memory, key_sum), "seq", merge_states, neutral)
    prior_memory = carried[1]
    prior_keys = carried[2]
    highest = lax.Precision.HIGHEST
    growth = jnp.exp(jnp.cumsum(decay_rate, axis=0))
    query_feat = features(queries.astype(jnp.float32).reshape(local_len, head_count, feat_in))
    added = jnp.einsum(
        "thf,fhv->thv",
        query_feat,
        prior_memory.reshape(feat_len, head_count, value_len),
        precision=highest,
    )
    numerator = numerator + (added * growth[:, :, None]).reshape(local_len, -1)
    denominator = (
        denominator + jnp.einsum("thf,fh->th", query_feat, prior_keys, precision=highest) * growth
    )
    span_factor = jnp.exp(span_decay)
    end_state = prior_memory * jnp.repeat(span_factor, value_len)[None, :] + flat_memory
    end_norm = prior_keys * span_factor[None, :] + key_sum
    return numerator, denominator, end_state, end_norm


def permute(array, target):
    count = lax.axis_size("req")
    return lax.ppermute(array, "req", [(i, target(i)) for i in range(count)])


def flip_core(array):
    return permute(array, lambda i: i ^ 1)


def flip_near(array):
    return permute(array, lambda i: i ^ 2)


def flip_far(array):
    return permute(array, lambda i: i ^ 4)


def next_plane(array):
    count = lax.axis_size("req")
    return permute(array, lambda i: (i + 8) % count)


def together(*arrays):
    return lax.optimization_barrier(arrays)


def slot(*sends):
    operands = together(*[array for _, array in sends])
    return together(*[send(array) for (send, _), array in zip(sends, operands)])


def vmem(count):
    return [pl.BlockSpec(memory_space=pltpu.VMEM)] * count


def kernel_call(body, name, out_shape, *operands, scratch=(), aliases=None, specs=None, mib=24):
    many = isinstance(out_shape, tuple)
    return pl.pallas_call(
        body,
        out_shape=out_shape,
        in_specs=specs or vmem(len(operands)),
        out_specs=tuple(vmem(len(out_shape))) if many else vmem(1)[0],
        scratch_shapes=list(scratch),
        input_output_aliases=aliases or {},
        compiler_params=pltpu.CompilerParams(vmem_limit_bytes=mib * 1024 * 1024),
        cost_estimate=pl.CostEstimate(flops=1000, bytes_accessed=1000, transcendentals=0),
        name=name,
    )(*operands)


def like(rows, columns, dtype):
    return jax.ShapeDtypeStruct((rows, columns), dtype)


NT = (((1,), (1,)), ((), ()))


def unit_rows(rows, gain):
    factor = lax.rsqrt(jnp.mean(rows * rows, axis=-1, keepdims=True) + 1e-05)
    return (rows * factor * gain).astype(jnp.bfloat16).astype(jnp.float32)


def project_body(
    step,
    scale,
    rows_ref,
    edge_ref,
    gain_ref,
    conv_ref,
    query_ref,
    key_ref,
    value_ref,
    queries_ref,
    keys_ref,
    values_ref,
    normed,
    gated,
):
    gain = gain_ref[...]
    count = rows_ref.shape[0]
    lead = edge_ref.shape[0]
    taps = conv_ref.shape[0]
    normed[:lead] = unit_rows(edge_ref[...].astype(jnp.float32), gain)

    @pl.loop(0, count // step)
    def _(block):
        at = pl.multiple_of(block * step, step)
        rows = rows_ref[pl.ds(at, step), :].astype(jnp.float32)
        normed[pl.ds(lead + at, step), :] = unit_rows(rows, gain)

    @pl.loop(0, count // step)
    def _(block):
        at = pl.multiple_of(block * step, step)
        window = normed[pl.ds(at, step + lead), :]
        here = window[lead:]
        total = conv_ref[0:1] * here
        for tap in range(1, taps):
            total = total + conv_ref[tap : tap + 1] * window[lead - tap : lead - tap + step]
        gated[pl.ds(at, step), :] = (total * jax.nn.sigmoid(here)).astype(jnp.bfloat16)

    rows = gated[...]
    for weight_ref, out_ref, factor in (
        (query_ref, queries_ref, scale),
        (key_ref, keys_ref, scale),
        (value_ref, values_ref, None),
    ):
        product = jnp.dot(rows, weight_ref[...], preferred_element_type=jnp.float32)
        if factor is not None:
            product = product * factor
        out_ref[...] = product.astype(jnp.bfloat16)


def project(rows, edge, mix_gain, conv_weight, query_weight, key_weight, value_weight, scale):
    count, width = rows.shape
    step = 32
    return kernel_call(
        functools.partial(project_body, step, scale),
        "project",
        tuple(like(count, w.shape[1], jnp.bfloat16) for w in (query_weight, key_weight, value_weight)),
        rows,
        edge,
        mix_gain[None],
        conv_weight,
        query_weight,
        key_weight,
        value_weight,
        scratch=(
            pltpu.VMEM((count + edge.shape[0], width), jnp.float32),
            pltpu.VMEM((count, width), jnp.bfloat16),
        ),
    )


def attend_body(
    feat_in,
    value_len,
    count_ref,
    rate_ref,
    queries_ref,
    keys_ref,
    values_ref,
    numer_ref,
    denom_ref,
    state_ref,
    norm_ref,
    turned,
    total,
    norms,
):
    heads, count = rate_ref.shape
    columns = values_ref.shape[1]
    lane = lax.broadcasted_iota(jnp.int32, (count, count), 1)
    row = lax.broadcasted_iota(jnp.int32, (count, count), 0)
    valid = (lane[:1] < count_ref[0]).astype(jnp.float32)
    rate = jnp.where(valid > 0, rate_ref[...], 0.0)
    upto = (row <= lane).astype(jnp.float32)
    across = jnp.dot(
        rate, upto, precision=lax.Precision.HIGHEST, preferred_element_type=jnp.float32
    )
    down = across.T
    closing = across[:, count - 1 : count]
    fading = jnp.exp(closing - across) * valid
    causal = row >= lane
    keys = keys_ref[...]
    turned[...] = keys.astype(jnp.float32).T
    owner = lax.broadcasted_iota(jnp.int32, queries_ref.shape, 1)
    spare = lax.broadcasted_iota(jnp.int32, (8, count), 0) == 0
    head_lane = lax.broadcasted_iota(jnp.int32, (count, 128), 1)
    numer_ref[...] = jnp.zeros(numer_ref.shape, jnp.float32)
    total[...] = jnp.zeros(total.shape, jnp.float32)
    norms[...] = jnp.zeros(norms.shape, jnp.float32)
    norm_total = jnp.zeros((total.shape[0], 128), jnp.float32)
    denominators = jnp.zeros((count, 128), jnp.float32)
    for h in range(heads):
        low = min(h * value_len // 128 * 128, max(columns - 256, 0))
        high = min(low + 256, columns)
        mine = lax.broadcasted_iota(jnp.int32, (count, high - low), 1) + low
        mine = (mine >= h * value_len) & (mine < (h + 1) * value_len)
        values = jnp.where(mine, values_ref[:, low:high].astype(jnp.float32), 0.0)
        values = values.astype(jnp.bfloat16)
        asks = (owner >= h * feat_in) & (owner < (h + 1) * feat_in)
        queries = jnp.where(asks, queries_ref[...].astype(jnp.float32), 0.0)
        scores = lax.dot_general(
            queries.astype(jnp.bfloat16), keys, NT, preferred_element_type=jnp.float32
        )
        gap = down[:, h : h + 1] - across[h : h + 1]
        weights = jnp.where(causal, jnp.exp(jnp.minimum(gap, 0.0)) * valid, 0.0)
        weights = weights * (1.0 + scores + 0.5 * scores * scores)
        numer_ref[:, low:high] += jnp.dot(
            weights.astype(jnp.bfloat16), values, preferred_element_type=jnp.float32
        )
        sums = jnp.sum(weights, axis=1, keepdims=True)
        denominators = jnp.where(head_lane == h, sums, denominators)
        own = turned[h * feat_in : (h + 1) * feat_in]
        fade = fading[h : h + 1]
        faded = own * fade
        scaled = faded * 0.5**0.5
        parts = [own[i : i + 1] * scaled for i in range(feat_in)]
        parts += [faded, jnp.where(spare, fade, 0.0)]
        feats = jnp.concatenate(parts, axis=0).astype(jnp.bfloat16)
        total[:, low:high] += jnp.dot(feats, values, preferred_element_type=jnp.float32)
        mark = (head_lane == h).astype(jnp.bfloat16)
        norm_total = norm_total + jnp.dot(feats, mark, preferred_element_type=jnp.float32)
    denom_ref[...] = denominators[:, :heads]
    pairs = feat_in * feat_in
    state_ref[0] = total[pairs + feat_in : pairs + feat_in + 1, :]
    for f in range(feat_in):
        state_ref[1 + f] = total[pairs + f : pairs + f + 1, :]

    @pl.loop(0, pairs // 8)
    def _(block):
        for k in range(8):
            f = block * 8 + k
            state_ref[1 + feat_in + f] = total[pl.ds(f, 1), :]

    norms[0:1, :] = norm_total[pairs + feat_in : pairs + feat_in + 1]
    norms[1 : 1 + feat_in, :] = norm_total[pairs : pairs + feat_in]
    norms[1 + feat_in : 1 + feat_in + pairs, :] = norm_total[:pairs]
    norm_ref[...] = norms[...].T[:heads, : 1 + feat_in + pairs]


def attend(valid_count, rate, queries, keys, values, feat_in, value_len):
    heads, count = rate.shape
    columns = values.shape[1]
    feat_len = 1 + feat_in + feat_in * feat_in
    padded = feat_in * feat_in + feat_in + 8
    return kernel_call(
        functools.partial(attend_body, feat_in, value_len),
        "attend",
        (
            like(count, columns, jnp.float32),
            like(count, heads, jnp.float32),
            jax.ShapeDtypeStruct((feat_len, 1, columns), jnp.float32),
            like(heads, feat_len, jnp.float32),
        ),
        valid_count,
        rate,
        queries,
        keys,
        values,
        specs=[pl.BlockSpec(memory_space=pltpu.SMEM)] + vmem(4),
        scratch=(
            pltpu.VMEM((queries.shape[1], count), jnp.float32),
            pltpu.VMEM((padded, columns), jnp.float32),
            pltpu.VMEM(((feat_len + 127) // 128 * 128, 128), jnp.float32),
        ),
    )


def mix_body(
    value_len, step, numer_ref, denom_ref, rows_ref, out_ref, gain_ref, mixed_ref, mlp_ref, sums
):
    count, columns = numer_ref.shape
    heads = denom_ref.shape[1]
    column = lax.broadcasted_iota(jnp.int32, (1, columns), 1)
    inverse = 1.0 / denom_ref[...]
    spread = jnp.zeros((count, columns), jnp.float32)
    for h in range(heads):
        here = (column >= h * value_len) & (column < (h + 1) * value_len)
        spread = jnp.where(here, inverse[:, h : h + 1], spread)
    attended = (numer_ref[...] * spread).astype(jnp.bfloat16)
    sums[...] = jnp.dot(attended, out_ref[...], preferred_element_type=jnp.float32)
    gain = gain_ref[...]

    @pl.loop(0, count // step)
    def _(block):
        at = pl.ds(pl.multiple_of(block * step, step), step)
        mixed = (rows_ref[at, :].astype(jnp.float32) + sums[at, :]).astype(jnp.bfloat16)
        mixed_ref[at, :] = mixed
        mlp_ref[at, :] = unit_rows(mixed.astype(jnp.float32), gain).astype(jnp.bfloat16)


def mix(numer, denom, rows, out_weight, mlp_gain, value_len):
    count, width = rows.shape
    shape = like(count, width, jnp.bfloat16)
    return kernel_call(
        functools.partial(mix_body, value_len, 32),
        "mix",
        (shape, shape),
        numer,
        denom,
        rows,
        out_weight,
        mlp_gain[None],
        scratch=(pltpu.VMEM((count, width), jnp.float32),),
    )


def swiglu_terms(rows, gate_rows, up_rows, down_rows):
    gate_act = lax.dot_general(rows, gate_rows, NT, preferred_element_type=jnp.float32)
    up_act = lax.dot_general(rows, up_rows, NT, preferred_element_type=jnp.float32)
    hidden_units = (gate_act * jax.nn.sigmoid(gate_act) * up_act).astype(jnp.bfloat16)
    return jnp.dot(hidden_units, down_rows, preferred_element_type=jnp.float32)


def on_grid(run):
    return all(low % 16 == 0 and high % 16 == 0 for _, low, high in run)


def read_units(refs, units):
    parts = []
    for k in range(3):
        rows = [refs[run[k][0]][run[k][1] : run[k][2]] for run in units if on_grid(run)]
        rest = [
            refs[run[k][0]][...].astype(jnp.float32)[run[k][1] : run[k][2]]
            for run in units
            if not on_grid(run)
        ]
        if rest:
            rows.append(jnp.concatenate(rest, axis=0).astype(jnp.bfloat16))
        parts.append(jnp.concatenate(rows, axis=0))
    return parts


def accumulate_body(units, n_weights, n_rows, n_acc, residual, *refs):
    weights = refs[:n_weights]
    rows = refs[n_weights : n_weights + n_rows]
    acc = refs[n_weights + n_rows : n_weights + n_rows + n_acc]
    parts = read_units(weights, units)
    for k, rows_ref in enumerate(rows):
        out_ref = refs[len(refs) - n_rows + k]
        terms = swiglu_terms(rows_ref[...], *parts)
        if n_acc:
            terms = terms + acc[k][...]
        if residual:
            terms = terms + refs[n_weights + n_rows + n_acc][...].astype(jnp.float32)
        out_ref[...] = terms.astype(out_ref.dtype)


def accumulate(rows, weights, units, acc, dtype, name, residual=None):
    shapes = tuple(like(*array.shape, dtype) for array in rows)
    start = len(weights) + len(rows)
    aliases = {start + k: k for k in range(len(acc))} if dtype == jnp.float32 else {}
    extra = () if residual is None else (residual,)
    body = functools.partial(
        accumulate_body, tuple(units), len(weights), len(rows), len(acc), bool(extra)
    )
    return kernel_call(body, name, shapes, *weights, *rows, *acc, *extra, aliases=aliases)


def runs(which, low, size):
    return tuple((which, low + k * size, low + (k + 1) * size) for k in range(3))


def split_runs(first, second, main):
    (i, at), (j, then) = first, second
    held = 2 * main // 3
    rest = main - held
    return (
        ((i, at, at + held), (i, at + main, at + main + held), (j, then + rest, then + main)),
        ((i, at + held, at + main), (j, then, then + rest), (j, then + main, then + rest + main)),
    )


def collect_body(plans, *refs):
    outs = refs[len(refs) - len(plans) :]
    for out_ref, plan in zip(outs, plans):
        rows = [refs[i][...].astype(jnp.float32)[low:high] for i, low, high in plan]
        out_ref[...] = jnp.concatenate(rows, axis=0).astype(jnp.bfloat16)


def collect(arrays, plans, name):
    columns = arrays[0].shape[1]
    shapes = tuple(like(sum(h - l for _, l, h in plan), columns, jnp.bfloat16) for plan in plans)
    return kernel_call(functools.partial(collect_body, plans), name, shapes, *arrays)


def shard_body(main, gate_ref, up_ref, down_ref, shard_ref, *rest):
    buffers, sems = rest[:3], rest[3]
    sources = (gate_ref, up_ref, down_ref)
    copies = []
    for k, source in enumerate(sources):
        copies.append(pltpu.make_async_copy(source, buffers[k], sems.at[k]))
        copies[-1].start()
    for k, source in enumerate(sources):
        place = shard_ref.at[pl.ds(k * main, main), :]
        copies.append(pltpu.make_async_copy(source.at[pl.ds(0, main), :], place, sems.at[3 + k]))
        copies[-1].start()
    for copy in copies:
        copy.wait()
    ends = [buffer[...].astype(jnp.float32)[main:] for buffer in buffers]
    shard_ref[3 * main :, :] = jnp.concatenate(ends, axis=0).astype(jnp.bfloat16)


def final_body(step, count_ref, kept_ref, given_ref, out_ref):
    count = kept_ref.shape[0]

    @pl.loop(0, count // step)
    def _(block):
        first = pl.multiple_of(block * step, step)
        at = pl.ds(first, step)
        total = kept_ref[at, :] + given_ref[at, :].astype(jnp.float32)
        row = lax.broadcasted_iota(jnp.int32, total.shape, 0) + first
        out_ref[at, :] = jnp.where(row < count_ref[0], total, 0.0).astype(out_ref.dtype)


def local(
    hidden_in,
    lengths,
    log_decay,
    mix_gain,
    conv_weight,
    query_weight,
    key_weight,
    value_weight,
    out_weight,
    mlp_gain,
    gate_weight,
    up_weight,
    down_weight,
):
    local_len = hidden_in.shape[1]
    rows_in = hidden_in[0]
    decays = log_decay[0]
    head_count = log_decay.shape[2]
    value_len = value_weight.shape[1] // head_count
    feat_in = query_weight.shape[1] // head_count
    feature_scale = feat_in ** (-0.25)
    valid_count = lengths - lax.axis_index("seq") * local_len
    spans = lax.axis_size("seq")
    units, model = gate_weight.shape[1], gate_weight.shape[0]
    edge = units // 7
    main = units - edge
    wide = 3 * main
    full = 3 * units
    narrow = full - wide
    cut = main + 2 * main // 3

    shard = kernel_call(
        functools.partial(shard_body, main),
        "shard",
        like(full, model, jnp.bfloat16),
        gate_weight.T,
        up_weight.T,
        down_weight.T,
        specs=[pl.BlockSpec(memory_space=pl.ANY)] * 3,
        scratch=[pltpu.VMEM((units, model), jnp.bfloat16)] * 3 + [pltpu.SemaphoreType.DMA((6,))],
        mib=56,
    )
    near, far, deep = slot((flip_near, shard), (flip_far, shard), (next_plane, shard))

    lead = 16
    if spans > 1:
        edge_in = from_behind(rows_in[local_len - lead :], "seq", 1)
    else:
        edge_in = jnp.zeros((lead, model), jnp.bfloat16)
    queries, key_rows, values = project(
        rows_in, edge_in, mix_gain, conv_weight, query_weight, key_weight, value_weight, feature_scale
    )
    near, far, deep, queries, key_rows, values = together(
        near, far, deep, queries, key_rows, values
    )

    sends = collect(
        (shard, near, far, deep),
        (
            ((3, 0, wide), (2, 0, cut)),
            ((3, 0, wide), (1, cut, full)),
            ((3, 0, full), (1, wide, full), (2, wide, full)),
        ),
        "collect_second",
    )
    near1, far1, deep1 = slot(*zip((flip_near, flip_far, next_plane), sends))

    numerator, denominator, end_state, end_norm = attend(
        valid_count, log_decay[0].T, queries, key_rows, values, feat_in, value_len
    )
    if spans > 1:
        positions = jnp.arange(local_len, dtype=jnp.int32)
        numerator, denominator, end_state, end_norm = carry_in(
            (positions < valid_count).astype(jnp.float32),
            decays,
            queries,
            numerator,
            denominator,
            end_state[:, 0],
            end_norm.T,
        )
    else:
        end_norm = end_norm.T
    mixed_rows, mlp_in = mix(numerator, denominator, rows_in, out_weight, mlp_gain, value_len)
    near1, far1, deep1, mixed_rows, mlp_in, end_state, end_norm = together(
        near1, far1, deep1, mixed_rows, mlp_in, end_state, end_norm
    )

    sends = collect(
        (near1, far1, deep1),
        (
            ((2, 0, wide), (1, 0, cut)),
            ((2, 0, wide), (0, cut, wide)),
            ((2, 0, wide + 3 * narrow), (1, wide + wide - cut, wide + full - cut)),
        ),
        "collect_third",
    )
    near2, far2, deep2 = slot(*zip((flip_near, flip_far, next_plane), sends))
    rows = (mlp_in, flip_core(mlp_in))
    acc = accumulate(
        rows,
        (shard, near, far, deep, near1, far1, deep1),
        [runs(i, 0, main) for i in range(7)] + list(split_runs((4, wide), (5, wide), main)),
        (),
        jnp.float32,
        "accumulate_second",
    )
    near2, far2, deep2 = together(near2, far2, deep2)

    deep3_main, line = collect(
        (far2, deep2),
        (
            ((1, 0, wide),),
            ((1, full, full + 3 * narrow), (0, wide + wide - cut - main, wide + wide - cut)),
        ),
        "collect_fourth",
    )
    near3, far3, deep3 = slot((flip_near, deep3_main), (flip_far, deep3_main), (next_plane, line))
    acc = accumulate(
        rows,
        (shard, near, far, deep, far1, deep1, near2, far2, deep2),
        [runs(i, 0, main) for i in (6, 7, 8)]
        + list(split_runs((6, wide), (7, wide), main))
        + [runs(i, wide, edge) for i in (0, 1, 2, 3)]
        + [runs(4, wide + wide - cut, edge)]
        + [runs(5, wide + k * narrow, edge) for k in range(3)]
        + [runs(8, wide + k * narrow, edge) for k in range(4)],
        tuple(acc),
        jnp.float32,
        "accumulate_third",
    )
    near3, far3, deep3, *acc = together(near3, far3, deep3, *acc)

    sends = collect(
        (near2, far2, near3, far3, deep3),
        (
            ((1, 0, main), (3, 0, main)),
            ((0, main, 2 * main), (2, main, 2 * main)),
            ((4, 2 * narrow, 3 * narrow + main),),
        ),
        "collect_fifth",
    )
    near4, far4, deep4 = slot(*zip((flip_near, flip_far, next_plane), sends))
    acc = accumulate(
        rows,
        (near3, far3, deep3),
        [runs(0, 0, main), runs(1, 0, main)] + [runs(2, k * narrow, edge) for k in range(3)],
        tuple(acc),
        jnp.float32,
        "accumulate_fourth",
    )
    weights = (near4, far4, deep3, deep4)
    last = [
        ((0, 0, main), (1, 0, main), (2, 3 * narrow, 3 * narrow + main)),
        ((0, main, 2 * main), (1, main, 2 * main), (3, narrow, narrow + main)),
        runs(3, 0, edge),
    ]
    (given,) = accumulate(rows[1:], weights, last, acc[1:], jnp.bfloat16, "finish_other")
    (kept,) = accumulate(
        rows[:1], weights, last, acc[:1], jnp.float32, "finish_own", residual=mixed_rows
    )
    result = kernel_call(
        functools.partial(final_body, 64),
        "final",
        like(local_len, model, jnp.bfloat16),
        valid_count,
        kept,
        flip_core(given),
        specs=[pl.BlockSpec(memory_space=pltpu.SMEM)] + vmem(2),
    )
    return (
        result[None],
        end_state.reshape((1, 1) + end_state.shape[:1] + end_state.shape[-1:]),
        end_norm[None, None],
    )


def solution(mesh):
    return jax.shard_map(
        local,
        mesh=mesh,
        in_specs=(
            P("req", "seq", None),
            P("req"),
            P("req", "seq", None),
            P(),
            P(),
            P(),
            P(),
            P(),
            P(),
            P(),
            P(None, "req"),
            P(None, "req"),
            P(None, "req"),
        ),
        out_specs=(P("req", "seq", None), P("req", "seq", None, None), P("req", "seq", None, None)),
        check_vma=False,
    )
```

```python
import functools

import jax
import jax.numpy as jnp
from jax import lax
from jax.experimental import pallas as pl
from jax.experimental.pallas import tpu as pltpu
from jax.sharding import PartitionSpec as P


def from_behind(array, axis, by):
    count = lax.axis_size(axis)
    pairs = [(i, i + by) for i in range(count) if 0 <= i + by < count]
    return lax.ppermute(array, axis, pairs)


def entering(array, axis, combine, identity):
    count, here = (lax.axis_size(axis), lax.axis_index(axis))
    everything = jax.tree.map(
        lambda part, kind: lax.all_gather(part.astype(kind), axis),
        array,
        (jnp.bfloat16, jnp.bfloat16, jnp.bfloat16),
    )
    start = jax.tree.map(
        lambda part, zero: jnp.broadcast_to(jnp.asarray(zero, part.dtype), part.shape),
        array,
        identity,
    )

    def hop(k, before):
        reached = k < here
        new = combine(
            before, jax.tree.map(lambda part, own: part[k].astype(own.dtype), everything, array)
        )
        return jax.tree.map(lambda a, b: jnp.where(reached, a, b), new, before)

    return lax.fori_loop(0, count, hop, start)


def features(vectors):
    constant = jnp.ones(vectors.shape[:-1] + (1,), jnp.float32)
    width = vectors.shape[-1]
    squares = (vectors[..., :, None] * vectors[..., None, :]).reshape(
        vectors.shape[:-1] + (width * width,)
    )
    return jnp.concatenate([constant, vectors, squares * 0.5**0.5], axis=-1)


def carry_in(valid_mask, decays, queries, numerator, denominator, flat_memory, key_sum):
    local_len = numerator.shape[0]
    feat_len, head_count = key_sum.shape
    value_len = flat_memory.shape[1] // head_count
    feat_in = queries.shape[1] // head_count
    decay_rate = jnp.where(valid_mask[:, None] > 0, decays, 0.0)
    span_decay = jnp.sum(decay_rate, axis=0)

    def merge_states(earlier, later):
        factor = jnp.exp(later[0])
        return (
            earlier[0] + later[0],
            earlier[1] * jnp.repeat(factor, value_len)[None, :] + later[1],
            earlier[2] * factor[None, :] + later[2],
        )

    neutral = (jnp.zeros_like(span_decay), jnp.zeros_like(flat_memory), jnp.zeros_like(key_sum))
    carried = entering((span_decay, flat_memory, key_sum), "seq", merge_states, neutral)
    prior_memory = carried[1]
    prior_keys = carried[2]
    highest = lax.Precision.HIGHEST
    growth = jnp.exp(jnp.cumsum(decay_rate, axis=0))
    query_feat = features(queries.astype(jnp.float32).reshape(local_len, head_count, feat_in))
    added = jnp.einsum(
        "thf,fhv->thv",
        query_feat,
        prior_memory.reshape(feat_len, head_count, value_len),
        precision=highest,
    )
    numerator = numerator + (added * growth[:, :, None]).reshape(local_len, -1)
    denominator = (
        denominator + jnp.einsum("thf,fh->th", query_feat, prior_keys, precision=highest) * growth
    )
    span_factor = jnp.exp(span_decay)
    end_state = prior_memory * jnp.repeat(span_factor, value_len)[None, :] + flat_memory
    end_norm = prior_keys * span_factor[None, :] + key_sum
    return numerator, denominator, end_state, end_norm


def permute(array, target):
    count = lax.axis_size("req")
    return lax.ppermute(array, "req", [(i, target(i)) for i in range(count)])


def flip_core(array):
    return permute(array, lambda i: i ^ 1)


def flip_near(array):
    return permute(array, lambda i: i ^ (4 if i % 2 else 2))


def flip_far(array):
    return permute(array, lambda i: i ^ (2 if i % 2 else 4))


def next_plane(array):
    count = lax.axis_size("req")
    return permute(array, lambda i: (i + 8) % count)


def together(*arrays):
    return lax.optimization_barrier(arrays)


def slot(*sends):
    operands = together(*[array for _, array in sends])
    return together(*[send(array) for (send, _), array in zip(sends, operands)])


def vmem(count):
    return [pl.BlockSpec(memory_space=pltpu.VMEM)] * count


def kernel_call(body, name, out_shape, *operands, scratch=(), aliases=None, specs=None, mib=24):
    many = isinstance(out_shape, tuple)
    return pl.pallas_call(
        body,
        out_shape=out_shape,
        in_specs=specs or vmem(len(operands)),
        out_specs=tuple(vmem(len(out_shape))) if many else vmem(1)[0],
        scratch_shapes=list(scratch),
        input_output_aliases=aliases or {},
        compiler_params=pltpu.CompilerParams(vmem_limit_bytes=mib * 1024 * 1024),
        cost_estimate=pl.CostEstimate(flops=1000, bytes_accessed=1000, transcendentals=0),
        name=name,
    )(*operands)


def like(rows, columns, dtype):
    return jax.ShapeDtypeStruct((rows, columns), dtype)


NT = (((1,), (1,)), ((), ()))


def unit_rows(rows, gain):
    factor = lax.rsqrt(jnp.mean(rows * rows, axis=-1, keepdims=True) + 1e-05)
    return (rows * factor * gain).astype(jnp.bfloat16).astype(jnp.float32)


def project_body(
    step,
    scale,
    rows_ref,
    edge_ref,
    gain_ref,
    conv_ref,
    query_ref,
    key_ref,
    value_ref,
    queries_ref,
    keys_ref,
    values_ref,
    normed,
    gated,
):
    gain = gain_ref[...]
    count = rows_ref.shape[0]
    lead = edge_ref.shape[0]
    taps = conv_ref.shape[0]
    normed[:lead] = unit_rows(edge_ref[...].astype(jnp.float32), gain)

    @pl.loop(0, count // step)
    def _(block):
        at = pl.multiple_of(block * step, step)
        rows = rows_ref[pl.ds(at, step), :].astype(jnp.float32)
        normed[pl.ds(lead + at, step), :] = unit_rows(rows, gain)

    @pl.loop(0, count // step)
    def _(block):
        at = pl.multiple_of(block * step, step)
        window = normed[pl.ds(at, step + lead), :]
        here = window[lead:]
        total = conv_ref[0:1] * here
        for tap in range(1, taps):
            total = total + conv_ref[tap : tap + 1] * window[lead - tap : lead - tap + step]
        gated[pl.ds(at, step), :] = (total * jax.nn.sigmoid(here)).astype(jnp.bfloat16)

    rows = gated[...]
    for weight_ref, out_ref, factor in (
        (query_ref, queries_ref, scale),
        (key_ref, keys_ref, scale),
        (value_ref, values_ref, None),
    ):
        product = jnp.dot(rows, weight_ref[...], preferred_element_type=jnp.float32)
        if factor is not None:
            product = product * factor
        out_ref[...] = product.astype(jnp.bfloat16)


def project(rows, edge, mix_gain, conv_weight, query_weight, key_weight, value_weight, scale):
    count, width = rows.shape
    step = 32
    return kernel_call(
        functools.partial(project_body, step, scale),
        "project",
        tuple(like(count, w.shape[1], jnp.bfloat16) for w in (query_weight, key_weight, value_weight)),
        rows,
        edge,
        mix_gain[None],
        conv_weight,
        query_weight,
        key_weight,
        value_weight,
        scratch=(
            pltpu.VMEM((count + edge.shape[0], width), jnp.float32),
            pltpu.VMEM((count, width), jnp.bfloat16),
        ),
    )


def attend_body(
    feat_in,
    value_len,
    count_ref,
    rate_ref,
    queries_ref,
    keys_ref,
    values_ref,
    numer_ref,
    denom_ref,
    state_ref,
    norm_ref,
    turned,
    total,
    norms,
):
    heads, count = rate_ref.shape
    columns = values_ref.shape[1]
    lane = lax.broadcasted_iota(jnp.int32, (count, count), 1)
    row = lax.broadcasted_iota(jnp.int32, (count, count), 0)
    valid = (lane[:1] < count_ref[0]).astype(jnp.float32)
    rate = jnp.where(valid > 0, rate_ref[...], 0.0)
    upto = (row <= lane).astype(jnp.float32)
    across = jnp.dot(
        rate, upto, precision=lax.Precision.HIGHEST, preferred_element_type=jnp.float32
    )
    down = across.T
    closing = across[:, count - 1 : count]
    fading = jnp.exp(closing - across) * valid
    causal = row >= lane
    keys = keys_ref[...]
    turned[...] = keys.astype(jnp.float32).T
    owner = lax.broadcasted_iota(jnp.int32, queries_ref.shape, 1)
    spare = lax.broadcasted_iota(jnp.int32, (8, count), 0) == 0
    head_lane = lax.broadcasted_iota(jnp.int32, (count, 128), 1)
    numer_ref[...] = jnp.zeros(numer_ref.shape, jnp.float32)
    total[...] = jnp.zeros(total.shape, jnp.float32)
    norms[...] = jnp.zeros(norms.shape, jnp.float32)
    norm_total = jnp.zeros((total.shape[0], 128), jnp.float32)
    denominators = jnp.zeros((count, 128), jnp.float32)
    for h in range(heads):
        low = min(h * value_len // 128 * 128, max(columns - 256, 0))
        high = min(low + 256, columns)
        mine = lax.broadcasted_iota(jnp.int32, (count, high - low), 1) + low
        mine = (mine >= h * value_len) & (mine < (h + 1) * value_len)
        values = jnp.where(mine, values_ref[:, low:high].astype(jnp.float32), 0.0)
        values = values.astype(jnp.bfloat16)
        asks = (owner >= h * feat_in) & (owner < (h + 1) * feat_in)
        queries = jnp.where(asks, queries_ref[...].astype(jnp.float32), 0.0)
        scores = lax.dot_general(
            queries.astype(jnp.bfloat16), keys, NT, preferred_element_type=jnp.float32
        )
        gap = down[:, h : h + 1] - across[h : h + 1]
        weights = jnp.where(causal, jnp.exp(jnp.minimum(gap, 0.0)) * valid, 0.0)
        weights = weights * (1.0 + scores + 0.5 * scores * scores)
        numer_ref[:, low:high] += jnp.dot(
            weights.astype(jnp.bfloat16), values, preferred_element_type=jnp.float32
        )
        sums = jnp.sum(weights, axis=1, keepdims=True)
        denominators = jnp.where(head_lane == h, sums, denominators)
        own = turned[h * feat_in : (h + 1) * feat_in]
        fade = fading[h : h + 1]
        faded = own * fade
        scaled = faded * 0.5**0.5
        parts = [own[i : i + 1] * scaled for i in range(feat_in)]
        parts += [faded, jnp.where(spare, fade, 0.0)]
        feats = jnp.concatenate(parts, axis=0).astype(jnp.bfloat16)
        total[:, low:high] += jnp.dot(feats, values, preferred_element_type=jnp.float32)
        mark = (head_lane == h).astype(jnp.bfloat16)
        norm_total = norm_total + jnp.dot(feats, mark, preferred_element_type=jnp.float32)
    denom_ref[...] = denominators[:, :heads]
    pairs = feat_in * feat_in
    state_ref[0] = total[pairs + feat_in : pairs + feat_in + 1, :]
    for f in range(feat_in):
        state_ref[1 + f] = total[pairs + f : pairs + f + 1, :]

    @pl.loop(0, pairs // 8)
    def _(block):
        for k in range(8):
            f = block * 8 + k
            state_ref[1 + feat_in + f] = total[pl.ds(f, 1), :]

    norms[0:1, :] = norm_total[pairs + feat_in : pairs + feat_in + 1]
    norms[1 : 1 + feat_in, :] = norm_total[pairs : pairs + feat_in]
    norms[1 + feat_in : 1 + feat_in + pairs, :] = norm_total[:pairs]
    norm_ref[...] = norms[...].T[:heads, : 1 + feat_in + pairs]


def attend(valid_count, rate, queries, keys, values, feat_in, value_len):
    heads, count = rate.shape
    columns = values.shape[1]
    feat_len = 1 + feat_in + feat_in * feat_in
    padded = feat_in * feat_in + feat_in + 8
    return kernel_call(
        functools.partial(attend_body, feat_in, value_len),
        "attend",
        (
            like(count, columns, jnp.float32),
            like(count, heads, jnp.float32),
            jax.ShapeDtypeStruct((feat_len, 1, columns), jnp.float32),
            like(heads, feat_len, jnp.float32),
        ),
        valid_count,
        rate,
        queries,
        keys,
        values,
        specs=[pl.BlockSpec(memory_space=pltpu.SMEM)] + vmem(4),
        scratch=(
            pltpu.VMEM((queries.shape[1], count), jnp.float32),
            pltpu.VMEM((padded, columns), jnp.float32),
            pltpu.VMEM(((feat_len + 127) // 128 * 128, 128), jnp.float32),
        ),
    )


def mix_body(
    value_len, step, numer_ref, denom_ref, rows_ref, out_ref, gain_ref, mixed_ref, mlp_ref, sums
):
    count, columns = numer_ref.shape
    heads = denom_ref.shape[1]
    column = lax.broadcasted_iota(jnp.int32, (1, columns), 1)
    inverse = 1.0 / denom_ref[...]
    spread = jnp.zeros((count, columns), jnp.float32)
    for h in range(heads):
        here = (column >= h * value_len) & (column < (h + 1) * value_len)
        spread = jnp.where(here, inverse[:, h : h + 1], spread)
    attended = (numer_ref[...] * spread).astype(jnp.bfloat16)
    sums[...] = jnp.dot(attended, out_ref[...], preferred_element_type=jnp.float32)
    gain = gain_ref[...]

    @pl.loop(0, count // step)
    def _(block):
        at = pl.ds(pl.multiple_of(block * step, step), step)
        mixed = (rows_ref[at, :].astype(jnp.float32) + sums[at, :]).astype(jnp.bfloat16)
        mixed_ref[at, :] = mixed
        mlp_ref[at, :] = unit_rows(mixed.astype(jnp.float32), gain).astype(jnp.bfloat16)


def mix(numer, denom, rows, out_weight, mlp_gain, value_len):
    count, width = rows.shape
    shape = like(count, width, jnp.bfloat16)
    return kernel_call(
        functools.partial(mix_body, value_len, 32),
        "mix",
        (shape, shape),
        numer,
        denom,
        rows,
        out_weight,
        mlp_gain[None],
        scratch=(pltpu.VMEM((count, width), jnp.float32),),
    )


def swiglu_terms(rows, gate_rows, up_rows, down_rows):
    gate_act = lax.dot_general(rows, gate_rows, NT, preferred_element_type=jnp.float32)
    up_act = lax.dot_general(rows, up_rows, NT, preferred_element_type=jnp.float32)
    hidden_units = (gate_act * jax.nn.sigmoid(gate_act) * up_act).astype(jnp.bfloat16)
    return jnp.dot(hidden_units, down_rows, preferred_element_type=jnp.float32)


def on_grid(run):
    return all(low % 16 == 0 and high % 16 == 0 for _, low, high in run)


def read_units(refs, units):
    parts = []
    for k in range(3):
        rows = [refs[run[k][0]][run[k][1] : run[k][2]] for run in units if on_grid(run)]
        rest = [
            refs[run[k][0]][...].astype(jnp.float32)[run[k][1] : run[k][2]]
            for run in units
            if not on_grid(run)
        ]
        if rest:
            rows.append(jnp.concatenate(rest, axis=0).astype(jnp.bfloat16))
        parts.append(jnp.concatenate(rows, axis=0))
    return parts


def accumulate_body(units, n_weights, n_rows, n_acc, residual, *refs):
    weights = refs[:n_weights]
    rows = refs[n_weights : n_weights + n_rows]
    acc = refs[n_weights + n_rows : n_weights + n_rows + n_acc]
    parts = read_units(weights, units)
    for k, rows_ref in enumerate(rows):
        out_ref = refs[len(refs) - n_rows + k]
        terms = swiglu_terms(rows_ref[...], *parts)
        if n_acc:
            terms = terms + acc[k][...]
        if residual:
            terms = terms + refs[n_weights + n_rows + n_acc][...].astype(jnp.float32)
        out_ref[...] = terms.astype(out_ref.dtype)


def accumulate(rows, weights, units, acc, dtype, name, residual=None):
    shapes = tuple(like(*array.shape, dtype) for array in rows)
    start = len(weights) + len(rows)
    aliases = {start + k: k for k in range(len(acc))} if dtype == jnp.float32 else {}
    extra = () if residual is None else (residual,)
    body = functools.partial(
        accumulate_body, tuple(units), len(weights), len(rows), len(acc), bool(extra)
    )
    return kernel_call(body, name, shapes, *weights, *rows, *acc, *extra, aliases=aliases)


def runs(which, low, size):
    return tuple((which, low + k * size, low + (k + 1) * size) for k in range(3))


def split_runs(first, second, main):
    (i, at), (j, then) = first, second
    held = 2 * main // 3
    rest = main - held
    return (
        ((i, at, at + held), (i, at + main, at + main + held), (j, then + rest, then + main)),
        ((i, at + held, at + main), (j, then, then + rest), (j, then + main, then + rest + main)),
    )


def collect_body(plans, *refs):
    outs = refs[len(refs) - len(plans) :]
    for out_ref, plan in zip(outs, plans):
        rows = [refs[i][...].astype(jnp.float32)[low:high] for i, low, high in plan]
        out_ref[...] = jnp.concatenate(rows, axis=0).astype(jnp.bfloat16)


def collect(arrays, plans, name):
    columns = arrays[0].shape[1]
    shapes = tuple(like(sum(h - l for _, l, h in plan), columns, jnp.bfloat16) for plan in plans)
    return kernel_call(functools.partial(collect_body, plans), name, shapes, *arrays)


def shard_body(main, gate_ref, up_ref, down_ref, shard_ref, main_ref, *rest):
    buffers, sems = rest[:3], rest[3]
    copies = [
        pltpu.make_async_copy(source, buffer, sems.at[k])
        for k, (source, buffer) in enumerate(zip((gate_ref, up_ref, down_ref), buffers))
    ]
    for copy in copies:
        copy.start()
    for copy in copies:
        copy.wait()
    arrays = [buffer[...].astype(jnp.float32) for buffer in buffers]
    tops = [array[:main] for array in arrays]
    ends = [array[main:] for array in arrays]
    shard_ref[...] = jnp.concatenate(tops + ends, axis=0).astype(jnp.bfloat16)
    main_ref[...] = jnp.concatenate(tops, axis=0).astype(jnp.bfloat16)


def final_body(step, count_ref, kept_ref, given_ref, out_ref):
    count = kept_ref.shape[0]

    @pl.loop(0, count // step)
    def _(block):
        first = pl.multiple_of(block * step, step)
        at = pl.ds(first, step)
        total = kept_ref[at, :] + given_ref[at, :].astype(jnp.float32)
        row = lax.broadcasted_iota(jnp.int32, total.shape, 0) + first
        out_ref[at, :] = jnp.where(row < count_ref[0], total, 0.0).astype(out_ref.dtype)


def local(
    hidden_in,
    lengths,
    log_decay,
    mix_gain,
    conv_weight,
    query_weight,
    key_weight,
    value_weight,
    out_weight,
    mlp_gain,
    gate_weight,
    up_weight,
    down_weight,
):
    local_len = hidden_in.shape[1]
    rows_in = hidden_in[0]
    decays = log_decay[0]
    head_count = log_decay.shape[2]
    value_len = value_weight.shape[1] // head_count
    feat_in = query_weight.shape[1] // head_count
    feature_scale = feat_in ** (-0.25)
    valid_count = lengths - lax.axis_index("seq") * local_len
    spans = lax.axis_size("seq")
    units, model = gate_weight.shape[1], gate_weight.shape[0]
    edge = units // 7
    main = units - edge
    wide = 3 * main
    full = 3 * units
    narrow = full - wide
    cut = main + 2 * main // 3

    shard, shard_main = kernel_call(
        functools.partial(shard_body, main),
        "shard",
        (like(full, model, jnp.bfloat16), like(wide, model, jnp.bfloat16)),
        gate_weight.T,
        up_weight.T,
        down_weight.T,
        specs=[pl.BlockSpec(memory_space=pl.ANY)] * 3,
        scratch=[pltpu.VMEM((units, model), jnp.bfloat16)] * 3 + [pltpu.SemaphoreType.DMA((3,))],
        mib=56,
    )
    near, far, deep = slot((flip_near, shard), (flip_far, shard), (next_plane, shard_main))

    lead = 16
    if spans > 1:
        edge_in = from_behind(rows_in[local_len - lead :], "seq", 1)
    else:
        edge_in = jnp.zeros((lead, model), jnp.bfloat16)
    queries, key_rows, values = project(
        rows_in, edge_in, mix_gain, conv_weight, query_weight, key_weight, value_weight, feature_scale
    )
    near, far, deep, queries, key_rows, values = together(
        near, far, deep, queries, key_rows, values
    )

    sends = collect(
        (shard, near, far, deep),
        (
            ((3, 0, wide), (2, 0, cut)),
            ((3, 0, wide), (1, cut, full)),
            ((3, 0, wide), (0, wide, full), (1, wide, full), (2, wide, full)),
        ),
        "collect_second",
    )
    near1, far1, deep1 = slot(*zip((flip_near, flip_far, next_plane), sends))

    numerator, denominator, end_state, end_norm = attend(
        valid_count, log_decay[0].T, queries, key_rows, values, feat_in, value_len
    )
    if spans > 1:
        positions = jnp.arange(local_len, dtype=jnp.int32)
        numerator, denominator, end_state, end_norm = carry_in(
            (positions < valid_count).astype(jnp.float32),
            decays,
            queries,
            numerator,
            denominator,
            end_state[:, 0],
            end_norm.T,
        )
    else:
        end_norm = end_norm.T
    mixed_rows, mlp_in = mix(numerator, denominator, rows_in, out_weight, mlp_gain, value_len)
    near1, far1, deep1, mixed_rows, mlp_in, end_state, end_norm = together(
        near1, far1, deep1, mixed_rows, mlp_in, end_state, end_norm
    )

    sends = collect(
        (near1, far1, deep1),
        (
            ((2, 0, wide), (1, 0, cut)),
            ((2, 0, wide), (0, cut, wide)),
            ((2, 0, wide + 3 * narrow), (1, wide + wide - cut, wide + full - cut)),
        ),
        "collect_third",
    )
    near2, far2, deep2 = slot(*zip((flip_near, flip_far, next_plane), sends))
    rows = (mlp_in, flip_core(mlp_in))
    acc = accumulate(
        rows,
        (shard, near, far, deep, near1, far1, deep1),
        [runs(i, 0, main) for i in range(7)] + list(split_runs((4, wide), (5, wide), main)),
        (),
        jnp.float32,
        "accumulate_second",
    )
    near2, far2, deep2 = together(near2, far2, deep2)

    deep3_main, line = collect(
        (far2, deep2),
        (
            ((1, 0, wide),),
            ((1, wide, wide + 4 * narrow), (0, wide + wide - cut - main, wide + wide - cut)),
        ),
        "collect_fourth",
    )
    near3, far3, deep3 = slot((flip_near, deep3_main), (flip_far, deep3_main), (next_plane, line))
    acc = accumulate(
        rows,
        (shard, near, far, far1, deep1, near2, far2, deep2),
        [runs(i, 0, main) for i in (5, 6, 7)]
        + list(split_runs((5, wide), (6, wide), main))
        + [runs(i, wide, edge) for i in (0, 1, 2)]
        + [runs(3, wide + wide - cut, edge)]
        + [runs(4, wide + k * narrow, edge) for k in range(3)]
        + [runs(7, wide + k * narrow, edge) for k in range(4)],
        tuple(acc),
        jnp.float32,
        "accumulate_third",
    )
    near3, far3, deep3, *acc = together(near3, far3, deep3, *acc)

    sends = collect(
        (near2, far2, near3, far3, deep3),
        (
            ((1, 0, main), (3, 0, main)),
            ((0, main, 2 * main), (2, main, 2 * main)),
            ((4, 3 * narrow, 4 * narrow + main),),
        ),
        "collect_fifth",
    )
    near4, far4, deep4 = slot(*zip((flip_near, flip_far, next_plane), sends))
    acc = accumulate(
        rows,
        (near3, far3, deep3),
        [runs(0, 0, main), runs(1, 0, main)] + [runs(2, k * narrow, edge) for k in range(4)],
        tuple(acc),
        jnp.float32,
        "accumulate_fourth",
    )
    weights = (near4, far4, deep3, deep4)
    last = [
        ((0, 0, main), (1, 0, main), (2, 4 * narrow, 4 * narrow + main)),
        ((0, main, 2 * main), (1, main, 2 * main), (3, narrow, narrow + main)),
        runs(3, 0, edge),
    ]
    (given,) = accumulate(rows[1:], weights, last, acc[1:], jnp.bfloat16, "finish_other")
    (kept,) = accumulate(
        rows[:1], weights, last, acc[:1], jnp.float32, "finish_own", residual=mixed_rows
    )
    result = kernel_call(
        functools.partial(final_body, 64),
        "final",
        like(local_len, model, jnp.bfloat16),
        valid_count,
        kept,
        flip_core(given),
        specs=[pl.BlockSpec(memory_space=pltpu.SMEM)] + vmem(2),
    )
    return (
        result[None],
        end_state.reshape((1, 1) + end_state.shape[:1] + end_state.shape[-1:]),
        end_norm[None, None],
    )


def solution(mesh):
    return jax.shard_map(
        local,
        mesh=mesh,
        in_specs=(
            P("req", "seq", None),
            P("req"),
            P("req", "seq", None),
            P(),
            P(),
            P(),
            P(),
            P(),
            P(),
            P(),
            P(None, "req"),
            P(None, "req"),
            P(None, "req"),
        ),
        out_specs=(P("req", "seq", None), P("req", "seq", None, None), P("req", "seq", None, None)),
        check_vma=False,
    )
```

```python
import functools

import jax
import jax.numpy as jnp
from jax import lax
from jax.experimental import pallas as pl
from jax.experimental.pallas import tpu as pltpu
from jax.sharding import PartitionSpec as P


def from_behind(array, axis, by):
    count = lax.axis_size(axis)
    pairs = [(i, i + by) for i in range(count) if 0 <= i + by < count]
    return lax.ppermute(array, axis, pairs)


def entering(array, axis, combine, identity):
    count, here = (lax.axis_size(axis), lax.axis_index(axis))
    everything = jax.tree.map(
        lambda part, kind: lax.all_gather(part.astype(kind), axis),
        array,
        (jnp.bfloat16, jnp.bfloat16, jnp.bfloat16),
    )
    start = jax.tree.map(
        lambda part, zero: jnp.broadcast_to(jnp.asarray(zero, part.dtype), part.shape),
        array,
        identity,
    )

    def hop(k, before):
        reached = k < here
        new = combine(
            before, jax.tree.map(lambda part, own: part[k].astype(own.dtype), everything, array)
        )
        return jax.tree.map(lambda a, b: jnp.where(reached, a, b), new, before)

    return lax.fori_loop(0, count, hop, start)


def features(vectors):
    constant = jnp.ones(vectors.shape[:-1] + (1,), jnp.float32)
    width = vectors.shape[-1]
    squares = (vectors[..., :, None] * vectors[..., None, :]).reshape(
        vectors.shape[:-1] + (width * width,)
    )
    return jnp.concatenate([constant, vectors, squares * 0.5**0.5], axis=-1)


def carry_in(valid_mask, decays, queries, numerator, denominator, flat_memory, key_sum):
    local_len = numerator.shape[0]
    feat_len, head_count = key_sum.shape
    value_len = flat_memory.shape[1] // head_count
    feat_in = queries.shape[1] // head_count
    decay_rate = jnp.where(valid_mask[:, None] > 0, decays, 0.0)
    span_decay = jnp.sum(decay_rate, axis=0)

    def merge_states(earlier, later):
        factor = jnp.exp(later[0])
        return (
            earlier[0] + later[0],
            earlier[1] * jnp.repeat(factor, value_len)[None, :] + later[1],
            earlier[2] * factor[None, :] + later[2],
        )

    neutral = (jnp.zeros_like(span_decay), jnp.zeros_like(flat_memory), jnp.zeros_like(key_sum))
    carried = entering((span_decay, flat_memory, key_sum), "seq", merge_states, neutral)
    prior_memory = carried[1]
    prior_keys = carried[2]
    highest = lax.Precision.HIGHEST
    growth = jnp.exp(jnp.cumsum(decay_rate, axis=0))
    query_feat = features(queries.astype(jnp.float32).reshape(local_len, head_count, feat_in))
    added = jnp.einsum(
        "thf,fhv->thv",
        query_feat,
        prior_memory.reshape(feat_len, head_count, value_len),
        precision=highest,
    )
    numerator = numerator + (added * growth[:, :, None]).reshape(local_len, -1)
    denominator = (
        denominator + jnp.einsum("thf,fh->th", query_feat, prior_keys, precision=highest) * growth
    )
    span_factor = jnp.exp(span_decay)
    end_state = prior_memory * jnp.repeat(span_factor, value_len)[None, :] + flat_memory
    end_norm = prior_keys * span_factor[None, :] + key_sum
    return numerator, denominator, end_state, end_norm


def permute(array, target):
    count = lax.axis_size("req")
    return lax.ppermute(array, "req", [(i, target(i)) for i in range(count)])


def flip_core(array):
    return permute(array, lambda i: i ^ 1)


def flip_near(array):
    return permute(array, lambda i: i ^ 2)


def flip_far(array):
    return permute(array, lambda i: i ^ 4)


def next_plane(array):
    count = lax.axis_size("req")
    return permute(array, lambda i: (i + 8) % count)


def together(*arrays):
    return lax.optimization_barrier(arrays)


def slot(*sends):
    operands = together(*[array for _, array in sends])
    return together(*[send(array) for (send, _), array in zip(sends, operands)])


def vmem(count):
    return [pl.BlockSpec(memory_space=pltpu.VMEM)] * count


def kernel_call(body, name, out_shape, *operands, scratch=(), aliases=None, specs=None, mib=24):
    many = isinstance(out_shape, tuple)
    return pl.pallas_call(
        body,
        out_shape=out_shape,
        in_specs=specs or vmem(len(operands)),
        out_specs=tuple(vmem(len(out_shape))) if many else vmem(1)[0],
        scratch_shapes=list(scratch),
        input_output_aliases=aliases or {},
        compiler_params=pltpu.CompilerParams(vmem_limit_bytes=mib * 1024 * 1024),
        cost_estimate=pl.CostEstimate(flops=1000, bytes_accessed=1000, transcendentals=0),
        name=name,
    )(*operands)


def like(rows, columns, dtype):
    return jax.ShapeDtypeStruct((rows, columns), dtype)


NT = (((1,), (1,)), ((), ()))


def unit_rows(rows, gain):
    factor = lax.rsqrt(jnp.mean(rows * rows, axis=-1, keepdims=True) + 1e-05)
    return (rows * factor * gain).astype(jnp.bfloat16).astype(jnp.float32)


def project_body(
    step,
    scale,
    rows_ref,
    edge_ref,
    gain_ref,
    conv_ref,
    query_ref,
    key_ref,
    value_ref,
    queries_ref,
    keys_ref,
    values_ref,
    normed,
    gated,
):
    gain = gain_ref[...]
    count = rows_ref.shape[0]
    lead = edge_ref.shape[0]
    taps = conv_ref.shape[0]
    normed[:lead] = unit_rows(edge_ref[...].astype(jnp.float32), gain)

    @pl.loop(0, count // step)
    def _(block):
        at = pl.multiple_of(block * step, step)
        rows = rows_ref[pl.ds(at, step), :].astype(jnp.float32)
        normed[pl.ds(lead + at, step), :] = unit_rows(rows, gain)

    @pl.loop(0, count // step)
    def _(block):
        at = pl.multiple_of(block * step, step)
        window = normed[pl.ds(at, step + lead), :]
        here = window[lead:]
        total = conv_ref[0:1] * here
        for tap in range(1, taps):
            total = total + conv_ref[tap : tap + 1] * window[lead - tap : lead - tap + step]
        gated[pl.ds(at, step), :] = (total * jax.nn.sigmoid(here)).astype(jnp.bfloat16)

    rows = gated[...]
    for weight_ref, out_ref, factor in (
        (query_ref, queries_ref, scale),
        (key_ref, keys_ref, scale),
        (value_ref, values_ref, None),
    ):
        product = jnp.dot(rows, weight_ref[...], preferred_element_type=jnp.float32)
        if factor is not None:
            product = product * factor
        out_ref[...] = product.astype(jnp.bfloat16)


def project(rows, edge, mix_gain, conv_weight, query_weight, key_weight, value_weight, scale):
    count, width = rows.shape
    step = 32
    return kernel_call(
        functools.partial(project_body, step, scale),
        "project",
        tuple(like(count, w.shape[1], jnp.bfloat16) for w in (query_weight, key_weight, value_weight)),
        rows,
        edge,
        mix_gain[None],
        conv_weight,
        query_weight,
        key_weight,
        value_weight,
        scratch=(
            pltpu.VMEM((count + edge.shape[0], width), jnp.float32),
            pltpu.VMEM((count, width), jnp.bfloat16),
        ),
    )


def attend_body(
    feat_in,
    value_len,
    count_ref,
    rate_ref,
    queries_ref,
    keys_ref,
    values_ref,
    numer_ref,
    denom_ref,
    state_ref,
    norm_ref,
    turned,
    total,
    norms,
):
    heads, count = rate_ref.shape
    columns = values_ref.shape[1]
    lane = lax.broadcasted_iota(jnp.int32, (count, count), 1)
    row = lax.broadcasted_iota(jnp.int32, (count, count), 0)
    valid = (lane[:1] < count_ref[0]).astype(jnp.float32)
    rate = jnp.where(valid > 0, rate_ref[...], 0.0)
    upto = (row <= lane).astype(jnp.float32)
    across = jnp.dot(
        rate, upto, precision=lax.Precision.HIGHEST, preferred_element_type=jnp.float32
    )
    down = across.T
    closing = across[:, count - 1 : count]
    fading = jnp.exp(closing - across) * valid
    causal = row >= lane
    keys = keys_ref[...]
    turned[...] = keys.astype(jnp.float32).T
    owner = lax.broadcasted_iota(jnp.int32, queries_ref.shape, 1)
    spare = lax.broadcasted_iota(jnp.int32, (8, count), 0) == 0
    head_lane = lax.broadcasted_iota(jnp.int32, (count, 128), 1)
    numer_ref[...] = jnp.zeros(numer_ref.shape, jnp.float32)
    total[...] = jnp.zeros(total.shape, jnp.float32)
    norms[...] = jnp.zeros(norms.shape, jnp.float32)
    norm_total = jnp.zeros((total.shape[0], 128), jnp.float32)
    denominators = jnp.zeros((count, 128), jnp.float32)
    for h in range(heads):
        low = min(h * value_len // 128 * 128, max(columns - 256, 0))
        high = min(low + 256, columns)
        mine = lax.broadcasted_iota(jnp.int32, (count, high - low), 1) + low
        mine = (mine >= h * value_len) & (mine < (h + 1) * value_len)
        values = jnp.where(mine, values_ref[:, low:high].astype(jnp.float32), 0.0)
        values = values.astype(jnp.bfloat16)
        asks = (owner >= h * feat_in) & (owner < (h + 1) * feat_in)
        queries = jnp.where(asks, queries_ref[...].astype(jnp.float32), 0.0)
        scores = lax.dot_general(
            queries.astype(jnp.bfloat16), keys, NT, preferred_element_type=jnp.float32
        )
        gap = down[:, h : h + 1] - across[h : h + 1]
        weights = jnp.where(causal, jnp.exp(jnp.minimum(gap, 0.0)) * valid, 0.0)
        weights = weights * (1.0 + scores + 0.5 * scores * scores)
        numer_ref[:, low:high] += jnp.dot(
            weights.astype(jnp.bfloat16), values, preferred_element_type=jnp.float32
        )
        sums = jnp.sum(weights, axis=1, keepdims=True)
        denominators = jnp.where(head_lane == h, sums, denominators)
        own = turned[h * feat_in : (h + 1) * feat_in]
        fade = fading[h : h + 1]
        faded = own * fade
        scaled = faded * 0.5**0.5
        parts = [own[i : i + 1] * scaled for i in range(feat_in)]
        parts += [faded, jnp.where(spare, fade, 0.0)]
        feats = jnp.concatenate(parts, axis=0).astype(jnp.bfloat16)
        total[:, low:high] += jnp.dot(feats, values, preferred_element_type=jnp.float32)
        mark = (head_lane == h).astype(jnp.bfloat16)
        norm_total = norm_total + jnp.dot(feats, mark, preferred_element_type=jnp.float32)
    denom_ref[...] = denominators[:, :heads]
    pairs = feat_in * feat_in
    state_ref[0] = total[pairs + feat_in : pairs + feat_in + 1, :]
    for f in range(feat_in):
        state_ref[1 + f] = total[pairs + f : pairs + f + 1, :]

    @pl.loop(0, pairs // 8)
    def _(block):
        for k in range(8):
            f = block * 8 + k
            state_ref[1 + feat_in + f] = total[pl.ds(f, 1), :]

    norms[0:1, :] = norm_total[pairs + feat_in : pairs + feat_in + 1]
    norms[1 : 1 + feat_in, :] = norm_total[pairs : pairs + feat_in]
    norms[1 + feat_in : 1 + feat_in + pairs, :] = norm_total[:pairs]
    norm_ref[...] = norms[...].T[:heads, : 1 + feat_in + pairs]


def attend(valid_count, rate, queries, keys, values, feat_in, value_len):
    heads, count = rate.shape
    columns = values.shape[1]
    feat_len = 1 + feat_in + feat_in * feat_in
    padded = feat_in * feat_in + feat_in + 8
    return kernel_call(
        functools.partial(attend_body, feat_in, value_len),
        "attend",
        (
            like(count, columns, jnp.float32),
            like(count, heads, jnp.float32),
            jax.ShapeDtypeStruct((feat_len, 1, columns), jnp.float32),
            like(heads, feat_len, jnp.float32),
        ),
        valid_count,
        rate,
        queries,
        keys,
        values,
        specs=[pl.BlockSpec(memory_space=pltpu.SMEM)] + vmem(4),
        scratch=(
            pltpu.VMEM((queries.shape[1], count), jnp.float32),
            pltpu.VMEM((padded, columns), jnp.float32),
            pltpu.VMEM(((feat_len + 127) // 128 * 128, 128), jnp.float32),
        ),
    )


def mix_body(
    value_len, step, numer_ref, denom_ref, rows_ref, out_ref, gain_ref, mixed_ref, mlp_ref, sums
):
    count, columns = numer_ref.shape
    heads = denom_ref.shape[1]
    column = lax.broadcasted_iota(jnp.int32, (1, columns), 1)
    inverse = 1.0 / denom_ref[...]
    spread = jnp.zeros((count, columns), jnp.float32)
    for h in range(heads):
        here = (column >= h * value_len) & (column < (h + 1) * value_len)
        spread = jnp.where(here, inverse[:, h : h + 1], spread)
    attended = (numer_ref[...] * spread).astype(jnp.bfloat16)
    sums[...] = jnp.dot(attended, out_ref[...], preferred_element_type=jnp.float32)
    gain = gain_ref[...]

    @pl.loop(0, count // step)
    def _(block):
        at = pl.ds(pl.multiple_of(block * step, step), step)
        mixed = (rows_ref[at, :].astype(jnp.float32) + sums[at, :]).astype(jnp.bfloat16)
        mixed_ref[at, :] = mixed
        mlp_ref[at, :] = unit_rows(mixed.astype(jnp.float32), gain).astype(jnp.bfloat16)


def mix(numer, denom, rows, out_weight, mlp_gain, value_len):
    count, width = rows.shape
    shape = like(count, width, jnp.bfloat16)
    return kernel_call(
        functools.partial(mix_body, value_len, 32),
        "mix",
        (shape, shape),
        numer,
        denom,
        rows,
        out_weight,
        mlp_gain[None],
        scratch=(pltpu.VMEM((count, width), jnp.float32),),
    )


def swiglu_terms(rows, gate_rows, up_rows, down_rows):
    gate_act = lax.dot_general(rows, gate_rows, NT, preferred_element_type=jnp.float32)
    up_act = lax.dot_general(rows, up_rows, NT, preferred_element_type=jnp.float32)
    hidden_units = (gate_act * jax.nn.sigmoid(gate_act) * up_act).astype(jnp.bfloat16)
    return jnp.dot(hidden_units, down_rows, preferred_element_type=jnp.float32)


def on_grid(run):
    return all(low % 16 == 0 and high % 16 == 0 for _, low, high in run)


def read_units(refs, units):
    parts = []
    for k in range(3):
        rows = [refs[run[k][0]][run[k][1] : run[k][2]] for run in units if on_grid(run)]
        rest = [
            refs[run[k][0]][...].astype(jnp.float32)[run[k][1] : run[k][2]]
            for run in units
            if not on_grid(run)
        ]
        if rest:
            rows.append(jnp.concatenate(rest, axis=0).astype(jnp.bfloat16))
        parts.append(jnp.concatenate(rows, axis=0))
    return parts


def accumulate_body(units, n_weights, n_rows, n_acc, residual, *refs):
    weights = refs[:n_weights]
    rows = refs[n_weights : n_weights + n_rows]
    acc = refs[n_weights + n_rows : n_weights + n_rows + n_acc]
    parts = read_units(weights, units)
    for k, rows_ref in enumerate(rows):
        out_ref = refs[len(refs) - n_rows + k]
        terms = swiglu_terms(rows_ref[...], *parts)
        if n_acc:
            terms = terms + acc[k][...]
        if residual:
            terms = terms + refs[n_weights + n_rows + n_acc][...].astype(jnp.float32)
        out_ref[...] = terms.astype(out_ref.dtype)


def accumulate(rows, weights, units, acc, dtype, name, residual=None):
    shapes = tuple(like(*array.shape, dtype) for array in rows)
    start = len(weights) + len(rows)
    aliases = {start + k: k for k in range(len(acc))} if dtype == jnp.float32 else {}
    extra = () if residual is None else (residual,)
    body = functools.partial(
        accumulate_body, tuple(units), len(weights), len(rows), len(acc), bool(extra)
    )
    return kernel_call(body, name, shapes, *weights, *rows, *acc, *extra, aliases=aliases)


def runs(which, low, size):
    return tuple((which, low + k * size, low + (k + 1) * size) for k in range(3))


def split_runs(first, second, main):
    (i, at), (j, then) = first, second
    held = 2 * main // 3
    rest = main - held
    return (
        ((i, at, at + held), (i, at + main, at + main + held), (j, then + rest, then + main)),
        ((i, at + held, at + main), (j, then, then + rest), (j, then + main, then + rest + main)),
    )


def collect_body(plans, *refs):
    outs = refs[len(refs) - len(plans) :]
    for out_ref, plan in zip(outs, plans):
        rows = [refs[i][...].astype(jnp.float32)[low:high] for i, low, high in plan]
        out_ref[...] = jnp.concatenate(rows, axis=0).astype(jnp.bfloat16)


def collect(arrays, plans, name):
    columns = arrays[0].shape[1]
    shapes = tuple(like(sum(h - l for _, l, h in plan), columns, jnp.bfloat16) for plan in plans)
    return kernel_call(functools.partial(collect_body, plans), name, shapes, *arrays)


def shard_body(main, gate_ref, up_ref, down_ref, shard_ref, main_ref, *rest):
    buffers, sems = rest[:3], rest[3]
    copies = [
        pltpu.make_async_copy(source, buffer, sems.at[k])
        for k, (source, buffer) in enumerate(zip((gate_ref, up_ref, down_ref), buffers))
    ]
    for copy in copies:
        copy.start()
    for copy in copies:
        copy.wait()
    arrays = [buffer[...].astype(jnp.float32) for buffer in buffers]
    tops = [array[:main] for array in arrays]
    ends = [array[main:] for array in arrays]
    shard_ref[...] = jnp.concatenate(tops + ends, axis=0).astype(jnp.bfloat16)
    main_ref[...] = jnp.concatenate(tops, axis=0).astype(jnp.bfloat16)


def final_body(step, count_ref, kept_ref, given_ref, out_ref):
    count = kept_ref.shape[0]

    @pl.loop(0, count // step)
    def _(block):
        first = pl.multiple_of(block * step, step)
        at = pl.ds(first, step)
        total = kept_ref[at, :] + given_ref[at, :].astype(jnp.float32)
        row = lax.broadcasted_iota(jnp.int32, total.shape, 0) + first
        out_ref[at, :] = jnp.where(row < count_ref[0], total, 0.0).astype(out_ref.dtype)


def local(
    hidden_in,
    lengths,
    log_decay,
    mix_gain,
    conv_weight,
    query_weight,
    key_weight,
    value_weight,
    out_weight,
    mlp_gain,
    gate_weight,
    up_weight,
    down_weight,
):
    local_len = hidden_in.shape[1]
    rows_in = hidden_in[0]
    decays = log_decay[0]
    head_count = log_decay.shape[2]
    value_len = value_weight.shape[1] // head_count
    feat_in = query_weight.shape[1] // head_count
    feature_scale = feat_in ** (-0.25)
    valid_count = lengths - lax.axis_index("seq") * local_len
    spans = lax.axis_size("seq")
    units, model = gate_weight.shape[1], gate_weight.shape[0]
    edge = units // 7
    main = units - edge
    wide = 3 * main
    full = 3 * units
    narrow = full - wide
    cut = main + 2 * main // 3

    shard, shard_main = kernel_call(
        functools.partial(shard_body, main),
        "shard",
        (like(full, model, jnp.bfloat16), like(wide, model, jnp.bfloat16)),
        gate_weight.T,
        up_weight.T,
        down_weight.T,
        specs=[pl.BlockSpec(memory_space=pl.ANY)] * 3,
        scratch=[pltpu.VMEM((units, model), jnp.bfloat16)] * 3 + [pltpu.SemaphoreType.DMA((3,))],
        mib=56,
    )
    near, far, deep = slot((flip_near, shard), (flip_far, shard), (next_plane, shard_main))

    lead = 16
    if spans > 1:
        edge_in = from_behind(rows_in[local_len - lead :], "seq", 1)
    else:
        edge_in = jnp.zeros((lead, model), jnp.bfloat16)
    queries, key_rows, values = project(
        rows_in, edge_in, mix_gain, conv_weight, query_weight, key_weight, value_weight, feature_scale
    )
    near, far, deep, queries, key_rows, values = together(
        near, far, deep, queries, key_rows, values
    )

    sends = collect(
        (shard, near, far, deep),
        (
            ((3, 0, wide), (2, 0, cut)),
            ((3, 0, wide), (1, cut, full)),
            ((3, 0, wide), (0, wide, full), (1, wide, full), (2, wide, full)),
        ),
        "collect_second",
    )
    near1, far1, deep1 = slot(*zip((flip_near, flip_far, next_plane), sends))

    numerator, denominator, end_state, end_norm = attend(
        valid_count, log_decay[0].T, queries, key_rows, values, feat_in, value_len
    )
    if spans > 1:
        positions = jnp.arange(local_len, dtype=jnp.int32)
        numerator, denominator, end_state, end_norm = carry_in(
            (positions < valid_count).astype(jnp.float32),
            decays,
            queries,
            numerator,
            denominator,
            end_state[:, 0],
            end_norm.T,
        )
    else:
        end_norm = end_norm.T
    mixed_rows, mlp_in = mix(numerator, denominator, rows_in, out_weight, mlp_gain, value_len)
    near1, far1, deep1, mixed_rows, mlp_in, end_state, end_norm = together(
        near1, far1, deep1, mixed_rows, mlp_in, end_state, end_norm
    )

    sends = collect(
        (near1, far1, deep1),
        (
            ((2, 0, wide), (1, 0, cut)),
            ((2, 0, wide), (0, cut, wide)),
            ((2, 0, wide + 3 * narrow), (1, wide + wide - cut, wide + full - cut)),
        ),
        "collect_third",
    )
    near2, far2, deep2 = slot(*zip((flip_near, flip_far, next_plane), sends))
    rows = (mlp_in, flip_core(mlp_in))
    acc = accumulate(
        rows,
        (shard, near, far, deep, near1, far1, deep1),
        [runs(i, 0, main) for i in range(7)] + list(split_runs((4, wide), (5, wide), main)),
        (),
        jnp.float32,
        "accumulate_second",
    )
    near2, far2, deep2 = together(near2, far2, deep2)

    deep3_main, line = collect(
        (far2, deep2),
        (
            ((1, 0, wide),),
            ((1, wide, wide + 4 * narrow), (0, wide + wide - cut - main, wide + wide - cut)),
        ),
        "collect_fourth",
    )
    near3, far3, deep3 = slot((flip_near, deep3_main), (flip_far, deep3_main), (next_plane, line))
    acc = accumulate(
        rows,
        (shard, near, far, far1, deep1, near2, far2, deep2),
        [runs(i, 0, main) for i in (5, 6, 7)]
        + list(split_runs((5, wide), (6, wide), main))
        + [runs(i, wide, edge) for i in (0, 1, 2)]
        + [runs(3, wide + wide - cut, edge)]
        + [runs(4, wide + k * narrow, edge) for k in range(3)]
        + [runs(7, wide + k * narrow, edge) for k in range(4)],
        tuple(acc),
        jnp.float32,
        "accumulate_third",
    )
    near3, far3, deep3, *acc = together(near3, far3, deep3, *acc)

    held = 2 * main // 3
    sends = collect(
        (near2, far2, near3, far3, deep3),
        (
            ((1, 0, main), (3, 0, main), (3, 2 * main, 2 * main + held)),
            ((0, main, 2 * main), (2, main, 2 * main), (2, 2 * main + held, wide))
            + ((4, narrow, 2 * narrow),),
        ),
        "collect_fifth",
    )
    near4, far4 = slot(*zip((flip_near, flip_far), sends))
    acc = accumulate(
        rows,
        (near3, far3, deep3),
        [runs(0, 0, main), runs(1, 0, main)] + [runs(2, k * narrow, edge) for k in range(4)],
        tuple(acc),
        jnp.float32,
        "accumulate_fourth",
    )
    weights = (near4, far4, deep3)
    two, tail = 2 * main, 2 * main + main - held
    last = [
        ((0, 0, main), (1, 0, main), (2, 4 * narrow, 4 * narrow + main)),
        ((0, main, main + held), (1, main, main + held), (0, two, two + held)),
        ((0, main + held, two), (1, main + held, two), (1, two, tail)),
        runs(1, tail, edge),
    ]
    (given,) = accumulate(rows[1:], weights, last, acc[1:], jnp.bfloat16, "finish_other")
    (kept,) = accumulate(
        rows[:1], weights, last, acc[:1], jnp.float32, "finish_own", residual=mixed_rows
    )
    result = kernel_call(
        functools.partial(final_body, 64),
        "final",
        like(local_len, model, jnp.bfloat16),
        valid_count,
        kept,
        flip_core(given),
        specs=[pl.BlockSpec(memory_space=pltpu.SMEM)] + vmem(2),
    )
    return (
        result[None],
        end_state.reshape((1, 1) + end_state.shape[:1] + end_state.shape[-1:]),
        end_norm[None, None],
    )


def solution(mesh):
    return jax.shard_map(
        local,
        mesh=mesh,
        in_specs=(
            P("req", "seq", None),
            P("req"),
            P("req", "seq", None),
            P(),
            P(),
            P(),
            P(),
            P(),
            P(),
            P(),
            P(None, "req"),
            P(None, "req"),
            P(None, "req"),
        ),
        out_specs=(P("req", "seq", None), P("req", "seq", None, None), P("req", "seq", None, None)),
        check_vma=False,
    )
```

```python
import functools

import jax
import jax.numpy as jnp
from jax import lax
from jax.experimental import pallas as pl
from jax.experimental.pallas import tpu as pltpu
from jax.sharding import PartitionSpec as P


def from_behind(array, axis, by):
    count = lax.axis_size(axis)
    pairs = [(i, i + by) for i in range(count) if 0 <= i + by < count]
    return lax.ppermute(array, axis, pairs)


def entering(array, axis, combine, identity):
    count, here = (lax.axis_size(axis), lax.axis_index(axis))
    everything = jax.tree.map(
        lambda part, kind: lax.all_gather(part.astype(kind), axis),
        array,
        (jnp.bfloat16, jnp.bfloat16, jnp.bfloat16),
    )
    start = jax.tree.map(
        lambda part, zero: jnp.broadcast_to(jnp.asarray(zero, part.dtype), part.shape),
        array,
        identity,
    )

    def hop(k, before):
        reached = k < here
        new = combine(
            before, jax.tree.map(lambda part, own: part[k].astype(own.dtype), everything, array)
        )
        return jax.tree.map(lambda a, b: jnp.where(reached, a, b), new, before)

    return lax.fori_loop(0, count, hop, start)


def features(vectors):
    constant = jnp.ones(vectors.shape[:-1] + (1,), jnp.float32)
    width = vectors.shape[-1]
    squares = (vectors[..., :, None] * vectors[..., None, :]).reshape(
        vectors.shape[:-1] + (width * width,)
    )
    return jnp.concatenate([constant, vectors, squares * 0.5**0.5], axis=-1)


def carry_in(valid_mask, decays, queries, numerator, denominator, flat_memory, key_sum):
    local_len = numerator.shape[0]
    feat_len, head_count = key_sum.shape
    value_len = flat_memory.shape[1] // head_count
    feat_in = queries.shape[1] // head_count
    decay_rate = jnp.where(valid_mask[:, None] > 0, decays, 0.0)
    span_decay = jnp.sum(decay_rate, axis=0)

    def merge_states(earlier, later):
        factor = jnp.exp(later[0])
        return (
            earlier[0] + later[0],
            earlier[1] * jnp.repeat(factor, value_len)[None, :] + later[1],
            earlier[2] * factor[None, :] + later[2],
        )

    neutral = (jnp.zeros_like(span_decay), jnp.zeros_like(flat_memory), jnp.zeros_like(key_sum))
    carried = entering((span_decay, flat_memory, key_sum), "seq", merge_states, neutral)
    prior_memory = carried[1]
    prior_keys = carried[2]
    highest = lax.Precision.HIGHEST
    growth = jnp.exp(jnp.cumsum(decay_rate, axis=0))
    query_feat = features(queries.astype(jnp.float32).reshape(local_len, head_count, feat_in))
    added = jnp.einsum(
        "thf,fhv->thv",
        query_feat,
        prior_memory.reshape(feat_len, head_count, value_len),
        precision=highest,
    )
    numerator = numerator + (added * growth[:, :, None]).reshape(local_len, -1)
    denominator = (
        denominator + jnp.einsum("thf,fh->th", query_feat, prior_keys, precision=highest) * growth
    )
    span_factor = jnp.exp(span_decay)
    end_state = prior_memory * jnp.repeat(span_factor, value_len)[None, :] + flat_memory
    end_norm = prior_keys * span_factor[None, :] + key_sum
    return numerator, denominator, end_state, end_norm


def permute(array, target):
    count = lax.axis_size("req")
    return lax.ppermute(array, "req", [(i, target(i)) for i in range(count)])


def flip_core(array):
    return permute(array, lambda i: i ^ 1)


def flip_near(array):
    return permute(array, lambda i: i ^ 2)


def flip_far(array):
    return permute(array, lambda i: i ^ 4)


def next_plane(array):
    count = lax.axis_size("req")
    return permute(array, lambda i: (i + 8) % count)


def together(*arrays):
    return lax.optimization_barrier(arrays)


def slot(*sends):
    operands = together(*[array for _, array in sends])
    return together(*[send(array) for (send, _), array in zip(sends, operands)])


def vmem(count):
    return [pl.BlockSpec(memory_space=pltpu.VMEM)] * count


def kernel_call(body, name, out_shape, *operands, scratch=(), aliases=None, specs=None, mib=24):
    many = isinstance(out_shape, tuple)
    return pl.pallas_call(
        body,
        out_shape=out_shape,
        in_specs=specs or vmem(len(operands)),
        out_specs=tuple(vmem(len(out_shape))) if many else vmem(1)[0],
        scratch_shapes=list(scratch),
        input_output_aliases=aliases or {},
        compiler_params=pltpu.CompilerParams(vmem_limit_bytes=mib * 1024 * 1024),
        cost_estimate=pl.CostEstimate(flops=1000, bytes_accessed=1000, transcendentals=0),
        name=name,
    )(*operands)


def like(rows, columns, dtype):
    return jax.ShapeDtypeStruct((rows, columns), dtype)


NT = (((1,), (1,)), ((), ()))


def unit_rows(rows, gain):
    factor = lax.rsqrt(jnp.mean(rows * rows, axis=-1, keepdims=True) + 1e-05)
    return (rows * factor * gain).astype(jnp.bfloat16).astype(jnp.float32)


def project_body(
    step,
    scale,
    rows_ref,
    edge_ref,
    gain_ref,
    conv_ref,
    query_ref,
    key_ref,
    value_ref,
    queries_ref,
    keys_ref,
    values_ref,
    normed,
    gated,
):
    gain = gain_ref[...]
    count = rows_ref.shape[0]
    lead = edge_ref.shape[0]
    taps = conv_ref.shape[0]
    normed[:lead] = unit_rows(edge_ref[...].astype(jnp.float32), gain)

    @pl.loop(0, count // step)
    def _(block):
        at = pl.multiple_of(block * step, step)
        rows = rows_ref[pl.ds(at, step), :].astype(jnp.float32)
        normed[pl.ds(lead + at, step), :] = unit_rows(rows, gain)

    @pl.loop(0, count // step)
    def _(block):
        at = pl.multiple_of(block * step, step)
        window = normed[pl.ds(at, step + lead), :]
        here = window[lead:]
        total = conv_ref[0:1] * here
        for tap in range(1, taps):
            total = total + conv_ref[tap : tap + 1] * window[lead - tap : lead - tap + step]
        gated[pl.ds(at, step), :] = (total * jax.nn.sigmoid(here)).astype(jnp.bfloat16)

    rows = gated[...]
    for weight_ref, out_ref, factor in (
        (query_ref, queries_ref, scale),
        (key_ref, keys_ref, scale),
        (value_ref, values_ref, None),
    ):
        product = jnp.dot(rows, weight_ref[...], preferred_element_type=jnp.float32)
        if factor is not None:
            product = product * factor
        out_ref[...] = product.astype(jnp.bfloat16)


def project(rows, edge, mix_gain, conv_weight, query_weight, key_weight, value_weight, scale):
    count, width = rows.shape
    step = 32
    return kernel_call(
        functools.partial(project_body, step, scale),
        "project",
        tuple(like(count, w.shape[1], jnp.bfloat16) for w in (query_weight, key_weight, value_weight)),
        rows,
        edge,
        mix_gain[None],
        conv_weight,
        query_weight,
        key_weight,
        value_weight,
        scratch=(
            pltpu.VMEM((count + edge.shape[0], width), jnp.float32),
            pltpu.VMEM((count, width), jnp.bfloat16),
        ),
    )


def attend_body(
    feat_in,
    value_len,
    count_ref,
    rate_ref,
    queries_ref,
    keys_ref,
    values_ref,
    numer_ref,
    denom_ref,
    state_ref,
    norm_ref,
    turned,
    total,
    norms,
):
    heads, count = rate_ref.shape
    columns = values_ref.shape[1]
    lane = lax.broadcasted_iota(jnp.int32, (count, count), 1)
    row = lax.broadcasted_iota(jnp.int32, (count, count), 0)
    valid = (lane[:1] < count_ref[0]).astype(jnp.float32)
    rate = jnp.where(valid > 0, rate_ref[...], 0.0)
    upto = (row <= lane).astype(jnp.float32)
    across = jnp.dot(
        rate, upto, precision=lax.Precision.HIGHEST, preferred_element_type=jnp.float32
    )
    down = across.T
    closing = across[:, count - 1 : count]
    fading = jnp.exp(closing - across) * valid
    causal = row >= lane
    keys = keys_ref[...]
    turned[...] = keys.astype(jnp.float32).T
    owner = lax.broadcasted_iota(jnp.int32, queries_ref.shape, 1)
    spare = lax.broadcasted_iota(jnp.int32, (8, count), 0) == 0
    head_lane = lax.broadcasted_iota(jnp.int32, (count, 128), 1)
    numer_ref[...] = jnp.zeros(numer_ref.shape, jnp.float32)
    total[...] = jnp.zeros(total.shape, jnp.float32)
    norms[...] = jnp.zeros(norms.shape, jnp.float32)
    norm_total = jnp.zeros((total.shape[0], 128), jnp.float32)
    denominators = jnp.zeros((count, 128), jnp.float32)
    for h in range(heads):
        low = min(h * value_len // 128 * 128, max(columns - 256, 0))
        high = min(low + 256, columns)
        mine = lax.broadcasted_iota(jnp.int32, (count, high - low), 1) + low
        mine = (mine >= h * value_len) & (mine < (h + 1) * value_len)
        values = jnp.where(mine, values_ref[:, low:high].astype(jnp.float32), 0.0)
        values = values.astype(jnp.bfloat16)
        asks = (owner >= h * feat_in) & (owner < (h + 1) * feat_in)
        queries = jnp.where(asks, queries_ref[...].astype(jnp.float32), 0.0)
        scores = lax.dot_general(
            queries.astype(jnp.bfloat16), keys, NT, preferred_element_type=jnp.float32
        )
        gap = down[:, h : h + 1] - across[h : h + 1]
        weights = jnp.where(causal, jnp.exp(jnp.minimum(gap, 0.0)) * valid, 0.0)
        weights = weights * (1.0 + scores + 0.5 * scores * scores)
        numer_ref[:, low:high] += jnp.dot(
            weights.astype(jnp.bfloat16), values, preferred_element_type=jnp.float32
        )
        sums = jnp.sum(weights, axis=1, keepdims=True)
        denominators = jnp.where(head_lane == h, sums, denominators)
        own = turned[h * feat_in : (h + 1) * feat_in]
        fade = fading[h : h + 1]
        faded = own * fade
        scaled = faded * 0.5**0.5
        parts = [own[i : i + 1] * scaled for i in range(feat_in)]
        parts += [faded, jnp.where(spare, fade, 0.0)]
        feats = jnp.concatenate(parts, axis=0).astype(jnp.bfloat16)
        total[:, low:high] += jnp.dot(feats, values, preferred_element_type=jnp.float32)
        mark = (head_lane == h).astype(jnp.bfloat16)
        norm_total = norm_total + jnp.dot(feats, mark, preferred_element_type=jnp.float32)
    denom_ref[...] = denominators[:, :heads]
    pairs = feat_in * feat_in
    state_ref[0] = total[pairs + feat_in : pairs + feat_in + 1, :]
    for f in range(feat_in):
        state_ref[1 + f] = total[pairs + f : pairs + f + 1, :]

    @pl.loop(0, pairs // 8)
    def _(block):
        for k in range(8):
            f = block * 8 + k
            state_ref[1 + feat_in + f] = total[pl.ds(f, 1), :]

    norms[0:1, :] = norm_total[pairs + feat_in : pairs + feat_in + 1]
    norms[1 : 1 + feat_in, :] = norm_total[pairs : pairs + feat_in]
    norms[1 + feat_in : 1 + feat_in + pairs, :] = norm_total[:pairs]
    norm_ref[...] = norms[...].T[:heads, : 1 + feat_in + pairs]


def attend(valid_count, rate, queries, keys, values, feat_in, value_len):
    heads, count = rate.shape
    columns = values.shape[1]
    feat_len = 1 + feat_in + feat_in * feat_in
    padded = feat_in * feat_in + feat_in + 8
    return kernel_call(
        functools.partial(attend_body, feat_in, value_len),
        "attend",
        (
            like(count, columns, jnp.float32),
            like(count, heads, jnp.float32),
            jax.ShapeDtypeStruct((feat_len, 1, columns), jnp.float32),
            like(heads, feat_len, jnp.float32),
        ),
        valid_count,
        rate,
        queries,
        keys,
        values,
        specs=[pl.BlockSpec(memory_space=pltpu.SMEM)] + vmem(4),
        scratch=(
            pltpu.VMEM((queries.shape[1], count), jnp.float32),
            pltpu.VMEM((padded, columns), jnp.float32),
            pltpu.VMEM(((feat_len + 127) // 128 * 128, 128), jnp.float32),
        ),
    )


def mix_body(
    value_len, step, numer_ref, denom_ref, rows_ref, out_ref, gain_ref, mixed_ref, mlp_ref, sums
):
    count, columns = numer_ref.shape
    heads = denom_ref.shape[1]
    column = lax.broadcasted_iota(jnp.int32, (1, columns), 1)
    inverse = 1.0 / denom_ref[...]
    spread = jnp.zeros((count, columns), jnp.float32)
    for h in range(heads):
        here = (column >= h * value_len) & (column < (h + 1) * value_len)
        spread = jnp.where(here, inverse[:, h : h + 1], spread)
    attended = (numer_ref[...] * spread).astype(jnp.bfloat16)
    sums[...] = jnp.dot(attended, out_ref[...], preferred_element_type=jnp.float32)
    gain = gain_ref[...]

    @pl.loop(0, count // step)
    def _(block):
        at = pl.ds(pl.multiple_of(block * step, step), step)
        mixed = (rows_ref[at, :].astype(jnp.float32) + sums[at, :]).astype(jnp.bfloat16)
        mixed_ref[at, :] = mixed
        mlp_ref[at, :] = unit_rows(mixed.astype(jnp.float32), gain).astype(jnp.bfloat16)


def mix(numer, denom, rows, out_weight, mlp_gain, value_len):
    count, width = rows.shape
    shape = like(count, width, jnp.bfloat16)
    return kernel_call(
        functools.partial(mix_body, value_len, 32),
        "mix",
        (shape, shape),
        numer,
        denom,
        rows,
        out_weight,
        mlp_gain[None],
        scratch=(pltpu.VMEM((count, width), jnp.float32),),
    )


def swiglu_terms(rows, gate_rows, up_rows, down_rows):
    gate_act = lax.dot_general(rows, gate_rows, NT, preferred_element_type=jnp.float32)
    up_act = lax.dot_general(rows, up_rows, NT, preferred_element_type=jnp.float32)
    hidden_units = (gate_act * jax.nn.sigmoid(gate_act) * up_act).astype(jnp.bfloat16)
    return jnp.dot(hidden_units, down_rows, preferred_element_type=jnp.float32)


def on_grid(run):
    return all(low % 16 == 0 and high % 16 == 0 for _, low, high in run)


def read_units(refs, units):
    parts = []
    for k in range(3):
        rows = [refs[run[k][0]][run[k][1] : run[k][2]] for run in units if on_grid(run)]
        rest = [
            refs[run[k][0]][...].astype(jnp.float32)[run[k][1] : run[k][2]]
            for run in units
            if not on_grid(run)
        ]
        if rest:
            rows.append(jnp.concatenate(rest, axis=0).astype(jnp.bfloat16))
        parts.append(jnp.concatenate(rows, axis=0))
    return parts


def accumulate_body(units, n_weights, n_rows, n_acc, residual, *refs):
    weights = refs[:n_weights]
    rows = refs[n_weights : n_weights + n_rows]
    acc = refs[n_weights + n_rows : n_weights + n_rows + n_acc]
    parts = read_units(weights, units)
    for k, rows_ref in enumerate(rows):
        out_ref = refs[len(refs) - n_rows + k]
        terms = swiglu_terms(rows_ref[...], *parts)
        if n_acc:
            terms = terms + acc[k][...]
        if residual:
            terms = terms + refs[n_weights + n_rows + n_acc][...].astype(jnp.float32)
        out_ref[...] = terms.astype(out_ref.dtype)


def accumulate(rows, weights, units, acc, dtype, name, residual=None):
    shapes = tuple(like(*array.shape, dtype) for array in rows)
    start = len(weights) + len(rows)
    aliases = {start + k: k for k in range(len(acc))} if dtype == jnp.float32 else {}
    extra = () if residual is None else (residual,)
    body = functools.partial(
        accumulate_body, tuple(units), len(weights), len(rows), len(acc), bool(extra)
    )
    return kernel_call(body, name, shapes, *weights, *rows, *acc, *extra, aliases=aliases)


def runs(which, low, size):
    return tuple((which, low + k * size, low + (k + 1) * size) for k in range(3))


def split_runs(first, second, main):
    (i, at), (j, then) = first, second
    held = 2 * main // 3
    rest = main - held
    return (
        ((i, at, at + held), (i, at + main, at + main + held), (j, then + rest, then + main)),
        ((i, at + held, at + main), (j, then, then + rest), (j, then + main, then + rest + main)),
    )


def collect_body(plans, *refs):
    outs = refs[len(refs) - len(plans) :]
    for out_ref, plan in zip(outs, plans):
        rows = [refs[i][...].astype(jnp.float32)[low:high] for i, low, high in plan]
        out_ref[...] = jnp.concatenate(rows, axis=0).astype(jnp.bfloat16)


def collect(arrays, plans, name):
    columns = arrays[0].shape[1]
    shapes = tuple(like(sum(h - l for _, l, h in plan), columns, jnp.bfloat16) for plan in plans)
    return kernel_call(functools.partial(collect_body, plans), name, shapes, *arrays)


def shard_body(main, gate_ref, up_ref, down_ref, shard_ref, main_ref, *rest):
    buffers, sems = rest[:3], rest[3]
    copies = [
        pltpu.make_async_copy(source, buffer, sems.at[k])
        for k, (source, buffer) in enumerate(zip((gate_ref, up_ref, down_ref), buffers))
    ]
    for copy in copies:
        copy.start()
    for copy in copies:
        copy.wait()
    arrays = [buffer[...].astype(jnp.float32) for buffer in buffers]
    tops = [array[:main] for array in arrays]
    ends = [array[main:] for array in arrays]
    shard_ref[...] = jnp.concatenate(tops + ends, axis=0).astype(jnp.bfloat16)
    main_ref[...] = jnp.concatenate(tops, axis=0).astype(jnp.bfloat16)


def final_body(step, count_ref, kept_ref, given_ref, out_ref):
    count = kept_ref.shape[0]

    @pl.loop(0, count // step)
    def _(block):
        first = pl.multiple_of(block * step, step)
        at = pl.ds(first, step)
        total = kept_ref[at, :] + given_ref[at, :].astype(jnp.float32)
        row = lax.broadcasted_iota(jnp.int32, total.shape, 0) + first
        out_ref[at, :] = jnp.where(row < count_ref[0], total, 0.0).astype(out_ref.dtype)


def local(
    hidden_in,
    lengths,
    log_decay,
    mix_gain,
    conv_weight,
    query_weight,
    key_weight,
    value_weight,
    out_weight,
    mlp_gain,
    gate_weight,
    up_weight,
    down_weight,
):
    local_len = hidden_in.shape[1]
    rows_in = hidden_in[0]
    decays = log_decay[0]
    head_count = log_decay.shape[2]
    value_len = value_weight.shape[1] // head_count
    feat_in = query_weight.shape[1] // head_count
    feature_scale = feat_in ** (-0.25)
    valid_count = lengths - lax.axis_index("seq") * local_len
    spans = lax.axis_size("seq")
    units, model = gate_weight.shape[1], gate_weight.shape[0]
    edge = units // 7
    main = units - edge
    wide = 3 * main
    full = 3 * units
    narrow = full - wide
    cut = main + 2 * main // 3

    shard, shard_main = kernel_call(
        functools.partial(shard_body, main),
        "shard",
        (like(full, model, jnp.bfloat16), like(wide, model, jnp.bfloat16)),
        gate_weight.T,
        up_weight.T,
        down_weight.T,
        specs=[pl.BlockSpec(memory_space=pl.ANY)] * 3,
        scratch=[pltpu.VMEM((units, model), jnp.bfloat16)] * 3 + [pltpu.SemaphoreType.DMA((3,))],
        mib=56,
    )
    near, far, deep = slot((flip_near, shard), (flip_far, shard), (next_plane, shard_main))

    lead = 16
    if spans > 1:
        edge_in = from_behind(rows_in[local_len - lead :], "seq", 1)
    else:
        edge_in = jnp.zeros((lead, model), jnp.bfloat16)
    queries, key_rows, values = project(
        rows_in, edge_in, mix_gain, conv_weight, query_weight, key_weight, value_weight, feature_scale
    )
    near, far, deep, queries, key_rows, values = together(
        near, far, deep, queries, key_rows, values
    )

    sends = collect(
        (shard, near, far, deep),
        (
            ((3, 0, wide), (2, 0, cut)),
            ((3, 0, wide), (1, cut, full)),
            ((3, 0, wide), (0, wide, full), (1, wide, full), (2, wide, full)),
        ),
        "collect_second",
    )
    near1, far1, deep1 = slot(*zip((flip_near, flip_far, next_plane), sends))

    numerator, denominator, end_state, end_norm = attend(
        valid_count, log_decay[0].T, queries, key_rows, values, feat_in, value_len
    )
    if spans > 1:
        positions = jnp.arange(local_len, dtype=jnp.int32)
        numerator, denominator, end_state, end_norm = carry_in(
            (positions < valid_count).astype(jnp.float32),
            decays,
            queries,
            numerator,
            denominator,
            end_state[:, 0],
            end_norm.T,
        )
    else:
        end_norm = end_norm.T
    mixed_rows, mlp_in = mix(numerator, denominator, rows_in, out_weight, mlp_gain, value_len)
    near1, far1, deep1, mixed_rows, mlp_in, end_state, end_norm = together(
        near1, far1, deep1, mixed_rows, mlp_in, end_state, end_norm
    )

    sends = collect(
        (near1, far1, deep1),
        (
            ((2, 0, wide), (1, 0, cut)),
            ((2, 0, wide), (0, cut, wide)),
            ((2, 0, wide + 3 * narrow), (1, wide + wide - cut, wide + full - cut)),
        ),
        "collect_third",
    )
    near2, far2, deep2 = slot(*zip((flip_near, flip_far, next_plane), sends))
    rows = (mlp_in, flip_core(mlp_in))
    acc = accumulate(
        rows,
        (shard, near, far, deep, near1, far1, deep1),
        [runs(i, 0, main) for i in range(7)] + list(split_runs((4, wide), (5, wide), main)),
        (),
        jnp.float32,
        "accumulate_second",
    )
    near2, far2, deep2 = together(near2, far2, deep2)

    held = 2 * main // 3
    deep3_main, line = collect(
        (far2, deep2),
        (
            ((1, 0, wide),),
            ((1, wide, wide + 4 * narrow), (0, 2 * wide - cut - main, 2 * wide - cut - main + held)),
        ),
        "collect_fourth",
    )
    near3, far3, deep3 = slot((flip_near, deep3_main), (flip_far, deep3_main), (next_plane, line))
    acc = accumulate(
        rows,
        (shard, near, far, far1, deep1, near2, far2, deep2),
        [runs(i, 0, main) for i in (5, 6, 7)]
        + list(split_runs((5, wide), (6, wide), main))
        + [runs(i, wide, edge) for i in (0, 1, 2)]
        + [runs(3, wide + wide - cut, edge)]
        + [runs(4, wide + k * narrow, edge) for k in range(3)]
        + [runs(7, wide + k * narrow, edge) for k in range(4)],
        tuple(acc),
        jnp.float32,
        "accumulate_third",
    )
    near3, far3, deep3, *acc = together(near3, far3, deep3, *acc)

    two = 2 * main
    sends = collect(
        (near2, far2, near3, far3, deep3),
        (
            ((1, 0, main), (1, two + held, wide), (3, 0, main), (3, two, two + held)),
            ((0, main, two), (2, main, two), (2, two + held, wide), (4, narrow, 2 * narrow)),
        ),
        "collect_fifth",
    )
    near4, far4 = slot(*zip((flip_near, flip_far), sends))
    acc = accumulate(
        rows,
        (near3, far3, deep3),
        [runs(0, 0, main), runs(1, 0, main)] + [runs(2, k * narrow, edge) for k in range(4)],
        tuple(acc),
        jnp.float32,
        "accumulate_fourth",
    )
    weights = (near4, far4, deep3)
    line, then = 4 * narrow, two - held
    last = [
        ((0, 0, held), (1, 0, held), (2, line, line + held)),
        ((0, held, main), (1, held, main), (0, main, then)),
        ((0, then, then + held), (1, main, main + held), (0, then + main, then + main + held)),
        ((0, then + held, then + main), (1, main + held, two), (1, two, two + main - held)),
        runs(1, two + main - held, edge),
    ]
    (given,) = accumulate(rows[1:], weights, last, acc[1:], jnp.bfloat16, "finish_other")
    (kept,) = accumulate(
        rows[:1], weights, last, acc[:1], jnp.float32, "finish_own", residual=mixed_rows
    )
    result = kernel_call(
        functools.partial(final_body, 64),
        "final",
        like(local_len, model, jnp.bfloat16),
        valid_count,
        kept,
        flip_core(given),
        specs=[pl.BlockSpec(memory_space=pltpu.SMEM)] + vmem(2),
    )
    return (
        result[None],
        end_state.reshape((1, 1) + end_state.shape[:1] + end_state.shape[-1:]),
        end_norm[None, None],
    )


def solution(mesh):
    return jax.shard_map(
        local,
        mesh=mesh,
        in_specs=(
            P("req", "seq", None),
            P("req"),
            P("req", "seq", None),
            P(),
            P(),
            P(),
            P(),
            P(),
            P(),
            P(),
            P(None, "req"),
            P(None, "req"),
            P(None, "req"),
        ),
        out_specs=(P("req", "seq", None), P("req", "seq", None, None), P("req", "seq", None, None)),
        check_vma=False,
    )
```

```python
import functools

import jax
import jax.numpy as jnp
from jax import lax
from jax.experimental import pallas as pl
from jax.experimental.pallas import tpu as pltpu
from jax.sharding import PartitionSpec as P


def from_behind(array, axis, by):
    count = lax.axis_size(axis)
    pairs = [(i, i + by) for i in range(count) if 0 <= i + by < count]
    return lax.ppermute(array, axis, pairs)


def entering(array, axis, combine, identity):
    count, here = (lax.axis_size(axis), lax.axis_index(axis))
    everything = jax.tree.map(
        lambda part, kind: lax.all_gather(part.astype(kind), axis),
        array,
        (jnp.bfloat16, jnp.bfloat16, jnp.bfloat16),
    )
    start = jax.tree.map(
        lambda part, zero: jnp.broadcast_to(jnp.asarray(zero, part.dtype), part.shape),
        array,
        identity,
    )

    def hop(k, before):
        reached = k < here
        new = combine(
            before, jax.tree.map(lambda part, own: part[k].astype(own.dtype), everything, array)
        )
        return jax.tree.map(lambda a, b: jnp.where(reached, a, b), new, before)

    return lax.fori_loop(0, count, hop, start)


def features(vectors):
    constant = jnp.ones(vectors.shape[:-1] + (1,), jnp.float32)
    width = vectors.shape[-1]
    squares = (vectors[..., :, None] * vectors[..., None, :]).reshape(
        vectors.shape[:-1] + (width * width,)
    )
    return jnp.concatenate([constant, vectors, squares * 0.5**0.5], axis=-1)


def carry_in(valid_mask, decays, queries, numerator, denominator, flat_memory, key_sum):
    local_len = numerator.shape[0]
    feat_len, head_count = key_sum.shape
    value_len = flat_memory.shape[1] // head_count
    feat_in = queries.shape[1] // head_count
    decay_rate = jnp.where(valid_mask[:, None] > 0, decays, 0.0)
    span_decay = jnp.sum(decay_rate, axis=0)

    def merge_states(earlier, later):
        factor = jnp.exp(later[0])
        return (
            earlier[0] + later[0],
            earlier[1] * jnp.repeat(factor, value_len)[None, :] + later[1],
            earlier[2] * factor[None, :] + later[2],
        )

    neutral = (jnp.zeros_like(span_decay), jnp.zeros_like(flat_memory), jnp.zeros_like(key_sum))
    carried = entering((span_decay, flat_memory, key_sum), "seq", merge_states, neutral)
    prior_memory = carried[1]
    prior_keys = carried[2]
    highest = lax.Precision.HIGHEST
    growth = jnp.exp(jnp.cumsum(decay_rate, axis=0))
    query_feat = features(queries.astype(jnp.float32).reshape(local_len, head_count, feat_in))
    added = jnp.einsum(
        "thf,fhv->thv",
        query_feat,
        prior_memory.reshape(feat_len, head_count, value_len),
        precision=highest,
    )
    numerator = numerator + (added * growth[:, :, None]).reshape(local_len, -1)
    denominator = (
        denominator + jnp.einsum("thf,fh->th", query_feat, prior_keys, precision=highest) * growth
    )
    span_factor = jnp.exp(span_decay)
    end_state = prior_memory * jnp.repeat(span_factor, value_len)[None, :] + flat_memory
    end_norm = prior_keys * span_factor[None, :] + key_sum
    return numerator, denominator, end_state, end_norm


def permute(array, target):
    count = lax.axis_size("req")
    return lax.ppermute(array, "req", [(i, target(i)) for i in range(count)])


def flip_core(array):
    return permute(array, lambda i: i ^ 1)


def flip_near(array):
    return permute(array, lambda i: i ^ 2)


def flip_far(array):
    return permute(array, lambda i: i ^ 4)


def next_plane(array):
    count = lax.axis_size("req")
    return permute(array, lambda i: (i + (8 if i % 2 else count - 8)) % count)


def together(*arrays):
    return lax.optimization_barrier(arrays)


def slot(*sends):
    operands = together(*[array for _, array in sends])
    return together(*[send(array) for (send, _), array in zip(sends, operands)])


def vmem(count):
    return [pl.BlockSpec(memory_space=pltpu.VMEM)] * count


def kernel_call(body, name, out_shape, *operands, scratch=(), aliases=None, specs=None, mib=24):
    many = isinstance(out_shape, tuple)
    return pl.pallas_call(
        body,
        out_shape=out_shape,
        in_specs=specs or vmem(len(operands)),
        out_specs=tuple(vmem(len(out_shape))) if many else vmem(1)[0],
        scratch_shapes=list(scratch),
        input_output_aliases=aliases or {},
        compiler_params=pltpu.CompilerParams(vmem_limit_bytes=mib * 1024 * 1024),
        cost_estimate=pl.CostEstimate(flops=1000, bytes_accessed=1000, transcendentals=0),
        name=name,
    )(*operands)


def like(rows, columns, dtype):
    return jax.ShapeDtypeStruct((rows, columns), dtype)


NT = (((1,), (1,)), ((), ()))


def unit_rows(rows, gain):
    factor = lax.rsqrt(jnp.mean(rows * rows, axis=-1, keepdims=True) + 1e-05)
    return (rows * factor * gain).astype(jnp.bfloat16).astype(jnp.float32)


def project_body(
    step,
    scale,
    rows_ref,
    edge_ref,
    gain_ref,
    conv_ref,
    query_ref,
    key_ref,
    value_ref,
    queries_ref,
    keys_ref,
    values_ref,
    normed,
    gated,
):
    gain = gain_ref[...]
    count = rows_ref.shape[0]
    lead = edge_ref.shape[0]
    taps = conv_ref.shape[0]
    normed[:lead] = unit_rows(edge_ref[...].astype(jnp.float32), gain)

    @pl.loop(0, count // step)
    def _(block):
        at = pl.multiple_of(block * step, step)
        rows = rows_ref[pl.ds(at, step), :].astype(jnp.float32)
        normed[pl.ds(lead + at, step), :] = unit_rows(rows, gain)

    @pl.loop(0, count // step)
    def _(block):
        at = pl.multiple_of(block * step, step)
        window = normed[pl.ds(at, step + lead), :]
        here = window[lead:]
        total = conv_ref[0:1] * here
        for tap in range(1, taps):
            total = total + conv_ref[tap : tap + 1] * window[lead - tap : lead - tap + step]
        gated[pl.ds(at, step), :] = (total * jax.nn.sigmoid(here)).astype(jnp.bfloat16)

    rows = gated[...]
    for weight_ref, out_ref, factor in (
        (query_ref, queries_ref, scale),
        (key_ref, keys_ref, scale),
        (value_ref, values_ref, None),
    ):
        product = jnp.dot(rows, weight_ref[...], preferred_element_type=jnp.float32)
        if factor is not None:
            product = product * factor
        out_ref[...] = product.astype(jnp.bfloat16)


def project(rows, edge, mix_gain, conv_weight, query_weight, key_weight, value_weight, scale):
    count, width = rows.shape
    step = 32
    return kernel_call(
        functools.partial(project_body, step, scale),
        "project",
        tuple(like(count, w.shape[1], jnp.bfloat16) for w in (query_weight, key_weight, value_weight)),
        rows,
        edge,
        mix_gain[None],
        conv_weight,
        query_weight,
        key_weight,
        value_weight,
        scratch=(
            pltpu.VMEM((count + edge.shape[0], width), jnp.float32),
            pltpu.VMEM((count, width), jnp.bfloat16),
        ),
    )


def attend_body(
    feat_in,
    value_len,
    count_ref,
    rate_ref,
    queries_ref,
    keys_ref,
    values_ref,
    numer_ref,
    denom_ref,
    state_ref,
    norm_ref,
    turned,
    total,
    norms,
):
    heads, count = rate_ref.shape
    columns = values_ref.shape[1]
    lane = lax.broadcasted_iota(jnp.int32, (count, count), 1)
    row = lax.broadcasted_iota(jnp.int32, (count, count), 0)
    valid = (lane[:1] < count_ref[0]).astype(jnp.float32)
    rate = jnp.where(valid > 0, rate_ref[...], 0.0)
    upto = (row <= lane).astype(jnp.float32)
    across = jnp.dot(
        rate, upto, precision=lax.Precision.HIGHEST, preferred_element_type=jnp.float32
    )
    down = across.T
    closing = across[:, count - 1 : count]
    fading = jnp.exp(closing - across) * valid
    causal = row >= lane
    keys = keys_ref[...]
    turned[...] = keys.astype(jnp.float32).T
    owner = lax.broadcasted_iota(jnp.int32, queries_ref.shape, 1)
    spare = lax.broadcasted_iota(jnp.int32, (8, count), 0) == 0
    head_lane = lax.broadcasted_iota(jnp.int32, (count, 128), 1)
    numer_ref[...] = jnp.zeros(numer_ref.shape, jnp.float32)
    total[...] = jnp.zeros(total.shape, jnp.float32)
    norms[...] = jnp.zeros(norms.shape, jnp.float32)
    norm_total = jnp.zeros((total.shape[0], 128), jnp.float32)
    denominators = jnp.zeros((count, 128), jnp.float32)
    for h in range(heads):
        low = min(h * value_len // 128 * 128, max(columns - 256, 0))
        high = min(low + 256, columns)
        mine = lax.broadcasted_iota(jnp.int32, (count, high - low), 1) + low
        mine = (mine >= h * value_len) & (mine < (h + 1) * value_len)
        values = jnp.where(mine, values_ref[:, low:high].astype(jnp.float32), 0.0)
        values = values.astype(jnp.bfloat16)
        asks = (owner >= h * feat_in) & (owner < (h + 1) * feat_in)
        queries = jnp.where(asks, queries_ref[...].astype(jnp.float32), 0.0)
        scores = lax.dot_general(
            queries.astype(jnp.bfloat16), keys, NT, preferred_element_type=jnp.float32
        )
        gap = down[:, h : h + 1] - across[h : h + 1]
        weights = jnp.where(causal, jnp.exp(jnp.minimum(gap, 0.0)) * valid, 0.0)
        weights = weights * (1.0 + scores + 0.5 * scores * scores)
        numer_ref[:, low:high] += jnp.dot(
            weights.astype(jnp.bfloat16), values, preferred_element_type=jnp.float32
        )
        sums = jnp.sum(weights, axis=1, keepdims=True)
        denominators = jnp.where(head_lane == h, sums, denominators)
        own = turned[h * feat_in : (h + 1) * feat_in]
        fade = fading[h : h + 1]
        faded = own * fade
        scaled = faded * 0.5**0.5
        parts = [own[i : i + 1] * scaled for i in range(feat_in)]
        parts += [faded, jnp.where(spare, fade, 0.0)]
        feats = jnp.concatenate(parts, axis=0).astype(jnp.bfloat16)
        total[:, low:high] += jnp.dot(feats, values, preferred_element_type=jnp.float32)
        mark = (head_lane == h).astype(jnp.bfloat16)
        norm_total = norm_total + jnp.dot(feats, mark, preferred_element_type=jnp.float32)
    denom_ref[...] = denominators[:, :heads]
    pairs = feat_in * feat_in
    state_ref[0] = total[pairs + feat_in : pairs + feat_in + 1, :]
    for f in range(feat_in):
        state_ref[1 + f] = total[pairs + f : pairs + f + 1, :]

    @pl.loop(0, pairs // 8)
    def _(block):
        for k in range(8):
            f = block * 8 + k
            state_ref[1 + feat_in + f] = total[pl.ds(f, 1), :]

    norms[0:1, :] = norm_total[pairs + feat_in : pairs + feat_in + 1]
    norms[1 : 1 + feat_in, :] = norm_total[pairs : pairs + feat_in]
    norms[1 + feat_in : 1 + feat_in + pairs, :] = norm_total[:pairs]
    norm_ref[...] = norms[...].T[:heads, : 1 + feat_in + pairs]


def attend(valid_count, rate, queries, keys, values, feat_in, value_len):
    heads, count = rate.shape
    columns = values.shape[1]
    feat_len = 1 + feat_in + feat_in * feat_in
    padded = feat_in * feat_in + feat_in + 8
    return kernel_call(
        functools.partial(attend_body, feat_in, value_len),
        "attend",
        (
            like(count, columns, jnp.float32),
            like(count, heads, jnp.float32),
            jax.ShapeDtypeStruct((feat_len, 1, columns), jnp.float32),
            like(heads, feat_len, jnp.float32),
        ),
        valid_count,
        rate,
        queries,
        keys,
        values,
        specs=[pl.BlockSpec(memory_space=pltpu.SMEM)] + vmem(4),
        scratch=(
            pltpu.VMEM((queries.shape[1], count), jnp.float32),
            pltpu.VMEM((padded, columns), jnp.float32),
            pltpu.VMEM(((feat_len + 127) // 128 * 128, 128), jnp.float32),
        ),
    )


def mix_body(
    value_len, step, numer_ref, denom_ref, rows_ref, out_ref, gain_ref, mixed_ref, mlp_ref, sums
):
    count, columns = numer_ref.shape
    heads = denom_ref.shape[1]
    column = lax.broadcasted_iota(jnp.int32, (1, columns), 1)
    inverse = 1.0 / denom_ref[...]
    spread = jnp.zeros((count, columns), jnp.float32)
    for h in range(heads):
        here = (column >= h * value_len) & (column < (h + 1) * value_len)
        spread = jnp.where(here, inverse[:, h : h + 1], spread)
    attended = (numer_ref[...] * spread).astype(jnp.bfloat16)
    sums[...] = jnp.dot(attended, out_ref[...], preferred_element_type=jnp.float32)
    gain = gain_ref[...]

    @pl.loop(0, count // step)
    def _(block):
        at = pl.ds(pl.multiple_of(block * step, step), step)
        mixed = (rows_ref[at, :].astype(jnp.float32) + sums[at, :]).astype(jnp.bfloat16)
        mixed_ref[at, :] = mixed
        mlp_ref[at, :] = unit_rows(mixed.astype(jnp.float32), gain).astype(jnp.bfloat16)


def mix(numer, denom, rows, out_weight, mlp_gain, value_len):
    count, width = rows.shape
    shape = like(count, width, jnp.bfloat16)
    return kernel_call(
        functools.partial(mix_body, value_len, 32),
        "mix",
        (shape, shape),
        numer,
        denom,
        rows,
        out_weight,
        mlp_gain[None],
        scratch=(pltpu.VMEM((count, width), jnp.float32),),
    )


def swiglu_terms(rows, gate_rows, up_rows, down_rows):
    gate_act = lax.dot_general(rows, gate_rows, NT, preferred_element_type=jnp.float32)
    up_act = lax.dot_general(rows, up_rows, NT, preferred_element_type=jnp.float32)
    hidden_units = (gate_act * jax.nn.sigmoid(gate_act) * up_act).astype(jnp.bfloat16)
    return jnp.dot(hidden_units, down_rows, preferred_element_type=jnp.float32)


def on_grid(run):
    return all(low % 16 == 0 and high % 16 == 0 for _, low, high in run)


def read_units(refs, units):
    parts = []
    for k in range(3):
        rows = [refs[run[k][0]][run[k][1] : run[k][2]] for run in units if on_grid(run)]
        rest = [
            refs[run[k][0]][...].astype(jnp.float32)[run[k][1] : run[k][2]]
            for run in units
            if not on_grid(run)
        ]
        if rest:
            rows.append(jnp.concatenate(rest, axis=0).astype(jnp.bfloat16))
        parts.append(jnp.concatenate(rows, axis=0))
    return parts


def accumulate_body(units, n_weights, n_rows, n_acc, residual, *refs):
    weights = refs[:n_weights]
    rows = refs[n_weights : n_weights + n_rows]
    acc = refs[n_weights + n_rows : n_weights + n_rows + n_acc]
    parts = read_units(weights, units)
    for k, rows_ref in enumerate(rows):
        out_ref = refs[len(refs) - n_rows + k]
        terms = swiglu_terms(rows_ref[...], *parts)
        if n_acc:
            terms = terms + acc[k][...]
        if residual:
            terms = terms + refs[n_weights + n_rows + n_acc][...].astype(jnp.float32)
        out_ref[...] = terms.astype(out_ref.dtype)


def accumulate(rows, weights, units, acc, dtype, name, residual=None):
    shapes = tuple(like(*array.shape, dtype) for array in rows)
    start = len(weights) + len(rows)
    aliases = {start + k: k for k in range(len(acc))} if dtype == jnp.float32 else {}
    extra = () if residual is None else (residual,)
    body = functools.partial(
        accumulate_body, tuple(units), len(weights), len(rows), len(acc), bool(extra)
    )
    return kernel_call(body, name, shapes, *weights, *rows, *acc, *extra, aliases=aliases)


def runs(which, low, size):
    return tuple((which, low + k * size, low + (k + 1) * size) for k in range(3))


def split_runs(first, second, main):
    (i, at), (j, then) = first, second
    held = 2 * main // 3
    rest = main - held
    return (
        ((i, at, at + held), (i, at + main, at + main + held), (j, then + rest, then + main)),
        ((i, at + held, at + main), (j, then, then + rest), (j, then + main, then + rest + main)),
    )


def collect_body(plans, *refs):
    outs = refs[len(refs) - len(plans) :]
    for out_ref, plan in zip(outs, plans):
        rows = [refs[i][...].astype(jnp.float32)[low:high] for i, low, high in plan]
        out_ref[...] = jnp.concatenate(rows, axis=0).astype(jnp.bfloat16)


def collect(arrays, plans, name):
    columns = arrays[0].shape[1]
    shapes = tuple(like(sum(h - l for _, l, h in plan), columns, jnp.bfloat16) for plan in plans)
    return kernel_call(functools.partial(collect_body, plans), name, shapes, *arrays)


def shard_body(main, gate_ref, up_ref, down_ref, shard_ref, main_ref, *rest):
    buffers, sems = rest[:3], rest[3]
    copies = [
        pltpu.make_async_copy(source, buffer, sems.at[k])
        for k, (source, buffer) in enumerate(zip((gate_ref, up_ref, down_ref), buffers))
    ]
    for copy in copies:
        copy.start()
    for copy in copies:
        copy.wait()
    arrays = [buffer[...].astype(jnp.float32) for buffer in buffers]
    tops = [array[:main] for array in arrays]
    ends = [array[main:] for array in arrays]
    shard_ref[...] = jnp.concatenate(tops + ends, axis=0).astype(jnp.bfloat16)
    main_ref[...] = jnp.concatenate(tops, axis=0).astype(jnp.bfloat16)


def final_body(step, count_ref, kept_ref, given_ref, out_ref):
    count = kept_ref.shape[0]

    @pl.loop(0, count // step)
    def _(block):
        first = pl.multiple_of(block * step, step)
        at = pl.ds(first, step)
        total = kept_ref[at, :] + given_ref[at, :].astype(jnp.float32)
        row = lax.broadcasted_iota(jnp.int32, total.shape, 0) + first
        out_ref[at, :] = jnp.where(row < count_ref[0], total, 0.0).astype(out_ref.dtype)


def local(
    hidden_in,
    lengths,
    log_decay,
    mix_gain,
    conv_weight,
    query_weight,
    key_weight,
    value_weight,
    out_weight,
    mlp_gain,
    gate_weight,
    up_weight,
    down_weight,
):
    local_len = hidden_in.shape[1]
    rows_in = hidden_in[0]
    decays = log_decay[0]
    head_count = log_decay.shape[2]
    value_len = value_weight.shape[1] // head_count
    feat_in = query_weight.shape[1] // head_count
    feature_scale = feat_in ** (-0.25)
    valid_count = lengths - lax.axis_index("seq") * local_len
    spans = lax.axis_size("seq")
    units, model = gate_weight.shape[1], gate_weight.shape[0]
    edge = units // 7
    main = units - edge
    wide = 3 * main
    full = 3 * units
    narrow = full - wide
    cut = main + 2 * main // 3

    shard, shard_main = kernel_call(
        functools.partial(shard_body, main),
        "shard",
        (like(full, model, jnp.bfloat16), like(wide, model, jnp.bfloat16)),
        gate_weight.T,
        up_weight.T,
        down_weight.T,
        specs=[pl.BlockSpec(memory_space=pl.ANY)] * 3,
        scratch=[pltpu.VMEM((units, model), jnp.bfloat16)] * 3 + [pltpu.SemaphoreType.DMA((3,))],
        mib=56,
    )
    near, far, deep = slot((flip_near, shard), (flip_far, shard), (next_plane, shard_main))

    lead = 16
    if spans > 1:
        edge_in = from_behind(rows_in[local_len - lead :], "seq", 1)
    else:
        edge_in = jnp.zeros((lead, model), jnp.bfloat16)
    queries, key_rows, values = project(
        rows_in, edge_in, mix_gain, conv_weight, query_weight, key_weight, value_weight, feature_scale
    )
    near, far, deep, queries, key_rows, values = together(
        near, far, deep, queries, key_rows, values
    )

    sends = collect(
        (shard, near, far, deep),
        (
            ((3, 0, wide), (2, 0, cut)),
            ((3, 0, wide), (1, cut, full)),
            ((3, 0, wide), (0, wide, full), (1, wide, full), (2, wide, full)),
        ),
        "collect_second",
    )
    near1, far1, deep1 = slot(*zip((flip_near, flip_far, next_plane), sends))

    numerator, denominator, end_state, end_norm = attend(
        valid_count, log_decay[0].T, queries, key_rows, values, feat_in, value_len
    )
    if spans > 1:
        positions = jnp.arange(local_len, dtype=jnp.int32)
        numerator, denominator, end_state, end_norm = carry_in(
            (positions < valid_count).astype(jnp.float32),
            decays,
            queries,
            numerator,
            denominator,
            end_state[:, 0],
            end_norm.T,
        )
    else:
        end_norm = end_norm.T
    mixed_rows, mlp_in = mix(numerator, denominator, rows_in, out_weight, mlp_gain, value_len)
    near1, far1, deep1, mixed_rows, mlp_in, end_state, end_norm = together(
        near1, far1, deep1, mixed_rows, mlp_in, end_state, end_norm
    )

    sends = collect(
        (near1, far1, deep1),
        (
            ((2, 0, wide), (1, 0, cut)),
            ((2, 0, wide), (0, cut, wide)),
            ((2, 0, wide + 3 * narrow), (1, wide + wide - cut, wide + full - cut)),
        ),
        "collect_third",
    )
    near2, far2, deep2 = slot(*zip((flip_near, flip_far, next_plane), sends))
    rows = (mlp_in, flip_core(mlp_in))
    acc = accumulate(
        rows,
        (shard, near, far, deep, near1, far1, deep1),
        [runs(i, 0, main) for i in range(7)] + list(split_runs((4, wide), (5, wide), main)),
        (),
        jnp.float32,
        "accumulate_second",
    )
    near2, far2, deep2 = together(near2, far2, deep2)

    held = 2 * main // 3
    deep3_main, line = collect(
        (far2, deep2),
        (
            ((1, 0, wide),),
            ((1, wide, wide + 4 * narrow), (0, 2 * wide - cut - main, 2 * wide - cut - main + held)),
        ),
        "collect_fourth",
    )
    near3, far3, deep3 = slot((flip_near, deep3_main), (flip_far, deep3_main), (next_plane, line))
    acc = accumulate(
        rows,
        (shard, near, far, far1, deep1, near2, far2, deep2),
        [runs(i, 0, main) for i in (5, 6, 7)]
        + list(split_runs((5, wide), (6, wide), main))
        + [runs(i, wide, edge) for i in (0, 1, 2)]
        + [runs(3, wide + wide - cut, edge)]
        + [runs(4, wide + k * narrow, edge) for k in range(3)]
        + [runs(7, wide + k * narrow, edge) for k in range(4)],
        tuple(acc),
        jnp.float32,
        "accumulate_third",
    )
    near3, far3, deep3, *acc = together(near3, far3, deep3, *acc)

    two = 2 * main
    sends = collect(
        (near2, far2, near3, far3, deep3),
        (
            ((1, 0, main), (1, two + held, wide), (3, 0, main), (3, two, two + held)),
            ((0, main, two), (2, main, two), (2, two + held, wide), (4, narrow, 2 * narrow)),
        ),
        "collect_fifth",
    )
    near4, far4 = slot(*zip((flip_near, flip_far), sends))
    acc = accumulate(
        rows,
        (near3, far3, deep3),
        [runs(0, 0, main), runs(1, 0, main)] + [runs(2, k * narrow, edge) for k in range(4)],
        tuple(acc),
        jnp.float32,
        "accumulate_fourth",
    )
    weights = (near4, far4, deep3)
    line, then = 4 * narrow, two - held
    last = [
        ((0, 0, held), (1, 0, held), (2, line, line + held)),
        ((0, held, main), (1, held, main), (0, main, then)),
        ((0, then, then + held), (1, main, main + held), (0, then + main, then + main + held)),
        ((0, then + held, then + main), (1, main + held, two), (1, two, two + main - held)),
        runs(1, two + main - held, edge),
    ]
    (given,) = accumulate(rows[1:], weights, last, acc[1:], jnp.bfloat16, "finish_other")
    (kept,) = accumulate(
        rows[:1], weights, last, acc[:1], jnp.float32, "finish_own", residual=mixed_rows
    )
    result = kernel_call(
        functools.partial(final_body, 64),
        "final",
        like(local_len, model, jnp.bfloat16),
        valid_count,
        kept,
        flip_core(given),
        specs=[pl.BlockSpec(memory_space=pltpu.SMEM)] + vmem(2),
    )
    return (
        result[None],
        end_state.reshape((1, 1) + end_state.shape[:1] + end_state.shape[-1:]),
        end_norm[None, None],
    )


def solution(mesh):
    return jax.shard_map(
        local,
        mesh=mesh,
        in_specs=(
            P("req", "seq", None),
            P("req"),
            P("req", "seq", None),
            P(),
            P(),
            P(),
            P(),
            P(),
            P(),
            P(),
            P(None, "req"),
            P(None, "req"),
            P(None, "req"),
        ),
        out_specs=(P("req", "seq", None), P("req", "seq", None, None), P("req", "seq", None, None)),
        check_vma=False,
    )
```

```python
import functools

import jax
import jax.numpy as jnp
from jax import lax
from jax.experimental import pallas as pl
from jax.experimental.pallas import tpu as pltpu
from jax.sharding import PartitionSpec as P


def from_behind(array, axis, by):
    count = lax.axis_size(axis)
    pairs = [(i, i + by) for i in range(count) if 0 <= i + by < count]
    return lax.ppermute(array, axis, pairs)


def entering(array, axis, combine, identity):
    count, here = (lax.axis_size(axis), lax.axis_index(axis))
    everything = jax.tree.map(
        lambda part, kind: lax.all_gather(part.astype(kind), axis),
        array,
        (jnp.bfloat16, jnp.bfloat16, jnp.bfloat16),
    )
    start = jax.tree.map(
        lambda part, zero: jnp.broadcast_to(jnp.asarray(zero, part.dtype), part.shape),
        array,
        identity,
    )

    def hop(k, before):
        reached = k < here
        new = combine(
            before, jax.tree.map(lambda part, own: part[k].astype(own.dtype), everything, array)
        )
        return jax.tree.map(lambda a, b: jnp.where(reached, a, b), new, before)

    return lax.fori_loop(0, count, hop, start)


def features(vectors):
    constant = jnp.ones(vectors.shape[:-1] + (1,), jnp.float32)
    width = vectors.shape[-1]
    squares = (vectors[..., :, None] * vectors[..., None, :]).reshape(
        vectors.shape[:-1] + (width * width,)
    )
    return jnp.concatenate([constant, vectors, squares * 0.5**0.5], axis=-1)


def carry_in(valid_mask, decays, queries, numerator, denominator, flat_memory, key_sum):
    local_len = numerator.shape[0]
    feat_len, head_count = key_sum.shape
    value_len = flat_memory.shape[1] // head_count
    feat_in = queries.shape[1] // head_count
    decay_rate = jnp.where(valid_mask[:, None] > 0, decays, 0.0)
    span_decay = jnp.sum(decay_rate, axis=0)

    def merge_states(earlier, later):
        factor = jnp.exp(later[0])
        return (
            earlier[0] + later[0],
            earlier[1] * jnp.repeat(factor, value_len)[None, :] + later[1],
            earlier[2] * factor[None, :] + later[2],
        )

    neutral = (jnp.zeros_like(span_decay), jnp.zeros_like(flat_memory), jnp.zeros_like(key_sum))
    carried = entering((span_decay, flat_memory, key_sum), "seq", merge_states, neutral)
    prior_memory = carried[1]
    prior_keys = carried[2]
    highest = lax.Precision.HIGHEST
    growth = jnp.exp(jnp.cumsum(decay_rate, axis=0))
    query_feat = features(queries.astype(jnp.float32).reshape(local_len, head_count, feat_in))
    added = jnp.einsum(
        "thf,fhv->thv",
        query_feat,
        prior_memory.reshape(feat_len, head_count, value_len),
        precision=highest,
    )
    numerator = numerator + (added * growth[:, :, None]).reshape(local_len, -1)
    denominator = (
        denominator + jnp.einsum("thf,fh->th", query_feat, prior_keys, precision=highest) * growth
    )
    span_factor = jnp.exp(span_decay)
    end_state = prior_memory * jnp.repeat(span_factor, value_len)[None, :] + flat_memory
    end_norm = prior_keys * span_factor[None, :] + key_sum
    return numerator, denominator, end_state, end_norm


def permute(array, target):
    count = lax.axis_size("req")
    return lax.ppermute(array, "req", [(i, target(i)) for i in range(count)])


def flip_core(array):
    return permute(array, lambda i: i ^ 1)


def flip_near(array):
    return permute(array, lambda i: i ^ 2)


def flip_far(array):
    return permute(array, lambda i: i ^ 4)


def next_plane(array):
    count = lax.axis_size("req")
    return permute(array, lambda i: (i + 8) % count)


def together(*arrays):
    return lax.optimization_barrier(arrays)


def slot(*sends):
    operands = together(*[array for _, array in sends])
    return together(*[send(array) for (send, _), array in zip(sends, operands)])


def vmem(count):
    return [pl.BlockSpec(memory_space=pltpu.VMEM)] * count


def kernel_call(body, name, out_shape, *operands, scratch=(), aliases=None, specs=None, mib=24):
    many = isinstance(out_shape, tuple)
    return pl.pallas_call(
        body,
        out_shape=out_shape,
        in_specs=specs or vmem(len(operands)),
        out_specs=tuple(vmem(len(out_shape))) if many else vmem(1)[0],
        scratch_shapes=list(scratch),
        input_output_aliases=aliases or {},
        compiler_params=pltpu.CompilerParams(vmem_limit_bytes=mib * 1024 * 1024),
        cost_estimate=pl.CostEstimate(flops=1000, bytes_accessed=1000, transcendentals=0),
        name=name,
    )(*operands)


def like(rows, columns, dtype):
    return jax.ShapeDtypeStruct((rows, columns), dtype)


NT = (((1,), (1,)), ((), ()))


def unit_rows(rows, gain):
    factor = lax.rsqrt(jnp.mean(rows * rows, axis=-1, keepdims=True) + 1e-05)
    return (rows * factor * gain).astype(jnp.bfloat16).astype(jnp.float32)


def project_body(
    step,
    scale,
    rows_ref,
    edge_ref,
    gain_ref,
    conv_ref,
    query_ref,
    key_ref,
    value_ref,
    queries_ref,
    keys_ref,
    values_ref,
    normed,
    gated,
):
    gain = gain_ref[...]
    count = rows_ref.shape[0]
    lead = edge_ref.shape[0]
    taps = conv_ref.shape[0]
    normed[:lead] = unit_rows(edge_ref[...].astype(jnp.float32), gain)

    @pl.loop(0, count // step)
    def _(block):
        at = pl.multiple_of(block * step, step)
        rows = rows_ref[pl.ds(at, step), :].astype(jnp.float32)
        normed[pl.ds(lead + at, step), :] = unit_rows(rows, gain)

    @pl.loop(0, count // step)
    def _(block):
        at = pl.multiple_of(block * step, step)
        window = normed[pl.ds(at, step + lead), :]
        here = window[lead:]
        total = conv_ref[0:1] * here
        for tap in range(1, taps):
            total = total + conv_ref[tap : tap + 1] * window[lead - tap : lead - tap + step]
        gated[pl.ds(at, step), :] = (total * jax.nn.sigmoid(here)).astype(jnp.bfloat16)

    rows = gated[...]
    for weight_ref, out_ref, factor in (
        (query_ref, queries_ref, scale),
        (key_ref, keys_ref, scale),
        (value_ref, values_ref, None),
    ):
        product = jnp.dot(rows, weight_ref[...], preferred_element_type=jnp.float32)
        if factor is not None:
            product = product * factor
        out_ref[...] = product.astype(jnp.bfloat16)


def project(rows, edge, mix_gain, conv_weight, query_weight, key_weight, value_weight, scale):
    count, width = rows.shape
    step = 32
    return kernel_call(
        functools.partial(project_body, step, scale),
        "project",
        tuple(like(count, w.shape[1], jnp.bfloat16) for w in (query_weight, key_weight, value_weight)),
        rows,
        edge,
        mix_gain[None],
        conv_weight,
        query_weight,
        key_weight,
        value_weight,
        scratch=(
            pltpu.VMEM((count + edge.shape[0], width), jnp.float32),
            pltpu.VMEM((count, width), jnp.bfloat16),
        ),
    )


def attend_body(
    feat_in,
    value_len,
    count_ref,
    rate_ref,
    queries_ref,
    keys_ref,
    values_ref,
    numer_ref,
    denom_ref,
    state_ref,
    norm_ref,
    turned,
    total,
    norms,
):
    heads, count = rate_ref.shape
    columns = values_ref.shape[1]
    lane = lax.broadcasted_iota(jnp.int32, (count, count), 1)
    row = lax.broadcasted_iota(jnp.int32, (count, count), 0)
    valid = (lane[:1] < count_ref[0]).astype(jnp.float32)
    rate = jnp.where(valid > 0, rate_ref[...], 0.0)
    upto = (row <= lane).astype(jnp.float32)
    across = jnp.dot(
        rate, upto, precision=lax.Precision.HIGHEST, preferred_element_type=jnp.float32
    )
    down = across.T
    closing = across[:, count - 1 : count]
    fading = jnp.exp(closing - across) * valid
    causal = row >= lane
    keys = keys_ref[...]
    turned[...] = keys.astype(jnp.float32).T
    owner = lax.broadcasted_iota(jnp.int32, queries_ref.shape, 1)
    spare = lax.broadcasted_iota(jnp.int32, (8, count), 0) == 0
    head_lane = lax.broadcasted_iota(jnp.int32, (count, 128), 1)
    numer_ref[...] = jnp.zeros(numer_ref.shape, jnp.float32)
    total[...] = jnp.zeros(total.shape, jnp.float32)
    norms[...] = jnp.zeros(norms.shape, jnp.float32)
    norm_total = jnp.zeros((total.shape[0], 128), jnp.float32)
    denominators = jnp.zeros((count, 128), jnp.float32)
    for h in range(heads):
        low = min(h * value_len // 128 * 128, max(columns - 256, 0))
        high = min(low + 256, columns)
        mine = lax.broadcasted_iota(jnp.int32, (count, high - low), 1) + low
        mine = (mine >= h * value_len) & (mine < (h + 1) * value_len)
        values = jnp.where(mine, values_ref[:, low:high].astype(jnp.float32), 0.0)
        values = values.astype(jnp.bfloat16)
        asks = (owner >= h * feat_in) & (owner < (h + 1) * feat_in)
        queries = jnp.where(asks, queries_ref[...].astype(jnp.float32), 0.0)
        scores = lax.dot_general(
            queries.astype(jnp.bfloat16), keys, NT, preferred_element_type=jnp.float32
        )
        gap = down[:, h : h + 1] - across[h : h + 1]
        weights = jnp.where(causal, jnp.exp(jnp.minimum(gap, 0.0)) * valid, 0.0)
        weights = weights * (1.0 + scores + 0.5 * scores * scores)
        numer_ref[:, low:high] += jnp.dot(
            weights.astype(jnp.bfloat16), values, preferred_element_type=jnp.float32
        )
        sums = jnp.sum(weights, axis=1, keepdims=True)
        denominators = jnp.where(head_lane == h, sums, denominators)
        own = turned[h * feat_in : (h + 1) * feat_in]
        fade = fading[h : h + 1]
        faded = own * fade
        scaled = faded * 0.5**0.5
        parts = [own[i : i + 1] * scaled for i in range(feat_in)]
        parts += [faded, jnp.where(spare, fade, 0.0)]
        feats = jnp.concatenate(parts, axis=0).astype(jnp.bfloat16)
        total[:, low:high] += jnp.dot(feats, values, preferred_element_type=jnp.float32)
        mark = (head_lane == h).astype(jnp.bfloat16)
        norm_total = norm_total + jnp.dot(feats, mark, preferred_element_type=jnp.float32)
    denom_ref[...] = denominators[:, :heads]
    pairs = feat_in * feat_in
    state_ref[0] = total[pairs + feat_in : pairs + feat_in + 1, :]
    for f in range(feat_in):
        state_ref[1 + f] = total[pairs + f : pairs + f + 1, :]

    @pl.loop(0, pairs // 8)
    def _(block):
        for k in range(8):
            f = block * 8 + k
            state_ref[1 + feat_in + f] = total[pl.ds(f, 1), :]

    norms[0:1, :] = norm_total[pairs + feat_in : pairs + feat_in + 1]
    norms[1 : 1 + feat_in, :] = norm_total[pairs : pairs + feat_in]
    norms[1 + feat_in : 1 + feat_in + pairs, :] = norm_total[:pairs]
    norm_ref[...] = norms[...].T[:heads, : 1 + feat_in + pairs]


def attend(valid_count, rate, queries, keys, values, feat_in, value_len):
    heads, count = rate.shape
    columns = values.shape[1]
    feat_len = 1 + feat_in + feat_in * feat_in
    padded = feat_in * feat_in + feat_in + 8
    return kernel_call(
        functools.partial(attend_body, feat_in, value_len),
        "attend",
        (
            like(count, columns, jnp.float32),
            like(count, heads, jnp.float32),
            jax.ShapeDtypeStruct((feat_len, 1, columns), jnp.float32),
            like(heads, feat_len, jnp.float32),
        ),
        valid_count,
        rate,
        queries,
        keys,
        values,
        specs=[pl.BlockSpec(memory_space=pltpu.SMEM)] + vmem(4),
        scratch=(
            pltpu.VMEM((queries.shape[1], count), jnp.float32),
            pltpu.VMEM((padded, columns), jnp.float32),
            pltpu.VMEM(((feat_len + 127) // 128 * 128, 128), jnp.float32),
        ),
    )


def mix_body(
    value_len, step, numer_ref, denom_ref, rows_ref, out_ref, gain_ref, mixed_ref, mlp_ref, sums
):
    count, columns = numer_ref.shape
    heads = denom_ref.shape[1]
    column = lax.broadcasted_iota(jnp.int32, (1, columns), 1)
    inverse = 1.0 / denom_ref[...]
    spread = jnp.zeros((count, columns), jnp.float32)
    for h in range(heads):
        here = (column >= h * value_len) & (column < (h + 1) * value_len)
        spread = jnp.where(here, inverse[:, h : h + 1], spread)
    attended = (numer_ref[...] * spread).astype(jnp.bfloat16)
    sums[...] = jnp.dot(attended, out_ref[...], preferred_element_type=jnp.float32)
    gain = gain_ref[...]

    @pl.loop(0, count // step)
    def _(block):
        at = pl.ds(pl.multiple_of(block * step, step), step)
        mixed = (rows_ref[at, :].astype(jnp.float32) + sums[at, :]).astype(jnp.bfloat16)
        mixed_ref[at, :] = mixed
        mlp_ref[at, :] = unit_rows(mixed.astype(jnp.float32), gain).astype(jnp.bfloat16)


def mix(numer, denom, rows, out_weight, mlp_gain, value_len):
    count, width = rows.shape
    shape = like(count, width, jnp.bfloat16)
    return kernel_call(
        functools.partial(mix_body, value_len, 32),
        "mix",
        (shape, shape),
        numer,
        denom,
        rows,
        out_weight,
        mlp_gain[None],
        scratch=(pltpu.VMEM((count, width), jnp.float32),),
    )


def swiglu_terms(rows, gate_rows, up_rows, down_rows):
    gate_act = lax.dot_general(rows, gate_rows, NT, preferred_element_type=jnp.float32)
    up_act = lax.dot_general(rows, up_rows, NT, preferred_element_type=jnp.float32)
    hidden_units = (gate_act * jax.nn.sigmoid(gate_act) * up_act).astype(jnp.bfloat16)
    return jnp.dot(hidden_units, down_rows, preferred_element_type=jnp.float32)


def on_grid(run):
    return all(low % 16 == 0 and high % 16 == 0 for _, low, high in run)


def read_units(refs, units):
    parts = []
    for k in range(3):
        rows = [refs[run[k][0]][run[k][1] : run[k][2]] for run in units if on_grid(run)]
        rest = [
            refs[run[k][0]][...].astype(jnp.float32)[run[k][1] : run[k][2]]
            for run in units
            if not on_grid(run)
        ]
        if rest:
            rows.append(jnp.concatenate(rest, axis=0).astype(jnp.bfloat16))
        parts.append(jnp.concatenate(rows, axis=0))
    return parts


def accumulate_body(units, n_weights, n_rows, n_acc, residual, *refs):
    weights = refs[:n_weights]
    rows = refs[n_weights : n_weights + n_rows]
    acc = refs[n_weights + n_rows : n_weights + n_rows + n_acc]
    parts = read_units(weights, units)
    for k, rows_ref in enumerate(rows):
        out_ref = refs[len(refs) - n_rows + k]
        terms = swiglu_terms(rows_ref[...], *parts)
        if n_acc:
            terms = terms + acc[k][...]
        if residual:
            terms = terms + refs[n_weights + n_rows + n_acc][...].astype(jnp.float32)
        out_ref[...] = terms.astype(out_ref.dtype)


def accumulate(rows, weights, units, acc, dtype, name, residual=None):
    shapes = tuple(like(*array.shape, dtype) for array in rows)
    start = len(weights) + len(rows)
    aliases = {start + k: k for k in range(len(acc))} if dtype == jnp.float32 else {}
    extra = () if residual is None else (residual,)
    body = functools.partial(
        accumulate_body, tuple(units), len(weights), len(rows), len(acc), bool(extra)
    )
    return kernel_call(body, name, shapes, *weights, *rows, *acc, *extra, aliases=aliases)


def runs(which, low, size):
    return tuple((which, low + k * size, low + (k + 1) * size) for k in range(3))


def split_runs(first, second, main):
    (i, at), (j, then) = first, second
    held = 2 * main // 3
    rest = main - held
    return (
        ((i, at, at + held), (i, at + main, at + main + held), (j, then + rest, then + main)),
        ((i, at + held, at + main), (j, then, then + rest), (j, then + main, then + rest + main)),
    )


def collect_body(plans, *refs):
    outs = refs[len(refs) - len(plans) :]
    for out_ref, plan in zip(outs, plans):
        rows = [refs[i][...].astype(jnp.float32)[low:high] for i, low, high in plan]
        out_ref[...] = jnp.concatenate(rows, axis=0).astype(jnp.bfloat16)


def collect(arrays, plans, name):
    columns = arrays[0].shape[1]
    shapes = tuple(like(sum(h - l for _, l, h in plan), columns, jnp.bfloat16) for plan in plans)
    return kernel_call(functools.partial(collect_body, plans), name, shapes, *arrays)


def shard_body(main, gate_ref, up_ref, down_ref, shard_ref, main_ref, *rest):
    buffers, sems = rest[:3], rest[3]
    copies = [
        pltpu.make_async_copy(source, buffer, sems.at[k])
        for k, (source, buffer) in enumerate(zip((gate_ref, up_ref, down_ref), buffers))
    ]
    for copy in copies:
        copy.start()
    for copy in copies:
        copy.wait()
    arrays = [buffer[...].astype(jnp.float32) for buffer in buffers]
    tops = [array[:main] for array in arrays]
    ends = [array[main:] for array in arrays]
    shard_ref[...] = jnp.concatenate(tops + ends, axis=0).astype(jnp.bfloat16)
    main_ref[...] = jnp.concatenate(tops, axis=0).astype(jnp.bfloat16)


def final_body(step, count_ref, kept_ref, given_ref, out_ref):
    count = kept_ref.shape[0]

    @pl.loop(0, count // step)
    def _(block):
        first = pl.multiple_of(block * step, step)
        at = pl.ds(first, step)
        total = kept_ref[at, :] + given_ref[at, :].astype(jnp.float32)
        row = lax.broadcasted_iota(jnp.int32, total.shape, 0) + first
        out_ref[at, :] = jnp.where(row < count_ref[0], total, 0.0).astype(out_ref.dtype)


def local(
    hidden_in,
    lengths,
    log_decay,
    mix_gain,
    conv_weight,
    query_weight,
    key_weight,
    value_weight,
    out_weight,
    mlp_gain,
    gate_weight,
    up_weight,
    down_weight,
):
    local_len = hidden_in.shape[1]
    rows_in = hidden_in[0]
    decays = log_decay[0]
    head_count = log_decay.shape[2]
    value_len = value_weight.shape[1] // head_count
    feat_in = query_weight.shape[1] // head_count
    feature_scale = feat_in ** (-0.25)
    valid_count = lengths - lax.axis_index("seq") * local_len
    spans = lax.axis_size("seq")
    units, model = gate_weight.shape[1], gate_weight.shape[0]
    edge = units // 7
    main = units - edge
    wide = 3 * main
    full = 3 * units
    narrow = full - wide
    cut = main + 2 * main // 3

    shard, shard_main = kernel_call(
        functools.partial(shard_body, main),
        "shard",
        (like(full, model, jnp.bfloat16), like(wide, model, jnp.bfloat16)),
        gate_weight.T,
        up_weight.T,
        down_weight.T,
        specs=[pl.BlockSpec(memory_space=pl.ANY)] * 3,
        scratch=[pltpu.VMEM((units, model), jnp.bfloat16)] * 3 + [pltpu.SemaphoreType.DMA((3,))],
        mib=56,
    )
    near, far, deep = slot((flip_near, shard), (flip_far, shard), (next_plane, shard_main))

    lead = 16
    if spans > 1:
        edge_in = from_behind(rows_in[local_len - lead :], "seq", 1)
    else:
        edge_in = jnp.zeros((lead, model), jnp.bfloat16)
    queries, key_rows, values = project(
        rows_in, edge_in, mix_gain, conv_weight, query_weight, key_weight, value_weight, feature_scale
    )
    near, far, deep, queries, key_rows, values = together(
        near, far, deep, queries, key_rows, values
    )

    sends = collect(
        (shard, near, far, deep),
        (
            ((3, 0, wide), (2, 0, cut)),
            ((3, 0, wide), (1, cut, full)),
            ((3, 0, wide), (0, wide, full), (1, wide, full), (2, wide, full)),
        ),
        "collect_second",
    )
    near1, far1, deep1 = slot(*zip((flip_near, flip_far, next_plane), sends))

    numerator, denominator, end_state, end_norm = attend(
        valid_count, log_decay[0].T, queries, key_rows, values, feat_in, value_len
    )
    if spans > 1:
        positions = jnp.arange(local_len, dtype=jnp.int32)
        numerator, denominator, end_state, end_norm = carry_in(
            (positions < valid_count).astype(jnp.float32),
            decays,
            queries,
            numerator,
            denominator,
            end_state[:, 0],
            end_norm.T,
        )
    else:
        end_norm = end_norm.T
    mixed_rows, mlp_in = mix(numerator, denominator, rows_in, out_weight, mlp_gain, value_len)
    near1, far1, deep1, mixed_rows, mlp_in, end_state, end_norm = together(
        near1, far1, deep1, mixed_rows, mlp_in, end_state, end_norm
    )

    sends = collect(
        (near1, far1, deep1),
        (
            ((2, 0, wide), (1, 0, cut)),
            ((2, 0, wide), (0, cut, wide)),
            ((2, 0, wide + 3 * narrow), (1, wide + wide - cut, wide + full - cut)),
        ),
        "collect_third",
    )
    near2, far2, deep2 = slot(*zip((flip_near, flip_far, next_plane), sends))
    rows = (mlp_in, flip_core(mlp_in))
    acc = accumulate(
        rows,
        (shard, near, far, deep, near1, far1, deep1),
        [runs(i, 0, main) for i in range(7)] + list(split_runs((4, wide), (5, wide), main)),
        (),
        jnp.float32,
        "accumulate_second",
    )
    near2, far2, deep2 = together(near2, far2, deep2)

    held = 2 * main // 3
    deep3_main, line = collect(
        (far2, deep2),
        (
            ((1, 0, wide),),
            ((1, wide, wide + 4 * narrow), (0, 2 * wide - cut - main, 2 * wide - cut - main + held)),
        ),
        "collect_fourth",
    )
    near3, far3, deep3 = slot((flip_near, deep3_main), (flip_far, deep3_main), (next_plane, line))
    acc = accumulate(
        rows,
        (shard, near, far, far1, deep1, near2, far2, deep2),
        [runs(i, 0, main) for i in (5, 6, 7)]
        + list(split_runs((5, wide), (6, wide), main))
        + [runs(i, wide, edge) for i in (0, 1, 2)]
        + [runs(3, wide + wide - cut, edge)]
        + [runs(4, wide + k * narrow, edge) for k in range(3)]
        + [runs(7, wide + k * narrow, edge) for k in range(4)],
        tuple(acc),
        jnp.float32,
        "accumulate_third",
    )
    near3, far3, deep3, *acc = together(near3, far3, deep3, *acc)

    two = 2 * main
    sends = collect(
        (near2, far2, near3, far3, deep3),
        (
            ((1, 0, main), (1, two + held, wide), (3, 0, main)),
            ((0, main, two), (2, main, two), (2, two + held, wide)),
            ((4, 3 * narrow, 4 * narrow + held),),
        ),
        "collect_fifth",
    )
    near4, far4, deep4 = slot(*zip((flip_near, flip_far, next_plane), sends))
    acc = accumulate(
        rows,
        (near3, far3, deep3),
        [runs(0, 0, main), runs(1, 0, main)] + [runs(2, k * narrow, edge) for k in range(4)],
        tuple(acc),
        jnp.float32,
        "accumulate_fourth",
    )
    weights = (near4, far4, deep3, deep4)
    line, then = 4 * narrow, two - held
    last = [
        ((0, 0, held), (1, 0, held), (2, line, line + held)),
        ((0, held, main), (1, held, main), (0, main, then)),
        ((0, then, then + held), (1, main, main + held), (3, narrow, narrow + held)),
        ((0, then + held, then + main), (1, main + held, two), (1, two, two + main - held)),
        runs(3, 0, edge),
    ]
    (given,) = accumulate(rows[1:], weights, last, acc[1:], jnp.bfloat16, "finish_other")
    (kept,) = accumulate(
        rows[:1], weights, last, acc[:1], jnp.float32, "finish_own", residual=mixed_rows
    )
    result = kernel_call(
        functools.partial(final_body, 64),
        "final",
        like(local_len, model, jnp.bfloat16),
        valid_count,
        kept,
        flip_core(given),
        specs=[pl.BlockSpec(memory_space=pltpu.SMEM)] + vmem(2),
    )
    return (
        result[None],
        end_state.reshape((1, 1) + end_state.shape[:1] + end_state.shape[-1:]),
        end_norm[None, None],
    )


def solution(mesh):
    return jax.shard_map(
        local,
        mesh=mesh,
        in_specs=(
            P("req", "seq", None),
            P("req"),
            P("req", "seq", None),
            P(),
            P(),
            P(),
            P(),
            P(),
            P(),
            P(),
            P(None, "req"),
            P(None, "req"),
            P(None, "req"),
        ),
        out_specs=(P("req", "seq", None), P("req", "seq", None, None), P("req", "seq", None, None)),
        check_vma=False,
    )
```

```python
import functools

import jax
import jax.numpy as jnp
from jax import lax
from jax.experimental import pallas as pl
from jax.experimental.pallas import tpu as pltpu
from jax.sharding import PartitionSpec as P


def from_behind(array, axis, by):
    count = lax.axis_size(axis)
    pairs = [(i, i + by) for i in range(count) if 0 <= i + by < count]
    return lax.ppermute(array, axis, pairs)


def entering(array, axis, combine, identity):
    count, here = (lax.axis_size(axis), lax.axis_index(axis))
    everything = jax.tree.map(
        lambda part, kind: lax.all_gather(part.astype(kind), axis),
        array,
        (jnp.bfloat16, jnp.bfloat16, jnp.bfloat16),
    )
    start = jax.tree.map(
        lambda part, zero: jnp.broadcast_to(jnp.asarray(zero, part.dtype), part.shape),
        array,
        identity,
    )

    def hop(k, before):
        reached = k < here
        new = combine(
            before, jax.tree.map(lambda part, own: part[k].astype(own.dtype), everything, array)
        )
        return jax.tree.map(lambda a, b: jnp.where(reached, a, b), new, before)

    return lax.fori_loop(0, count, hop, start)


def features(vectors):
    constant = jnp.ones(vectors.shape[:-1] + (1,), jnp.float32)
    width = vectors.shape[-1]
    squares = (vectors[..., :, None] * vectors[..., None, :]).reshape(
        vectors.shape[:-1] + (width * width,)
    )
    return jnp.concatenate([constant, vectors, squares * 0.5**0.5], axis=-1)


def carry_in(valid_mask, decays, queries, numerator, denominator, flat_memory, key_sum):
    local_len = numerator.shape[0]
    feat_len, head_count = key_sum.shape
    value_len = flat_memory.shape[1] // head_count
    feat_in = queries.shape[1] // head_count
    decay_rate = jnp.where(valid_mask[:, None] > 0, decays, 0.0)
    span_decay = jnp.sum(decay_rate, axis=0)

    def merge_states(earlier, later):
        factor = jnp.exp(later[0])
        return (
            earlier[0] + later[0],
            earlier[1] * jnp.repeat(factor, value_len)[None, :] + later[1],
            earlier[2] * factor[None, :] + later[2],
        )

    neutral = (jnp.zeros_like(span_decay), jnp.zeros_like(flat_memory), jnp.zeros_like(key_sum))
    carried = entering((span_decay, flat_memory, key_sum), "seq", merge_states, neutral)
    prior_memory = carried[1]
    prior_keys = carried[2]
    highest = lax.Precision.HIGHEST
    growth = jnp.exp(jnp.cumsum(decay_rate, axis=0))
    query_feat = features(queries.astype(jnp.float32).reshape(local_len, head_count, feat_in))
    added = jnp.einsum(
        "thf,fhv->thv",
        query_feat,
        prior_memory.reshape(feat_len, head_count, value_len),
        precision=highest,
    )
    numerator = numerator + (added * growth[:, :, None]).reshape(local_len, -1)
    denominator = (
        denominator + jnp.einsum("thf,fh->th", query_feat, prior_keys, precision=highest) * growth
    )
    span_factor = jnp.exp(span_decay)
    end_state = prior_memory * jnp.repeat(span_factor, value_len)[None, :] + flat_memory
    end_norm = prior_keys * span_factor[None, :] + key_sum
    return numerator, denominator, end_state, end_norm


def permute(array, target):
    count = lax.axis_size("req")
    return lax.ppermute(array, "req", [(i, target(i)) for i in range(count)])


def flip_core(array):
    return permute(array, lambda i: i ^ 1)


def flip_near(array):
    return permute(array, lambda i: i ^ 2)


def flip_far(array):
    return permute(array, lambda i: i ^ 4)


def next_plane(array):
    return permute(array, lambda i: i ^ (16 if i // 8 in (1, 2) else 8))


def together(*arrays):
    return lax.optimization_barrier(arrays)


def slot(*sends):
    operands = together(*[array for _, array in sends])
    return together(*[send(array) for (send, _), array in zip(sends, operands)])


def vmem(count):
    return [pl.BlockSpec(memory_space=pltpu.VMEM)] * count


def kernel_call(body, name, out_shape, *operands, scratch=(), aliases=None, specs=None, mib=24):
    many = isinstance(out_shape, tuple)
    return pl.pallas_call(
        body,
        out_shape=out_shape,
        in_specs=specs or vmem(len(operands)),
        out_specs=tuple(vmem(len(out_shape))) if many else vmem(1)[0],
        scratch_shapes=list(scratch),
        input_output_aliases=aliases or {},
        compiler_params=pltpu.CompilerParams(vmem_limit_bytes=mib * 1024 * 1024),
        cost_estimate=pl.CostEstimate(flops=1000, bytes_accessed=1000, transcendentals=0),
        name=name,
    )(*operands)


def like(rows, columns, dtype):
    return jax.ShapeDtypeStruct((rows, columns), dtype)


NT = (((1,), (1,)), ((), ()))


def unit_rows(rows, gain):
    factor = lax.rsqrt(jnp.mean(rows * rows, axis=-1, keepdims=True) + 1e-05)
    return (rows * factor * gain).astype(jnp.bfloat16).astype(jnp.float32)


def project_body(
    step,
    scale,
    rows_ref,
    edge_ref,
    gain_ref,
    conv_ref,
    query_ref,
    key_ref,
    value_ref,
    queries_ref,
    keys_ref,
    values_ref,
    normed,
    gated,
):
    gain = gain_ref[...]
    count = rows_ref.shape[0]
    lead = edge_ref.shape[0]
    taps = conv_ref.shape[0]
    normed[:lead] = unit_rows(edge_ref[...].astype(jnp.float32), gain)

    @pl.loop(0, count // step)
    def _(block):
        at = pl.multiple_of(block * step, step)
        rows = rows_ref[pl.ds(at, step), :].astype(jnp.float32)
        normed[pl.ds(lead + at, step), :] = unit_rows(rows, gain)

    @pl.loop(0, count // step)
    def _(block):
        at = pl.multiple_of(block * step, step)
        window = normed[pl.ds(at, step + lead), :]
        here = window[lead:]
        total = conv_ref[0:1] * here
        for tap in range(1, taps):
            total = total + conv_ref[tap : tap + 1] * window[lead - tap : lead - tap + step]
        gated[pl.ds(at, step), :] = (total * jax.nn.sigmoid(here)).astype(jnp.bfloat16)

    rows = gated[...]
    for weight_ref, out_ref, factor in (
        (query_ref, queries_ref, scale),
        (key_ref, keys_ref, scale),
        (value_ref, values_ref, None),
    ):
        product = jnp.dot(rows, weight_ref[...], preferred_element_type=jnp.float32)
        if factor is not None:
            product = product * factor
        out_ref[...] = product.astype(jnp.bfloat16)


def project(rows, edge, mix_gain, conv_weight, query_weight, key_weight, value_weight, scale):
    count, width = rows.shape
    step = 32
    return kernel_call(
        functools.partial(project_body, step, scale),
        "project",
        tuple(like(count, w.shape[1], jnp.bfloat16) for w in (query_weight, key_weight, value_weight)),
        rows,
        edge,
        mix_gain[None],
        conv_weight,
        query_weight,
        key_weight,
        value_weight,
        scratch=(
            pltpu.VMEM((count + edge.shape[0], width), jnp.float32),
            pltpu.VMEM((count, width), jnp.bfloat16),
        ),
    )


def attend_body(
    feat_in,
    value_len,
    count_ref,
    rate_ref,
    queries_ref,
    keys_ref,
    values_ref,
    numer_ref,
    denom_ref,
    state_ref,
    norm_ref,
    turned,
    total,
    norms,
):
    heads, count = rate_ref.shape
    columns = values_ref.shape[1]
    lane = lax.broadcasted_iota(jnp.int32, (count, count), 1)
    row = lax.broadcasted_iota(jnp.int32, (count, count), 0)
    valid = (lane[:1] < count_ref[0]).astype(jnp.float32)
    rate = jnp.where(valid > 0, rate_ref[...], 0.0)
    upto = (row <= lane).astype(jnp.float32)
    across = jnp.dot(
        rate, upto, precision=lax.Precision.HIGHEST, preferred_element_type=jnp.float32
    )
    down = across.T
    closing = across[:, count - 1 : count]
    fading = jnp.exp(closing - across) * valid
    causal = row >= lane
    keys = keys_ref[...]
    turned[...] = keys.astype(jnp.float32).T
    owner = lax.broadcasted_iota(jnp.int32, queries_ref.shape, 1)
    spare = lax.broadcasted_iota(jnp.int32, (8, count), 0) == 0
    head_lane = lax.broadcasted_iota(jnp.int32, (count, 128), 1)
    numer_ref[...] = jnp.zeros(numer_ref.shape, jnp.float32)
    total[...] = jnp.zeros(total.shape, jnp.float32)
    norms[...] = jnp.zeros(norms.shape, jnp.float32)
    norm_total = jnp.zeros((total.shape[0], 128), jnp.float32)
    denominators = jnp.zeros((count, 128), jnp.float32)
    for h in range(heads):
        low = min(h * value_len // 128 * 128, max(columns - 256, 0))
        high = min(low + 256, columns)
        mine = lax.broadcasted_iota(jnp.int32, (count, high - low), 1) + low
        mine = (mine >= h * value_len) & (mine < (h + 1) * value_len)
        values = jnp.where(mine, values_ref[:, low:high].astype(jnp.float32), 0.0)
        values = values.astype(jnp.bfloat16)
        asks = (owner >= h * feat_in) & (owner < (h + 1) * feat_in)
        queries = jnp.where(asks, queries_ref[...].astype(jnp.float32), 0.0)
        scores = lax.dot_general(
            queries.astype(jnp.bfloat16), keys, NT, preferred_element_type=jnp.float32
        )
        gap = down[:, h : h + 1] - across[h : h + 1]
        weights = jnp.where(causal, jnp.exp(jnp.minimum(gap, 0.0)) * valid, 0.0)
        weights = weights * (1.0 + scores + 0.5 * scores * scores)
        numer_ref[:, low:high] += jnp.dot(
            weights.astype(jnp.bfloat16), values, preferred_element_type=jnp.float32
        )
        sums = jnp.sum(weights, axis=1, keepdims=True)
        denominators = jnp.where(head_lane == h, sums, denominators)
        own = turned[h * feat_in : (h + 1) * feat_in]
        fade = fading[h : h + 1]
        faded = own * fade
        scaled = faded * 0.5**0.5
        parts = [own[i : i + 1] * scaled for i in range(feat_in)]
        parts += [faded, jnp.where(spare, fade, 0.0)]
        feats = jnp.concatenate(parts, axis=0).astype(jnp.bfloat16)
        total[:, low:high] += jnp.dot(feats, values, preferred_element_type=jnp.float32)
        mark = (head_lane == h).astype(jnp.bfloat16)
        norm_total = norm_total + jnp.dot(feats, mark, preferred_element_type=jnp.float32)
    denom_ref[...] = denominators[:, :heads]
    pairs = feat_in * feat_in
    state_ref[0] = total[pairs + feat_in : pairs + feat_in + 1, :]
    for f in range(feat_in):
        state_ref[1 + f] = total[pairs + f : pairs + f + 1, :]

    @pl.loop(0, pairs // 8)
    def _(block):
        for k in range(8):
            f = block * 8 + k
            state_ref[1 + feat_in + f] = total[pl.ds(f, 1), :]

    norms[0:1, :] = norm_total[pairs + feat_in : pairs + feat_in + 1]
    norms[1 : 1 + feat_in, :] = norm_total[pairs : pairs + feat_in]
    norms[1 + feat_in : 1 + feat_in + pairs, :] = norm_total[:pairs]
    norm_ref[...] = norms[...].T[:heads, : 1 + feat_in + pairs]


def attend(valid_count, rate, queries, keys, values, feat_in, value_len):
    heads, count = rate.shape
    columns = values.shape[1]
    feat_len = 1 + feat_in + feat_in * feat_in
    padded = feat_in * feat_in + feat_in + 8
    return kernel_call(
        functools.partial(attend_body, feat_in, value_len),
        "attend",
        (
            like(count, columns, jnp.float32),
            like(count, heads, jnp.float32),
            jax.ShapeDtypeStruct((feat_len, 1, columns), jnp.float32),
            like(heads, feat_len, jnp.float32),
        ),
        valid_count,
        rate,
        queries,
        keys,
        values,
        specs=[pl.BlockSpec(memory_space=pltpu.SMEM)] + vmem(4),
        scratch=(
            pltpu.VMEM((queries.shape[1], count), jnp.float32),
            pltpu.VMEM((padded, columns), jnp.float32),
            pltpu.VMEM(((feat_len + 127) // 128 * 128, 128), jnp.float32),
        ),
    )


def mix_body(
    value_len, step, numer_ref, denom_ref, rows_ref, out_ref, gain_ref, mixed_ref, mlp_ref, sums
):
    count, columns = numer_ref.shape
    heads = denom_ref.shape[1]
    column = lax.broadcasted_iota(jnp.int32, (1, columns), 1)
    inverse = 1.0 / denom_ref[...]
    spread = jnp.zeros((count, columns), jnp.float32)
    for h in range(heads):
        here = (column >= h * value_len) & (column < (h + 1) * value_len)
        spread = jnp.where(here, inverse[:, h : h + 1], spread)
    attended = (numer_ref[...] * spread).astype(jnp.bfloat16)
    sums[...] = jnp.dot(attended, out_ref[...], preferred_element_type=jnp.float32)
    gain = gain_ref[...]

    @pl.loop(0, count // step)
    def _(block):
        at = pl.ds(pl.multiple_of(block * step, step), step)
        mixed = (rows_ref[at, :].astype(jnp.float32) + sums[at, :]).astype(jnp.bfloat16)
        mixed_ref[at, :] = mixed
        mlp_ref[at, :] = unit_rows(mixed.astype(jnp.float32), gain).astype(jnp.bfloat16)


def mix(numer, denom, rows, out_weight, mlp_gain, value_len):
    count, width = rows.shape
    shape = like(count, width, jnp.bfloat16)
    return kernel_call(
        functools.partial(mix_body, value_len, 32),
        "mix",
        (shape, shape),
        numer,
        denom,
        rows,
        out_weight,
        mlp_gain[None],
        scratch=(pltpu.VMEM((count, width), jnp.float32),),
    )


def swiglu_terms(rows, gate_rows, up_rows, down_rows):
    gate_act = lax.dot_general(rows, gate_rows, NT, preferred_element_type=jnp.float32)
    up_act = lax.dot_general(rows, up_rows, NT, preferred_element_type=jnp.float32)
    hidden_units = (gate_act * jax.nn.sigmoid(gate_act) * up_act).astype(jnp.bfloat16)
    return jnp.dot(hidden_units, down_rows, preferred_element_type=jnp.float32)


def on_grid(run):
    return all(low % 16 == 0 and high % 16 == 0 for _, low, high in run)


def read_units(refs, units):
    parts = []
    for k in range(3):
        rows = [refs[run[k][0]][run[k][1] : run[k][2]] for run in units if on_grid(run)]
        rest = [
            refs[run[k][0]][...].astype(jnp.float32)[run[k][1] : run[k][2]]
            for run in units
            if not on_grid(run)
        ]
        if rest:
            rows.append(jnp.concatenate(rest, axis=0).astype(jnp.bfloat16))
        parts.append(jnp.concatenate(rows, axis=0))
    return parts


def accumulate_body(units, n_weights, n_rows, n_acc, residual, *refs):
    weights = refs[:n_weights]
    rows = refs[n_weights : n_weights + n_rows]
    acc = refs[n_weights + n_rows : n_weights + n_rows + n_acc]
    parts = read_units(weights, units)
    for k, rows_ref in enumerate(rows):
        out_ref = refs[len(refs) - n_rows + k]
        terms = swiglu_terms(rows_ref[...], *parts)
        if n_acc:
            terms = terms + acc[k][...]
        if residual:
            terms = terms + refs[n_weights + n_rows + n_acc][...].astype(jnp.float32)
        out_ref[...] = terms.astype(out_ref.dtype)


def accumulate(rows, weights, units, acc, dtype, name, residual=None):
    shapes = tuple(like(*array.shape, dtype) for array in rows)
    start = len(weights) + len(rows)
    aliases = {start + k: k for k in range(len(acc))} if dtype == jnp.float32 else {}
    extra = () if residual is None else (residual,)
    body = functools.partial(
        accumulate_body, tuple(units), len(weights), len(rows), len(acc), bool(extra)
    )
    return kernel_call(body, name, shapes, *weights, *rows, *acc, *extra, aliases=aliases)


def runs(which, low, size):
    return tuple((which, low + k * size, low + (k + 1) * size) for k in range(3))


def split_runs(first, second, main):
    (i, at), (j, then) = first, second
    held = 2 * main // 3
    rest = main - held
    return (
        ((i, at, at + held), (i, at + main, at + main + held), (j, then + rest, then + main)),
        ((i, at + held, at + main), (j, then, then + rest), (j, then + main, then + rest + main)),
    )


def collect_body(plans, *refs):
    outs = refs[len(refs) - len(plans) :]
    for out_ref, plan in zip(outs, plans):
        rows = [refs[i][...].astype(jnp.float32)[low:high] for i, low, high in plan]
        out_ref[...] = jnp.concatenate(rows, axis=0).astype(jnp.bfloat16)


def collect(arrays, plans, name):
    columns = arrays[0].shape[1]
    shapes = tuple(like(sum(h - l for _, l, h in plan), columns, jnp.bfloat16) for plan in plans)
    return kernel_call(functools.partial(collect_body, plans), name, shapes, *arrays)


def shard_body(main, gate_ref, up_ref, down_ref, shard_ref, main_ref, *rest):
    buffers, sems = rest[:3], rest[3]
    copies = [
        pltpu.make_async_copy(source, buffer, sems.at[k])
        for k, (source, buffer) in enumerate(zip((gate_ref, up_ref, down_ref), buffers))
    ]
    for copy in copies:
        copy.start()
    for copy in copies:
        copy.wait()
    arrays = [buffer[...].astype(jnp.float32) for buffer in buffers]
    tops = [array[:main] for array in arrays]
    ends = [array[main:] for array in arrays]
    shard_ref[...] = jnp.concatenate(tops + ends, axis=0).astype(jnp.bfloat16)
    main_ref[...] = jnp.concatenate(tops, axis=0).astype(jnp.bfloat16)


def final_body(step, count_ref, kept_ref, given_ref, out_ref):
    count = kept_ref.shape[0]

    @pl.loop(0, count // step)
    def _(block):
        first = pl.multiple_of(block * step, step)
        at = pl.ds(first, step)
        total = kept_ref[at, :] + given_ref[at, :].astype(jnp.float32)
        row = lax.broadcasted_iota(jnp.int32, total.shape, 0) + first
        out_ref[at, :] = jnp.where(row < count_ref[0], total, 0.0).astype(out_ref.dtype)


def local(
    hidden_in,
    lengths,
    log_decay,
    mix_gain,
    conv_weight,
    query_weight,
    key_weight,
    value_weight,
    out_weight,
    mlp_gain,
    gate_weight,
    up_weight,
    down_weight,
):
    local_len = hidden_in.shape[1]
    rows_in = hidden_in[0]
    decays = log_decay[0]
    head_count = log_decay.shape[2]
    value_len = value_weight.shape[1] // head_count
    feat_in = query_weight.shape[1] // head_count
    feature_scale = feat_in ** (-0.25)
    valid_count = lengths - lax.axis_index("seq") * local_len
    spans = lax.axis_size("seq")
    units, model = gate_weight.shape[1], gate_weight.shape[0]
    edge = units // 7
    main = units - edge
    wide = 3 * main
    full = 3 * units
    narrow = full - wide
    cut = main + 2 * main // 3

    shard, shard_main = kernel_call(
        functools.partial(shard_body, main),
        "shard",
        (like(full, model, jnp.bfloat16), like(wide, model, jnp.bfloat16)),
        gate_weight.T,
        up_weight.T,
        down_weight.T,
        specs=[pl.BlockSpec(memory_space=pl.ANY)] * 3,
        scratch=[pltpu.VMEM((units, model), jnp.bfloat16)] * 3 + [pltpu.SemaphoreType.DMA((3,))],
        mib=56,
    )
    near, far, deep = slot((flip_near, shard), (flip_far, shard), (next_plane, shard_main))

    lead = 16
    if spans > 1:
        edge_in = from_behind(rows_in[local_len - lead :], "seq", 1)
    else:
        edge_in = jnp.zeros((lead, model), jnp.bfloat16)
    queries, key_rows, values = project(
        rows_in, edge_in, mix_gain, conv_weight, query_weight, key_weight, value_weight, feature_scale
    )
    near, far, deep, queries, key_rows, values = together(
        near, far, deep, queries, key_rows, values
    )

    sends = collect(
        (shard, near, far, deep),
        (
            ((3, 0, wide), (2, 0, cut)),
            ((3, 0, wide), (1, cut, full)),
            ((3, 0, wide), (0, wide, full), (1, wide, full), (2, wide, full)),
        ),
        "collect_second",
    )
    near1, far1, deep1 = slot(*zip((flip_near, flip_far, next_plane), sends))

    numerator, denominator, end_state, end_norm = attend(
        valid_count, log_decay[0].T, queries, key_rows, values, feat_in, value_len
    )
    if spans > 1:
        positions = jnp.arange(local_len, dtype=jnp.int32)
        numerator, denominator, end_state, end_norm = carry_in(
            (positions < valid_count).astype(jnp.float32),
            decays,
            queries,
            numerator,
            denominator,
            end_state[:, 0],
            end_norm.T,
        )
    else:
        end_norm = end_norm.T
    mixed_rows, mlp_in = mix(numerator, denominator, rows_in, out_weight, mlp_gain, value_len)
    near1, far1, deep1, mixed_rows, mlp_in, end_state, end_norm = together(
        near1, far1, deep1, mixed_rows, mlp_in, end_state, end_norm
    )

    sends = collect(
        (near1, far1, deep1),
        (
            ((2, 0, wide), (1, 0, cut)),
            ((2, 0, wide), (0, cut, wide)),
            ((2, 0, wide + 3 * narrow), (1, wide + wide - cut, wide + full - cut)),
        ),
        "collect_third",
    )
    near2, far2, deep2 = slot(*zip((flip_near, flip_far, next_plane), sends))
    rows = (mlp_in, flip_core(mlp_in))
    acc = accumulate(
        rows,
        (shard, near, far, deep, near1, far1, deep1),
        [runs(i, 0, main) for i in range(7)] + list(split_runs((4, wide), (5, wide), main)),
        (),
        jnp.float32,
        "accumulate_second",
    )
    near2, far2, deep2 = together(near2, far2, deep2)

    held = 2 * main // 3
    deep3_main, line = collect(
        (far2, deep2),
        (
            ((1, 0, wide),),
            ((1, wide, wide + 4 * narrow), (0, 2 * wide - cut - main, 2 * wide - cut - main + held)),
        ),
        "collect_fourth",
    )
    near3, far3, deep3 = slot((flip_near, deep3_main), (flip_far, deep3_main), (next_plane, line))
    acc = accumulate(
        rows,
        (shard, near, far, far1, deep1, near2, far2, deep2),
        [runs(i, 0, main) for i in (5, 6, 7)]
        + list(split_runs((5, wide), (6, wide), main))
        + [runs(i, wide, edge) for i in (0, 1, 2)]
        + [runs(3, wide + wide - cut, edge)]
        + [runs(4, wide + k * narrow, edge) for k in range(3)]
        + [runs(7, wide + k * narrow, edge) for k in range(4)],
        tuple(acc),
        jnp.float32,
        "accumulate_third",
    )
    near3, far3, deep3, *acc = together(near3, far3, deep3, *acc)

    two = 2 * main
    sends = collect(
        (near2, far2, near3, far3, deep3),
        (
            ((1, 0, main), (1, two + held, wide), (3, 0, main)),
            ((0, main, two), (2, main, two), (2, two + held, wide)),
            ((4, 3 * narrow, 4 * narrow + held),),
        ),
        "collect_fifth",
    )
    near4, far4, deep4 = slot(*zip((flip_near, flip_far, next_plane), sends))
    acc = accumulate(
        rows,
        (near3, far3, deep3),
        [runs(0, 0, main), runs(1, 0, main)] + [runs(2, k * narrow, edge) for k in range(4)],
        tuple(acc),
        jnp.float32,
        "accumulate_fourth",
    )
    weights = (near4, far4, deep3, deep4)
    line, then = 4 * narrow, two - held
    last = [
        ((0, 0, held), (1, 0, held), (2, line, line + held)),
        ((0, held, main), (1, held, main), (0, main, then)),
        ((0, then, then + held), (1, main, main + held), (3, narrow, narrow + held)),
        ((0, then + held, then + main), (1, main + held, two), (1, two, two + main - held)),
        runs(3, 0, edge),
    ]
    (given,) = accumulate(rows[1:], weights, last, acc[1:], jnp.bfloat16, "finish_other")
    (kept,) = accumulate(
        rows[:1], weights, last, acc[:1], jnp.float32, "finish_own", residual=mixed_rows
    )
    result = kernel_call(
        functools.partial(final_body, 64),
        "final",
        like(local_len, model, jnp.bfloat16),
        valid_count,
        kept,
        flip_core(given),
        specs=[pl.BlockSpec(memory_space=pltpu.SMEM)] + vmem(2),
    )
    return (
        result[None],
        end_state.reshape((1, 1) + end_state.shape[:1] + end_state.shape[-1:]),
        end_norm[None, None],
    )


def solution(mesh):
    return jax.shard_map(
        local,
        mesh=mesh,
        in_specs=(
            P("req", "seq", None),
            P("req"),
            P("req", "seq", None),
            P(),
            P(),
            P(),
            P(),
            P(),
            P(),
            P(),
            P(None, "req"),
            P(None, "req"),
            P(None, "req"),
        ),
        out_specs=(P("req", "seq", None), P("req", "seq", None, None), P("req", "seq", None, None)),
        check_vma=False,
    )
```

```python
import functools

import jax
import jax.numpy as jnp
from jax import lax
from jax.experimental import pallas as pl
from jax.experimental.pallas import tpu as pltpu
from jax.sharding import PartitionSpec as P


def from_behind(array, axis, by):
    count = lax.axis_size(axis)
    pairs = [(i, i + by) for i in range(count) if 0 <= i + by < count]
    return lax.ppermute(array, axis, pairs)


def entering(array, axis, combine, identity):
    count, here = (lax.axis_size(axis), lax.axis_index(axis))
    everything = jax.tree.map(
        lambda part, kind: lax.all_gather(part.astype(kind), axis),
        array,
        (jnp.bfloat16, jnp.bfloat16, jnp.bfloat16),
    )
    start = jax.tree.map(
        lambda part, zero: jnp.broadcast_to(jnp.asarray(zero, part.dtype), part.shape),
        array,
        identity,
    )

    def hop(k, before):
        reached = k < here
        new = combine(
            before, jax.tree.map(lambda part, own: part[k].astype(own.dtype), everything, array)
        )
        return jax.tree.map(lambda a, b: jnp.where(reached, a, b), new, before)

    return lax.fori_loop(0, count, hop, start)


def features(vectors):
    constant = jnp.ones(vectors.shape[:-1] + (1,), jnp.float32)
    width = vectors.shape[-1]
    squares = (vectors[..., :, None] * vectors[..., None, :]).reshape(
        vectors.shape[:-1] + (width * width,)
    )
    return jnp.concatenate([constant, vectors, squares * 0.5**0.5], axis=-1)


def carry_in(valid_mask, decays, queries, numerator, denominator, flat_memory, key_sum):
    local_len = numerator.shape[0]
    feat_len, head_count = key_sum.shape
    value_len = flat_memory.shape[1] // head_count
    feat_in = queries.shape[1] // head_count
    decay_rate = jnp.where(valid_mask[:, None] > 0, decays, 0.0)
    span_decay = jnp.sum(decay_rate, axis=0)

    def merge_states(earlier, later):
        factor = jnp.exp(later[0])
        return (
            earlier[0] + later[0],
            earlier[1] * jnp.repeat(factor, value_len)[None, :] + later[1],
            earlier[2] * factor[None, :] + later[2],
        )

    neutral = (jnp.zeros_like(span_decay), jnp.zeros_like(flat_memory), jnp.zeros_like(key_sum))
    carried = entering((span_decay, flat_memory, key_sum), "seq", merge_states, neutral)
    prior_memory = carried[1]
    prior_keys = carried[2]
    highest = lax.Precision.HIGHEST
    growth = jnp.exp(jnp.cumsum(decay_rate, axis=0))
    query_feat = features(queries.astype(jnp.float32).reshape(local_len, head_count, feat_in))
    added = jnp.einsum(
        "thf,fhv->thv",
        query_feat,
        prior_memory.reshape(feat_len, head_count, value_len),
        precision=highest,
    )
    numerator = numerator + (added * growth[:, :, None]).reshape(local_len, -1)
    denominator = (
        denominator + jnp.einsum("thf,fh->th", query_feat, prior_keys, precision=highest) * growth
    )
    span_factor = jnp.exp(span_decay)
    end_state = prior_memory * jnp.repeat(span_factor, value_len)[None, :] + flat_memory
    end_norm = prior_keys * span_factor[None, :] + key_sum
    return numerator, denominator, end_state, end_norm


def permute(array, target):
    count = lax.axis_size("req")
    return lax.ppermute(array, "req", [(i, target(i)) for i in range(count)])


def flip_core(array):
    return permute(array, lambda i: i ^ 1)


def flip_near(array):
    return permute(array, lambda i: i ^ 2)


def flip_far(array):
    return permute(array, lambda i: i ^ 4)


def next_plane(array):
    return permute(array, lambda i: i ^ (16 if i // 8 in (1, 2) else 8))


def together(*arrays):
    return lax.optimization_barrier(arrays)


def slot(*sends):
    operands = together(*[array for _, array in sends])
    return together(*[send(array) for (send, _), array in zip(sends, operands)])


def vmem(count):
    return [pl.BlockSpec(memory_space=pltpu.VMEM)] * count


def kernel_call(body, name, out_shape, *operands, scratch=(), aliases=None, specs=None, mib=24):
    many = isinstance(out_shape, tuple)
    return pl.pallas_call(
        body,
        out_shape=out_shape,
        in_specs=specs or vmem(len(operands)),
        out_specs=tuple(vmem(len(out_shape))) if many else vmem(1)[0],
        scratch_shapes=list(scratch),
        input_output_aliases=aliases or {},
        compiler_params=pltpu.CompilerParams(vmem_limit_bytes=mib * 1024 * 1024),
        cost_estimate=pl.CostEstimate(flops=1000, bytes_accessed=1000, transcendentals=0),
        name=name,
    )(*operands)


def like(rows, columns, dtype):
    return jax.ShapeDtypeStruct((rows, columns), dtype)


NT = (((1,), (1,)), ((), ()))


def unit_rows(rows, gain):
    factor = lax.rsqrt(jnp.mean(rows * rows, axis=-1, keepdims=True) + 1e-05)
    return (rows * factor * gain).astype(jnp.bfloat16).astype(jnp.float32)


def project_body(
    step,
    scale,
    rows_ref,
    edge_ref,
    gain_ref,
    conv_ref,
    query_ref,
    key_ref,
    value_ref,
    queries_ref,
    keys_ref,
    values_ref,
    normed,
    gated,
):
    gain = gain_ref[...]
    count = rows_ref.shape[0]
    lead = edge_ref.shape[0]
    taps = conv_ref.shape[0]
    normed[:lead] = unit_rows(edge_ref[...].astype(jnp.float32), gain)

    @pl.loop(0, count // step)
    def _(block):
        at = pl.multiple_of(block * step, step)
        rows = rows_ref[pl.ds(at, step), :].astype(jnp.float32)
        normed[pl.ds(lead + at, step), :] = unit_rows(rows, gain)

    @pl.loop(0, count // step)
    def _(block):
        at = pl.multiple_of(block * step, step)
        window = normed[pl.ds(at, step + lead), :]
        here = window[lead:]
        total = conv_ref[0:1] * here
        for tap in range(1, taps):
            total = total + conv_ref[tap : tap + 1] * window[lead - tap : lead - tap + step]
        gated[pl.ds(at, step), :] = (total * jax.nn.sigmoid(here)).astype(jnp.bfloat16)

    rows = gated[...]
    for weight_ref, out_ref, factor in (
        (query_ref, queries_ref, scale),
        (key_ref, keys_ref, scale),
        (value_ref, values_ref, None),
    ):
        product = jnp.dot(rows, weight_ref[...], preferred_element_type=jnp.float32)
        if factor is not None:
            product = product * factor
        out_ref[...] = product.astype(jnp.bfloat16)


def project(rows, edge, mix_gain, conv_weight, query_weight, key_weight, value_weight, scale):
    count, width = rows.shape
    step = 32
    return kernel_call(
        functools.partial(project_body, step, scale),
        "project",
        tuple(like(count, w.shape[1], jnp.bfloat16) for w in (query_weight, key_weight, value_weight)),
        rows,
        edge,
        mix_gain[None],
        conv_weight,
        query_weight,
        key_weight,
        value_weight,
        scratch=(
            pltpu.VMEM((count + edge.shape[0], width), jnp.float32),
            pltpu.VMEM((count, width), jnp.bfloat16),
        ),
    )


def attend_body(
    feat_in,
    value_len,
    count_ref,
    rate_ref,
    queries_ref,
    keys_ref,
    values_ref,
    numer_ref,
    denom_ref,
    state_ref,
    norm_ref,
    turned,
    total,
    norms,
):
    heads, count = rate_ref.shape
    columns = values_ref.shape[1]
    lane = lax.broadcasted_iota(jnp.int32, (count, count), 1)
    row = lax.broadcasted_iota(jnp.int32, (count, count), 0)
    valid = (lane[:1] < count_ref[0]).astype(jnp.float32)
    rate = jnp.where(valid > 0, rate_ref[...], 0.0)
    upto = (row <= lane).astype(jnp.float32)
    across = jnp.dot(
        rate, upto, precision=lax.Precision.HIGHEST, preferred_element_type=jnp.float32
    )
    down = across.T
    closing = across[:, count - 1 : count]
    fading = jnp.exp(closing - across) * valid
    causal = row >= lane
    keys = keys_ref[...]
    turned[...] = keys.astype(jnp.float32).T
    owner = lax.broadcasted_iota(jnp.int32, queries_ref.shape, 1)
    spare = lax.broadcasted_iota(jnp.int32, (8, count), 0) == 0
    head_lane = lax.broadcasted_iota(jnp.int32, (count, 128), 1)
    numer_ref[...] = jnp.zeros(numer_ref.shape, jnp.float32)
    total[...] = jnp.zeros(total.shape, jnp.float32)
    norms[...] = jnp.zeros(norms.shape, jnp.float32)
    norm_total = jnp.zeros((total.shape[0], 128), jnp.float32)
    denominators = jnp.zeros((count, 128), jnp.float32)
    for h in range(heads):
        low = min(h * value_len // 128 * 128, max(columns - 256, 0))
        high = min(low + 256, columns)
        mine = lax.broadcasted_iota(jnp.int32, (count, high - low), 1) + low
        mine = (mine >= h * value_len) & (mine < (h + 1) * value_len)
        values = jnp.where(mine, values_ref[:, low:high].astype(jnp.float32), 0.0)
        values = values.astype(jnp.bfloat16)
        asks = (owner >= h * feat_in) & (owner < (h + 1) * feat_in)
        queries = jnp.where(asks, queries_ref[...].astype(jnp.float32), 0.0)
        scores = lax.dot_general(
            queries.astype(jnp.bfloat16), keys, NT, preferred_element_type=jnp.float32
        )
        gap = down[:, h : h + 1] - across[h : h + 1]
        weights = jnp.where(causal, jnp.exp(jnp.minimum(gap, 0.0)) * valid, 0.0)
        weights = weights * (1.0 + scores + 0.5 * scores * scores)
        numer_ref[:, low:high] += jnp.dot(
            weights.astype(jnp.bfloat16), values, preferred_element_type=jnp.float32
        )
        sums = jnp.sum(weights, axis=1, keepdims=True)
        denominators = jnp.where(head_lane == h, sums, denominators)
        own = turned[h * feat_in : (h + 1) * feat_in]
        fade = fading[h : h + 1]
        faded = own * fade
        scaled = faded * 0.5**0.5
        parts = [own[i : i + 1] * scaled for i in range(feat_in)]
        parts += [faded, jnp.where(spare, fade, 0.0)]
        feats = jnp.concatenate(parts, axis=0).astype(jnp.bfloat16)
        total[:, low:high] += jnp.dot(feats, values, preferred_element_type=jnp.float32)
        mark = (head_lane == h).astype(jnp.bfloat16)
        norm_total = norm_total + jnp.dot(feats, mark, preferred_element_type=jnp.float32)
    denom_ref[...] = denominators[:, :heads]
    pairs = feat_in * feat_in
    state_ref[0] = total[pairs + feat_in : pairs + feat_in + 1, :]
    for f in range(feat_in):
        state_ref[1 + f] = total[pairs + f : pairs + f + 1, :]

    @pl.loop(0, pairs // 8)
    def _(block):
        for k in range(8):
            f = block * 8 + k
            state_ref[1 + feat_in + f] = total[pl.ds(f, 1), :]

    norms[0:1, :] = norm_total[pairs + feat_in : pairs + feat_in + 1]
    norms[1 : 1 + feat_in, :] = norm_total[pairs : pairs + feat_in]
    norms[1 + feat_in : 1 + feat_in + pairs, :] = norm_total[:pairs]
    norm_ref[...] = norms[...].T[:heads, : 1 + feat_in + pairs]


def attend(valid_count, rate, queries, keys, values, feat_in, value_len):
    heads, count = rate.shape
    columns = values.shape[1]
    feat_len = 1 + feat_in + feat_in * feat_in
    padded = feat_in * feat_in + feat_in + 8
    return kernel_call(
        functools.partial(attend_body, feat_in, value_len),
        "attend",
        (
            like(count, columns, jnp.float32),
            like(count, heads, jnp.float32),
            jax.ShapeDtypeStruct((feat_len, 1, columns), jnp.float32),
            like(heads, feat_len, jnp.float32),
        ),
        valid_count,
        rate,
        queries,
        keys,
        values,
        specs=[pl.BlockSpec(memory_space=pltpu.SMEM)] + vmem(4),
        scratch=(
            pltpu.VMEM((queries.shape[1], count), jnp.float32),
            pltpu.VMEM((padded, columns), jnp.float32),
            pltpu.VMEM(((feat_len + 127) // 128 * 128, 128), jnp.float32),
        ),
    )


def mix_body(
    value_len, step, numer_ref, denom_ref, rows_ref, out_ref, gain_ref, mixed_ref, mlp_ref, sums
):
    count, columns = numer_ref.shape
    heads = denom_ref.shape[1]
    column = lax.broadcasted_iota(jnp.int32, (1, columns), 1)
    inverse = 1.0 / denom_ref[...]
    spread = jnp.zeros((count, columns), jnp.float32)
    for h in range(heads):
        here = (column >= h * value_len) & (column < (h + 1) * value_len)
        spread = jnp.where(here, inverse[:, h : h + 1], spread)
    attended = (numer_ref[...] * spread).astype(jnp.bfloat16)
    sums[...] = jnp.dot(attended, out_ref[...], preferred_element_type=jnp.float32)
    gain = gain_ref[...]

    @pl.loop(0, count // step)
    def _(block):
        at = pl.ds(pl.multiple_of(block * step, step), step)
        mixed = (rows_ref[at, :].astype(jnp.float32) + sums[at, :]).astype(jnp.bfloat16)
        mixed_ref[at, :] = mixed
        mlp_ref[at, :] = unit_rows(mixed.astype(jnp.float32), gain).astype(jnp.bfloat16)


def mix(numer, denom, rows, out_weight, mlp_gain, value_len):
    count, width = rows.shape
    shape = like(count, width, jnp.bfloat16)
    return kernel_call(
        functools.partial(mix_body, value_len, 32),
        "mix",
        (shape, shape),
        numer,
        denom,
        rows,
        out_weight,
        mlp_gain[None],
        scratch=(pltpu.VMEM((count, width), jnp.float32),),
    )


def swiglu_terms(rows, gate_rows, up_rows, down_rows):
    gate_act = lax.dot_general(rows, gate_rows, NT, preferred_element_type=jnp.float32)
    up_act = lax.dot_general(rows, up_rows, NT, preferred_element_type=jnp.float32)
    hidden_units = (gate_act * jax.nn.sigmoid(gate_act) * up_act).astype(jnp.bfloat16)
    return jnp.dot(hidden_units, down_rows, preferred_element_type=jnp.float32)


def on_grid(run):
    return all(low % 16 == 0 and high % 16 == 0 for _, low, high in run)


def read_units(refs, units):
    parts = []
    for k in range(3):
        rows = [refs[run[k][0]][run[k][1] : run[k][2]] for run in units if on_grid(run)]
        rest = [
            refs[run[k][0]][...].astype(jnp.float32)[run[k][1] : run[k][2]]
            for run in units
            if not on_grid(run)
        ]
        if rest:
            rows.append(jnp.concatenate(rest, axis=0).astype(jnp.bfloat16))
        parts.append(jnp.concatenate(rows, axis=0))
    return parts


def accumulate_body(units, n_weights, n_rows, n_acc, residual, *refs):
    weights = refs[:n_weights]
    rows = refs[n_weights : n_weights + n_rows]
    acc = refs[n_weights + n_rows : n_weights + n_rows + n_acc]
    parts = read_units(weights, units)
    for k, rows_ref in enumerate(rows):
        out_ref = refs[len(refs) - n_rows + k]
        terms = swiglu_terms(rows_ref[...], *parts)
        if n_acc:
            terms = terms + acc[k][...]
        if residual:
            terms = terms + refs[n_weights + n_rows + n_acc][...].astype(jnp.float32)
        out_ref[...] = terms.astype(out_ref.dtype)


def accumulate(rows, weights, units, acc, dtype, name, residual=None):
    shapes = tuple(like(*array.shape, dtype) for array in rows)
    start = len(weights) + len(rows)
    aliases = {start + k: k for k in range(len(acc))} if dtype == jnp.float32 else {}
    extra = () if residual is None else (residual,)
    body = functools.partial(
        accumulate_body, tuple(units), len(weights), len(rows), len(acc), bool(extra)
    )
    return kernel_call(body, name, shapes, *weights, *rows, *acc, *extra, aliases=aliases)


def runs(which, low, size):
    return tuple((which, low + k * size, low + (k + 1) * size) for k in range(3))


def split_runs(first, second, main):
    (i, at), (j, then) = first, second
    held = 2 * main // 3
    rest = main - held
    return (
        ((i, at, at + held), (i, at + main, at + main + held), (j, then + rest, then + main)),
        ((i, at + held, at + main), (j, then, then + rest), (j, then + main, then + rest + main)),
    )


def collect_body(plans, *refs):
    outs = refs[len(refs) - len(plans) :]
    for out_ref, plan in zip(outs, plans):
        rows = [refs[i][...].astype(jnp.float32)[low:high] for i, low, high in plan]
        out_ref[...] = jnp.concatenate(rows, axis=0).astype(jnp.bfloat16)


def collect(arrays, plans, name):
    columns = arrays[0].shape[1]
    shapes = tuple(like(sum(h - l for _, l, h in plan), columns, jnp.bfloat16) for plan in plans)
    return kernel_call(functools.partial(collect_body, plans), name, shapes, *arrays)


def shard_body(main, gate_ref, up_ref, down_ref, shard_ref, main_ref, *rest):
    buffers, sems = rest[:3], rest[3]
    copies = [
        pltpu.make_async_copy(source, buffer, sems.at[k])
        for k, (source, buffer) in enumerate(zip((gate_ref, up_ref, down_ref), buffers))
    ]
    for copy in copies:
        copy.start()
    for copy in copies:
        copy.wait()
    arrays = [buffer[...].astype(jnp.float32) for buffer in buffers]
    tops = [array[:main] for array in arrays]
    ends = [array[main:] for array in arrays]
    shard_ref[...] = jnp.concatenate(tops + ends, axis=0).astype(jnp.bfloat16)
    main_ref[...] = jnp.concatenate(tops, axis=0).astype(jnp.bfloat16)


def final_body(step, count_ref, kept_ref, given_ref, out_ref):
    count = kept_ref.shape[0]

    @pl.loop(0, count // step)
    def _(block):
        first = pl.multiple_of(block * step, step)
        at = pl.ds(first, step)
        total = kept_ref[at, :] + given_ref[at, :].astype(jnp.float32)
        row = lax.broadcasted_iota(jnp.int32, total.shape, 0) + first
        out_ref[at, :] = jnp.where(row < count_ref[0], total, 0.0).astype(out_ref.dtype)


def local(
    hidden_in,
    lengths,
    log_decay,
    mix_gain,
    conv_weight,
    query_weight,
    key_weight,
    value_weight,
    out_weight,
    mlp_gain,
    gate_weight,
    up_weight,
    down_weight,
):
    local_len = hidden_in.shape[1]
    rows_in = hidden_in[0]
    decays = log_decay[0]
    head_count = log_decay.shape[2]
    value_len = value_weight.shape[1] // head_count
    feat_in = query_weight.shape[1] // head_count
    feature_scale = feat_in ** (-0.25)
    valid_count = lengths - lax.axis_index("seq") * local_len
    spans = lax.axis_size("seq")
    units, model = gate_weight.shape[1], gate_weight.shape[0]
    edge = units // 7
    main = units - edge
    wide = 3 * main
    full = 3 * units
    narrow = full - wide
    cut = main + 2 * main // 3

    shard, shard_main = kernel_call(
        functools.partial(shard_body, main),
        "shard",
        (like(full, model, jnp.bfloat16), like(wide, model, jnp.bfloat16)),
        gate_weight.T,
        up_weight.T,
        down_weight.T,
        specs=[pl.BlockSpec(memory_space=pl.ANY)] * 3,
        scratch=[pltpu.VMEM((units, model), jnp.bfloat16)] * 3 + [pltpu.SemaphoreType.DMA((3,))],
        mib=56,
    )
    near, far, deep = slot((flip_near, shard), (flip_far, shard), (next_plane, shard_main))

    lead = 16
    if spans > 1:
        edge_in = from_behind(rows_in[local_len - lead :], "seq", 1)
    else:
        edge_in = jnp.zeros((lead, model), jnp.bfloat16)
    queries, key_rows, values = project(
        rows_in, edge_in, mix_gain, conv_weight, query_weight, key_weight, value_weight, feature_scale
    )
    near, far, deep, queries, key_rows, values = together(
        near, far, deep, queries, key_rows, values
    )

    sends = collect(
        (shard, near, far, deep),
        (
            ((3, 0, wide), (2, 0, cut)),
            ((3, 0, wide), (1, cut, full)),
            ((3, 0, wide), (0, wide, full), (1, wide, full), (2, wide, full)),
        ),
        "collect_second",
    )
    near1, far1, deep1 = slot(*zip((flip_near, flip_far, next_plane), sends))

    numerator, denominator, end_state, end_norm = attend(
        valid_count, log_decay[0].T, queries, key_rows, values, feat_in, value_len
    )
    if spans > 1:
        positions = jnp.arange(local_len, dtype=jnp.int32)
        numerator, denominator, end_state, end_norm = carry_in(
            (positions < valid_count).astype(jnp.float32),
            decays,
            queries,
            numerator,
            denominator,
            end_state[:, 0],
            end_norm.T,
        )
    else:
        end_norm = end_norm.T
    mixed_rows, mlp_in = mix(numerator, denominator, rows_in, out_weight, mlp_gain, value_len)
    near1, far1, deep1, mixed_rows, mlp_in, end_state, end_norm = together(
        near1, far1, deep1, mixed_rows, mlp_in, end_state, end_norm
    )

    sends = collect(
        (near1, far1, deep1),
        (
            ((2, 0, wide), (1, 0, cut)),
            ((2, 0, wide), (0, cut, wide)),
            ((2, 0, wide + 3 * narrow), (1, wide + wide - cut, wide + full - cut)),
        ),
        "collect_third",
    )
    near2, far2, deep2 = slot(*zip((flip_near, flip_far, next_plane), sends))
    rows = (mlp_in, flip_core(mlp_in))
    acc = accumulate(
        rows,
        (shard, near, far, deep, near1, far1, deep1),
        [runs(i, 0, main) for i in range(7)] + list(split_runs((4, wide), (5, wide), main)),
        (),
        jnp.float32,
        "accumulate_second",
    )
    near2, far2, deep2 = together(near2, far2, deep2)

    held = 2 * main // 3
    two = 2 * main
    sends = collect(
        (near2, far2, deep2),
        (
            ((2, main, wide),),
            ((2, 0, main), (2, two, wide)),
            ((2, wide, wide + 4 * narrow), (1, 2 * wide - cut - main, 2 * wide - cut - main + held)),
            ((2, 0, main), (1, 0, main), (1, two + held, wide)),
            ((2, main, two), (0, main, two)),
        ),
        "collect_fourth",
    )
    sends = together(*sends)
    near3, far3, deep3 = flip_near(sends[0]), flip_far(sends[1]), next_plane(sends[2])
    near3_more, far3_more = flip_near(sends[3]), flip_far(sends[4])
    acc = accumulate(
        rows,
        (shard, near, far, far1, deep1, near2, far2, deep2),
        [runs(i, 0, main) for i in (5, 6, 7)]
        + list(split_runs((5, wide), (6, wide), main))
        + [runs(i, wide, edge) for i in (0, 1, 2)]
        + [runs(3, wide + wide - cut, edge)]
        + [runs(4, wide + k * narrow, edge) for k in range(3)]
        + [runs(7, wide + k * narrow, edge) for k in range(4)],
        tuple(acc),
        jnp.float32,
        "accumulate_third",
    )
    near3, far3, deep3, *acc = together(near3, far3, deep3, *acc)

    sends = collect(
        (near3, far3, deep3),
        (
            ((1, 0, main),),
            ((0, 0, main), (0, main + held, two)),
            ((2, 3 * narrow, 4 * narrow + held),),
        ),
        "collect_fifth",
    )
    near4, far4, deep4 = slot(*zip((flip_near, flip_far, next_plane), sends))
    line = 4 * narrow
    acc = accumulate(
        rows,
        (near3, near3_more, far3, far3_more, deep3),
        [((1, 0, main), (0, 0, main), (0, main, two)), ((2, 0, main), (3, 0, main), (2, main, two))]
        + [((1, main, main + held), (3, main, main + held), (4, line, line + held))]
        + [((1, main + held, two), (3, main + held, two), (1, two, two + main - held))]
        + [runs(4, k * narrow, edge) for k in range(4)],
        tuple(acc),
        jnp.float32,
        "accumulate_fourth",
    )
    weights = (near4, far4, deep4)
    last = [
        ((0, 0, held), (1, 0, held), (2, narrow, narrow + held)),
        ((0, held, main), (1, held, main), (1, main, two - held)),
        runs(2, 0, edge),
    ]
    (given,) = accumulate(rows[1:], weights, last, acc[1:], jnp.bfloat16, "finish_other")
    (kept,) = accumulate(
        rows[:1], weights, last, acc[:1], jnp.float32, "finish_own", residual=mixed_rows
    )
    result = kernel_call(
        functools.partial(final_body, 64),
        "final",
        like(local_len, model, jnp.bfloat16),
        valid_count,
        kept,
        flip_core(given),
        specs=[pl.BlockSpec(memory_space=pltpu.SMEM)] + vmem(2),
    )
    return (
        result[None],
        end_state.reshape((1, 1) + end_state.shape[:1] + end_state.shape[-1:]),
        end_norm[None, None],
    )


def solution(mesh):
    return jax.shard_map(
        local,
        mesh=mesh,
        in_specs=(
            P("req", "seq", None),
            P("req"),
            P("req", "seq", None),
            P(),
            P(),
            P(),
            P(),
            P(),
            P(),
            P(),
            P(None, "req"),
            P(None, "req"),
            P(None, "req"),
        ),
        out_specs=(P("req", "seq", None), P("req", "seq", None, None), P("req", "seq", None, None)),
        check_vma=False,
    )
```

```python
import functools

import jax
import jax.numpy as jnp
from jax import lax
from jax.experimental import pallas as pl
from jax.experimental.pallas import tpu as pltpu
from jax.sharding import PartitionSpec as P


def from_behind(array, axis, by):
    count = lax.axis_size(axis)
    pairs = [(i, i + by) for i in range(count) if 0 <= i + by < count]
    return lax.ppermute(array, axis, pairs)


def entering(array, axis, combine, identity):
    count, here = (lax.axis_size(axis), lax.axis_index(axis))
    everything = jax.tree.map(
        lambda part, kind: lax.all_gather(part.astype(kind), axis),
        array,
        (jnp.bfloat16, jnp.bfloat16, jnp.bfloat16),
    )
    start = jax.tree.map(
        lambda part, zero: jnp.broadcast_to(jnp.asarray(zero, part.dtype), part.shape),
        array,
        identity,
    )

    def hop(k, before):
        reached = k < here
        new = combine(
            before, jax.tree.map(lambda part, own: part[k].astype(own.dtype), everything, array)
        )
        return jax.tree.map(lambda a, b: jnp.where(reached, a, b), new, before)

    return lax.fori_loop(0, count, hop, start)


def features(vectors):
    constant = jnp.ones(vectors.shape[:-1] + (1,), jnp.float32)
    width = vectors.shape[-1]
    squares = (vectors[..., :, None] * vectors[..., None, :]).reshape(
        vectors.shape[:-1] + (width * width,)
    )
    return jnp.concatenate([constant, vectors, squares * 0.5**0.5], axis=-1)


def carry_in(valid_mask, decays, queries, numerator, denominator, flat_memory, key_sum):
    local_len = numerator.shape[0]
    feat_len, head_count = key_sum.shape
    value_len = flat_memory.shape[1] // head_count
    feat_in = queries.shape[1] // head_count
    decay_rate = jnp.where(valid_mask[:, None] > 0, decays, 0.0)
    span_decay = jnp.sum(decay_rate, axis=0)

    def merge_states(earlier, later):
        factor = jnp.exp(later[0])
        return (
            earlier[0] + later[0],
            earlier[1] * jnp.repeat(factor, value_len)[None, :] + later[1],
            earlier[2] * factor[None, :] + later[2],
        )

    neutral = (jnp.zeros_like(span_decay), jnp.zeros_like(flat_memory), jnp.zeros_like(key_sum))
    carried = entering((span_decay, flat_memory, key_sum), "seq", merge_states, neutral)
    prior_memory = carried[1]
    prior_keys = carried[2]
    highest = lax.Precision.HIGHEST
    growth = jnp.exp(jnp.cumsum(decay_rate, axis=0))
    query_feat = features(queries.astype(jnp.float32).reshape(local_len, head_count, feat_in))
    added = jnp.einsum(
        "thf,fhv->thv",
        query_feat,
        prior_memory.reshape(feat_len, head_count, value_len),
        precision=highest,
    )
    numerator = numerator + (added * growth[:, :, None]).reshape(local_len, -1)
    denominator = (
        denominator + jnp.einsum("thf,fh->th", query_feat, prior_keys, precision=highest) * growth
    )
    span_factor = jnp.exp(span_decay)
    end_state = prior_memory * jnp.repeat(span_factor, value_len)[None, :] + flat_memory
    end_norm = prior_keys * span_factor[None, :] + key_sum
    return numerator, denominator, end_state, end_norm


def permute(array, target):
    count = lax.axis_size("req")
    return lax.ppermute(array, "req", [(i, target(i)) for i in range(count)])


def flip_core(array):
    return permute(array, lambda i: i ^ 1)


def flip_near(array):
    return permute(array, lambda i: i ^ 2)


def flip_far(array):
    return permute(array, lambda i: i ^ 4)


def next_plane(array):
    return permute(array, lambda i: i ^ (16 if i // 8 in (1, 2) else 8))


def together(*arrays):
    return lax.optimization_barrier(arrays)


def slot(*sends):
    operands = together(*[array for _, array in sends])
    return together(*[send(array) for (send, _), array in zip(sends, operands)])


def vmem(count):
    return [pl.BlockSpec(memory_space=pltpu.VMEM)] * count


def kernel_call(body, name, out_shape, *operands, scratch=(), aliases=None, specs=None, mib=24):
    many = isinstance(out_shape, tuple)
    return pl.pallas_call(
        body,
        out_shape=out_shape,
        in_specs=specs or vmem(len(operands)),
        out_specs=tuple(vmem(len(out_shape))) if many else vmem(1)[0],
        scratch_shapes=list(scratch),
        input_output_aliases=aliases or {},
        compiler_params=pltpu.CompilerParams(vmem_limit_bytes=mib * 1024 * 1024),
        cost_estimate=pl.CostEstimate(flops=1000, bytes_accessed=1000, transcendentals=0),
        name=name,
    )(*operands)


def like(rows, columns, dtype):
    return jax.ShapeDtypeStruct((rows, columns), dtype)


NT = (((1,), (1,)), ((), ()))


def unit_rows(rows, gain):
    factor = lax.rsqrt(jnp.mean(rows * rows, axis=-1, keepdims=True) + 1e-05)
    return (rows * factor * gain).astype(jnp.bfloat16).astype(jnp.float32)


def project_body(
    step,
    scale,
    rows_ref,
    edge_ref,
    gain_ref,
    conv_ref,
    query_ref,
    key_ref,
    value_ref,
    queries_ref,
    keys_ref,
    values_ref,
    normed,
    gated,
):
    gain = gain_ref[...]
    count = rows_ref.shape[0]
    lead = edge_ref.shape[0]
    taps = conv_ref.shape[0]
    normed[:lead] = unit_rows(edge_ref[...].astype(jnp.float32), gain)

    @pl.loop(0, count // step)
    def _(block):
        at = pl.multiple_of(block * step, step)
        rows = rows_ref[pl.ds(at, step), :].astype(jnp.float32)
        normed[pl.ds(lead + at, step), :] = unit_rows(rows, gain)

    @pl.loop(0, count // step)
    def _(block):
        at = pl.multiple_of(block * step, step)
        window = normed[pl.ds(at, step + lead), :]
        here = window[lead:]
        total = conv_ref[0:1] * here
        for tap in range(1, taps):
            total = total + conv_ref[tap : tap + 1] * window[lead - tap : lead - tap + step]
        gated[pl.ds(at, step), :] = (total * jax.nn.sigmoid(here)).astype(jnp.bfloat16)

    rows = gated[...]
    for weight_ref, out_ref, factor in (
        (query_ref, queries_ref, scale),
        (key_ref, keys_ref, scale),
        (value_ref, values_ref, None),
    ):
        product = jnp.dot(rows, weight_ref[...], preferred_element_type=jnp.float32)
        if factor is not None:
            product = product * factor
        out_ref[...] = product.astype(jnp.bfloat16)


def project(rows, edge, mix_gain, conv_weight, query_weight, key_weight, value_weight, scale):
    count, width = rows.shape
    step = 32
    return kernel_call(
        functools.partial(project_body, step, scale),
        "project",
        tuple(like(count, w.shape[1], jnp.bfloat16) for w in (query_weight, key_weight, value_weight)),
        rows,
        edge,
        mix_gain[None],
        conv_weight,
        query_weight,
        key_weight,
        value_weight,
        scratch=(
            pltpu.VMEM((count + edge.shape[0], width), jnp.float32),
            pltpu.VMEM((count, width), jnp.bfloat16),
        ),
    )


def attend_body(
    feat_in,
    value_len,
    count_ref,
    rate_ref,
    queries_ref,
    keys_ref,
    values_ref,
    numer_ref,
    denom_ref,
    state_ref,
    norm_ref,
    turned,
    total,
    norms,
):
    heads, count = rate_ref.shape
    columns = values_ref.shape[1]
    lane = lax.broadcasted_iota(jnp.int32, (count, count), 1)
    row = lax.broadcasted_iota(jnp.int32, (count, count), 0)
    valid = (lane[:1] < count_ref[0]).astype(jnp.float32)
    rate = jnp.where(valid > 0, rate_ref[...], 0.0)
    upto = (row <= lane).astype(jnp.float32)
    across = jnp.dot(
        rate, upto, precision=lax.Precision.HIGHEST, preferred_element_type=jnp.float32
    )
    down = across.T
    closing = across[:, count - 1 : count]
    fading = jnp.exp(closing - across) * valid
    causal = row >= lane
    keys = keys_ref[...]
    turned[...] = keys.astype(jnp.float32).T
    owner = lax.broadcasted_iota(jnp.int32, queries_ref.shape, 1)
    spare = lax.broadcasted_iota(jnp.int32, (8, count), 0) == 0
    head_lane = lax.broadcasted_iota(jnp.int32, (count, 128), 1)
    numer_ref[...] = jnp.zeros(numer_ref.shape, jnp.float32)
    total[...] = jnp.zeros(total.shape, jnp.float32)
    norms[...] = jnp.zeros(norms.shape, jnp.float32)
    norm_total = jnp.zeros((total.shape[0], 128), jnp.float32)
    denominators = jnp.zeros((count, 128), jnp.float32)
    for h in range(heads):
        low = min(h * value_len // 128 * 128, max(columns - 256, 0))
        high = min(low + 256, columns)
        mine = lax.broadcasted_iota(jnp.int32, (count, high - low), 1) + low
        mine = (mine >= h * value_len) & (mine < (h + 1) * value_len)
        values = jnp.where(mine, values_ref[:, low:high].astype(jnp.float32), 0.0)
        values = values.astype(jnp.bfloat16)
        asks = (owner >= h * feat_in) & (owner < (h + 1) * feat_in)
        queries = jnp.where(asks, queries_ref[...].astype(jnp.float32), 0.0)
        scores = lax.dot_general(
            queries.astype(jnp.bfloat16), keys, NT, preferred_element_type=jnp.float32
        )
        gap = down[:, h : h + 1] - across[h : h + 1]
        weights = jnp.where(causal, jnp.exp(jnp.minimum(gap, 0.0)) * valid, 0.0)
        weights = weights * (1.0 + scores + 0.5 * scores * scores)
        numer_ref[:, low:high] += jnp.dot(
            weights.astype(jnp.bfloat16), values, preferred_element_type=jnp.float32
        )
        sums = jnp.sum(weights, axis=1, keepdims=True)
        denominators = jnp.where(head_lane == h, sums, denominators)
        own = turned[h * feat_in : (h + 1) * feat_in]
        fade = fading[h : h + 1]
        faded = own * fade
        scaled = faded * 0.5**0.5
        parts = [own[i : i + 1] * scaled for i in range(feat_in)]
        parts += [faded, jnp.where(spare, fade, 0.0)]
        feats = jnp.concatenate(parts, axis=0).astype(jnp.bfloat16)
        total[:, low:high] += jnp.dot(feats, values, preferred_element_type=jnp.float32)
        mark = (head_lane == h).astype(jnp.bfloat16)
        norm_total = norm_total + jnp.dot(feats, mark, preferred_element_type=jnp.float32)
    denom_ref[...] = denominators[:, :heads]
    pairs = feat_in * feat_in
    state_ref[0] = total[pairs + feat_in : pairs + feat_in + 1, :]
    for f in range(feat_in):
        state_ref[1 + f] = total[pairs + f : pairs + f + 1, :]

    @pl.loop(0, pairs // 8)
    def _(block):
        for k in range(8):
            f = block * 8 + k
            state_ref[1 + feat_in + f] = total[pl.ds(f, 1), :]

    norms[0:1, :] = norm_total[pairs + feat_in : pairs + feat_in + 1]
    norms[1 : 1 + feat_in, :] = norm_total[pairs : pairs + feat_in]
    norms[1 + feat_in : 1 + feat_in + pairs, :] = norm_total[:pairs]
    norm_ref[...] = norms[...].T[:heads, : 1 + feat_in + pairs]


def attend(valid_count, rate, queries, keys, values, feat_in, value_len):
    heads, count = rate.shape
    columns = values.shape[1]
    feat_len = 1 + feat_in + feat_in * feat_in
    padded = feat_in * feat_in + feat_in + 8
    return kernel_call(
        functools.partial(attend_body, feat_in, value_len),
        "attend",
        (
            like(count, columns, jnp.float32),
            like(count, heads, jnp.float32),
            jax.ShapeDtypeStruct((feat_len, 1, columns), jnp.float32),
            like(heads, feat_len, jnp.float32),
        ),
        valid_count,
        rate,
        queries,
        keys,
        values,
        specs=[pl.BlockSpec(memory_space=pltpu.SMEM)] + vmem(4),
        scratch=(
            pltpu.VMEM((queries.shape[1], count), jnp.float32),
            pltpu.VMEM((padded, columns), jnp.float32),
            pltpu.VMEM(((feat_len + 127) // 128 * 128, 128), jnp.float32),
        ),
    )


def mix_body(
    value_len, step, numer_ref, denom_ref, rows_ref, out_ref, gain_ref, mixed_ref, mlp_ref, sums
):
    count, columns = numer_ref.shape
    heads = denom_ref.shape[1]
    column = lax.broadcasted_iota(jnp.int32, (1, columns), 1)
    inverse = 1.0 / denom_ref[...]
    spread = jnp.zeros((count, columns), jnp.float32)
    for h in range(heads):
        here = (column >= h * value_len) & (column < (h + 1) * value_len)
        spread = jnp.where(here, inverse[:, h : h + 1], spread)
    attended = (numer_ref[...] * spread).astype(jnp.bfloat16)
    sums[...] = jnp.dot(attended, out_ref[...], preferred_element_type=jnp.float32)
    gain = gain_ref[...]

    @pl.loop(0, count // step)
    def _(block):
        at = pl.ds(pl.multiple_of(block * step, step), step)
        mixed = (rows_ref[at, :].astype(jnp.float32) + sums[at, :]).astype(jnp.bfloat16)
        mixed_ref[at, :] = mixed
        mlp_ref[at, :] = unit_rows(mixed.astype(jnp.float32), gain).astype(jnp.bfloat16)


def mix(numer, denom, rows, out_weight, mlp_gain, value_len):
    count, width = rows.shape
    shape = like(count, width, jnp.bfloat16)
    return kernel_call(
        functools.partial(mix_body, value_len, 32),
        "mix",
        (shape, shape),
        numer,
        denom,
        rows,
        out_weight,
        mlp_gain[None],
        scratch=(pltpu.VMEM((count, width), jnp.float32),),
    )


def swiglu_terms(rows, gate_rows, up_rows, down_rows):
    gate_act = lax.dot_general(rows, gate_rows, NT, preferred_element_type=jnp.float32)
    up_act = lax.dot_general(rows, up_rows, NT, preferred_element_type=jnp.float32)
    hidden_units = (gate_act * jax.nn.sigmoid(gate_act) * up_act).astype(jnp.bfloat16)
    return jnp.dot(hidden_units, down_rows, preferred_element_type=jnp.float32)


def on_grid(run):
    return all(low % 16 == 0 and high % 16 == 0 for _, low, high in run)


def read_units(refs, units):
    parts = []
    for k in range(3):
        rows = [refs[run[k][0]][run[k][1] : run[k][2]] for run in units if on_grid(run)]
        rest = [
            refs[run[k][0]][...].astype(jnp.float32)[run[k][1] : run[k][2]]
            for run in units
            if not on_grid(run)
        ]
        if rest:
            rows.append(jnp.concatenate(rest, axis=0).astype(jnp.bfloat16))
        parts.append(jnp.concatenate(rows, axis=0))
    return parts


def accumulate_body(units, n_weights, n_rows, n_acc, residual, *refs):
    weights = refs[:n_weights]
    rows = refs[n_weights : n_weights + n_rows]
    acc = refs[n_weights + n_rows : n_weights + n_rows + n_acc]
    parts = read_units(weights, units)
    for k, rows_ref in enumerate(rows):
        out_ref = refs[len(refs) - n_rows + k]
        terms = swiglu_terms(rows_ref[...], *parts)
        if n_acc:
            terms = terms + acc[k][...]
        if residual:
            terms = terms + refs[n_weights + n_rows + n_acc][...].astype(jnp.float32)
        out_ref[...] = terms.astype(out_ref.dtype)


def accumulate(rows, weights, units, acc, dtype, name, residual=None):
    shapes = tuple(like(*array.shape, dtype) for array in rows)
    start = len(weights) + len(rows)
    aliases = {start + k: k for k in range(len(acc))} if dtype == jnp.float32 else {}
    extra = () if residual is None else (residual,)
    body = functools.partial(
        accumulate_body, tuple(units), len(weights), len(rows), len(acc), bool(extra)
    )
    return kernel_call(body, name, shapes, *weights, *rows, *acc, *extra, aliases=aliases)


def runs(which, low, size):
    return tuple((which, low + k * size, low + (k + 1) * size) for k in range(3))


def split_runs(first, second, main):
    (i, at), (j, then) = first, second
    held = 2 * main // 3
    rest = main - held
    return (
        ((i, at, at + held), (i, at + main, at + main + held), (j, then + rest, then + main)),
        ((i, at + held, at + main), (j, then, then + rest), (j, then + main, then + rest + main)),
    )


def collect_body(plans, *refs):
    outs = refs[len(refs) - len(plans) :]
    for out_ref, plan in zip(outs, plans):
        rows = [refs[i][...].astype(jnp.float32)[low:high] for i, low, high in plan]
        out_ref[...] = jnp.concatenate(rows, axis=0).astype(jnp.bfloat16)


def collect(arrays, plans, name):
    columns = arrays[0].shape[1]
    shapes = tuple(like(sum(h - l for _, l, h in plan), columns, jnp.bfloat16) for plan in plans)
    return kernel_call(functools.partial(collect_body, plans), name, shapes, *arrays)


def shard_body(main, gate_ref, up_ref, down_ref, shard_ref, main_ref, *rest):
    buffers, sems = rest[:3], rest[3]
    copies = [
        pltpu.make_async_copy(source, buffer, sems.at[k])
        for k, (source, buffer) in enumerate(zip((gate_ref, up_ref, down_ref), buffers))
    ]
    for copy in copies:
        copy.start()
    for copy in copies:
        copy.wait()
    arrays = [buffer[...].astype(jnp.float32) for buffer in buffers]
    tops = [array[:main] for array in arrays]
    ends = [array[main:] for array in arrays]
    shard_ref[...] = jnp.concatenate(tops + ends, axis=0).astype(jnp.bfloat16)
    main_ref[...] = jnp.concatenate(tops, axis=0).astype(jnp.bfloat16)


def final_body(step, count_ref, kept_ref, given_ref, out_ref):
    count = kept_ref.shape[0]

    @pl.loop(0, count // step)
    def _(block):
        first = pl.multiple_of(block * step, step)
        at = pl.ds(first, step)
        total = kept_ref[at, :] + given_ref[at, :].astype(jnp.float32)
        row = lax.broadcasted_iota(jnp.int32, total.shape, 0) + first
        out_ref[at, :] = jnp.where(row < count_ref[0], total, 0.0).astype(out_ref.dtype)


def local(
    hidden_in,
    lengths,
    log_decay,
    mix_gain,
    conv_weight,
    query_weight,
    key_weight,
    value_weight,
    out_weight,
    mlp_gain,
    gate_weight,
    up_weight,
    down_weight,
):
    local_len = hidden_in.shape[1]
    rows_in = hidden_in[0]
    decays = log_decay[0]
    head_count = log_decay.shape[2]
    value_len = value_weight.shape[1] // head_count
    feat_in = query_weight.shape[1] // head_count
    feature_scale = feat_in ** (-0.25)
    valid_count = lengths - lax.axis_index("seq") * local_len
    spans = lax.axis_size("seq")
    units, model = gate_weight.shape[1], gate_weight.shape[0]
    edge = units // 7
    main = units - edge
    wide = 3 * main
    full = 3 * units
    narrow = full - wide
    cut = main + 2 * main // 3

    shard, shard_main = kernel_call(
        functools.partial(shard_body, main),
        "shard",
        (like(full, model, jnp.bfloat16), like(wide, model, jnp.bfloat16)),
        gate_weight.T,
        up_weight.T,
        down_weight.T,
        specs=[pl.BlockSpec(memory_space=pl.ANY)] * 3,
        scratch=[pltpu.VMEM((units, model), jnp.bfloat16)] * 3 + [pltpu.SemaphoreType.DMA((3,))],
        mib=56,
    )
    near, far, deep = slot((flip_near, shard), (flip_far, shard), (next_plane, shard_main))

    lead = 16
    if spans > 1:
        edge_in = from_behind(rows_in[local_len - lead :], "seq", 1)
    else:
        edge_in = jnp.zeros((lead, model), jnp.bfloat16)
    queries, key_rows, values = project(
        rows_in, edge_in, mix_gain, conv_weight, query_weight, key_weight, value_weight, feature_scale
    )
    near, far, deep, queries, key_rows, values = together(
        near, far, deep, queries, key_rows, values
    )

    sends = collect(
        (shard, near, far, deep),
        (
            ((3, 0, wide), (2, 0, cut)),
            ((3, 0, wide), (1, cut, full)),
            ((3, 0, wide), (0, wide, full), (1, wide, full), (2, wide, full)),
        ),
        "collect_second",
    )
    near1, far1, deep1 = slot(*zip((flip_near, flip_far, next_plane), sends))

    numerator, denominator, end_state, end_norm = attend(
        valid_count, log_decay[0].T, queries, key_rows, values, feat_in, value_len
    )
    if spans > 1:
        positions = jnp.arange(local_len, dtype=jnp.int32)
        numerator, denominator, end_state, end_norm = carry_in(
            (positions < valid_count).astype(jnp.float32),
            decays,
            queries,
            numerator,
            denominator,
            end_state[:, 0],
            end_norm.T,
        )
    else:
        end_norm = end_norm.T
    mixed_rows, mlp_in = mix(numerator, denominator, rows_in, out_weight, mlp_gain, value_len)
    middle = local_len // 2
    other_top, other_end = flip_core(mlp_in[:middle]), flip_core(mlp_in[middle:])
    near1, far1, deep1, mixed_rows, mlp_in, other_top, other_end, end_state, end_norm = together(
        near1, far1, deep1, mixed_rows, mlp_in, other_top, other_end, end_state, end_norm
    )

    *sends, other_in = collect(
        (near1, far1, deep1, other_top, other_end),
        (
            ((2, 0, wide), (1, 0, cut)),
            ((2, 0, wide), (0, cut, wide)),
            ((2, 0, wide + 3 * narrow), (1, wide + wide - cut, wide + full - cut)),
            ((3, 0, middle), (4, 0, local_len - middle)),
        ),
        "collect_third",
    )
    near2, far2, deep2 = slot(*zip((flip_near, flip_far, next_plane), sends))
    rows = (mlp_in, other_in)
    acc = accumulate(
        rows,
        (shard, near, far, deep, near1, far1, deep1),
        [runs(i, 0, main) for i in range(7)] + list(split_runs((4, wide), (5, wide), main)),
        (),
        jnp.float32,
        "accumulate_second",
    )
    near2, far2, deep2, *acc = together(near2, far2, deep2, *acc)

    held = 2 * main // 3
    two = 2 * main
    sends = collect(
        (near2, far2, deep2),
        (
            ((2, main, wide),),
            ((2, 0, main), (2, two, wide)),
            ((2, wide, wide + 4 * narrow), (1, 2 * wide - cut - main, 2 * wide - cut - main + held)),
            ((2, 0, main), (1, 0, main), (1, two + held, wide)),
            ((2, main, two), (0, main, two)),
        ),
        "collect_fourth",
    )
    sends = together(*sends)
    near3, far3, deep3 = flip_near(sends[0]), flip_far(sends[1]), next_plane(sends[2])
    near3_more, far3_more = flip_near(sends[3]), flip_far(sends[4])
    acc = accumulate(
        rows,
        (shard, near, far, far1, deep1, near2, far2, deep2),
        [runs(i, 0, main) for i in (5, 6, 7)]
        + list(split_runs((5, wide), (6, wide), main))
        + [runs(i, wide, edge) for i in (0, 1, 2)]
        + [runs(3, wide + wide - cut, edge)]
        + [runs(4, wide + k * narrow, edge) for k in range(3)]
        + [runs(7, wide + k * narrow, edge) for k in range(4)],
        tuple(acc),
        jnp.float32,
        "accumulate_third",
    )
    near3, far3, deep3, *acc = together(near3, far3, deep3, *acc)

    sends = collect(
        (near3, far3, deep3),
        (
            ((1, 0, main),),
            ((0, 0, main), (0, main + held, two)),
            ((2, 3 * narrow, 4 * narrow + held),),
        ),
        "collect_fifth",
    )
    near4, far4, deep4 = slot(*zip((flip_near, flip_far, next_plane), sends))
    line = 4 * narrow
    weights = (near3, near3_more, far3, far3_more, deep3, near4, far4, deep4)
    last = [
        ((1, 0, main), (0, 0, main), (0, main, two)),
        ((2, 0, main), (3, 0, main), (2, main, two)),
        ((1, main, main + held), (3, main, main + held), (4, line, line + held)),
        ((1, main + held, two), (3, main + held, two), (1, two, two + main - held)),
        ((5, 0, held), (6, 0, held), (7, narrow, narrow + held)),
        ((5, held, main), (6, held, main), (6, main, two - held)),
    ]
    last += [runs(4, k * narrow, edge) for k in range(4)] + [runs(7, 0, edge)]
    (given,) = accumulate(rows[1:], weights, last, acc[1:], jnp.bfloat16, "finish_other")
    (kept,) = accumulate(
        rows[:1], weights, last, acc[:1], jnp.float32, "finish_own", residual=mixed_rows
    )
    result = kernel_call(
        functools.partial(final_body, 64),
        "final",
        like(local_len, model, jnp.bfloat16),
        valid_count,
        kept,
        flip_core(given),
        specs=[pl.BlockSpec(memory_space=pltpu.SMEM)] + vmem(2),
    )
    return (
        result[None],
        end_state.reshape((1, 1) + end_state.shape[:1] + end_state.shape[-1:]),
        end_norm[None, None],
    )


def solution(mesh):
    return jax.shard_map(
        local,
        mesh=mesh,
        in_specs=(
            P("req", "seq", None),
            P("req"),
            P("req", "seq", None),
            P(),
            P(),
            P(),
            P(),
            P(),
            P(),
            P(),
            P(None, "req"),
            P(None, "req"),
            P(None, "req"),
        ),
        out_specs=(P("req", "seq", None), P("req", "seq", None, None), P("req", "seq", None, None)),
        check_vma=False,
    )
```

```python
import functools

import jax
import jax.numpy as jnp
from jax import lax
from jax.experimental import pallas as pl
from jax.experimental.pallas import tpu as pltpu
from jax.sharding import PartitionSpec as P


def from_behind(array, axis, by):
    count = lax.axis_size(axis)
    pairs = [(i, i + by) for i in range(count) if 0 <= i + by < count]
    return lax.ppermute(array, axis, pairs)


def entering(array, axis, combine, identity):
    count, here = (lax.axis_size(axis), lax.axis_index(axis))
    everything = jax.tree.map(
        lambda part, kind: lax.all_gather(part.astype(kind), axis),
        array,
        (jnp.bfloat16, jnp.bfloat16, jnp.bfloat16),
    )
    start = jax.tree.map(
        lambda part, zero: jnp.broadcast_to(jnp.asarray(zero, part.dtype), part.shape),
        array,
        identity,
    )

    def hop(k, before):
        reached = k < here
        new = combine(
            before, jax.tree.map(lambda part, own: part[k].astype(own.dtype), everything, array)
        )
        return jax.tree.map(lambda a, b: jnp.where(reached, a, b), new, before)

    return lax.fori_loop(0, count, hop, start)


def features(vectors):
    constant = jnp.ones(vectors.shape[:-1] + (1,), jnp.float32)
    width = vectors.shape[-1]
    squares = (vectors[..., :, None] * vectors[..., None, :]).reshape(
        vectors.shape[:-1] + (width * width,)
    )
    return jnp.concatenate([constant, vectors, squares * 0.5**0.5], axis=-1)


def carry_in(valid_mask, decays, queries, numerator, denominator, flat_memory, key_sum):
    local_len = numerator.shape[0]
    feat_len, head_count = key_sum.shape
    value_len = flat_memory.shape[1] // head_count
    feat_in = queries.shape[1] // head_count
    decay_rate = jnp.where(valid_mask[:, None] > 0, decays, 0.0)
    span_decay = jnp.sum(decay_rate, axis=0)

    def merge_states(earlier, later):
        factor = jnp.exp(later[0])
        return (
            earlier[0] + later[0],
            earlier[1] * jnp.repeat(factor, value_len)[None, :] + later[1],
            earlier[2] * factor[None, :] + later[2],
        )

    neutral = (jnp.zeros_like(span_decay), jnp.zeros_like(flat_memory), jnp.zeros_like(key_sum))
    carried = entering((span_decay, flat_memory, key_sum), "seq", merge_states, neutral)
    prior_memory = carried[1]
    prior_keys = carried[2]
    highest = lax.Precision.HIGHEST
    growth = jnp.exp(jnp.cumsum(decay_rate, axis=0))
    query_feat = features(queries.astype(jnp.float32).reshape(local_len, head_count, feat_in))
    added = jnp.einsum(
        "thf,fhv->thv",
        query_feat,
        prior_memory.reshape(feat_len, head_count, value_len),
        precision=highest,
    )
    numerator = numerator + (added * growth[:, :, None]).reshape(local_len, -1)
    denominator = (
        denominator + jnp.einsum("thf,fh->th", query_feat, prior_keys, precision=highest) * growth
    )
    span_factor = jnp.exp(span_decay)
    end_state = prior_memory * jnp.repeat(span_factor, value_len)[None, :] + flat_memory
    end_norm = prior_keys * span_factor[None, :] + key_sum
    return numerator, denominator, end_state, end_norm


def permute(array, target):
    count = lax.axis_size("req")
    return lax.ppermute(array, "req", [(i, target(i)) for i in range(count)])


def flip_core(array):
    return permute(array, lambda i: i ^ 1)


def flip_near(array):
    return permute(array, lambda i: i ^ 2)


def flip_far(array):
    return permute(array, lambda i: i ^ 4)


def next_plane(array):
    return permute(array, lambda i: i ^ (16 if i // 8 in (1, 2) else 8))


def together(*arrays):
    return lax.optimization_barrier(arrays)


def slot(*sends):
    operands = together(*[array for _, array in sends])
    return together(*[send(array) for (send, _), array in zip(sends, operands)])


def vmem(count):
    return [pl.BlockSpec(memory_space=pltpu.VMEM)] * count


def kernel_call(body, name, out_shape, *operands, scratch=(), aliases=None, specs=None, mib=24):
    many = isinstance(out_shape, tuple)
    return pl.pallas_call(
        body,
        out_shape=out_shape,
        in_specs=specs or vmem(len(operands)),
        out_specs=tuple(vmem(len(out_shape))) if many else vmem(1)[0],
        scratch_shapes=list(scratch),
        input_output_aliases=aliases or {},
        compiler_params=pltpu.CompilerParams(vmem_limit_bytes=mib * 1024 * 1024),
        cost_estimate=pl.CostEstimate(flops=1000, bytes_accessed=1000, transcendentals=0),
        name=name,
    )(*operands)


def like(rows, columns, dtype):
    return jax.ShapeDtypeStruct((rows, columns), dtype)


NT = (((1,), (1,)), ((), ()))


def unit_rows(rows, gain):
    factor = lax.rsqrt(jnp.mean(rows * rows, axis=-1, keepdims=True) + 1e-05)
    return (rows * factor * gain).astype(jnp.bfloat16).astype(jnp.float32)


def project_body(
    step,
    scale,
    rows_ref,
    edge_ref,
    gain_ref,
    conv_ref,
    query_ref,
    key_ref,
    value_ref,
    queries_ref,
    keys_ref,
    values_ref,
    normed,
    gated,
):
    gain = gain_ref[...]
    count = rows_ref.shape[0]
    lead = edge_ref.shape[0]
    taps = conv_ref.shape[0]
    normed[:lead] = unit_rows(edge_ref[...].astype(jnp.float32), gain)

    @pl.loop(0, count // step)
    def _(block):
        at = pl.multiple_of(block * step, step)
        rows = rows_ref[pl.ds(at, step), :].astype(jnp.float32)
        normed[pl.ds(lead + at, step), :] = unit_rows(rows, gain)

    @pl.loop(0, count // step)
    def _(block):
        at = pl.multiple_of(block * step, step)
        window = normed[pl.ds(at, step + lead), :]
        here = window[lead:]
        total = conv_ref[0:1] * here
        for tap in range(1, taps):
            total = total + conv_ref[tap : tap + 1] * window[lead - tap : lead - tap + step]
        gated[pl.ds(at, step), :] = (total * jax.nn.sigmoid(here)).astype(jnp.bfloat16)

    rows = gated[...]
    for weight_ref, out_ref, factor in (
        (query_ref, queries_ref, scale),
        (key_ref, keys_ref, scale),
        (value_ref, values_ref, None),
    ):
        product = jnp.dot(rows, weight_ref[...], preferred_element_type=jnp.float32)
        if factor is not None:
            product = product * factor
        out_ref[...] = product.astype(jnp.bfloat16)


def project(rows, edge, mix_gain, conv_weight, query_weight, key_weight, value_weight, scale):
    count, width = rows.shape
    step = 32
    return kernel_call(
        functools.partial(project_body, step, scale),
        "project",
        tuple(like(count, w.shape[1], jnp.bfloat16) for w in (query_weight, key_weight, value_weight)),
        rows,
        edge,
        mix_gain[None],
        conv_weight,
        query_weight,
        key_weight,
        value_weight,
        scratch=(
            pltpu.VMEM((count + edge.shape[0], width), jnp.float32),
            pltpu.VMEM((count, width), jnp.bfloat16),
        ),
    )


def attend_body(
    feat_in,
    value_len,
    count_ref,
    rate_ref,
    queries_ref,
    keys_ref,
    values_ref,
    numer_ref,
    denom_ref,
    state_ref,
    norm_ref,
    turned,
    total,
    norms,
):
    heads, count = rate_ref.shape
    columns = values_ref.shape[1]
    lane = lax.broadcasted_iota(jnp.int32, (count, count), 1)
    row = lax.broadcasted_iota(jnp.int32, (count, count), 0)
    valid = (lane[:1] < count_ref[0]).astype(jnp.float32)
    rate = jnp.where(valid > 0, rate_ref[...], 0.0)
    upto = (row <= lane).astype(jnp.float32)
    across = jnp.dot(
        rate, upto, precision=lax.Precision.HIGHEST, preferred_element_type=jnp.float32
    )
    down = across.T
    closing = across[:, count - 1 : count]
    fading = jnp.exp(closing - across) * valid
    causal = row >= lane
    keys = keys_ref[...]
    turned[...] = keys.astype(jnp.float32).T
    owner = lax.broadcasted_iota(jnp.int32, queries_ref.shape, 1)
    spare = lax.broadcasted_iota(jnp.int32, (8, count), 0) == 0
    head_lane = lax.broadcasted_iota(jnp.int32, (count, 128), 1)
    numer_ref[...] = jnp.zeros(numer_ref.shape, jnp.float32)
    total[...] = jnp.zeros(total.shape, jnp.float32)
    norms[...] = jnp.zeros(norms.shape, jnp.float32)
    norm_total = jnp.zeros((total.shape[0], 128), jnp.float32)
    denominators = jnp.zeros((count, 128), jnp.float32)
    for h in range(heads):
        low = min(h * value_len // 128 * 128, max(columns - 256, 0))
        high = min(low + 256, columns)
        mine = lax.broadcasted_iota(jnp.int32, (count, high - low), 1) + low
        mine = (mine >= h * value_len) & (mine < (h + 1) * value_len)
        values = jnp.where(mine, values_ref[:, low:high].astype(jnp.float32), 0.0)
        values = values.astype(jnp.bfloat16)
        asks = (owner >= h * feat_in) & (owner < (h + 1) * feat_in)
        queries = jnp.where(asks, queries_ref[...].astype(jnp.float32), 0.0)
        scores = lax.dot_general(
            queries.astype(jnp.bfloat16), keys, NT, preferred_element_type=jnp.float32
        )
        gap = down[:, h : h + 1] - across[h : h + 1]
        weights = jnp.where(causal, jnp.exp(jnp.minimum(gap, 0.0)) * valid, 0.0)
        weights = weights * (1.0 + scores + 0.5 * scores * scores)
        numer_ref[:, low:high] += jnp.dot(
            weights.astype(jnp.bfloat16), values, preferred_element_type=jnp.float32
        )
        sums = jnp.sum(weights, axis=1, keepdims=True)
        denominators = jnp.where(head_lane == h, sums, denominators)
        own = turned[h * feat_in : (h + 1) * feat_in]
        fade = fading[h : h + 1]
        faded = own * fade
        scaled = faded * 0.5**0.5
        parts = [own[i : i + 1] * scaled for i in range(feat_in)]
        parts += [faded, jnp.where(spare, fade, 0.0)]
        feats = jnp.concatenate(parts, axis=0).astype(jnp.bfloat16)
        total[:, low:high] += jnp.dot(feats, values, preferred_element_type=jnp.float32)
        mark = (head_lane == h).astype(jnp.bfloat16)
        norm_total = norm_total + jnp.dot(feats, mark, preferred_element_type=jnp.float32)
    denom_ref[...] = denominators[:, :heads]
    pairs = feat_in * feat_in
    state_ref[0] = total[pairs + feat_in : pairs + feat_in + 1, :]
    for f in range(feat_in):
        state_ref[1 + f] = total[pairs + f : pairs + f + 1, :]

    @pl.loop(0, pairs // 8)
    def _(block):
        for k in range(8):
            f = block * 8 + k
            state_ref[1 + feat_in + f] = total[pl.ds(f, 1), :]

    norms[0:1, :] = norm_total[pairs + feat_in : pairs + feat_in + 1]
    norms[1 : 1 + feat_in, :] = norm_total[pairs : pairs + feat_in]
    norms[1 + feat_in : 1 + feat_in + pairs, :] = norm_total[:pairs]
    norm_ref[...] = norms[...].T[:heads, : 1 + feat_in + pairs]


def attend(valid_count, rate, queries, keys, values, feat_in, value_len):
    heads, count = rate.shape
    columns = values.shape[1]
    feat_len = 1 + feat_in + feat_in * feat_in
    padded = feat_in * feat_in + feat_in + 8
    return kernel_call(
        functools.partial(attend_body, feat_in, value_len),
        "attend",
        (
            like(count, columns, jnp.float32),
            like(count, heads, jnp.float32),
            jax.ShapeDtypeStruct((feat_len, 1, columns), jnp.float32),
            like(heads, feat_len, jnp.float32),
        ),
        valid_count,
        rate,
        queries,
        keys,
        values,
        specs=[pl.BlockSpec(memory_space=pltpu.SMEM)] + vmem(4),
        scratch=(
            pltpu.VMEM((queries.shape[1], count), jnp.float32),
            pltpu.VMEM((padded, columns), jnp.float32),
            pltpu.VMEM(((feat_len + 127) // 128 * 128, 128), jnp.float32),
        ),
    )


def mix_body(
    value_len, step, numer_ref, denom_ref, rows_ref, out_ref, gain_ref, mixed_ref, mlp_ref, sums
):
    count, columns = numer_ref.shape
    heads = denom_ref.shape[1]
    column = lax.broadcasted_iota(jnp.int32, (1, columns), 1)
    inverse = 1.0 / denom_ref[...]
    spread = jnp.zeros((count, columns), jnp.float32)
    for h in range(heads):
        here = (column >= h * value_len) & (column < (h + 1) * value_len)
        spread = jnp.where(here, inverse[:, h : h + 1], spread)
    attended = (numer_ref[...] * spread).astype(jnp.bfloat16)
    sums[...] = jnp.dot(attended, out_ref[...], preferred_element_type=jnp.float32)
    gain = gain_ref[...]

    @pl.loop(0, count // step)
    def _(block):
        at = pl.ds(pl.multiple_of(block * step, step), step)
        mixed = (rows_ref[at, :].astype(jnp.float32) + sums[at, :]).astype(jnp.bfloat16)
        mixed_ref[at, :] = mixed
        mlp_ref[at, :] = unit_rows(mixed.astype(jnp.float32), gain).astype(jnp.bfloat16)


def mix(numer, denom, rows, out_weight, mlp_gain, value_len):
    count, width = rows.shape
    shape = like(count, width, jnp.bfloat16)
    return kernel_call(
        functools.partial(mix_body, value_len, 32),
        "mix",
        (shape, shape),
        numer,
        denom,
        rows,
        out_weight,
        mlp_gain[None],
        scratch=(pltpu.VMEM((count, width), jnp.float32),),
    )


def swiglu_terms(rows, gate_rows, up_rows, down_rows):
    gate_act = lax.dot_general(rows, gate_rows, NT, preferred_element_type=jnp.float32)
    up_act = lax.dot_general(rows, up_rows, NT, preferred_element_type=jnp.float32)
    hidden_units = (gate_act * jax.nn.sigmoid(gate_act) * up_act).astype(jnp.bfloat16)
    return jnp.dot(hidden_units, down_rows, preferred_element_type=jnp.float32)


def on_grid(run):
    return all(low % 16 == 0 and high % 16 == 0 for _, low, high in run)


def read_units(refs, units):
    parts = []
    for k in range(3):
        rows = [refs[run[k][0]][run[k][1] : run[k][2]] for run in units if on_grid(run)]
        rest = [
            refs[run[k][0]][...].astype(jnp.float32)[run[k][1] : run[k][2]]
            for run in units
            if not on_grid(run)
        ]
        if rest:
            rows.append(jnp.concatenate(rest, axis=0).astype(jnp.bfloat16))
        parts.append(jnp.concatenate(rows, axis=0))
    return parts


def accumulate_body(units, n_weights, n_rows, n_acc, residual, *refs):
    weights = refs[:n_weights]
    rows = refs[n_weights : n_weights + n_rows]
    acc = refs[n_weights + n_rows : n_weights + n_rows + n_acc]
    parts = read_units(weights, units)
    for k, rows_ref in enumerate(rows):
        out_ref = refs[len(refs) - n_rows + k]
        terms = swiglu_terms(rows_ref[...], *parts)
        if n_acc:
            terms = terms + acc[k][...]
        if residual:
            terms = terms + refs[n_weights + n_rows + n_acc][...].astype(jnp.float32)
        out_ref[...] = terms.astype(out_ref.dtype)


def accumulate(rows, weights, units, acc, dtype, name, residual=None):
    shapes = tuple(like(*array.shape, dtype) for array in rows)
    start = len(weights) + len(rows)
    aliases = {start + k: k for k in range(len(acc))} if dtype == jnp.float32 else {}
    extra = () if residual is None else (residual,)
    body = functools.partial(
        accumulate_body, tuple(units), len(weights), len(rows), len(acc), bool(extra)
    )
    return kernel_call(body, name, shapes, *weights, *rows, *acc, *extra, aliases=aliases)


def runs(which, low, size):
    return tuple((which, low + k * size, low + (k + 1) * size) for k in range(3))


def split_runs(first, second, main):
    (i, at), (j, then) = first, second
    held = 2 * main // 3
    rest = main - held
    return (
        ((i, at, at + held), (i, at + main, at + main + held), (j, then + rest, then + main)),
        ((i, at + held, at + main), (j, then, then + rest), (j, then + main, then + rest + main)),
    )


def collect_body(plans, *refs):
    outs = refs[len(refs) - len(plans) :]
    for out_ref, plan in zip(outs, plans):
        rows = [refs[i][...].astype(jnp.float32)[low:high] for i, low, high in plan]
        out_ref[...] = jnp.concatenate(rows, axis=0).astype(jnp.bfloat16)


def collect(arrays, plans, name):
    columns = arrays[0].shape[1]
    shapes = tuple(like(sum(h - l for _, l, h in plan), columns, jnp.bfloat16) for plan in plans)
    return kernel_call(functools.partial(collect_body, plans), name, shapes, *arrays)


def shard_body(main, gate_ref, up_ref, down_ref, shard_ref, main_ref, *rest):
    buffers, sems = rest[:3], rest[3]
    copies = [
        pltpu.make_async_copy(source, buffer, sems.at[k])
        for k, (source, buffer) in enumerate(zip((gate_ref, up_ref, down_ref), buffers))
    ]
    for copy in copies:
        copy.start()
    for copy in copies:
        copy.wait()
    arrays = [buffer[...].astype(jnp.float32) for buffer in buffers]
    tops = [array[:main] for array in arrays]
    ends = [array[main:] for array in arrays]
    shard_ref[...] = jnp.concatenate(tops + ends, axis=0).astype(jnp.bfloat16)
    main_ref[...] = jnp.concatenate(tops, axis=0).astype(jnp.bfloat16)


def final_body(step, count_ref, kept_ref, given_ref, out_ref):
    count = kept_ref.shape[0]

    @pl.loop(0, count // step)
    def _(block):
        first = pl.multiple_of(block * step, step)
        at = pl.ds(first, step)
        total = kept_ref[at, :] + given_ref[at, :].astype(jnp.float32)
        row = lax.broadcasted_iota(jnp.int32, total.shape, 0) + first
        out_ref[at, :] = jnp.where(row < count_ref[0], total, 0.0).astype(out_ref.dtype)


def local(
    hidden_in,
    lengths,
    log_decay,
    mix_gain,
    conv_weight,
    query_weight,
    key_weight,
    value_weight,
    out_weight,
    mlp_gain,
    gate_weight,
    up_weight,
    down_weight,
):
    local_len = hidden_in.shape[1]
    rows_in = hidden_in[0]
    decays = log_decay[0]
    head_count = log_decay.shape[2]
    value_len = value_weight.shape[1] // head_count
    feat_in = query_weight.shape[1] // head_count
    feature_scale = feat_in ** (-0.25)
    valid_count = lengths - lax.axis_index("seq") * local_len
    spans = lax.axis_size("seq")
    units, model = gate_weight.shape[1], gate_weight.shape[0]
    edge = units // 7
    main = units - edge
    wide = 3 * main
    full = 3 * units
    narrow = full - wide
    cut = main + 2 * main // 3

    shard, shard_main = kernel_call(
        functools.partial(shard_body, main),
        "shard",
        (like(full, model, jnp.bfloat16), like(wide, model, jnp.bfloat16)),
        gate_weight.T,
        up_weight.T,
        down_weight.T,
        specs=[pl.BlockSpec(memory_space=pl.ANY)] * 3,
        scratch=[pltpu.VMEM((units, model), jnp.bfloat16)] * 3 + [pltpu.SemaphoreType.DMA((3,))],
        mib=56,
    )
    near, far, deep = slot((flip_near, shard), (flip_far, shard), (next_plane, shard_main))

    lead = 16
    if spans > 1:
        edge_in = from_behind(rows_in[local_len - lead :], "seq", 1)
    else:
        edge_in = jnp.zeros((lead, model), jnp.bfloat16)
    queries, key_rows, values = project(
        rows_in, edge_in, mix_gain, conv_weight, query_weight, key_weight, value_weight, feature_scale
    )
    near, far, deep, queries, key_rows, values = together(
        near, far, deep, queries, key_rows, values
    )

    sends = collect(
        (shard, near, far, deep),
        (
            ((3, 0, wide), (2, 0, cut)),
            ((3, 0, wide), (1, cut, full)),
            ((3, 0, wide), (0, wide, full), (1, wide, full), (2, wide, full)),
        ),
        "collect_second",
    )
    near1, far1, deep1 = slot(*zip((flip_near, flip_far, next_plane), sends))

    numerator, denominator, end_state, end_norm = attend(
        valid_count, log_decay[0].T, queries, key_rows, values, feat_in, value_len
    )
    if spans > 1:
        positions = jnp.arange(local_len, dtype=jnp.int32)
        numerator, denominator, end_state, end_norm = carry_in(
            (positions < valid_count).astype(jnp.float32),
            decays,
            queries,
            numerator,
            denominator,
            end_state[:, 0],
            end_norm.T,
        )
    else:
        end_norm = end_norm.T
    mixed_rows, mlp_in = mix(numerator, denominator, rows_in, out_weight, mlp_gain, value_len)
    near1, far1, deep1, mixed_rows, mlp_in, end_state, end_norm = together(
        near1, far1, deep1, mixed_rows, mlp_in, end_state, end_norm
    )

    middle = local_len // 2
    *sends, top, end = collect(
        (near1, far1, deep1, mlp_in),
        (
            ((2, 0, wide), (1, 0, cut)),
            ((2, 0, wide), (0, cut, wide)),
            ((2, 0, wide + 3 * narrow), (1, wide + wide - cut, wide + full - cut)),
            ((3, 0, middle),),
            ((3, middle, local_len),),
        ),
        "collect_third",
    )
    near2, far2, deep2 = slot(*zip((flip_near, flip_far, next_plane), sends))
    (other_in,) = collect(
        (flip_core(top), flip_core(end)),
        (((0, 0, middle), (1, 0, local_len - middle)),),
        "collect_rows",
    )
    rows = (mlp_in, other_in)
    acc = accumulate(
        rows,
        (shard, near, far, deep, near1, far1, deep1),
        [runs(i, 0, main) for i in range(7)] + list(split_runs((4, wide), (5, wide), main)),
        (),
        jnp.float32,
        "accumulate_second",
    )
    near2, far2, deep2, *acc = together(near2, far2, deep2, *acc)

    held = 2 * main // 3
    two = 2 * main
    sends = collect(
        (near2, far2, deep2),
        (
            ((2, main, wide),),
            ((2, 0, main), (2, two, wide)),
            ((2, wide, wide + 4 * narrow), (1, 2 * wide - cut - main, 2 * wide - cut - main + held)),
            ((2, 0, main), (1, 0, main), (1, two + held, wide)),
            ((2, main, two), (0, main, two)),
        ),
        "collect_fourth",
    )
    sends = together(*sends)
    near3, far3, deep3 = flip_near(sends[0]), flip_far(sends[1]), next_plane(sends[2])
    near3_more, far3_more = flip_near(sends[3]), flip_far(sends[4])
    acc = accumulate(
        rows,
        (shard, near, far, far1, deep1, near2, far2, deep2),
        [runs(i, 0, main) for i in (5, 6, 7)]
        + list(split_runs((5, wide), (6, wide), main))
        + [runs(i, wide, edge) for i in (0, 1, 2)]
        + [runs(3, wide + wide - cut, edge)]
        + [runs(4, wide + k * narrow, edge) for k in range(3)]
        + [runs(7, wide + k * narrow, edge) for k in range(4)],
        tuple(acc),
        jnp.float32,
        "accumulate_third",
    )
    near3, far3, deep3, *acc = together(near3, far3, deep3, *acc)

    sends = collect(
        (near3, far3, deep3),
        (
            ((1, 0, main),),
            ((0, 0, main), (0, main + held, two)),
            ((2, 3 * narrow, 4 * narrow + held),),
        ),
        "collect_fifth",
    )
    near4, far4, deep4 = slot(*zip((flip_near, flip_far, next_plane), sends))
    line = 4 * narrow
    weights = (near3, near3_more, far3, far3_more, deep3, near4, far4, deep4)
    last = [
        ((1, 0, main), (0, 0, main), (0, main, two)),
        ((2, 0, main), (3, 0, main), (2, main, two)),
        ((1, main, main + held), (3, main, main + held), (4, line, line + held)),
        ((1, main + held, two), (3, main + held, two), (1, two, two + main - held)),
        ((5, 0, held), (6, 0, held), (7, narrow, narrow + held)),
        ((5, held, main), (6, held, main), (6, main, two - held)),
    ]
    last += [runs(4, k * narrow, edge) for k in range(4)] + [runs(7, 0, edge)]
    (given,) = accumulate(rows[1:], weights, last, acc[1:], jnp.bfloat16, "finish_other")
    (kept,) = accumulate(
        rows[:1], weights, last, acc[:1], jnp.float32, "finish_own", residual=mixed_rows
    )
    result = kernel_call(
        functools.partial(final_body, 64),
        "final",
        like(local_len, model, jnp.bfloat16),
        valid_count,
        kept,
        flip_core(given),
        specs=[pl.BlockSpec(memory_space=pltpu.SMEM)] + vmem(2),
    )
    return (
        result[None],
        end_state.reshape((1, 1) + end_state.shape[:1] + end_state.shape[-1:]),
        end_norm[None, None],
    )


def solution(mesh):
    return jax.shard_map(
        local,
        mesh=mesh,
        in_specs=(
            P("req", "seq", None),
            P("req"),
            P("req", "seq", None),
            P(),
            P(),
            P(),
            P(),
            P(),
            P(),
            P(),
            P(None, "req"),
            P(None, "req"),
            P(None, "req"),
        ),
        out_specs=(P("req", "seq", None), P("req", "seq", None, None), P("req", "seq", None, None)),
        check_vma=False,
    )
```

```python
import functools

import jax
import jax.numpy as jnp
from jax import lax
from jax.experimental import pallas as pl
from jax.experimental.pallas import tpu as pltpu
from jax.sharding import PartitionSpec as P


def from_behind(array, axis, by):
    count = lax.axis_size(axis)
    pairs = [(i, i + by) for i in range(count) if 0 <= i + by < count]
    return lax.ppermute(array, axis, pairs)


def entering(array, axis, combine, identity):
    count, here = (lax.axis_size(axis), lax.axis_index(axis))
    everything = jax.tree.map(
        lambda part, kind: lax.all_gather(part.astype(kind), axis),
        array,
        (jnp.bfloat16, jnp.bfloat16, jnp.bfloat16),
    )
    start = jax.tree.map(
        lambda part, zero: jnp.broadcast_to(jnp.asarray(zero, part.dtype), part.shape),
        array,
        identity,
    )

    def hop(k, before):
        reached = k < here
        new = combine(
            before, jax.tree.map(lambda part, own: part[k].astype(own.dtype), everything, array)
        )
        return jax.tree.map(lambda a, b: jnp.where(reached, a, b), new, before)

    return lax.fori_loop(0, count, hop, start)


def features(vectors):
    constant = jnp.ones(vectors.shape[:-1] + (1,), jnp.float32)
    width = vectors.shape[-1]
    squares = (vectors[..., :, None] * vectors[..., None, :]).reshape(
        vectors.shape[:-1] + (width * width,)
    )
    return jnp.concatenate([constant, vectors, squares * 0.5**0.5], axis=-1)


def carry_in(valid_mask, decays, queries, numerator, denominator, flat_memory, key_sum):
    local_len = numerator.shape[0]
    feat_len, head_count = key_sum.shape
    value_len = flat_memory.shape[1] // head_count
    feat_in = queries.shape[1] // head_count
    decay_rate = jnp.where(valid_mask[:, None] > 0, decays, 0.0)
    span_decay = jnp.sum(decay_rate, axis=0)

    def merge_states(earlier, later):
        factor = jnp.exp(later[0])
        return (
            earlier[0] + later[0],
            earlier[1] * jnp.repeat(factor, value_len)[None, :] + later[1],
            earlier[2] * factor[None, :] + later[2],
        )

    neutral = (jnp.zeros_like(span_decay), jnp.zeros_like(flat_memory), jnp.zeros_like(key_sum))
    carried = entering((span_decay, flat_memory, key_sum), "seq", merge_states, neutral)
    prior_memory = carried[1]
    prior_keys = carried[2]
    highest = lax.Precision.HIGHEST
    growth = jnp.exp(jnp.cumsum(decay_rate, axis=0))
    query_feat = features(queries.astype(jnp.float32).reshape(local_len, head_count, feat_in))
    added = jnp.einsum(
        "thf,fhv->thv",
        query_feat,
        prior_memory.reshape(feat_len, head_count, value_len),
        precision=highest,
    )
    numerator = numerator + (added * growth[:, :, None]).reshape(local_len, -1)
    denominator = (
        denominator + jnp.einsum("thf,fh->th", query_feat, prior_keys, precision=highest) * growth
    )
    span_factor = jnp.exp(span_decay)
    end_state = prior_memory * jnp.repeat(span_factor, value_len)[None, :] + flat_memory
    end_norm = prior_keys * span_factor[None, :] + key_sum
    return numerator, denominator, end_state, end_norm


def permute(array, target):
    count = lax.axis_size("req")
    return lax.ppermute(array, "req", [(i, target(i)) for i in range(count)])


def flip_core(array):
    return permute(array, lambda i: i ^ 1)


def flip_near(array):
    return permute(array, lambda i: i ^ 2)


def flip_far(array):
    return permute(array, lambda i: i ^ 4)


def next_plane(array):
    return permute(array, lambda i: i ^ (16 if i // 8 in (1, 2) else 8))


def together(*arrays):
    return lax.optimization_barrier(arrays)


def slot(*sends):
    operands = together(*[array for _, array in sends])
    return together(*[send(array) for (send, _), array in zip(sends, operands)])


def vmem(count):
    return [pl.BlockSpec(memory_space=pltpu.VMEM)] * count


def kernel_call(body, name, out_shape, *operands, scratch=(), aliases=None, specs=None, mib=24):
    many = isinstance(out_shape, tuple)
    return pl.pallas_call(
        body,
        out_shape=out_shape,
        in_specs=specs or vmem(len(operands)),
        out_specs=tuple(vmem(len(out_shape))) if many else vmem(1)[0],
        scratch_shapes=list(scratch),
        input_output_aliases=aliases or {},
        compiler_params=pltpu.CompilerParams(vmem_limit_bytes=mib * 1024 * 1024),
        cost_estimate=pl.CostEstimate(flops=1000, bytes_accessed=1000, transcendentals=0),
        name=name,
    )(*operands)


def like(rows, columns, dtype):
    return jax.ShapeDtypeStruct((rows, columns), dtype)


NT = (((1,), (1,)), ((), ()))


def unit_rows(rows, gain):
    factor = lax.rsqrt(jnp.mean(rows * rows, axis=-1, keepdims=True) + 1e-05)
    return (rows * factor * gain).astype(jnp.bfloat16).astype(jnp.float32)


def project_body(
    step,
    scale,
    rows_ref,
    edge_ref,
    gain_ref,
    conv_ref,
    query_ref,
    key_ref,
    value_ref,
    queries_ref,
    keys_ref,
    values_ref,
    normed,
    gated,
):
    gain = gain_ref[...]
    count = rows_ref.shape[0]
    lead = edge_ref.shape[0]
    taps = conv_ref.shape[0]
    normed[:lead] = unit_rows(edge_ref[...].astype(jnp.float32), gain)

    @pl.loop(0, count // step)
    def _(block):
        at = pl.multiple_of(block * step, step)
        rows = rows_ref[pl.ds(at, step), :].astype(jnp.float32)
        normed[pl.ds(lead + at, step), :] = unit_rows(rows, gain)

    @pl.loop(0, count // step)
    def _(block):
        at = pl.multiple_of(block * step, step)
        window = normed[pl.ds(at, step + lead), :]
        here = window[lead:]
        total = conv_ref[0:1] * here
        for tap in range(1, taps):
            total = total + conv_ref[tap : tap + 1] * window[lead - tap : lead - tap + step]
        gated[pl.ds(at, step), :] = (total * jax.nn.sigmoid(here)).astype(jnp.bfloat16)

    rows = gated[...]
    for weight_ref, out_ref, factor in (
        (query_ref, queries_ref, scale),
        (key_ref, keys_ref, scale),
        (value_ref, values_ref, None),
    ):
        product = jnp.dot(rows, weight_ref[...], preferred_element_type=jnp.float32)
        if factor is not None:
            product = product * factor
        out_ref[...] = product.astype(jnp.bfloat16)


def project(rows, edge, mix_gain, conv_weight, query_weight, key_weight, value_weight, scale):
    count, width = rows.shape
    step = 32
    return kernel_call(
        functools.partial(project_body, step, scale),
        "project",
        tuple(like(count, w.shape[1], jnp.bfloat16) for w in (query_weight, key_weight, value_weight)),
        rows,
        edge,
        mix_gain[None],
        conv_weight,
        query_weight,
        key_weight,
        value_weight,
        scratch=(
            pltpu.VMEM((count + edge.shape[0], width), jnp.float32),
            pltpu.VMEM((count, width), jnp.bfloat16),
        ),
    )


def attend_body(
    feat_in,
    value_len,
    count_ref,
    rate_ref,
    queries_ref,
    keys_ref,
    values_ref,
    numer_ref,
    denom_ref,
    state_ref,
    norm_ref,
    turned,
    total,
    norms,
):
    heads, count = rate_ref.shape
    columns = values_ref.shape[1]
    lane = lax.broadcasted_iota(jnp.int32, (count, count), 1)
    row = lax.broadcasted_iota(jnp.int32, (count, count), 0)
    valid = (lane[:1] < count_ref[0]).astype(jnp.float32)
    rate = jnp.where(valid > 0, rate_ref[...], 0.0)
    upto = (row <= lane).astype(jnp.float32)
    across = jnp.dot(
        rate, upto, precision=lax.Precision.HIGHEST, preferred_element_type=jnp.float32
    )
    down = across.T
    closing = across[:, count - 1 : count]
    fading = jnp.exp(closing - across) * valid
    causal = row >= lane
    keys = keys_ref[...]
    turned[...] = keys.astype(jnp.float32).T
    owner = lax.broadcasted_iota(jnp.int32, queries_ref.shape, 1)
    spare = lax.broadcasted_iota(jnp.int32, (8, count), 0) == 0
    head_lane = lax.broadcasted_iota(jnp.int32, (count, 128), 1)
    numer_ref[...] = jnp.zeros(numer_ref.shape, jnp.float32)
    total[...] = jnp.zeros(total.shape, jnp.float32)
    norms[...] = jnp.zeros(norms.shape, jnp.float32)
    norm_total = jnp.zeros((total.shape[0], 128), jnp.float32)
    denominators = jnp.zeros((count, 128), jnp.float32)
    for h in range(heads):
        low = min(h * value_len // 128 * 128, max(columns - 256, 0))
        high = min(low + 256, columns)
        mine = lax.broadcasted_iota(jnp.int32, (count, high - low), 1) + low
        mine = (mine >= h * value_len) & (mine < (h + 1) * value_len)
        values = jnp.where(mine, values_ref[:, low:high].astype(jnp.float32), 0.0)
        values = values.astype(jnp.bfloat16)
        asks = (owner >= h * feat_in) & (owner < (h + 1) * feat_in)
        queries = jnp.where(asks, queries_ref[...].astype(jnp.float32), 0.0)
        scores = lax.dot_general(
            queries.astype(jnp.bfloat16), keys, NT, preferred_element_type=jnp.float32
        )
        gap = down[:, h : h + 1] - across[h : h + 1]
        weights = jnp.where(causal, jnp.exp(jnp.minimum(gap, 0.0)) * valid, 0.0)
        weights = weights * (1.0 + scores + 0.5 * scores * scores)
        numer_ref[:, low:high] += jnp.dot(
            weights.astype(jnp.bfloat16), values, preferred_element_type=jnp.float32
        )
        sums = jnp.sum(weights, axis=1, keepdims=True)
        denominators = jnp.where(head_lane == h, sums, denominators)
        own = turned[h * feat_in : (h + 1) * feat_in]
        fade = fading[h : h + 1]
        faded = own * fade
        scaled = faded * 0.5**0.5
        parts = [own[i : i + 1] * scaled for i in range(feat_in)]
        parts += [faded, jnp.where(spare, fade, 0.0)]
        feats = jnp.concatenate(parts, axis=0).astype(jnp.bfloat16)
        total[:, low:high] += jnp.dot(feats, values, preferred_element_type=jnp.float32)
        mark = (head_lane == h).astype(jnp.bfloat16)
        norm_total = norm_total + jnp.dot(feats, mark, preferred_element_type=jnp.float32)
    denom_ref[...] = denominators[:, :heads]
    pairs = feat_in * feat_in
    state_ref[0] = total[pairs + feat_in : pairs + feat_in + 1, :]
    for f in range(feat_in):
        state_ref[1 + f] = total[pairs + f : pairs + f + 1, :]

    @pl.loop(0, pairs // 8)
    def _(block):
        for k in range(8):
            f = block * 8 + k
            state_ref[1 + feat_in + f] = total[pl.ds(f, 1), :]

    norms[0:1, :] = norm_total[pairs + feat_in : pairs + feat_in + 1]
    norms[1 : 1 + feat_in, :] = norm_total[pairs : pairs + feat_in]
    norms[1 + feat_in : 1 + feat_in + pairs, :] = norm_total[:pairs]
    norm_ref[...] = norms[...].T[:heads, : 1 + feat_in + pairs]


def attend(valid_count, rate, queries, keys, values, feat_in, value_len):
    heads, count = rate.shape
    columns = values.shape[1]
    feat_len = 1 + feat_in + feat_in * feat_in
    padded = feat_in * feat_in + feat_in + 8
    return kernel_call(
        functools.partial(attend_body, feat_in, value_len),
        "attend",
        (
            like(count, columns, jnp.float32),
            like(count, heads, jnp.float32),
            jax.ShapeDtypeStruct((feat_len, 1, columns), jnp.float32),
            like(heads, feat_len, jnp.float32),
        ),
        valid_count,
        rate,
        queries,
        keys,
        values,
        specs=[pl.BlockSpec(memory_space=pltpu.SMEM)] + vmem(4),
        scratch=(
            pltpu.VMEM((queries.shape[1], count), jnp.float32),
            pltpu.VMEM((padded, columns), jnp.float32),
            pltpu.VMEM(((feat_len + 127) // 128 * 128, 128), jnp.float32),
        ),
    )


def mix_body(
    value_len, step, numer_ref, denom_ref, rows_ref, out_ref, gain_ref, mixed_ref, mlp_ref, sums
):
    count, columns = numer_ref.shape
    heads = denom_ref.shape[1]
    column = lax.broadcasted_iota(jnp.int32, (1, columns), 1)
    inverse = 1.0 / denom_ref[...]
    spread = jnp.zeros((count, columns), jnp.float32)
    for h in range(heads):
        here = (column >= h * value_len) & (column < (h + 1) * value_len)
        spread = jnp.where(here, inverse[:, h : h + 1], spread)
    attended = (numer_ref[...] * spread).astype(jnp.bfloat16)
    sums[...] = jnp.dot(attended, out_ref[...], preferred_element_type=jnp.float32)
    gain = gain_ref[...]

    @pl.loop(0, count // step)
    def _(block):
        at = pl.ds(pl.multiple_of(block * step, step), step)
        mixed = (rows_ref[at, :].astype(jnp.float32) + sums[at, :]).astype(jnp.bfloat16)
        mixed_ref[at, :] = mixed
        mlp_ref[at, :] = unit_rows(mixed.astype(jnp.float32), gain).astype(jnp.bfloat16)


def mix(numer, denom, rows, out_weight, mlp_gain, value_len):
    count, width = rows.shape
    shape = like(count, width, jnp.bfloat16)
    return kernel_call(
        functools.partial(mix_body, value_len, 32),
        "mix",
        (shape, shape),
        numer,
        denom,
        rows,
        out_weight,
        mlp_gain[None],
        scratch=(pltpu.VMEM((count, width), jnp.float32),),
    )


def swiglu_terms(rows, gate_rows, up_rows, down_rows):
    gate_act = lax.dot_general(rows, gate_rows, NT, preferred_element_type=jnp.float32)
    up_act = lax.dot_general(rows, up_rows, NT, preferred_element_type=jnp.float32)
    hidden_units = (gate_act * jax.nn.sigmoid(gate_act) * up_act).astype(jnp.bfloat16)
    return jnp.dot(hidden_units, down_rows, preferred_element_type=jnp.float32)


def on_grid(run):
    return all(low % 16 == 0 and high % 16 == 0 for _, low, high in run)


def read_units(refs, units):
    parts = []
    for k in range(3):
        rows = [refs[run[k][0]][run[k][1] : run[k][2]] for run in units if on_grid(run)]
        rest = [
            refs[run[k][0]][...].astype(jnp.float32)[run[k][1] : run[k][2]]
            for run in units
            if not on_grid(run)
        ]
        if rest:
            rows.append(jnp.concatenate(rest, axis=0).astype(jnp.bfloat16))
        parts.append(jnp.concatenate(rows, axis=0))
    return parts


def accumulate_body(units, n_weights, n_rows, n_acc, residual, *refs):
    weights = refs[:n_weights]
    rows = refs[n_weights : n_weights + n_rows]
    acc = refs[n_weights + n_rows : n_weights + n_rows + n_acc]
    parts = read_units(weights, units)
    for k, rows_ref in enumerate(rows):
        out_ref = refs[len(refs) - n_rows + k]
        terms = swiglu_terms(rows_ref[...], *parts)
        if n_acc:
            terms = terms + acc[k][...]
        if residual:
            terms = terms + refs[n_weights + n_rows + n_acc][...].astype(jnp.float32)
        out_ref[...] = terms.astype(out_ref.dtype)


def accumulate(rows, weights, units, acc, dtype, name, residual=None):
    shapes = tuple(like(*array.shape, dtype) for array in rows)
    start = len(weights) + len(rows)
    aliases = {start + k: k for k in range(len(acc))} if dtype == jnp.float32 else {}
    extra = () if residual is None else (residual,)
    body = functools.partial(
        accumulate_body, tuple(units), len(weights), len(rows), len(acc), bool(extra)
    )
    return kernel_call(body, name, shapes, *weights, *rows, *acc, *extra, aliases=aliases)


def runs(which, low, size):
    return tuple((which, low + k * size, low + (k + 1) * size) for k in range(3))


def split_runs(first, second, main):
    (i, at), (j, then) = first, second
    held = 2 * main // 3
    rest = main - held
    return (
        ((i, at, at + held), (i, at + main, at + main + held), (j, then + rest, then + main)),
        ((i, at + held, at + main), (j, then, then + rest), (j, then + main, then + rest + main)),
    )


def collect_body(plans, *refs):
    outs = refs[len(refs) - len(plans) :]
    for out_ref, plan in zip(outs, plans):
        rows = [refs[i][...].astype(jnp.float32)[low:high] for i, low, high in plan]
        out_ref[...] = jnp.concatenate(rows, axis=0).astype(jnp.bfloat16)


def collect(arrays, plans, name):
    columns = arrays[0].shape[1]
    shapes = tuple(like(sum(h - l for _, l, h in plan), columns, jnp.bfloat16) for plan in plans)
    return kernel_call(functools.partial(collect_body, plans), name, shapes, *arrays)


def shard_body(main, gate_ref, up_ref, down_ref, shard_ref, main_ref, *rest):
    buffers, sems = rest[:3], rest[3]
    copies = [
        pltpu.make_async_copy(source, buffer, sems.at[k])
        for k, (source, buffer) in enumerate(zip((gate_ref, up_ref, down_ref), buffers))
    ]
    for copy in copies:
        copy.start()
    for copy in copies:
        copy.wait()
    arrays = [buffer[...].astype(jnp.float32) for buffer in buffers]
    tops = [array[:main] for array in arrays]
    ends = [array[main:] for array in arrays]
    shard_ref[...] = jnp.concatenate(tops + ends, axis=0).astype(jnp.bfloat16)
    main_ref[...] = jnp.concatenate(tops, axis=0).astype(jnp.bfloat16)


def final_body(step, count_ref, kept_ref, given_ref, out_ref):
    count = kept_ref.shape[0]

    @pl.loop(0, count // step)
    def _(block):
        first = pl.multiple_of(block * step, step)
        at = pl.ds(first, step)
        total = kept_ref[at, :] + given_ref[at, :].astype(jnp.float32)
        row = lax.broadcasted_iota(jnp.int32, total.shape, 0) + first
        out_ref[at, :] = jnp.where(row < count_ref[0], total, 0.0).astype(out_ref.dtype)


def local(
    hidden_in,
    lengths,
    log_decay,
    mix_gain,
    conv_weight,
    query_weight,
    key_weight,
    value_weight,
    out_weight,
    mlp_gain,
    gate_weight,
    up_weight,
    down_weight,
):
    local_len = hidden_in.shape[1]
    rows_in = hidden_in[0]
    decays = log_decay[0]
    head_count = log_decay.shape[2]
    value_len = value_weight.shape[1] // head_count
    feat_in = query_weight.shape[1] // head_count
    feature_scale = feat_in ** (-0.25)
    valid_count = lengths - lax.axis_index("seq") * local_len
    spans = lax.axis_size("seq")
    units, model = gate_weight.shape[1], gate_weight.shape[0]
    edge = units // 7
    main = units - edge
    wide = 3 * main
    full = 3 * units
    narrow = full - wide
    cut = main + 2 * main // 3

    shard, shard_main = kernel_call(
        functools.partial(shard_body, main),
        "shard",
        (like(full, model, jnp.bfloat16), like(wide, model, jnp.bfloat16)),
        gate_weight.T,
        up_weight.T,
        down_weight.T,
        specs=[pl.BlockSpec(memory_space=pl.ANY)] * 3,
        scratch=[pltpu.VMEM((units, model), jnp.bfloat16)] * 3 + [pltpu.SemaphoreType.DMA((3,))],
        mib=56,
    )
    near, far, deep = slot((flip_near, shard), (flip_far, shard), (next_plane, shard_main))

    lead = 16
    if spans > 1:
        edge_in = from_behind(rows_in[local_len - lead :], "seq", 1)
    else:
        edge_in = jnp.zeros((lead, model), jnp.bfloat16)
    queries, key_rows, values = project(
        rows_in, edge_in, mix_gain, conv_weight, query_weight, key_weight, value_weight, feature_scale
    )
    near, far, deep, queries, key_rows, values = together(
        near, far, deep, queries, key_rows, values
    )

    sends = collect(
        (shard, near, far, deep),
        (
            ((3, 0, wide), (2, 0, cut)),
            ((3, 0, wide), (1, cut, full)),
            ((3, 0, wide), (0, wide, full), (1, wide, full), (2, wide, full)),
        ),
        "collect_second",
    )
    near1, far1, deep1 = slot(*zip((flip_near, flip_far, next_plane), sends))

    numerator, denominator, end_state, end_norm = attend(
        valid_count, log_decay[0].T, queries, key_rows, values, feat_in, value_len
    )
    if spans > 1:
        positions = jnp.arange(local_len, dtype=jnp.int32)
        numerator, denominator, end_state, end_norm = carry_in(
            (positions < valid_count).astype(jnp.float32),
            decays,
            queries,
            numerator,
            denominator,
            end_state[:, 0],
            end_norm.T,
        )
    else:
        end_norm = end_norm.T
    mixed_rows, mlp_in = mix(numerator, denominator, rows_in, out_weight, mlp_gain, value_len)
    near1, far1, deep1, mixed_rows, mlp_in, end_state, end_norm = together(
        near1, far1, deep1, mixed_rows, mlp_in, end_state, end_norm
    )

    middle = local_len // 2
    *sends, top, end = collect(
        (near1, far1, deep1, mlp_in),
        (
            ((2, 0, wide), (1, 0, cut)),
            ((2, 0, wide), (0, cut, wide)),
            ((2, 0, wide + 3 * narrow), (1, wide + wide - cut, wide + full - cut)),
            ((3, 0, middle),),
            ((3, middle, local_len),),
        ),
        "collect_third",
    )
    near2, far2, deep2 = slot(*zip((flip_near, flip_far, next_plane), sends))
    (other_in,) = collect(
        (flip_core(top), flip_core(end)),
        (((0, 0, middle), (1, 0, local_len - middle)),),
        "collect_rows",
    )
    rows = (mlp_in, other_in)
    acc = accumulate(
        rows,
        (shard, near, far, deep, near1, far1, deep1),
        [runs(i, 0, main) for i in range(7)] + list(split_runs((4, wide), (5, wide), main)),
        (),
        jnp.float32,
        "accumulate_second",
    )
    near2, far2, deep2, *acc = together(near2, far2, deep2, *acc)

    two = 2 * main
    sends = collect(
        (near2, far2, deep2),
        (
            ((2, main, wide),),
            ((2, 0, main), (2, two, wide)),
            ((2, wide, wide + 4 * narrow), (1, 2 * wide - cut - main, 2 * wide - cut)),
            ((2, 0, main), (1, 0, main)),
            ((2, main, two), (0, main, two)),
        ),
        "collect_fourth",
    )
    sends = together(*sends)
    near3, far3, deep3 = flip_near(sends[0]), flip_far(sends[1]), next_plane(sends[2])
    near3_more, far3_more = flip_near(sends[3]), flip_far(sends[4])
    acc = accumulate(
        rows,
        (shard, near, far, far1, deep1, near2, far2, deep2),
        [runs(i, 0, main) for i in (5, 6, 7)]
        + list(split_runs((5, wide), (6, wide), main))
        + [runs(i, wide, edge) for i in (0, 1, 2)]
        + [runs(3, wide + wide - cut, edge)]
        + [runs(4, wide + k * narrow, edge) for k in range(3)]
        + [runs(7, wide + k * narrow, edge) for k in range(4)],
        tuple(acc),
        jnp.float32,
        "accumulate_third",
    )
    near3, far3, deep3, *acc = together(near3, far3, deep3, *acc)

    sends = collect(
        (near3, far3, deep3),
        (
            ((1, 0, main),),
            ((0, 0, main),),
            ((2, 3 * narrow, 4 * narrow + main),),
        ),
        "collect_fifth",
    )
    near4, far4, deep4 = slot(*zip((flip_near, flip_far, next_plane), sends))
    line = 4 * narrow
    weights = (near3, near3_more, far3, far3_more, deep3, near4, far4, deep4)
    last = [
        ((1, 0, main), (0, 0, main), (0, main, two)),
        ((2, 0, main), (3, 0, main), (2, main, two)),
        ((1, main, two), (3, main, two), (4, line, line + main)),
        ((5, 0, main), (6, 0, main), (7, narrow, narrow + main)),
    ]
    last += [runs(4, k * narrow, edge) for k in range(4)] + [runs(7, 0, edge)]
    (given,) = accumulate(rows[1:], weights, last, acc[1:], jnp.bfloat16, "finish_other")
    (kept,) = accumulate(
        rows[:1], weights, last, acc[:1], jnp.float32, "finish_own", residual=mixed_rows
    )
    result = kernel_call(
        functools.partial(final_body, 64),
        "final",
        like(local_len, model, jnp.bfloat16),
        valid_count,
        kept,
        flip_core(given),
        specs=[pl.BlockSpec(memory_space=pltpu.SMEM)] + vmem(2),
    )
    return (
        result[None],
        end_state.reshape((1, 1) + end_state.shape[:1] + end_state.shape[-1:]),
        end_norm[None, None],
    )


def solution(mesh):
    return jax.shard_map(
        local,
        mesh=mesh,
        in_specs=(
            P("req", "seq", None),
            P("req"),
            P("req", "seq", None),
            P(),
            P(),
            P(),
            P(),
            P(),
            P(),
            P(),
            P(None, "req"),
            P(None, "req"),
            P(None, "req"),
        ),
        out_specs=(P("req", "seq", None), P("req", "seq", None, None), P("req", "seq", None, None)),
        check_vma=False,
    )
```

```python
import functools

import jax
import jax.numpy as jnp
from jax import lax
from jax.experimental import pallas as pl
from jax.experimental.pallas import tpu as pltpu
from jax.sharding import PartitionSpec as P


def from_behind(array, axis, by):
    count = lax.axis_size(axis)
    pairs = [(i, i + by) for i in range(count) if 0 <= i + by < count]
    return lax.ppermute(array, axis, pairs)


def entering(array, axis, combine, identity):
    count, here = (lax.axis_size(axis), lax.axis_index(axis))
    everything = jax.tree.map(
        lambda part, kind: lax.all_gather(part.astype(kind), axis),
        array,
        (jnp.bfloat16, jnp.bfloat16, jnp.bfloat16),
    )
    start = jax.tree.map(
        lambda part, zero: jnp.broadcast_to(jnp.asarray(zero, part.dtype), part.shape),
        array,
        identity,
    )

    def hop(k, before):
        reached = k < here
        new = combine(
            before, jax.tree.map(lambda part, own: part[k].astype(own.dtype), everything, array)
        )
        return jax.tree.map(lambda a, b: jnp.where(reached, a, b), new, before)

    return lax.fori_loop(0, count, hop, start)


def features(vectors):
    constant = jnp.ones(vectors.shape[:-1] + (1,), jnp.float32)
    width = vectors.shape[-1]
    squares = (vectors[..., :, None] * vectors[..., None, :]).reshape(
        vectors.shape[:-1] + (width * width,)
    )
    return jnp.concatenate([constant, vectors, squares * 0.5**0.5], axis=-1)


def carry_in(valid_mask, decays, queries, numerator, denominator, flat_memory, key_sum):
    local_len = numerator.shape[0]
    feat_len, head_count = key_sum.shape
    value_len = flat_memory.shape[1] // head_count
    feat_in = queries.shape[1] // head_count
    decay_rate = jnp.where(valid_mask[:, None] > 0, decays, 0.0)
    span_decay = jnp.sum(decay_rate, axis=0)

    def merge_states(earlier, later):
        factor = jnp.exp(later[0])
        return (
            earlier[0] + later[0],
            earlier[1] * jnp.repeat(factor, value_len)[None, :] + later[1],
            earlier[2] * factor[None, :] + later[2],
        )

    neutral = (jnp.zeros_like(span_decay), jnp.zeros_like(flat_memory), jnp.zeros_like(key_sum))
    carried = entering((span_decay, flat_memory, key_sum), "seq", merge_states, neutral)
    prior_memory = carried[1]
    prior_keys = carried[2]
    highest = lax.Precision.HIGHEST
    growth = jnp.exp(jnp.cumsum(decay_rate, axis=0))
    query_feat = features(queries.astype(jnp.float32).reshape(local_len, head_count, feat_in))
    added = jnp.einsum(
        "thf,fhv->thv",
        query_feat,
        prior_memory.reshape(feat_len, head_count, value_len),
        precision=highest,
    )
    numerator = numerator + (added * growth[:, :, None]).reshape(local_len, -1)
    denominator = (
        denominator + jnp.einsum("thf,fh->th", query_feat, prior_keys, precision=highest) * growth
    )
    span_factor = jnp.exp(span_decay)
    end_state = prior_memory * jnp.repeat(span_factor, value_len)[None, :] + flat_memory
    end_norm = prior_keys * span_factor[None, :] + key_sum
    return numerator, denominator, end_state, end_norm


def permute(array, target):
    count = lax.axis_size("req")
    return lax.ppermute(array, "req", [(i, target(i)) for i in range(count)])


def flip_core(array):
    return permute(array, lambda i: i ^ 1)


def flip_near(array):
    return permute(array, lambda i: i ^ 2)


def flip_far(array):
    return permute(array, lambda i: i ^ 4)


def next_plane(array):
    return permute(array, lambda i: i ^ (8 if i // 8 in (1, 2) else 16))


def together(*arrays):
    return lax.optimization_barrier(arrays)


def slot(*sends):
    operands = together(*[array for _, array in sends])
    return together(*[send(array) for (send, _), array in zip(sends, operands)])


def vmem(count):
    return [pl.BlockSpec(memory_space=pltpu.VMEM)] * count


def kernel_call(body, name, out_shape, *operands, scratch=(), aliases=None, specs=None, mib=24):
    many = isinstance(out_shape, tuple)
    return pl.pallas_call(
        body,
        out_shape=out_shape,
        in_specs=specs or vmem(len(operands)),
        out_specs=tuple(vmem(len(out_shape))) if many else vmem(1)[0],
        scratch_shapes=list(scratch),
        input_output_aliases=aliases or {},
        compiler_params=pltpu.CompilerParams(vmem_limit_bytes=mib * 1024 * 1024),
        cost_estimate=pl.CostEstimate(flops=1000, bytes_accessed=1000, transcendentals=0),
        name=name,
    )(*operands)


def like(rows, columns, dtype):
    return jax.ShapeDtypeStruct((rows, columns), dtype)


NT = (((1,), (1,)), ((), ()))


def unit_rows(rows, gain):
    factor = lax.rsqrt(jnp.mean(rows * rows, axis=-1, keepdims=True) + 1e-05)
    return (rows * factor * gain).astype(jnp.bfloat16).astype(jnp.float32)


def project_body(
    step,
    scale,
    rows_ref,
    edge_ref,
    gain_ref,
    conv_ref,
    query_ref,
    key_ref,
    value_ref,
    queries_ref,
    keys_ref,
    values_ref,
    normed,
    gated,
):
    gain = gain_ref[...]
    count = rows_ref.shape[0]
    lead = edge_ref.shape[0]
    taps = conv_ref.shape[0]
    normed[:lead] = unit_rows(edge_ref[...].astype(jnp.float32), gain)

    @pl.loop(0, count // step)
    def _(block):
        at = pl.multiple_of(block * step, step)
        rows = rows_ref[pl.ds(at, step), :].astype(jnp.float32)
        normed[pl.ds(lead + at, step), :] = unit_rows(rows, gain)

    @pl.loop(0, count // step)
    def _(block):
        at = pl.multiple_of(block * step, step)
        window = normed[pl.ds(at, step + lead), :]
        here = window[lead:]
        total = conv_ref[0:1] * here
        for tap in range(1, taps):
            total = total + conv_ref[tap : tap + 1] * window[lead - tap : lead - tap + step]
        gated[pl.ds(at, step), :] = (total * jax.nn.sigmoid(here)).astype(jnp.bfloat16)

    rows = gated[...]
    for weight_ref, out_ref, factor in (
        (query_ref, queries_ref, scale),
        (key_ref, keys_ref, scale),
        (value_ref, values_ref, None),
    ):
        product = jnp.dot(rows, weight_ref[...], preferred_element_type=jnp.float32)
        if factor is not None:
            product = product * factor
        out_ref[...] = product.astype(jnp.bfloat16)


def project(rows, edge, mix_gain, conv_weight, query_weight, key_weight, value_weight, scale):
    count, width = rows.shape
    step = 32
    return kernel_call(
        functools.partial(project_body, step, scale),
        "project",
        tuple(like(count, w.shape[1], jnp.bfloat16) for w in (query_weight, key_weight, value_weight)),
        rows,
        edge,
        mix_gain[None],
        conv_weight,
        query_weight,
        key_weight,
        value_weight,
        scratch=(
            pltpu.VMEM((count + edge.shape[0], width), jnp.float32),
            pltpu.VMEM((count, width), jnp.bfloat16),
        ),
    )


def attend_body(
    feat_in,
    value_len,
    count_ref,
    rate_ref,
    queries_ref,
    keys_ref,
    values_ref,
    numer_ref,
    denom_ref,
    state_ref,
    norm_ref,
    turned,
    total,
    norms,
):
    heads, count = rate_ref.shape
    columns = values_ref.shape[1]
    lane = lax.broadcasted_iota(jnp.int32, (count, count), 1)
    row = lax.broadcasted_iota(jnp.int32, (count, count), 0)
    valid = (lane[:1] < count_ref[0]).astype(jnp.float32)
    rate = jnp.where(valid > 0, rate_ref[...], 0.0)
    upto = (row <= lane).astype(jnp.float32)
    across = jnp.dot(
        rate, upto, precision=lax.Precision.HIGHEST, preferred_element_type=jnp.float32
    )
    down = across.T
    closing = across[:, count - 1 : count]
    fading = jnp.exp(closing - across) * valid
    causal = row >= lane
    keys = keys_ref[...]
    turned[...] = keys.astype(jnp.float32).T
    owner = lax.broadcasted_iota(jnp.int32, queries_ref.shape, 1)
    spare = lax.broadcasted_iota(jnp.int32, (8, count), 0) == 0
    head_lane = lax.broadcasted_iota(jnp.int32, (count, 128), 1)
    numer_ref[...] = jnp.zeros(numer_ref.shape, jnp.float32)
    total[...] = jnp.zeros(total.shape, jnp.float32)
    norms[...] = jnp.zeros(norms.shape, jnp.float32)
    norm_total = jnp.zeros((total.shape[0], 128), jnp.float32)
    denominators = jnp.zeros((count, 128), jnp.float32)
    for h in range(heads):
        low = min(h * value_len // 128 * 128, max(columns - 256, 0))
        high = min(low + 256, columns)
        mine = lax.broadcasted_iota(jnp.int32, (count, high - low), 1) + low
        mine = (mine >= h * value_len) & (mine < (h + 1) * value_len)
        values = jnp.where(mine, values_ref[:, low:high].astype(jnp.float32), 0.0)
        values = values.astype(jnp.bfloat16)
        asks = (owner >= h * feat_in) & (owner < (h + 1) * feat_in)
        queries = jnp.where(asks, queries_ref[...].astype(jnp.float32), 0.0)
        scores = lax.dot_general(
            queries.astype(jnp.bfloat16), keys, NT, preferred_element_type=jnp.float32
        )
        gap = down[:, h : h + 1] - across[h : h + 1]
        weights = jnp.where(causal, jnp.exp(jnp.minimum(gap, 0.0)) * valid, 0.0)
        weights = weights * (1.0 + scores + 0.5 * scores * scores)
        numer_ref[:, low:high] += jnp.dot(
            weights.astype(jnp.bfloat16), values, preferred_element_type=jnp.float32
        )
        sums = jnp.sum(weights, axis=1, keepdims=True)
        denominators = jnp.where(head_lane == h, sums, denominators)
        own = turned[h * feat_in : (h + 1) * feat_in]
        fade = fading[h : h + 1]
        faded = own * fade
        scaled = faded * 0.5**0.5
        parts = [own[i : i + 1] * scaled for i in range(feat_in)]
        parts += [faded, jnp.where(spare, fade, 0.0)]
        feats = jnp.concatenate(parts, axis=0).astype(jnp.bfloat16)
        total[:, low:high] += jnp.dot(feats, values, preferred_element_type=jnp.float32)
        mark = (head_lane == h).astype(jnp.bfloat16)
        norm_total = norm_total + jnp.dot(feats, mark, preferred_element_type=jnp.float32)
    denom_ref[...] = denominators[:, :heads]
    pairs = feat_in * feat_in
    state_ref[0] = total[pairs + feat_in : pairs + feat_in + 1, :]
    for f in range(feat_in):
        state_ref[1 + f] = total[pairs + f : pairs + f + 1, :]

    @pl.loop(0, pairs // 8)
    def _(block):
        for k in range(8):
            f = block * 8 + k
            state_ref[1 + feat_in + f] = total[pl.ds(f, 1), :]

    norms[0:1, :] = norm_total[pairs + feat_in : pairs + feat_in + 1]
    norms[1 : 1 + feat_in, :] = norm_total[pairs : pairs + feat_in]
    norms[1 + feat_in : 1 + feat_in + pairs, :] = norm_total[:pairs]
    norm_ref[...] = norms[...].T[:heads, : 1 + feat_in + pairs]


def attend(valid_count, rate, queries, keys, values, feat_in, value_len):
    heads, count = rate.shape
    columns = values.shape[1]
    feat_len = 1 + feat_in + feat_in * feat_in
    padded = feat_in * feat_in + feat_in + 8
    return kernel_call(
        functools.partial(attend_body, feat_in, value_len),
        "attend",
        (
            like(count, columns, jnp.float32),
            like(count, heads, jnp.float32),
            jax.ShapeDtypeStruct((feat_len, 1, columns), jnp.float32),
            like(heads, feat_len, jnp.float32),
        ),
        valid_count,
        rate,
        queries,
        keys,
        values,
        specs=[pl.BlockSpec(memory_space=pltpu.SMEM)] + vmem(4),
        scratch=(
            pltpu.VMEM((queries.shape[1], count), jnp.float32),
            pltpu.VMEM((padded, columns), jnp.float32),
            pltpu.VMEM(((feat_len + 127) // 128 * 128, 128), jnp.float32),
        ),
    )


def mix_body(
    value_len, step, numer_ref, denom_ref, rows_ref, out_ref, gain_ref, mixed_ref, mlp_ref, sums
):
    count, columns = numer_ref.shape
    heads = denom_ref.shape[1]
    column = lax.broadcasted_iota(jnp.int32, (1, columns), 1)
    inverse = 1.0 / denom_ref[...]
    spread = jnp.zeros((count, columns), jnp.float32)
    for h in range(heads):
        here = (column >= h * value_len) & (column < (h + 1) * value_len)
        spread = jnp.where(here, inverse[:, h : h + 1], spread)
    attended = (numer_ref[...] * spread).astype(jnp.bfloat16)
    sums[...] = jnp.dot(attended, out_ref[...], preferred_element_type=jnp.float32)
    gain = gain_ref[...]

    @pl.loop(0, count // step)
    def _(block):
        at = pl.ds(pl.multiple_of(block * step, step), step)
        mixed = (rows_ref[at, :].astype(jnp.float32) + sums[at, :]).astype(jnp.bfloat16)
        mixed_ref[at, :] = mixed
        mlp_ref[at, :] = unit_rows(mixed.astype(jnp.float32), gain).astype(jnp.bfloat16)


def mix(numer, denom, rows, out_weight, mlp_gain, value_len):
    count, width = rows.shape
    shape = like(count, width, jnp.bfloat16)
    return kernel_call(
        functools.partial(mix_body, value_len, 32),
        "mix",
        (shape, shape),
        numer,
        denom,
        rows,
        out_weight,
        mlp_gain[None],
        scratch=(pltpu.VMEM((count, width), jnp.float32),),
    )


def swiglu_terms(rows, gate_rows, up_rows, down_rows):
    gate_act = lax.dot_general(rows, gate_rows, NT, preferred_element_type=jnp.float32)
    up_act = lax.dot_general(rows, up_rows, NT, preferred_element_type=jnp.float32)
    hidden_units = (gate_act * jax.nn.sigmoid(gate_act) * up_act).astype(jnp.bfloat16)
    return jnp.dot(hidden_units, down_rows, preferred_element_type=jnp.float32)


def on_grid(run):
    return all(low % 16 == 0 and high % 16 == 0 for _, low, high in run)


def read_units(refs, units):
    parts = []
    for k in range(3):
        rows = [refs[run[k][0]][run[k][1] : run[k][2]] for run in units if on_grid(run)]
        rest = [
            refs[run[k][0]][...].astype(jnp.float32)[run[k][1] : run[k][2]]
            for run in units
            if not on_grid(run)
        ]
        if rest:
            rows.append(jnp.concatenate(rest, axis=0).astype(jnp.bfloat16))
        parts.append(jnp.concatenate(rows, axis=0))
    return parts


def accumulate_body(units, n_weights, n_rows, n_acc, residual, *refs):
    weights = refs[:n_weights]
    rows = refs[n_weights : n_weights + n_rows]
    acc = refs[n_weights + n_rows : n_weights + n_rows + n_acc]
    parts = read_units(weights, units)
    for k, rows_ref in enumerate(rows):
        out_ref = refs[len(refs) - n_rows + k]
        terms = swiglu_terms(rows_ref[...], *parts)
        if n_acc:
            terms = terms + acc[k][...]
        if residual:
            terms = terms + refs[n_weights + n_rows + n_acc][...].astype(jnp.float32)
        out_ref[...] = terms.astype(out_ref.dtype)


def accumulate(rows, weights, units, acc, dtype, name, residual=None):
    shapes = tuple(like(*array.shape, dtype) for array in rows)
    start = len(weights) + len(rows)
    aliases = {start + k: k for k in range(len(acc))} if dtype == jnp.float32 else {}
    extra = () if residual is None else (residual,)
    body = functools.partial(
        accumulate_body, tuple(units), len(weights), len(rows), len(acc), bool(extra)
    )
    return kernel_call(body, name, shapes, *weights, *rows, *acc, *extra, aliases=aliases)


def runs(which, low, size):
    return tuple((which, low + k * size, low + (k + 1) * size) for k in range(3))


def split_runs(first, second, main):
    (i, at), (j, then) = first, second
    held = 2 * main // 3
    rest = main - held
    return (
        ((i, at, at + held), (i, at + main, at + main + held), (j, then + rest, then + main)),
        ((i, at + held, at + main), (j, then, then + rest), (j, then + main, then + rest + main)),
    )


def collect_body(plans, *refs):
    outs = refs[len(refs) - len(plans) :]
    for out_ref, plan in zip(outs, plans):
        rows = [refs[i][...].astype(jnp.float32)[low:high] for i, low, high in plan]
        out_ref[...] = jnp.concatenate(rows, axis=0).astype(jnp.bfloat16)


def collect(arrays, plans, name):
    columns = arrays[0].shape[1]
    shapes = tuple(like(sum(h - l for _, l, h in plan), columns, jnp.bfloat16) for plan in plans)
    return kernel_call(functools.partial(collect_body, plans), name, shapes, *arrays)


def shard_body(main, gate_ref, up_ref, down_ref, shard_ref, main_ref, *rest):
    buffers, sems = rest[:3], rest[3]
    copies = [
        pltpu.make_async_copy(source, buffer, sems.at[k])
        for k, (source, buffer) in enumerate(zip((gate_ref, up_ref, down_ref), buffers))
    ]
    for copy in copies:
        copy.start()
    for copy in copies:
        copy.wait()
    arrays = [buffer[...].astype(jnp.float32) for buffer in buffers]
    tops = [array[:main] for array in arrays]
    ends = [array[main:] for array in arrays]
    shard_ref[...] = jnp.concatenate(tops + ends, axis=0).astype(jnp.bfloat16)
    main_ref[...] = jnp.concatenate(tops, axis=0).astype(jnp.bfloat16)


def final_body(step, count_ref, kept_ref, given_ref, out_ref):
    count = kept_ref.shape[0]

    @pl.loop(0, count // step)
    def _(block):
        first = pl.multiple_of(block * step, step)
        at = pl.ds(first, step)
        total = kept_ref[at, :] + given_ref[at, :].astype(jnp.float32)
        row = lax.broadcasted_iota(jnp.int32, total.shape, 0) + first
        out_ref[at, :] = jnp.where(row < count_ref[0], total, 0.0).astype(out_ref.dtype)


def local(
    hidden_in,
    lengths,
    log_decay,
    mix_gain,
    conv_weight,
    query_weight,
    key_weight,
    value_weight,
    out_weight,
    mlp_gain,
    gate_weight,
    up_weight,
    down_weight,
):
    local_len = hidden_in.shape[1]
    rows_in = hidden_in[0]
    decays = log_decay[0]
    head_count = log_decay.shape[2]
    value_len = value_weight.shape[1] // head_count
    feat_in = query_weight.shape[1] // head_count
    feature_scale = feat_in ** (-0.25)
    valid_count = lengths - lax.axis_index("seq") * local_len
    spans = lax.axis_size("seq")
    units, model = gate_weight.shape[1], gate_weight.shape[0]
    edge = units // 7
    main = units - edge
    wide = 3 * main
    full = 3 * units
    narrow = full - wide
    cut = main + 2 * main // 3

    shard, shard_main = kernel_call(
        functools.partial(shard_body, main),
        "shard",
        (like(full, model, jnp.bfloat16), like(wide, model, jnp.bfloat16)),
        gate_weight.T,
        up_weight.T,
        down_weight.T,
        specs=[pl.BlockSpec(memory_space=pl.ANY)] * 3,
        scratch=[pltpu.VMEM((units, model), jnp.bfloat16)] * 3 + [pltpu.SemaphoreType.DMA((3,))],
        mib=56,
    )
    near, far, deep = slot((flip_near, shard), (flip_far, shard), (next_plane, shard_main))

    lead = 16
    if spans > 1:
        edge_in = from_behind(rows_in[local_len - lead :], "seq", 1)
    else:
        edge_in = jnp.zeros((lead, model), jnp.bfloat16)
    queries, key_rows, values = project(
        rows_in, edge_in, mix_gain, conv_weight, query_weight, key_weight, value_weight, feature_scale
    )
    near, far, deep, queries, key_rows, values = together(
        near, far, deep, queries, key_rows, values
    )

    sends = collect(
        (shard, near, far, deep),
        (
            ((3, 0, wide), (2, 0, cut)),
            ((3, 0, wide), (1, cut, full)),
            ((3, 0, wide), (0, wide, full), (1, wide, full), (2, wide, full)),
        ),
        "collect_second",
    )
    near1, far1, deep1 = slot(*zip((flip_near, flip_far, next_plane), sends))

    numerator, denominator, end_state, end_norm = attend(
        valid_count, log_decay[0].T, queries, key_rows, values, feat_in, value_len
    )
    if spans > 1:
        positions = jnp.arange(local_len, dtype=jnp.int32)
        numerator, denominator, end_state, end_norm = carry_in(
            (positions < valid_count).astype(jnp.float32),
            decays,
            queries,
            numerator,
            denominator,
            end_state[:, 0],
            end_norm.T,
        )
    else:
        end_norm = end_norm.T
    mixed_rows, mlp_in = mix(numerator, denominator, rows_in, out_weight, mlp_gain, value_len)
    near1, far1, deep1, mixed_rows, mlp_in, end_state, end_norm = together(
        near1, far1, deep1, mixed_rows, mlp_in, end_state, end_norm
    )

    middle = local_len // 2
    *sends, top, end = collect(
        (near1, far1, deep1, mlp_in),
        (
            ((2, 0, wide), (1, 0, cut)),
            ((2, 0, wide), (0, cut, wide)),
            ((2, 0, wide + 3 * narrow), (1, wide + wide - cut, wide + full - cut)),
            ((3, 0, middle),),
            ((3, middle, local_len),),
        ),
        "collect_third",
    )
    near2, far2, deep2 = slot(*zip((flip_near, flip_far, next_plane), sends))
    (other_in,) = collect(
        (flip_core(top), flip_core(end)),
        (((0, 0, middle), (1, 0, local_len - middle)),),
        "collect_rows",
    )
    rows = (mlp_in, other_in)
    acc = accumulate(
        rows,
        (shard, near, far, deep, near1, far1, deep1),
        [runs(i, 0, main) for i in range(7)] + list(split_runs((4, wide), (5, wide), main)),
        (),
        jnp.float32,
        "accumulate_second",
    )
    near2, far2, deep2, *acc = together(near2, far2, deep2, *acc)

    two = 2 * main
    sends = collect(
        (near2, far2, deep2),
        (
            ((2, main, wide),),
            ((2, 0, main), (2, two, wide)),
            ((2, wide, wide + 4 * narrow), (1, 2 * wide - cut - main, 2 * wide - cut)),
            ((2, 0, main), (1, 0, main)),
            ((2, main, two), (0, main, two)),
        ),
        "collect_fourth",
    )
    sends = together(*sends)
    near3, far3, deep3 = flip_near(sends[0]), flip_far(sends[1]), next_plane(sends[2])
    near3_more, far3_more = flip_near(sends[3]), flip_far(sends[4])
    acc = accumulate(
        rows,
        (shard, near, far, far1, deep1, near2, far2, deep2),
        [runs(i, 0, main) for i in (5, 6, 7)]
        + list(split_runs((5, wide), (6, wide), main))
        + [runs(i, wide, edge) for i in (0, 1, 2)]
        + [runs(3, wide + wide - cut, edge)]
        + [runs(4, wide + k * narrow, edge) for k in range(3)]
        + [runs(7, wide + k * narrow, edge) for k in range(4)],
        tuple(acc),
        jnp.float32,
        "accumulate_third",
    )
    near3, far3, deep3, *acc = together(near3, far3, deep3, *acc)

    sends = collect(
        (near3, far3, deep3),
        (
            ((1, 0, main),),
            ((0, 0, main),),
            ((2, 3 * narrow, 4 * narrow + main),),
        ),
        "collect_fifth",
    )
    near4, far4, deep4 = slot(*zip((flip_near, flip_far, next_plane), sends))
    line = 4 * narrow
    weights = (near3, near3_more, far3, far3_more, deep3, near4, far4, deep4)
    last = [
        ((1, 0, main), (0, 0, main), (0, main, two)),
        ((2, 0, main), (3, 0, main), (2, main, two)),
        ((1, main, two), (3, main, two), (4, line, line + main)),
        ((5, 0, main), (6, 0, main), (7, narrow, narrow + main)),
    ]
    last += [runs(4, k * narrow, edge) for k in range(4)] + [runs(7, 0, edge)]
    (given,) = accumulate(rows[1:], weights, last, acc[1:], jnp.bfloat16, "finish_other")
    (kept,) = accumulate(
        rows[:1], weights, last, acc[:1], jnp.float32, "finish_own", residual=mixed_rows
    )
    result = kernel_call(
        functools.partial(final_body, 64),
        "final",
        like(local_len, model, jnp.bfloat16),
        valid_count,
        kept,
        flip_core(given),
        specs=[pl.BlockSpec(memory_space=pltpu.SMEM)] + vmem(2),
    )
    return (
        result[None],
        end_state.reshape((1, 1) + end_state.shape[:1] + end_state.shape[-1:]),
        end_norm[None, None],
    )


def solution(mesh):
    return jax.shard_map(
        local,
        mesh=mesh,
        in_specs=(
            P("req", "seq", None),
            P("req"),
            P("req", "seq", None),
            P(),
            P(),
            P(),
            P(),
            P(),
            P(),
            P(),
            P(None, "req"),
            P(None, "req"),
            P(None, "req"),
        ),
        out_specs=(P("req", "seq", None), P("req", "seq", None, None), P("req", "seq", None, None)),
        check_vma=False,
    )
```

```python
import functools

import jax
import jax.numpy as jnp
from jax import lax
from jax.experimental import pallas as pl
from jax.experimental.pallas import tpu as pltpu
from jax.sharding import PartitionSpec as P


def from_behind(array, axis, by):
    count = lax.axis_size(axis)
    pairs = [(i, i + by) for i in range(count) if 0 <= i + by < count]
    return lax.ppermute(array, axis, pairs)


def entering(array, axis, combine, identity):
    count, here = (lax.axis_size(axis), lax.axis_index(axis))
    everything = jax.tree.map(
        lambda part, kind: lax.all_gather(part.astype(kind), axis),
        array,
        (jnp.bfloat16, jnp.bfloat16, jnp.bfloat16),
    )
    start = jax.tree.map(
        lambda part, zero: jnp.broadcast_to(jnp.asarray(zero, part.dtype), part.shape),
        array,
        identity,
    )

    def hop(k, before):
        reached = k < here
        new = combine(
            before, jax.tree.map(lambda part, own: part[k].astype(own.dtype), everything, array)
        )
        return jax.tree.map(lambda a, b: jnp.where(reached, a, b), new, before)

    return lax.fori_loop(0, count, hop, start)


def features(vectors):
    constant = jnp.ones(vectors.shape[:-1] + (1,), jnp.float32)
    width = vectors.shape[-1]
    squares = (vectors[..., :, None] * vectors[..., None, :]).reshape(
        vectors.shape[:-1] + (width * width,)
    )
    return jnp.concatenate([constant, vectors, squares * 0.5**0.5], axis=-1)


def carry_in(valid_mask, decays, queries, numerator, denominator, flat_memory, key_sum):
    local_len = numerator.shape[0]
    feat_len, head_count = key_sum.shape
    value_len = flat_memory.shape[1] // head_count
    feat_in = queries.shape[1] // head_count
    decay_rate = jnp.where(valid_mask[:, None] > 0, decays, 0.0)
    span_decay = jnp.sum(decay_rate, axis=0)

    def merge_states(earlier, later):
        factor = jnp.exp(later[0])
        return (
            earlier[0] + later[0],
            earlier[1] * jnp.repeat(factor, value_len)[None, :] + later[1],
            earlier[2] * factor[None, :] + later[2],
        )

    neutral = (jnp.zeros_like(span_decay), jnp.zeros_like(flat_memory), jnp.zeros_like(key_sum))
    carried = entering((span_decay, flat_memory, key_sum), "seq", merge_states, neutral)
    prior_memory = carried[1]
    prior_keys = carried[2]
    highest = lax.Precision.HIGHEST
    growth = jnp.exp(jnp.cumsum(decay_rate, axis=0))
    query_feat = features(queries.astype(jnp.float32).reshape(local_len, head_count, feat_in))
    added = jnp.einsum(
        "thf,fhv->thv",
        query_feat,
        prior_memory.reshape(feat_len, head_count, value_len),
        precision=highest,
    )
    numerator = numerator + (added * growth[:, :, None]).reshape(local_len, -1)
    denominator = (
        denominator + jnp.einsum("thf,fh->th", query_feat, prior_keys, precision=highest) * growth
    )
    span_factor = jnp.exp(span_decay)
    end_state = prior_memory * jnp.repeat(span_factor, value_len)[None, :] + flat_memory
    end_norm = prior_keys * span_factor[None, :] + key_sum
    return numerator, denominator, end_state, end_norm


def permute(array, target):
    count = lax.axis_size("req")
    return lax.ppermute(array, "req", [(i, target(i)) for i in range(count)])


def flip_core(array):
    return permute(array, lambda i: i ^ 1)


def flip_near(array):
    return permute(array, lambda i: i ^ 2)


def flip_far(array):
    return permute(array, lambda i: i ^ 4)


def next_plane(array):
    return permute(array, lambda i: i ^ (8 if i // 8 in (1, 2) else 16))


def together(*arrays):
    return lax.optimization_barrier(arrays)


def slot(*sends):
    operands = together(*[array for _, array in sends])
    return together(*[send(array) for (send, _), array in zip(sends, operands)])


def vmem(count):
    return [pl.BlockSpec(memory_space=pltpu.VMEM)] * count


def kernel_call(body, name, out_shape, *operands, scratch=(), aliases=None, specs=None, mib=24):
    many = isinstance(out_shape, tuple)
    return pl.pallas_call(
        body,
        out_shape=out_shape,
        in_specs=specs or vmem(len(operands)),
        out_specs=tuple(vmem(len(out_shape))) if many else vmem(1)[0],
        scratch_shapes=list(scratch),
        input_output_aliases=aliases or {},
        compiler_params=pltpu.CompilerParams(vmem_limit_bytes=mib * 1024 * 1024),
        cost_estimate=pl.CostEstimate(flops=1000, bytes_accessed=1000, transcendentals=0),
        name=name,
    )(*operands)


def like(rows, columns, dtype):
    return jax.ShapeDtypeStruct((rows, columns), dtype)


NT = (((1,), (1,)), ((), ()))


def unit_rows(rows, gain):
    factor = lax.rsqrt(jnp.mean(rows * rows, axis=-1, keepdims=True) + 1e-05)
    return (rows * factor * gain).astype(jnp.bfloat16).astype(jnp.float32)


def project_body(
    step,
    scale,
    rows_ref,
    edge_ref,
    gain_ref,
    conv_ref,
    query_ref,
    key_ref,
    value_ref,
    queries_ref,
    keys_ref,
    values_ref,
    normed,
    gated,
):
    gain = gain_ref[...]
    count = rows_ref.shape[0]
    lead = edge_ref.shape[0]
    taps = conv_ref.shape[0]
    normed[:lead] = unit_rows(edge_ref[...].astype(jnp.float32), gain)

    @pl.loop(0, count // step)
    def _(block):
        at = pl.multiple_of(block * step, step)
        rows = rows_ref[pl.ds(at, step), :].astype(jnp.float32)
        normed[pl.ds(lead + at, step), :] = unit_rows(rows, gain)

    @pl.loop(0, count // step)
    def _(block):
        at = pl.multiple_of(block * step, step)
        window = normed[pl.ds(at, step + lead), :]
        here = window[lead:]
        total = conv_ref[0:1] * here
        for tap in range(1, taps):
            total = total + conv_ref[tap : tap + 1] * window[lead - tap : lead - tap + step]
        gated[pl.ds(at, step), :] = (total * jax.nn.sigmoid(here)).astype(jnp.bfloat16)

    rows = gated[...]
    for weight_ref, out_ref, factor in (
        (query_ref, queries_ref, scale),
        (key_ref, keys_ref, scale),
        (value_ref, values_ref, None),
    ):
        product = jnp.dot(rows, weight_ref[...], preferred_element_type=jnp.float32)
        if factor is not None:
            product = product * factor
        out_ref[...] = product.astype(jnp.bfloat16)


def project(rows, edge, mix_gain, conv_weight, query_weight, key_weight, value_weight, scale):
    count, width = rows.shape
    step = 32
    return kernel_call(
        functools.partial(project_body, step, scale),
        "project",
        tuple(like(count, w.shape[1], jnp.bfloat16) for w in (query_weight, key_weight, value_weight)),
        rows,
        edge,
        mix_gain[None],
        conv_weight,
        query_weight,
        key_weight,
        value_weight,
        scratch=(
            pltpu.VMEM((count + edge.shape[0], width), jnp.float32),
            pltpu.VMEM((count, width), jnp.bfloat16),
        ),
    )


def attend_body(
    feat_in,
    value_len,
    count_ref,
    rate_ref,
    queries_ref,
    keys_ref,
    values_ref,
    numer_ref,
    denom_ref,
    state_ref,
    norm_ref,
    turned,
    total,
    norms,
):
    heads, count = rate_ref.shape
    columns = values_ref.shape[1]
    lane = lax.broadcasted_iota(jnp.int32, (count, count), 1)
    row = lax.broadcasted_iota(jnp.int32, (count, count), 0)
    valid = (lane[:1] < count_ref[0]).astype(jnp.float32)
    rate = jnp.where(valid > 0, rate_ref[...], 0.0)
    upto = (row <= lane).astype(jnp.float32)
    across = jnp.dot(
        rate, upto, precision=lax.Precision.HIGHEST, preferred_element_type=jnp.float32
    )
    down = across.T
    closing = across[:, count - 1 : count]
    fading = jnp.exp(closing - across) * valid
    causal = row >= lane
    keys = keys_ref[...]
    turned[...] = keys.astype(jnp.float32).T
    owner = lax.broadcasted_iota(jnp.int32, queries_ref.shape, 1)
    spare = lax.broadcasted_iota(jnp.int32, (8, count), 0) == 0
    head_lane = lax.broadcasted_iota(jnp.int32, (count, 128), 1)
    numer_ref[...] = jnp.zeros(numer_ref.shape, jnp.float32)
    total[...] = jnp.zeros(total.shape, jnp.float32)
    norms[...] = jnp.zeros(norms.shape, jnp.float32)
    norm_total = jnp.zeros((total.shape[0], 128), jnp.float32)
    denominators = jnp.zeros((count, 128), jnp.float32)
    for h in range(heads):
        low = min(h * value_len // 128 * 128, max(columns - 256, 0))
        high = min(low + 256, columns)
        mine = lax.broadcasted_iota(jnp.int32, (count, high - low), 1) + low
        mine = (mine >= h * value_len) & (mine < (h + 1) * value_len)
        values = jnp.where(mine, values_ref[:, low:high].astype(jnp.float32), 0.0)
        values = values.astype(jnp.bfloat16)
        asks = (owner >= h * feat_in) & (owner < (h + 1) * feat_in)
        queries = jnp.where(asks, queries_ref[...].astype(jnp.float32), 0.0)
        scores = lax.dot_general(
            queries.astype(jnp.bfloat16), keys, NT, preferred_element_type=jnp.float32
        )
        gap = down[:, h : h + 1] - across[h : h + 1]
        weights = jnp.where(causal, jnp.exp(jnp.minimum(gap, 0.0)) * valid, 0.0)
        weights = weights * (1.0 + scores + 0.5 * scores * scores)
        numer_ref[:, low:high] += jnp.dot(
            weights.astype(jnp.bfloat16), values, preferred_element_type=jnp.float32
        )
        sums = jnp.sum(weights, axis=1, keepdims=True)
        denominators = jnp.where(head_lane == h, sums, denominators)
        own = turned[h * feat_in : (h + 1) * feat_in]
        fade = fading[h : h + 1]
        faded = own * fade
        scaled = faded * 0.5**0.5
        parts = [own[i : i + 1] * scaled for i in range(feat_in)]
        parts += [faded, jnp.where(spare, fade, 0.0)]
        feats = jnp.concatenate(parts, axis=0).astype(jnp.bfloat16)
        total[:, low:high] += jnp.dot(feats, values, preferred_element_type=jnp.float32)
        mark = (head_lane == h).astype(jnp.bfloat16)
        norm_total = norm_total + jnp.dot(feats, mark, preferred_element_type=jnp.float32)
    denom_ref[...] = denominators[:, :heads]
    pairs = feat_in * feat_in
    state_ref[0] = total[pairs + feat_in : pairs + feat_in + 1, :]
    for f in range(feat_in):
        state_ref[1 + f] = total[pairs + f : pairs + f + 1, :]

    @pl.loop(0, pairs // 8)
    def _(block):
        for k in range(8):
            f = block * 8 + k
            state_ref[1 + feat_in + f] = total[pl.ds(f, 1), :]

    norms[0:1, :] = norm_total[pairs + feat_in : pairs + feat_in + 1]
    norms[1 : 1 + feat_in, :] = norm_total[pairs : pairs + feat_in]
    norms[1 + feat_in : 1 + feat_in + pairs, :] = norm_total[:pairs]
    norm_ref[...] = norms[...].T[:heads, : 1 + feat_in + pairs]


def attend(valid_count, rate, queries, keys, values, feat_in, value_len):
    heads, count = rate.shape
    columns = values.shape[1]
    feat_len = 1 + feat_in + feat_in * feat_in
    padded = feat_in * feat_in + feat_in + 8
    return kernel_call(
        functools.partial(attend_body, feat_in, value_len),
        "attend",
        (
            like(count, columns, jnp.float32),
            like(count, heads, jnp.float32),
            jax.ShapeDtypeStruct((feat_len, 1, columns), jnp.float32),
            like(heads, feat_len, jnp.float32),
        ),
        valid_count,
        rate,
        queries,
        keys,
        values,
        specs=[pl.BlockSpec(memory_space=pltpu.SMEM)] + vmem(4),
        scratch=(
            pltpu.VMEM((queries.shape[1], count), jnp.float32),
            pltpu.VMEM((padded, columns), jnp.float32),
            pltpu.VMEM(((feat_len + 127) // 128 * 128, 128), jnp.float32),
        ),
    )


def mix_body(
    value_len, step, numer_ref, denom_ref, rows_ref, out_ref, gain_ref, mixed_ref, mlp_ref, sums
):
    count, columns = numer_ref.shape
    heads = denom_ref.shape[1]
    column = lax.broadcasted_iota(jnp.int32, (1, columns), 1)
    inverse = 1.0 / denom_ref[...]
    spread = jnp.zeros((count, columns), jnp.float32)
    for h in range(heads):
        here = (column >= h * value_len) & (column < (h + 1) * value_len)
        spread = jnp.where(here, inverse[:, h : h + 1], spread)
    attended = (numer_ref[...] * spread).astype(jnp.bfloat16)
    sums[...] = jnp.dot(attended, out_ref[...], preferred_element_type=jnp.float32)
    gain = gain_ref[...]

    @pl.loop(0, count // step)
    def _(block):
        at = pl.ds(pl.multiple_of(block * step, step), step)
        mixed = (rows_ref[at, :].astype(jnp.float32) + sums[at, :]).astype(jnp.bfloat16)
        mixed_ref[at, :] = mixed
        mlp_ref[at, :] = unit_rows(mixed.astype(jnp.float32), gain).astype(jnp.bfloat16)


def mix(numer, denom, rows, out_weight, mlp_gain, value_len):
    count, width = rows.shape
    shape = like(count, width, jnp.bfloat16)
    return kernel_call(
        functools.partial(mix_body, value_len, 32),
        "mix",
        (shape, shape),
        numer,
        denom,
        rows,
        out_weight,
        mlp_gain[None],
        scratch=(pltpu.VMEM((count, width), jnp.float32),),
    )


def swiglu_terms(rows, gate_rows, up_rows, down_rows):
    gate_act = lax.dot_general(rows, gate_rows, NT, preferred_element_type=jnp.float32)
    up_act = lax.dot_general(rows, up_rows, NT, preferred_element_type=jnp.float32)
    hidden_units = (gate_act * jax.nn.sigmoid(gate_act) * up_act).astype(jnp.bfloat16)
    return jnp.dot(hidden_units, down_rows, preferred_element_type=jnp.float32)


def on_grid(run):
    return all(low % 16 == 0 and high % 16 == 0 for _, low, high in run)


def read_units(refs, units):
    parts = []
    for k in range(3):
        rows = [refs[run[k][0]][run[k][1] : run[k][2]] for run in units if on_grid(run)]
        rest = [
            refs[run[k][0]][...].astype(jnp.float32)[run[k][1] : run[k][2]]
            for run in units
            if not on_grid(run)
        ]
        if rest:
            rows.append(jnp.concatenate(rest, axis=0).astype(jnp.bfloat16))
        parts.append(jnp.concatenate(rows, axis=0))
    return parts


def accumulate_body(units, n_weights, n_rows, n_acc, residual, *refs):
    weights = refs[:n_weights]
    rows = refs[n_weights : n_weights + n_rows]
    acc = refs[n_weights + n_rows : n_weights + n_rows + n_acc]
    parts = read_units(weights, units)
    for k, rows_ref in enumerate(rows):
        out_ref = refs[len(refs) - n_rows + k]
        terms = swiglu_terms(rows_ref[...], *parts)
        if n_acc:
            terms = terms + acc[k][...]
        if residual:
            terms = terms + refs[n_weights + n_rows + n_acc][...].astype(jnp.float32)
        out_ref[...] = terms.astype(out_ref.dtype)


def accumulate(rows, weights, units, acc, dtype, name, residual=None):
    shapes = tuple(like(*array.shape, dtype) for array in rows)
    start = len(weights) + len(rows)
    aliases = {start + k: k for k in range(len(acc))} if dtype == jnp.float32 else {}
    extra = () if residual is None else (residual,)
    body = functools.partial(
        accumulate_body, tuple(units), len(weights), len(rows), len(acc), bool(extra)
    )
    return kernel_call(body, name, shapes, *weights, *rows, *acc, *extra, aliases=aliases)


def runs(which, low, size):
    return tuple((which, low + k * size, low + (k + 1) * size) for k in range(3))


def split_runs(first, second, main):
    (i, at), (j, then) = first, second
    held = 2 * main // 3
    rest = main - held
    return (
        ((i, at, at + held), (i, at + main, at + main + held), (j, then + rest, then + main)),
        ((i, at + held, at + main), (j, then, then + rest), (j, then + main, then + rest + main)),
    )


def collect_body(plans, *refs):
    outs = refs[len(refs) - len(plans) :]
    for out_ref, plan in zip(outs, plans):
        rows = [refs[i][...].astype(jnp.float32)[low:high] for i, low, high in plan]
        out_ref[...] = jnp.concatenate(rows, axis=0).astype(jnp.bfloat16)


def collect(arrays, plans, name):
    columns = arrays[0].shape[1]
    shapes = tuple(like(sum(h - l for _, l, h in plan), columns, jnp.bfloat16) for plan in plans)
    return kernel_call(functools.partial(collect_body, plans), name, shapes, *arrays)


def shard_body(main, gate_ref, up_ref, down_ref, shard_ref, main_ref, *rest):
    buffers, sems = rest[:3], rest[3]
    copies = [
        pltpu.make_async_copy(source, buffer, sems.at[k])
        for k, (source, buffer) in enumerate(zip((gate_ref, up_ref, down_ref), buffers))
    ]
    for copy in copies:
        copy.start()
    for copy in copies:
        copy.wait()
    arrays = [buffer[...].astype(jnp.float32) for buffer in buffers]
    tops = [array[:main] for array in arrays]
    ends = [array[main:] for array in arrays]
    shard_ref[...] = jnp.concatenate(tops + ends, axis=0).astype(jnp.bfloat16)
    main_ref[...] = jnp.concatenate(tops, axis=0).astype(jnp.bfloat16)


def final_body(step, count_ref, kept_ref, given_ref, out_ref):
    count = kept_ref.shape[0]

    @pl.loop(0, count // step)
    def _(block):
        first = pl.multiple_of(block * step, step)
        at = pl.ds(first, step)
        total = kept_ref[at, :] + given_ref[at, :].astype(jnp.float32)
        row = lax.broadcasted_iota(jnp.int32, total.shape, 0) + first
        out_ref[at, :] = jnp.where(row < count_ref[0], total, 0.0).astype(out_ref.dtype)


def local(
    hidden_in,
    lengths,
    log_decay,
    mix_gain,
    conv_weight,
    query_weight,
    key_weight,
    value_weight,
    out_weight,
    mlp_gain,
    gate_weight,
    up_weight,
    down_weight,
):
    local_len = hidden_in.shape[1]
    rows_in = hidden_in[0]
    decays = log_decay[0]
    head_count = log_decay.shape[2]
    value_len = value_weight.shape[1] // head_count
    feat_in = query_weight.shape[1] // head_count
    feature_scale = feat_in ** (-0.25)
    valid_count = lengths - lax.axis_index("seq") * local_len
    spans = lax.axis_size("seq")
    units, model = gate_weight.shape[1], gate_weight.shape[0]
    edge = units // 7
    main = units - edge
    wide = 3 * main
    full = 3 * units
    narrow = full - wide
    cut = main + 2 * main // 3

    shard, shard_main = kernel_call(
        functools.partial(shard_body, main),
        "shard",
        (like(full, model, jnp.bfloat16), like(wide, model, jnp.bfloat16)),
        gate_weight.T,
        up_weight.T,
        down_weight.T,
        specs=[pl.BlockSpec(memory_space=pl.ANY)] * 3,
        scratch=[pltpu.VMEM((units, model), jnp.bfloat16)] * 3 + [pltpu.SemaphoreType.DMA((3,))],
        mib=56,
    )
    near, far, deep = slot((flip_near, shard), (flip_far, shard), (next_plane, shard_main))

    lead = 16
    if spans > 1:
        edge_in = from_behind(rows_in[local_len - lead :], "seq", 1)
    else:
        edge_in = jnp.zeros((lead, model), jnp.bfloat16)
    queries, key_rows, values = project(
        rows_in, edge_in, mix_gain, conv_weight, query_weight, key_weight, value_weight, feature_scale
    )
    near, far, deep, queries, key_rows, values = together(
        near, far, deep, queries, key_rows, values
    )

    sends = collect(
        (shard, near, far, deep),
        (
            ((3, 0, wide), (2, 0, cut)),
            ((3, 0, wide), (1, cut, full)),
            ((3, 0, wide), (0, wide, full), (1, wide, full), (2, wide, full)),
        ),
        "collect_second",
    )
    near1, far1, deep1 = slot(*zip((flip_near, flip_far, next_plane), sends))

    numerator, denominator, end_state, end_norm = attend(
        valid_count, log_decay[0].T, queries, key_rows, values, feat_in, value_len
    )
    if spans > 1:
        positions = jnp.arange(local_len, dtype=jnp.int32)
        numerator, denominator, end_state, end_norm = carry_in(
            (positions < valid_count).astype(jnp.float32),
            decays,
            queries,
            numerator,
            denominator,
            end_state[:, 0],
            end_norm.T,
        )
    else:
        end_norm = end_norm.T
    mixed_rows, mlp_in = mix(numerator, denominator, rows_in, out_weight, mlp_gain, value_len)
    near1, far1, deep1, mixed_rows, mlp_in, end_state, end_norm = together(
        near1, far1, deep1, mixed_rows, mlp_in, end_state, end_norm
    )

    middle = local_len // 2
    *sends, top, end = collect(
        (near1, far1, deep1, mlp_in),
        (
            ((2, 0, wide), (1, 0, cut)),
            ((2, 0, wide), (0, cut, wide)),
            ((2, 0, wide + 3 * narrow), (1, wide + wide - cut, wide + full - cut)),
            ((3, 0, middle),),
            ((3, middle, local_len),),
        ),
        "collect_third",
    )
    near2, far2, deep2 = slot(*zip((flip_near, flip_far, next_plane), sends))
    (other_in,) = collect(
        (flip_core(top), flip_core(end)),
        (((0, 0, middle), (1, 0, local_len - middle)),),
        "collect_rows",
    )
    rows = (mlp_in, other_in)
    acc = accumulate(
        rows,
        (shard, near, far, deep, near1, far1, deep1),
        [runs(i, 0, main) for i in range(7)] + list(split_runs((4, wide), (5, wide), main)),
        (),
        jnp.float32,
        "accumulate_second",
    )
    near2, far2, deep2, *acc = together(near2, far2, deep2, *acc)

    two = 2 * main
    sends = collect(
        (near2, far2, deep2),
        (
            ((2, main, wide),),
            ((2, 0, main), (2, two, wide)),
            ((2, wide, wide + 4 * narrow), (1, 2 * wide - cut - main, 2 * wide - cut)),
            ((2, 0, main), (1, 0, main)),
            ((2, main, two), (0, main, two)),
        ),
        "collect_fourth",
    )
    near3, far3, deep3 = slot(*zip((flip_near, flip_far, next_plane), sends))
    acc = accumulate(
        rows,
        (shard, near, far, far1, deep1, near2, far2, deep2),
        [runs(i, 0, main) for i in (5, 6, 7)]
        + list(split_runs((5, wide), (6, wide), main))
        + [runs(i, wide, edge) for i in (0, 1, 2)]
        + [runs(3, wide + wide - cut, edge)]
        + [runs(4, wide + k * narrow, edge) for k in range(3)]
        + [runs(7, wide + k * narrow, edge) for k in range(4)],
        tuple(acc),
        jnp.float32,
        "accumulate_third",
    )
    near3_more, far3_more, *acc = together(*sends[3:], *acc)
    near3_more, far3_more = flip_near(near3_more), flip_far(far3_more)

    sends = collect(
        (near3, far3, deep3),
        (
            ((1, 0, main),),
            ((0, 0, main),),
            ((2, 3 * narrow, 4 * narrow + main),),
        ),
        "collect_fifth",
    )
    near4, far4, deep4 = slot(*zip((flip_near, flip_far, next_plane), sends))
    line = 4 * narrow
    weights = (near3, near3_more, far3, far3_more, deep3, near4, far4, deep4)
    last = [
        ((1, 0, main), (0, 0, main), (0, main, two)),
        ((2, 0, main), (3, 0, main), (2, main, two)),
        ((1, main, two), (3, main, two), (4, line, line + main)),
        ((5, 0, main), (6, 0, main), (7, narrow, narrow + main)),
    ]
    last += [runs(4, k * narrow, edge) for k in range(4)] + [runs(7, 0, edge)]
    (given,) = accumulate(rows[1:], weights, last, acc[1:], jnp.bfloat16, "finish_other")
    (kept,) = accumulate(
        rows[:1], weights, last, acc[:1], jnp.float32, "finish_own", residual=mixed_rows
    )
    result = kernel_call(
        functools.partial(final_body, 64),
        "final",
        like(local_len, model, jnp.bfloat16),
        valid_count,
        kept,
        flip_core(given),
        specs=[pl.BlockSpec(memory_space=pltpu.SMEM)] + vmem(2),
    )
    return (
        result[None],
        end_state.reshape((1, 1) + end_state.shape[:1] + end_state.shape[-1:]),
        end_norm[None, None],
    )


def solution(mesh):
    return jax.shard_map(
        local,
        mesh=mesh,
        in_specs=(
            P("req", "seq", None),
            P("req"),
            P("req", "seq", None),
            P(),
            P(),
            P(),
            P(),
            P(),
            P(),
            P(),
            P(None, "req"),
            P(None, "req"),
            P(None, "req"),
        ),
        out_specs=(P("req", "seq", None), P("req", "seq", None, None), P("req", "seq", None, None)),
        check_vma=False,
    )
```

```python
import functools

import jax
import jax.numpy as jnp
from jax import lax
from jax.experimental import pallas as pl
from jax.experimental.pallas import tpu as pltpu
from jax.sharding import PartitionSpec as P


def from_behind(array, axis, by):
    count = lax.axis_size(axis)
    pairs = [(i, i + by) for i in range(count) if 0 <= i + by < count]
    return lax.ppermute(array, axis, pairs)


def entering(array, axis, combine, identity):
    count, here = (lax.axis_size(axis), lax.axis_index(axis))
    everything = jax.tree.map(
        lambda part, kind: lax.all_gather(part.astype(kind), axis),
        array,
        (jnp.bfloat16, jnp.bfloat16, jnp.bfloat16),
    )
    start = jax.tree.map(
        lambda part, zero: jnp.broadcast_to(jnp.asarray(zero, part.dtype), part.shape),
        array,
        identity,
    )

    def hop(k, before):
        reached = k < here
        new = combine(
            before, jax.tree.map(lambda part, own: part[k].astype(own.dtype), everything, array)
        )
        return jax.tree.map(lambda a, b: jnp.where(reached, a, b), new, before)

    return lax.fori_loop(0, count, hop, start)


def features(vectors):
    constant = jnp.ones(vectors.shape[:-1] + (1,), jnp.float32)
    width = vectors.shape[-1]
    squares = (vectors[..., :, None] * vectors[..., None, :]).reshape(
        vectors.shape[:-1] + (width * width,)
    )
    return jnp.concatenate([constant, vectors, squares * 0.5**0.5], axis=-1)


def carry_in(valid_mask, decays, queries, numerator, denominator, flat_memory, key_sum):
    local_len = numerator.shape[0]
    feat_len, head_count = key_sum.shape
    value_len = flat_memory.shape[1] // head_count
    feat_in = queries.shape[1] // head_count
    decay_rate = jnp.where(valid_mask[:, None] > 0, decays, 0.0)
    span_decay = jnp.sum(decay_rate, axis=0)

    def merge_states(earlier, later):
        factor = jnp.exp(later[0])
        return (
            earlier[0] + later[0],
            earlier[1] * jnp.repeat(factor, value_len)[None, :] + later[1],
            earlier[2] * factor[None, :] + later[2],
        )

    neutral = (jnp.zeros_like(span_decay), jnp.zeros_like(flat_memory), jnp.zeros_like(key_sum))
    carried = entering((span_decay, flat_memory, key_sum), "seq", merge_states, neutral)
    prior_memory = carried[1]
    prior_keys = carried[2]
    highest = lax.Precision.HIGHEST
    growth = jnp.exp(jnp.cumsum(decay_rate, axis=0))
    query_feat = features(queries.astype(jnp.float32).reshape(local_len, head_count, feat_in))
    added = jnp.einsum(
        "thf,fhv->thv",
        query_feat,
        prior_memory.reshape(feat_len, head_count, value_len),
        precision=highest,
    )
    numerator = numerator + (added * growth[:, :, None]).reshape(local_len, -1)
    denominator = (
        denominator + jnp.einsum("thf,fh->th", query_feat, prior_keys, precision=highest) * growth
    )
    span_factor = jnp.exp(span_decay)
    end_state = prior_memory * jnp.repeat(span_factor, value_len)[None, :] + flat_memory
    end_norm = prior_keys * span_factor[None, :] + key_sum
    return numerator, denominator, end_state, end_norm


def permute(array, target):
    count = lax.axis_size("req")
    return lax.ppermute(array, "req", [(i, target(i)) for i in range(count)])


def flip_core(array):
    return permute(array, lambda i: i ^ 1)


def flip_near(array):
    return permute(array, lambda i: i ^ 2)


def flip_far(array):
    return permute(array, lambda i: i ^ 4)


def next_plane(array):
    return permute(array, lambda i: i ^ (8 if i // 8 in (1, 2) else 16))


def together(*arrays):
    return lax.optimization_barrier(arrays)


def slot(*sends):
    operands = together(*[array for _, array in sends])
    return together(*[send(array) for (send, _), array in zip(sends, operands)])


def vmem(count):
    return [pl.BlockSpec(memory_space=pltpu.VMEM)] * count


def kernel_call(body, name, out_shape, *operands, scratch=(), aliases=None, specs=None, mib=24):
    many = isinstance(out_shape, tuple)
    return pl.pallas_call(
        body,
        out_shape=out_shape,
        in_specs=specs or vmem(len(operands)),
        out_specs=tuple(vmem(len(out_shape))) if many else vmem(1)[0],
        scratch_shapes=list(scratch),
        input_output_aliases=aliases or {},
        compiler_params=pltpu.CompilerParams(vmem_limit_bytes=mib * 1024 * 1024),
        cost_estimate=pl.CostEstimate(flops=1000, bytes_accessed=1000, transcendentals=0),
        name=name,
    )(*operands)


def like(rows, columns, dtype):
    return jax.ShapeDtypeStruct((rows, columns), dtype)


NT = (((1,), (1,)), ((), ()))


def unit_rows(rows, gain):
    factor = lax.rsqrt(jnp.mean(rows * rows, axis=-1, keepdims=True) + 1e-05)
    return (rows * factor * gain).astype(jnp.bfloat16).astype(jnp.float32)


def project_body(
    step,
    scale,
    rows_ref,
    edge_ref,
    gain_ref,
    conv_ref,
    query_ref,
    key_ref,
    value_ref,
    queries_ref,
    keys_ref,
    values_ref,
    normed,
    gated,
):
    gain = gain_ref[...]
    count = rows_ref.shape[0]
    lead = edge_ref.shape[0]
    taps = conv_ref.shape[0]
    normed[:lead] = unit_rows(edge_ref[...].astype(jnp.float32), gain)

    @pl.loop(0, count // step)
    def _(block):
        at = pl.multiple_of(block * step, step)
        rows = rows_ref[pl.ds(at, step), :].astype(jnp.float32)
        normed[pl.ds(lead + at, step), :] = unit_rows(rows, gain)

    @pl.loop(0, count // step)
    def _(block):
        at = pl.multiple_of(block * step, step)
        window = normed[pl.ds(at, step + lead), :]
        here = window[lead:]
        total = conv_ref[0:1] * here
        for tap in range(1, taps):
            total = total + conv_ref[tap : tap + 1] * window[lead - tap : lead - tap + step]
        gated[pl.ds(at, step), :] = (total * jax.nn.sigmoid(here)).astype(jnp.bfloat16)

    rows = gated[...]
    for weight_ref, out_ref, factor in (
        (query_ref, queries_ref, scale),
        (key_ref, keys_ref, scale),
        (value_ref, values_ref, None),
    ):
        product = jnp.dot(rows, weight_ref[...], preferred_element_type=jnp.float32)
        if factor is not None:
            product = product * factor
        out_ref[...] = product.astype(jnp.bfloat16)


def project(rows, edge, mix_gain, conv_weight, query_weight, key_weight, value_weight, scale):
    count, width = rows.shape
    step = 32
    return kernel_call(
        functools.partial(project_body, step, scale),
        "project",
        tuple(like(count, w.shape[1], jnp.bfloat16) for w in (query_weight, key_weight, value_weight)),
        rows,
        edge,
        mix_gain[None],
        conv_weight,
        query_weight,
        key_weight,
        value_weight,
        scratch=(
            pltpu.VMEM((count + edge.shape[0], width), jnp.float32),
            pltpu.VMEM((count, width), jnp.bfloat16),
        ),
    )


def attend_body(
    feat_in,
    value_len,
    count_ref,
    rate_ref,
    queries_ref,
    keys_ref,
    values_ref,
    numer_ref,
    denom_ref,
    state_ref,
    norm_ref,
    turned,
    total,
    norms,
):
    heads, count = rate_ref.shape
    columns = values_ref.shape[1]
    lane = lax.broadcasted_iota(jnp.int32, (count, count), 1)
    row = lax.broadcasted_iota(jnp.int32, (count, count), 0)
    valid = (lane[:1] < count_ref[0]).astype(jnp.float32)
    rate = jnp.where(valid > 0, rate_ref[...], 0.0)
    upto = (row <= lane).astype(jnp.float32)
    across = jnp.dot(
        rate, upto, precision=lax.Precision.HIGHEST, preferred_element_type=jnp.float32
    )
    down = across.T
    closing = across[:, count - 1 : count]
    fading = jnp.exp(closing - across) * valid
    causal = row >= lane
    keys = keys_ref[...]
    turned[...] = keys.astype(jnp.float32).T
    owner = lax.broadcasted_iota(jnp.int32, queries_ref.shape, 1)
    spare = lax.broadcasted_iota(jnp.int32, (8, count), 0) == 0
    head_lane = lax.broadcasted_iota(jnp.int32, (count, 128), 1)
    numer_ref[...] = jnp.zeros(numer_ref.shape, jnp.float32)
    total[...] = jnp.zeros(total.shape, jnp.float32)
    norms[...] = jnp.zeros(norms.shape, jnp.float32)
    norm_total = jnp.zeros((total.shape[0], 128), jnp.float32)
    denominators = jnp.zeros((count, 128), jnp.float32)
    for h in range(heads):
        low = min(h * value_len // 128 * 128, max(columns - 256, 0))
        high = min(low + 256, columns)
        mine = lax.broadcasted_iota(jnp.int32, (count, high - low), 1) + low
        mine = (mine >= h * value_len) & (mine < (h + 1) * value_len)
        values = jnp.where(mine, values_ref[:, low:high].astype(jnp.float32), 0.0)
        values = values.astype(jnp.bfloat16)
        asks = (owner >= h * feat_in) & (owner < (h + 1) * feat_in)
        queries = jnp.where(asks, queries_ref[...].astype(jnp.float32), 0.0)
        scores = lax.dot_general(
            queries.astype(jnp.bfloat16), keys, NT, preferred_element_type=jnp.float32
        )
        gap = down[:, h : h + 1] - across[h : h + 1]
        weights = jnp.where(causal, jnp.exp(jnp.minimum(gap, 0.0)) * valid, 0.0)
        weights = weights * (1.0 + scores + 0.5 * scores * scores)
        numer_ref[:, low:high] += jnp.dot(
            weights.astype(jnp.bfloat16), values, preferred_element_type=jnp.float32
        )
        sums = jnp.sum(weights, axis=1, keepdims=True)
        denominators = jnp.where(head_lane == h, sums, denominators)
        own = turned[h * feat_in : (h + 1) * feat_in]
        fade = fading[h : h + 1]
        faded = own * fade
        scaled = faded * 0.5**0.5
        parts = [own[i : i + 1] * scaled for i in range(feat_in)]
        parts += [faded, jnp.where(spare, fade, 0.0)]
        feats = jnp.concatenate(parts, axis=0).astype(jnp.bfloat16)
        total[:, low:high] += jnp.dot(feats, values, preferred_element_type=jnp.float32)
        mark = (head_lane == h).astype(jnp.bfloat16)
        norm_total = norm_total + jnp.dot(feats, mark, preferred_element_type=jnp.float32)
    denom_ref[...] = denominators[:, :heads]
    pairs = feat_in * feat_in
    state_ref[0] = total[pairs + feat_in : pairs + feat_in + 1, :]
    for f in range(feat_in):
        state_ref[1 + f] = total[pairs + f : pairs + f + 1, :]

    @pl.loop(0, pairs // 8)
    def _(block):
        for k in range(8):
            f = block * 8 + k
            state_ref[1 + feat_in + f] = total[pl.ds(f, 1), :]

    norms[0:1, :] = norm_total[pairs + feat_in : pairs + feat_in + 1]
    norms[1 : 1 + feat_in, :] = norm_total[pairs : pairs + feat_in]
    norms[1 + feat_in : 1 + feat_in + pairs, :] = norm_total[:pairs]
    norm_ref[...] = norms[...].T[:heads, : 1 + feat_in + pairs]


def attend(valid_count, rate, queries, keys, values, feat_in, value_len):
    heads, count = rate.shape
    columns = values.shape[1]
    feat_len = 1 + feat_in + feat_in * feat_in
    padded = feat_in * feat_in + feat_in + 8
    return kernel_call(
        functools.partial(attend_body, feat_in, value_len),
        "attend",
        (
            like(count, columns, jnp.float32),
            like(count, heads, jnp.float32),
            jax.ShapeDtypeStruct((feat_len, 1, columns), jnp.float32),
            like(heads, feat_len, jnp.float32),
        ),
        valid_count,
        rate,
        queries,
        keys,
        values,
        specs=[pl.BlockSpec(memory_space=pltpu.SMEM)] + vmem(4),
        scratch=(
            pltpu.VMEM((queries.shape[1], count), jnp.float32),
            pltpu.VMEM((padded, columns), jnp.float32),
            pltpu.VMEM(((feat_len + 127) // 128 * 128, 128), jnp.float32),
        ),
    )


def mix_body(
    value_len, step, numer_ref, denom_ref, rows_ref, out_ref, gain_ref, mixed_ref, mlp_ref, sums
):
    count, columns = numer_ref.shape
    heads = denom_ref.shape[1]
    column = lax.broadcasted_iota(jnp.int32, (1, columns), 1)
    inverse = 1.0 / denom_ref[...]
    spread = jnp.zeros((count, columns), jnp.float32)
    for h in range(heads):
        here = (column >= h * value_len) & (column < (h + 1) * value_len)
        spread = jnp.where(here, inverse[:, h : h + 1], spread)
    attended = (numer_ref[...] * spread).astype(jnp.bfloat16)
    sums[...] = jnp.dot(attended, out_ref[...], preferred_element_type=jnp.float32)
    gain = gain_ref[...]

    @pl.loop(0, count // step)
    def _(block):
        at = pl.ds(pl.multiple_of(block * step, step), step)
        mixed = (rows_ref[at, :].astype(jnp.float32) + sums[at, :]).astype(jnp.bfloat16)
        mixed_ref[at, :] = mixed
        mlp_ref[at, :] = unit_rows(mixed.astype(jnp.float32), gain).astype(jnp.bfloat16)


def mix(numer, denom, rows, out_weight, mlp_gain, value_len):
    count, width = rows.shape
    shape = like(count, width, jnp.bfloat16)
    return kernel_call(
        functools.partial(mix_body, value_len, 32),
        "mix",
        (shape, shape),
        numer,
        denom,
        rows,
        out_weight,
        mlp_gain[None],
        scratch=(pltpu.VMEM((count, width), jnp.float32),),
    )


def swiglu_terms(rows, gate_rows, up_rows, down_rows):
    gate_act = lax.dot_general(rows, gate_rows, NT, preferred_element_type=jnp.float32)
    up_act = lax.dot_general(rows, up_rows, NT, preferred_element_type=jnp.float32)
    hidden_units = (gate_act * jax.nn.sigmoid(gate_act) * up_act).astype(jnp.bfloat16)
    return jnp.dot(hidden_units, down_rows, preferred_element_type=jnp.float32)


def on_grid(run):
    return all(low % 16 == 0 and high % 16 == 0 for _, low, high in run)


def read_units(refs, units):
    parts = []
    for k in range(3):
        rows = [refs[run[k][0]][run[k][1] : run[k][2]] for run in units if on_grid(run)]
        rest = [
            refs[run[k][0]][...].astype(jnp.float32)[run[k][1] : run[k][2]]
            for run in units
            if not on_grid(run)
        ]
        if rest:
            rows.append(jnp.concatenate(rest, axis=0).astype(jnp.bfloat16))
        parts.append(jnp.concatenate(rows, axis=0))
    return parts


def accumulate_body(units, n_weights, n_rows, n_acc, residual, *refs):
    weights = refs[:n_weights]
    rows = refs[n_weights : n_weights + n_rows]
    acc = refs[n_weights + n_rows : n_weights + n_rows + n_acc]
    parts = read_units(weights, units)
    for k, rows_ref in enumerate(rows):
        out_ref = refs[len(refs) - n_rows + k]
        terms = swiglu_terms(rows_ref[...], *parts)
        if n_acc:
            terms = terms + acc[k][...]
        if residual:
            terms = terms + refs[n_weights + n_rows + n_acc][...].astype(jnp.float32)
        out_ref[...] = terms.astype(out_ref.dtype)


def accumulate(rows, weights, units, acc, dtype, name, residual=None):
    shapes = tuple(like(*array.shape, dtype) for array in rows)
    start = len(weights) + len(rows)
    aliases = {start + k: k for k in range(len(acc))} if dtype == jnp.float32 else {}
    extra = () if residual is None else (residual,)
    body = functools.partial(
        accumulate_body, tuple(units), len(weights), len(rows), len(acc), bool(extra)
    )
    return kernel_call(body, name, shapes, *weights, *rows, *acc, *extra, aliases=aliases)


def runs(which, low, size):
    return tuple((which, low + k * size, low + (k + 1) * size) for k in range(3))


def split_runs(first, second, main):
    (i, at), (j, then) = first, second
    held = 2 * main // 3
    rest = main - held
    return (
        ((i, at, at + held), (i, at + main, at + main + held), (j, then + rest, then + main)),
        ((i, at + held, at + main), (j, then, then + rest), (j, then + main, then + rest + main)),
    )


def collect_body(plans, *refs):
    outs = refs[len(refs) - len(plans) :]
    for out_ref, plan in zip(outs, plans):
        rows = [refs[i][...].astype(jnp.float32)[low:high] for i, low, high in plan]
        out_ref[...] = jnp.concatenate(rows, axis=0).astype(jnp.bfloat16)


def collect(arrays, plans, name):
    columns = arrays[0].shape[1]
    shapes = tuple(like(sum(h - l for _, l, h in plan), columns, jnp.bfloat16) for plan in plans)
    return kernel_call(functools.partial(collect_body, plans), name, shapes, *arrays)


def shard_body(main, gate_ref, up_ref, down_ref, shard_ref, main_ref, *rest):
    buffers, sems = rest[:3], rest[3]
    copies = [
        pltpu.make_async_copy(source, buffer, sems.at[k])
        for k, (source, buffer) in enumerate(zip((gate_ref, up_ref, down_ref), buffers))
    ]
    for copy in copies:
        copy.start()
    for copy in copies:
        copy.wait()
    arrays = [buffer[...].astype(jnp.float32) for buffer in buffers]
    tops = [array[:main] for array in arrays]
    ends = [array[main:] for array in arrays]
    shard_ref[...] = jnp.concatenate(tops + ends, axis=0).astype(jnp.bfloat16)
    main_ref[...] = jnp.concatenate(tops, axis=0).astype(jnp.bfloat16)


def final_body(step, count_ref, kept_ref, given_ref, out_ref):
    count = kept_ref.shape[0]

    @pl.loop(0, count // step)
    def _(block):
        first = pl.multiple_of(block * step, step)
        at = pl.ds(first, step)
        total = kept_ref[at, :] + given_ref[at, :].astype(jnp.float32)
        row = lax.broadcasted_iota(jnp.int32, total.shape, 0) + first
        out_ref[at, :] = jnp.where(row < count_ref[0], total, 0.0).astype(out_ref.dtype)


def local(
    hidden_in,
    lengths,
    log_decay,
    mix_gain,
    conv_weight,
    query_weight,
    key_weight,
    value_weight,
    out_weight,
    mlp_gain,
    gate_weight,
    up_weight,
    down_weight,
):
    local_len = hidden_in.shape[1]
    rows_in = hidden_in[0]
    decays = log_decay[0]
    head_count = log_decay.shape[2]
    value_len = value_weight.shape[1] // head_count
    feat_in = query_weight.shape[1] // head_count
    feature_scale = feat_in ** (-0.25)
    valid_count = lengths - lax.axis_index("seq") * local_len
    spans = lax.axis_size("seq")
    units, model = gate_weight.shape[1], gate_weight.shape[0]
    edge = units // 7
    main = units - edge
    wide = 3 * main
    full = 3 * units
    narrow = full - wide
    cut = main + 2 * main // 3

    shard, shard_main = kernel_call(
        functools.partial(shard_body, main),
        "shard",
        (like(full, model, jnp.bfloat16), like(wide, model, jnp.bfloat16)),
        gate_weight.T,
        up_weight.T,
        down_weight.T,
        specs=[pl.BlockSpec(memory_space=pl.ANY)] * 3,
        scratch=[pltpu.VMEM((units, model), jnp.bfloat16)] * 3 + [pltpu.SemaphoreType.DMA((3,))],
        mib=56,
    )
    near, far, deep = slot((flip_near, shard), (flip_far, shard), (next_plane, shard_main))

    lead = 16
    if spans > 1:
        edge_in = from_behind(rows_in[local_len - lead :], "seq", 1)
    else:
        edge_in = jnp.zeros((lead, model), jnp.bfloat16)
    queries, key_rows, values = project(
        rows_in, edge_in, mix_gain, conv_weight, query_weight, key_weight, value_weight, feature_scale
    )
    near, far, deep, queries, key_rows, values = together(
        near, far, deep, queries, key_rows, values
    )

    sends = collect(
        (shard, near, far, deep),
        (
            ((3, 0, wide), (2, 0, cut)),
            ((3, 0, wide), (1, cut, full)),
            ((3, 0, wide), (0, wide, full), (1, wide, full), (2, wide, full)),
        ),
        "collect_second",
    )
    near1, far1, deep1 = slot(*zip((flip_near, flip_far, next_plane), sends))

    numerator, denominator, end_state, end_norm = attend(
        valid_count, log_decay[0].T, queries, key_rows, values, feat_in, value_len
    )
    if spans > 1:
        positions = jnp.arange(local_len, dtype=jnp.int32)
        numerator, denominator, end_state, end_norm = carry_in(
            (positions < valid_count).astype(jnp.float32),
            decays,
            queries,
            numerator,
            denominator,
            end_state[:, 0],
            end_norm.T,
        )
    else:
        end_norm = end_norm.T
    mixed_rows, mlp_in = mix(numerator, denominator, rows_in, out_weight, mlp_gain, value_len)
    near1, far1, deep1, mixed_rows, mlp_in, end_state, end_norm = together(
        near1, far1, deep1, mixed_rows, mlp_in, end_state, end_norm
    )

    middle = local_len // 2
    *sends, top, end = collect(
        (near1, far1, deep1, mlp_in),
        (
            ((2, 0, wide), (1, 0, cut)),
            ((2, 0, wide),),
            ((2, 0, wide + 3 * narrow), (1, wide + wide - cut, wide + full - cut)),
            ((0, cut, wide),),
            ((3, 0, middle),),
            ((3, middle, local_len),),
        ),
        "collect_third",
    )
    sends = together(*sends)
    near2, far2, deep2 = flip_near(sends[0]), flip_far(sends[1]), next_plane(sends[2])
    second2 = flip_far(sends[3])
    (other_in,) = collect(
        (flip_core(top), flip_core(end)),
        (((0, 0, middle), (1, 0, local_len - middle)),),
        "collect_rows",
    )
    rows = (mlp_in, other_in)
    acc = accumulate(
        rows,
        (shard, near, far, deep, near1, far1, deep1),
        [runs(i, 0, main) for i in range(7)] + list(split_runs((4, wide), (5, wide), main)),
        (),
        jnp.float32,
        "accumulate_second",
    )
    second2, deep2, *acc = together(second2, deep2, *acc)

    two = 2 * main
    sends = collect(
        (second2, deep2),
        (
            ((1, main, wide),),
            ((1, 0, main), (1, two, wide)),
            ((1, wide, wide + 4 * narrow), (0, wide - cut - main, wide - cut)),
        ),
        "collect_fourth",
    )
    near3, far3, deep3 = slot(*zip((flip_near, flip_far, next_plane), sends))
    acc = accumulate(
        rows,
        (shard, near, far, far1, deep1, near2, far2, second2, deep2),
        [runs(i, 0, main) for i in (5, 6, 8)]
        + list(split_runs((5, wide), (7, 0), main))
        + [runs(i, wide, edge) for i in (0, 1, 2)]
        + [runs(3, wide + wide - cut, edge)]
        + [runs(4, wide + k * narrow, edge) for k in range(3)]
        + [runs(8, wide + k * narrow, edge) for k in range(4)],
        tuple(acc),
        jnp.float32,
        "accumulate_third",
    )
    near2, far2, *acc = together(near2, far2, *acc)
    sends = collect(
        (near2, far2, deep2),
        (((2, 0, main), (1, 0, main)), ((2, main, two), (0, main, two))),
        "collect_more",
    )
    near3_more, far3_more = flip_near(sends[0]), flip_far(sends[1])

    sends = collect(
        (near3, far3, deep3),
        (
            ((1, 0, main),),
            ((0, 0, main),),
            ((2, 3 * narrow, 4 * narrow + main),),
        ),
        "collect_fifth",
    )
    near4, far4, deep4 = slot(*zip((flip_near, flip_far, next_plane), sends))
    line = 4 * narrow
    weights = (near3, near3_more, far3, far3_more, deep3, near4, far4, deep4)
    last = [
        ((1, 0, main), (0, 0, main), (0, main, two)),
        ((2, 0, main), (3, 0, main), (2, main, two)),
        ((1, main, two), (3, main, two), (4, line, line + main)),
        ((5, 0, main), (6, 0, main), (7, narrow, narrow + main)),
    ]
    last += [runs(4, k * narrow, edge) for k in range(4)] + [runs(7, 0, edge)]
    (given,) = accumulate(rows[1:], weights, last, acc[1:], jnp.bfloat16, "finish_other")
    (kept,) = accumulate(
        rows[:1], weights, last, acc[:1], jnp.float32, "finish_own", residual=mixed_rows
    )
    result = kernel_call(
        functools.partial(final_body, 64),
        "final",
        like(local_len, model, jnp.bfloat16),
        valid_count,
        kept,
        flip_core(given),
        specs=[pl.BlockSpec(memory_space=pltpu.SMEM)] + vmem(2),
    )
    return (
        result[None],
        end_state.reshape((1, 1) + end_state.shape[:1] + end_state.shape[-1:]),
        end_norm[None, None],
    )


def solution(mesh):
    return jax.shard_map(
        local,
        mesh=mesh,
        in_specs=(
            P("req", "seq", None),
            P("req"),
            P("req", "seq", None),
            P(),
            P(),
            P(),
            P(),
            P(),
            P(),
            P(),
            P(None, "req"),
            P(None, "req"),
            P(None, "req"),
        ),
        out_specs=(P("req", "seq", None), P("req", "seq", None, None), P("req", "seq", None, None)),
        check_vma=False,
    )
```

```python
import functools

import jax
import jax.numpy as jnp
from jax import lax
from jax.experimental import pallas as pl
from jax.experimental.pallas import tpu as pltpu
from jax.sharding import PartitionSpec as P


def from_behind(array, axis, by):
    count = lax.axis_size(axis)
    pairs = [(i, i + by) for i in range(count) if 0 <= i + by < count]
    return lax.ppermute(array, axis, pairs)


def entering(array, axis, combine, identity):
    count, here = (lax.axis_size(axis), lax.axis_index(axis))
    everything = jax.tree.map(
        lambda part, kind: lax.all_gather(part.astype(kind), axis),
        array,
        (jnp.bfloat16, jnp.bfloat16, jnp.bfloat16),
    )
    start = jax.tree.map(
        lambda part, zero: jnp.broadcast_to(jnp.asarray(zero, part.dtype), part.shape),
        array,
        identity,
    )

    def hop(k, before):
        reached = k < here
        new = combine(
            before, jax.tree.map(lambda part, own: part[k].astype(own.dtype), everything, array)
        )
        return jax.tree.map(lambda a, b: jnp.where(reached, a, b), new, before)

    return lax.fori_loop(0, count, hop, start)


def features(vectors):
    constant = jnp.ones(vectors.shape[:-1] + (1,), jnp.float32)
    width = vectors.shape[-1]
    squares = (vectors[..., :, None] * vectors[..., None, :]).reshape(
        vectors.shape[:-1] + (width * width,)
    )
    return jnp.concatenate([constant, vectors, squares * 0.5**0.5], axis=-1)


def carry_in(valid_mask, decays, queries, numerator, denominator, flat_memory, key_sum):
    local_len = numerator.shape[0]
    feat_len, head_count = key_sum.shape
    value_len = flat_memory.shape[1] // head_count
    feat_in = queries.shape[1] // head_count
    decay_rate = jnp.where(valid_mask[:, None] > 0, decays, 0.0)
    span_decay = jnp.sum(decay_rate, axis=0)

    def merge_states(earlier, later):
        factor = jnp.exp(later[0])
        return (
            earlier[0] + later[0],
            earlier[1] * jnp.repeat(factor, value_len)[None, :] + later[1],
            earlier[2] * factor[None, :] + later[2],
        )

    neutral = (jnp.zeros_like(span_decay), jnp.zeros_like(flat_memory), jnp.zeros_like(key_sum))
    carried = entering((span_decay, flat_memory, key_sum), "seq", merge_states, neutral)
    prior_memory = carried[1]
    prior_keys = carried[2]
    highest = lax.Precision.HIGHEST
    growth = jnp.exp(jnp.cumsum(decay_rate, axis=0))
    query_feat = features(queries.astype(jnp.float32).reshape(local_len, head_count, feat_in))
    added = jnp.einsum(
        "thf,fhv->thv",
        query_feat,
        prior_memory.reshape(feat_len, head_count, value_len),
        precision=highest,
    )
    numerator = numerator + (added * growth[:, :, None]).reshape(local_len, -1)
    denominator = (
        denominator + jnp.einsum("thf,fh->th", query_feat, prior_keys, precision=highest) * growth
    )
    span_factor = jnp.exp(span_decay)
    end_state = prior_memory * jnp.repeat(span_factor, value_len)[None, :] + flat_memory
    end_norm = prior_keys * span_factor[None, :] + key_sum
    return numerator, denominator, end_state, end_norm


def permute(array, target):
    count = lax.axis_size("req")
    return lax.ppermute(array, "req", [(i, target(i)) for i in range(count)])


def flip_core(array):
    return permute(array, lambda i: i ^ 1)


def flip_near(array):
    return permute(array, lambda i: i ^ 2)


def flip_far(array):
    return permute(array, lambda i: i ^ 4)


def next_plane(array):
    return permute(array, lambda i: i ^ (8 if i // 8 in (1, 2) else 16))


def together(*arrays):
    return lax.optimization_barrier(arrays)


def slot(*sends):
    operands = together(*[array for _, array in sends])
    return together(*[send(array) for (send, _), array in zip(sends, operands)])


def vmem(count):
    return [pl.BlockSpec(memory_space=pltpu.VMEM)] * count


def kernel_call(body, name, out_shape, *operands, scratch=(), aliases=None, specs=None, mib=24):
    many = isinstance(out_shape, tuple)
    return pl.pallas_call(
        body,
        out_shape=out_shape,
        in_specs=specs or vmem(len(operands)),
        out_specs=tuple(vmem(len(out_shape))) if many else vmem(1)[0],
        scratch_shapes=list(scratch),
        input_output_aliases=aliases or {},
        compiler_params=pltpu.CompilerParams(vmem_limit_bytes=mib * 1024 * 1024),
        cost_estimate=pl.CostEstimate(flops=1000, bytes_accessed=1000, transcendentals=0),
        name=name,
    )(*operands)


def like(rows, columns, dtype):
    return jax.ShapeDtypeStruct((rows, columns), dtype)


NT = (((1,), (1,)), ((), ()))


def unit_rows(rows, gain):
    factor = lax.rsqrt(jnp.mean(rows * rows, axis=-1, keepdims=True) + 1e-05)
    return (rows * factor * gain).astype(jnp.bfloat16).astype(jnp.float32)


def project_body(
    step,
    scale,
    rows_ref,
    edge_ref,
    gain_ref,
    conv_ref,
    query_ref,
    key_ref,
    value_ref,
    queries_ref,
    keys_ref,
    values_ref,
    normed,
    gated,
):
    gain = gain_ref[...]
    count = rows_ref.shape[0]
    lead = edge_ref.shape[0]
    taps = conv_ref.shape[0]
    normed[:lead] = unit_rows(edge_ref[...].astype(jnp.float32), gain)

    @pl.loop(0, count // step)
    def _(block):
        at = pl.multiple_of(block * step, step)
        rows = rows_ref[pl.ds(at, step), :].astype(jnp.float32)
        normed[pl.ds(lead + at, step), :] = unit_rows(rows, gain)

    @pl.loop(0, count // step)
    def _(block):
        at = pl.multiple_of(block * step, step)
        window = normed[pl.ds(at, step + lead), :]
        here = window[lead:]
        total = conv_ref[0:1] * here
        for tap in range(1, taps):
            total = total + conv_ref[tap : tap + 1] * window[lead - tap : lead - tap + step]
        gated[pl.ds(at, step), :] = (total * jax.nn.sigmoid(here)).astype(jnp.bfloat16)

    rows = gated[...]
    for weight_ref, out_ref, factor in (
        (query_ref, queries_ref, scale),
        (key_ref, keys_ref, scale),
        (value_ref, values_ref, None),
    ):
        product = jnp.dot(rows, weight_ref[...], preferred_element_type=jnp.float32)
        if factor is not None:
            product = product * factor
        out_ref[...] = product.astype(jnp.bfloat16)


def project(rows, edge, mix_gain, conv_weight, query_weight, key_weight, value_weight, scale):
    count, width = rows.shape
    step = 32
    return kernel_call(
        functools.partial(project_body, step, scale),
        "project",
        tuple(like(count, w.shape[1], jnp.bfloat16) for w in (query_weight, key_weight, value_weight)),
        rows,
        edge,
        mix_gain[None],
        conv_weight,
        query_weight,
        key_weight,
        value_weight,
        scratch=(
            pltpu.VMEM((count + edge.shape[0], width), jnp.float32),
            pltpu.VMEM((count, width), jnp.bfloat16),
        ),
    )


def attend_body(
    feat_in,
    value_len,
    count_ref,
    rate_ref,
    queries_ref,
    keys_ref,
    values_ref,
    numer_ref,
    denom_ref,
    state_ref,
    norm_ref,
    turned,
    total,
    norms,
):
    heads, count = rate_ref.shape
    columns = values_ref.shape[1]
    lane = lax.broadcasted_iota(jnp.int32, (count, count), 1)
    row = lax.broadcasted_iota(jnp.int32, (count, count), 0)
    valid = (lane[:1] < count_ref[0]).astype(jnp.float32)
    rate = jnp.where(valid > 0, rate_ref[...], 0.0)
    upto = (row <= lane).astype(jnp.float32)
    across = jnp.dot(
        rate, upto, precision=lax.Precision.HIGHEST, preferred_element_type=jnp.float32
    )
    down = across.T
    closing = across[:, count - 1 : count]
    fading = jnp.exp(closing - across) * valid
    causal = row >= lane
    keys = keys_ref[...]
    turned[...] = keys.astype(jnp.float32).T
    owner = lax.broadcasted_iota(jnp.int32, queries_ref.shape, 1)
    spare = lax.broadcasted_iota(jnp.int32, (8, count), 0) == 0
    head_lane = lax.broadcasted_iota(jnp.int32, (count, 128), 1)
    numer_ref[...] = jnp.zeros(numer_ref.shape, jnp.float32)
    total[...] = jnp.zeros(total.shape, jnp.float32)
    norms[...] = jnp.zeros(norms.shape, jnp.float32)
    norm_total = jnp.zeros((total.shape[0], 128), jnp.float32)
    denominators = jnp.zeros((count, 128), jnp.float32)
    for h in range(heads):
        low = min(h * value_len // 128 * 128, max(columns - 256, 0))
        high = min(low + 256, columns)
        mine = lax.broadcasted_iota(jnp.int32, (count, high - low), 1) + low
        mine = (mine >= h * value_len) & (mine < (h + 1) * value_len)
        values = jnp.where(mine, values_ref[:, low:high].astype(jnp.float32), 0.0)
        values = values.astype(jnp.bfloat16)
        asks = (owner >= h * feat_in) & (owner < (h + 1) * feat_in)
        queries = jnp.where(asks, queries_ref[...].astype(jnp.float32), 0.0)
        scores = lax.dot_general(
            queries.astype(jnp.bfloat16), keys, NT, preferred_element_type=jnp.float32
        )
        gap = down[:, h : h + 1] - across[h : h + 1]
        weights = jnp.where(causal, jnp.exp(jnp.minimum(gap, 0.0)) * valid, 0.0)
        weights = weights * (1.0 + scores + 0.5 * scores * scores)
        numer_ref[:, low:high] += jnp.dot(
            weights.astype(jnp.bfloat16), values, preferred_element_type=jnp.float32
        )
        sums = jnp.sum(weights, axis=1, keepdims=True)
        denominators = jnp.where(head_lane == h, sums, denominators)
        own = turned[h * feat_in : (h + 1) * feat_in]
        fade = fading[h : h + 1]
        faded = own * fade
        scaled = faded * 0.5**0.5
        parts = [own[i : i + 1] * scaled for i in range(feat_in)]
        parts += [faded, jnp.where(spare, fade, 0.0)]
        feats = jnp.concatenate(parts, axis=0).astype(jnp.bfloat16)
        total[:, low:high] += jnp.dot(feats, values, preferred_element_type=jnp.float32)
        mark = (head_lane == h).astype(jnp.bfloat16)
        norm_total = norm_total + jnp.dot(feats, mark, preferred_element_type=jnp.float32)
    denom_ref[...] = denominators[:, :heads]
    pairs = feat_in * feat_in
    state_ref[0] = total[pairs + feat_in : pairs + feat_in + 1, :]
    for f in range(feat_in):
        state_ref[1 + f] = total[pairs + f : pairs + f + 1, :]

    @pl.loop(0, pairs // 8)
    def _(block):
        for k in range(8):
            f = block * 8 + k
            state_ref[1 + feat_in + f] = total[pl.ds(f, 1), :]

    norms[0:1, :] = norm_total[pairs + feat_in : pairs + feat_in + 1]
    norms[1 : 1 + feat_in, :] = norm_total[pairs : pairs + feat_in]
    norms[1 + feat_in : 1 + feat_in + pairs, :] = norm_total[:pairs]
    norm_ref[...] = norms[...].T[:heads, : 1 + feat_in + pairs]


def attend(valid_count, rate, queries, keys, values, feat_in, value_len):
    heads, count = rate.shape
    columns = values.shape[1]
    feat_len = 1 + feat_in + feat_in * feat_in
    padded = feat_in * feat_in + feat_in + 8
    return kernel_call(
        functools.partial(attend_body, feat_in, value_len),
        "attend",
        (
            like(count, columns, jnp.float32),
            like(count, heads, jnp.float32),
            jax.ShapeDtypeStruct((feat_len, 1, columns), jnp.float32),
            like(heads, feat_len, jnp.float32),
        ),
        valid_count,
        rate,
        queries,
        keys,
        values,
        specs=[pl.BlockSpec(memory_space=pltpu.SMEM)] + vmem(4),
        scratch=(
            pltpu.VMEM((queries.shape[1], count), jnp.float32),
            pltpu.VMEM((padded, columns), jnp.float32),
            pltpu.VMEM(((feat_len + 127) // 128 * 128, 128), jnp.float32),
        ),
    )


def mix_body(
    value_len, step, numer_ref, denom_ref, rows_ref, out_ref, gain_ref, mixed_ref, mlp_ref, sums
):
    count, columns = numer_ref.shape
    heads = denom_ref.shape[1]
    column = lax.broadcasted_iota(jnp.int32, (1, columns), 1)
    inverse = 1.0 / denom_ref[...]
    spread = jnp.zeros((count, columns), jnp.float32)
    for h in range(heads):
        here = (column >= h * value_len) & (column < (h + 1) * value_len)
        spread = jnp.where(here, inverse[:, h : h + 1], spread)
    attended = (numer_ref[...] * spread).astype(jnp.bfloat16)
    sums[...] = jnp.dot(attended, out_ref[...], preferred_element_type=jnp.float32)
    gain = gain_ref[...]

    @pl.loop(0, count // step)
    def _(block):
        at = pl.ds(pl.multiple_of(block * step, step), step)
        mixed = (rows_ref[at, :].astype(jnp.float32) + sums[at, :]).astype(jnp.bfloat16)
        mixed_ref[at, :] = mixed
        mlp_ref[at, :] = unit_rows(mixed.astype(jnp.float32), gain).astype(jnp.bfloat16)


def mix(numer, denom, rows, out_weight, mlp_gain, value_len):
    count, width = rows.shape
    shape = like(count, width, jnp.bfloat16)
    return kernel_call(
        functools.partial(mix_body, value_len, 32),
        "mix",
        (shape, shape),
        numer,
        denom,
        rows,
        out_weight,
        mlp_gain[None],
        scratch=(pltpu.VMEM((count, width), jnp.float32),),
    )


def swiglu_terms(rows, gate_rows, up_rows, down_rows):
    gate_act = lax.dot_general(rows, gate_rows, NT, preferred_element_type=jnp.float32)
    up_act = lax.dot_general(rows, up_rows, NT, preferred_element_type=jnp.float32)
    hidden_units = (gate_act * jax.nn.sigmoid(gate_act) * up_act).astype(jnp.bfloat16)
    return jnp.dot(hidden_units, down_rows, preferred_element_type=jnp.float32)


def on_grid(run):
    return all(low % 16 == 0 and high % 16 == 0 for _, low, high in run)


def read_units(refs, units):
    parts = []
    for k in range(3):
        rows = [refs[run[k][0]][run[k][1] : run[k][2]] for run in units if on_grid(run)]
        rest = [
            refs[run[k][0]][...].astype(jnp.float32)[run[k][1] : run[k][2]]
            for run in units
            if not on_grid(run)
        ]
        if rest:
            rows.append(jnp.concatenate(rest, axis=0).astype(jnp.bfloat16))
        parts.append(jnp.concatenate(rows, axis=0))
    return parts


def accumulate_body(units, n_weights, n_rows, n_acc, residual, *refs):
    weights = refs[:n_weights]
    rows = refs[n_weights : n_weights + n_rows]
    acc = refs[n_weights + n_rows : n_weights + n_rows + n_acc]
    parts = read_units(weights, units)
    for k, rows_ref in enumerate(rows):
        out_ref = refs[len(refs) - n_rows + k]
        terms = swiglu_terms(rows_ref[...], *parts)
        if n_acc:
            terms = terms + acc[k][...]
        if residual:
            terms = terms + refs[n_weights + n_rows + n_acc][...].astype(jnp.float32)
        out_ref[...] = terms.astype(out_ref.dtype)


def accumulate(rows, weights, units, acc, dtype, name, residual=None):
    shapes = tuple(like(*array.shape, dtype) for array in rows)
    start = len(weights) + len(rows)
    aliases = {start + k: k for k in range(len(acc))} if dtype == jnp.float32 else {}
    extra = () if residual is None else (residual,)
    body = functools.partial(
        accumulate_body, tuple(units), len(weights), len(rows), len(acc), bool(extra)
    )
    return kernel_call(body, name, shapes, *weights, *rows, *acc, *extra, aliases=aliases)


def runs(which, low, size):
    return tuple((which, low + k * size, low + (k + 1) * size) for k in range(3))


def split_runs(first, second, main):
    (i, at), (j, then) = first, second
    held = 2 * main // 3
    rest = main - held
    return (
        ((i, at, at + held), (i, at + main, at + main + held), (j, then + rest, then + main)),
        ((i, at + held, at + main), (j, then, then + rest), (j, then + main, then + rest + main)),
    )


def collect_body(plans, *refs):
    outs = refs[len(refs) - len(plans) :]
    for out_ref, plan in zip(outs, plans):
        rows = [refs[i][...].astype(jnp.float32)[low:high] for i, low, high in plan]
        out_ref[...] = jnp.concatenate(rows, axis=0).astype(jnp.bfloat16)


def collect(arrays, plans, name):
    columns = arrays[0].shape[1]
    shapes = tuple(like(sum(h - l for _, l, h in plan), columns, jnp.bfloat16) for plan in plans)
    return kernel_call(functools.partial(collect_body, plans), name, shapes, *arrays)


def shard_body(main, gate_ref, up_ref, down_ref, shard_ref, main_ref, *rest):
    buffers, sems = rest[:3], rest[3]
    copies = [
        pltpu.make_async_copy(source, buffer, sems.at[k])
        for k, (source, buffer) in enumerate(zip((gate_ref, up_ref, down_ref), buffers))
    ]
    for copy in copies:
        copy.start()
    for copy in copies:
        copy.wait()
    arrays = [buffer[...].astype(jnp.float32) for buffer in buffers]
    tops = [array[:main] for array in arrays]
    ends = [array[main:] for array in arrays]
    shard_ref[...] = jnp.concatenate(tops + ends, axis=0).astype(jnp.bfloat16)
    main_ref[...] = jnp.concatenate(tops, axis=0).astype(jnp.bfloat16)


def final_body(step, count_ref, kept_ref, given_ref, out_ref):
    count = kept_ref.shape[0]

    @pl.loop(0, count // step)
    def _(block):
        first = pl.multiple_of(block * step, step)
        at = pl.ds(first, step)
        total = kept_ref[at, :] + given_ref[at, :].astype(jnp.float32)
        row = lax.broadcasted_iota(jnp.int32, total.shape, 0) + first
        out_ref[at, :] = jnp.where(row < count_ref[0], total, 0.0).astype(out_ref.dtype)


def local(
    hidden_in,
    lengths,
    log_decay,
    mix_gain,
    conv_weight,
    query_weight,
    key_weight,
    value_weight,
    out_weight,
    mlp_gain,
    gate_weight,
    up_weight,
    down_weight,
):
    local_len = hidden_in.shape[1]
    rows_in = hidden_in[0]
    decays = log_decay[0]
    head_count = log_decay.shape[2]
    value_len = value_weight.shape[1] // head_count
    feat_in = query_weight.shape[1] // head_count
    feature_scale = feat_in ** (-0.25)
    valid_count = lengths - lax.axis_index("seq") * local_len
    spans = lax.axis_size("seq")
    units, model = gate_weight.shape[1], gate_weight.shape[0]
    edge = units // 7
    main = units - edge
    wide = 3 * main
    full = 3 * units
    narrow = full - wide
    cut = main + 2 * main // 3

    shard, shard_main = kernel_call(
        functools.partial(shard_body, main),
        "shard",
        (like(full, model, jnp.bfloat16), like(wide, model, jnp.bfloat16)),
        gate_weight.T,
        up_weight.T,
        down_weight.T,
        specs=[pl.BlockSpec(memory_space=pl.ANY)] * 3,
        scratch=[pltpu.VMEM((units, model), jnp.bfloat16)] * 3 + [pltpu.SemaphoreType.DMA((3,))],
        mib=56,
    )
    near, far, deep = slot((flip_near, shard), (flip_far, shard), (next_plane, shard_main))

    lead = 16
    if spans > 1:
        edge_in = from_behind(rows_in[local_len - lead :], "seq", 1)
    else:
        edge_in = jnp.zeros((lead, model), jnp.bfloat16)
    queries, key_rows, values = project(
        rows_in, edge_in, mix_gain, conv_weight, query_weight, key_weight, value_weight, feature_scale
    )
    near, far, deep, queries, key_rows, values = together(
        near, far, deep, queries, key_rows, values
    )

    sends = collect(
        (shard, near, far, deep),
        (
            ((3, 0, wide), (2, 0, cut)),
            ((3, 0, wide), (1, cut, full)),
            ((3, 0, wide), (0, wide, full), (1, wide, full), (2, wide, full)),
        ),
        "collect_second",
    )
    near1, far1, deep1 = slot(*zip((flip_near, flip_far, next_plane), sends))

    numerator, denominator, end_state, end_norm = attend(
        valid_count, log_decay[0].T, queries, key_rows, values, feat_in, value_len
    )
    if spans > 1:
        positions = jnp.arange(local_len, dtype=jnp.int32)
        numerator, denominator, end_state, end_norm = carry_in(
            (positions < valid_count).astype(jnp.float32),
            decays,
            queries,
            numerator,
            denominator,
            end_state[:, 0],
            end_norm.T,
        )
    else:
        end_norm = end_norm.T
    mixed_rows, mlp_in = mix(numerator, denominator, rows_in, out_weight, mlp_gain, value_len)
    near1, far1, deep1, mixed_rows, mlp_in, end_state, end_norm = together(
        near1, far1, deep1, mixed_rows, mlp_in, end_state, end_norm
    )

    sends = collect(
        (near1, far1, deep1),
        (
            ((2, 0, wide), (1, 0, cut)),
            ((2, 0, wide), (0, cut, wide)),
            ((2, 0, wide + 3 * narrow), (1, wide + wide - cut, wide + full - cut)),
        ),
        "collect_third",
    )
    near2, far2, deep2 = slot(*zip((flip_near, flip_far, next_plane), sends))
    rows = (mlp_in, flip_core(mlp_in))
    acc = accumulate(
        rows,
        (shard, near, far, deep, near1, far1, deep1),
        [runs(i, 0, main) for i in range(7)] + list(split_runs((4, wide), (5, wide), main)),
        (),
        jnp.float32,
        "accumulate_second",
    )
    near2, far2, deep2 = together(near2, far2, deep2)

    held = 2 * main // 3
    deep3_main, line = collect(
        (far2, deep2),
        (
            ((1, 0, wide),),
            ((1, wide, wide + 4 * narrow), (0, 2 * wide - cut - main, 2 * wide - cut - main + held)),
        ),
        "collect_fourth",
    )
    near3, far3, deep3 = slot((flip_near, deep3_main), (flip_far, deep3_main), (next_plane, line))
    acc = accumulate(
        rows,
        (shard, near, far, far1, deep1, near2, far2, deep2),
        [runs(i, 0, main) for i in (5, 6, 7)]
        + list(split_runs((5, wide), (6, wide), main))
        + [runs(i, wide, edge) for i in (0, 1, 2)]
        + [runs(3, wide + wide - cut, edge)]
        + [runs(4, wide + k * narrow, edge) for k in range(3)]
        + [runs(7, wide + k * narrow, edge) for k in range(4)],
        tuple(acc),
        jnp.float32,
        "accumulate_third",
    )
    near3, far3, deep3, *acc = together(near3, far3, deep3, *acc)

    two = 2 * main
    sends = collect(
        (near2, far2, near3, far3, deep3),
        (
            ((1, 0, main), (1, two + held, wide), (3, 0, main)),
            ((0, main, two), (2, main, two), (2, two + held, wide)),
            ((4, 3 * narrow, 4 * narrow + held),),
        ),
        "collect_fifth",
    )
    near4, far4, deep4 = slot(*zip((flip_near, flip_far, next_plane), sends))
    acc = accumulate(
        rows,
        (near3, far3, deep3),
        [runs(0, 0, main), runs(1, 0, main)] + [runs(2, k * narrow, edge) for k in range(4)],
        tuple(acc),
        jnp.float32,
        "accumulate_fourth",
    )
    weights = (near4, far4, deep3, deep4)
    line, then = 4 * narrow, two - held
    last = [
        ((0, 0, held), (1, 0, held), (2, line, line + held)),
        ((0, held, main), (1, held, main), (0, main, then)),
        ((0, then, then + held), (1, main, main + held), (3, narrow, narrow + held)),
        ((0, then + held, then + main), (1, main + held, two), (1, two, two + main - held)),
        runs(3, 0, edge),
    ]
    (given,) = accumulate(rows[1:], weights, last, acc[1:], jnp.bfloat16, "finish_other")
    (kept,) = accumulate(
        rows[:1], weights, last, acc[:1], jnp.float32, "finish_own", residual=mixed_rows
    )
    result = kernel_call(
        functools.partial(final_body, 64),
        "final",
        like(local_len, model, jnp.bfloat16),
        valid_count,
        kept,
        flip_core(given),
        specs=[pl.BlockSpec(memory_space=pltpu.SMEM)] + vmem(2),
    )
    return (
        result[None],
        end_state.reshape((1, 1) + end_state.shape[:1] + end_state.shape[-1:]),
        end_norm[None, None],
    )


def solution(mesh):
    return jax.shard_map(
        local,
        mesh=mesh,
        in_specs=(
            P("req", "seq", None),
            P("req"),
            P("req", "seq", None),
            P(),
            P(),
            P(),
            P(),
            P(),
            P(),
            P(),
            P(None, "req"),
            P(None, "req"),
            P(None, "req"),
        ),
        out_specs=(P("req", "seq", None), P("req", "seq", None, None), P("req", "seq", None, None)),
        check_vma=False,
    )
```

```python
import functools

import jax
import jax.numpy as jnp
from jax import lax
from jax.experimental import pallas as pl
from jax.experimental.pallas import tpu as pltpu
from jax.sharding import PartitionSpec as P


def from_behind(array, axis, by):
    count = lax.axis_size(axis)
    pairs = [(i, i + by) for i in range(count) if 0 <= i + by < count]
    return lax.ppermute(array, axis, pairs)


def entering(array, axis, combine, identity):
    count, here = (lax.axis_size(axis), lax.axis_index(axis))
    everything = jax.tree.map(
        lambda part, kind: lax.all_gather(part.astype(kind), axis),
        array,
        (jnp.bfloat16, jnp.bfloat16, jnp.bfloat16),
    )
    start = jax.tree.map(
        lambda part, zero: jnp.broadcast_to(jnp.asarray(zero, part.dtype), part.shape),
        array,
        identity,
    )

    def hop(k, before):
        reached = k < here
        new = combine(
            before, jax.tree.map(lambda part, own: part[k].astype(own.dtype), everything, array)
        )
        return jax.tree.map(lambda a, b: jnp.where(reached, a, b), new, before)

    return lax.fori_loop(0, count, hop, start)


def features(vectors):
    constant = jnp.ones(vectors.shape[:-1] + (1,), jnp.float32)
    width = vectors.shape[-1]
    squares = (vectors[..., :, None] * vectors[..., None, :]).reshape(
        vectors.shape[:-1] + (width * width,)
    )
    return jnp.concatenate([constant, vectors, squares * 0.5**0.5], axis=-1)


def carry_in(valid_mask, decays, queries, numerator, denominator, flat_memory, key_sum):
    local_len = numerator.shape[0]
    feat_len, head_count = key_sum.shape
    value_len = flat_memory.shape[1] // head_count
    feat_in = queries.shape[1] // head_count
    decay_rate = jnp.where(valid_mask[:, None] > 0, decays, 0.0)
    span_decay = jnp.sum(decay_rate, axis=0)

    def merge_states(earlier, later):
        factor = jnp.exp(later[0])
        return (
            earlier[0] + later[0],
            earlier[1] * jnp.repeat(factor, value_len)[None, :] + later[1],
            earlier[2] * factor[None, :] + later[2],
        )

    neutral = (jnp.zeros_like(span_decay), jnp.zeros_like(flat_memory), jnp.zeros_like(key_sum))
    carried = entering((span_decay, flat_memory, key_sum), "seq", merge_states, neutral)
    prior_memory = carried[1]
    prior_keys = carried[2]
    highest = lax.Precision.HIGHEST
    growth = jnp.exp(jnp.cumsum(decay_rate, axis=0))
    query_feat = features(queries.astype(jnp.float32).reshape(local_len, head_count, feat_in))
    added = jnp.einsum(
        "thf,fhv->thv",
        query_feat,
        prior_memory.reshape(feat_len, head_count, value_len),
        precision=highest,
    )
    numerator = numerator + (added * growth[:, :, None]).reshape(local_len, -1)
    denominator = (
        denominator + jnp.einsum("thf,fh->th", query_feat, prior_keys, precision=highest) * growth
    )
    span_factor = jnp.exp(span_decay)
    end_state = prior_memory * jnp.repeat(span_factor, value_len)[None, :] + flat_memory
    end_norm = prior_keys * span_factor[None, :] + key_sum
    return numerator, denominator, end_state, end_norm


def permute(array, target):
    count = lax.axis_size("req")
    return lax.ppermute(array, "req", [(i, target(i)) for i in range(count)])


def flip_core(array):
    return permute(array, lambda i: i ^ 1)


def flip_near(array):
    return permute(array, lambda i: i ^ 2)


def flip_far(array):
    return permute(array, lambda i: i ^ 4)


def next_plane(array):
    return permute(array, lambda i: i ^ (8 if i // 8 in (1, 2) else 16))


def together(*arrays):
    return lax.optimization_barrier(arrays)


def slot(*sends):
    operands = together(*[array for _, array in sends])
    return together(*[send(array) for (send, _), array in zip(sends, operands)])


def vmem(count):
    return [pl.BlockSpec(memory_space=pltpu.VMEM)] * count


def kernel_call(body, name, out_shape, *operands, scratch=(), aliases=None, specs=None, mib=24):
    many = isinstance(out_shape, tuple)
    return pl.pallas_call(
        body,
        out_shape=out_shape,
        in_specs=specs or vmem(len(operands)),
        out_specs=tuple(vmem(len(out_shape))) if many else vmem(1)[0],
        scratch_shapes=list(scratch),
        input_output_aliases=aliases or {},
        compiler_params=pltpu.CompilerParams(vmem_limit_bytes=mib * 1024 * 1024),
        cost_estimate=pl.CostEstimate(flops=1000, bytes_accessed=1000, transcendentals=0),
        name=name,
    )(*operands)


def like(rows, columns, dtype):
    return jax.ShapeDtypeStruct((rows, columns), dtype)


NT = (((1,), (1,)), ((), ()))


def unit_rows(rows, gain):
    factor = lax.rsqrt(jnp.mean(rows * rows, axis=-1, keepdims=True) + 1e-05)
    return (rows * factor * gain).astype(jnp.bfloat16).astype(jnp.float32)


def project_body(
    step,
    scale,
    rows_ref,
    edge_ref,
    gain_ref,
    conv_ref,
    query_ref,
    key_ref,
    value_ref,
    queries_ref,
    keys_ref,
    values_ref,
    normed,
    gated,
):
    gain = gain_ref[...]
    count = rows_ref.shape[0]
    lead = edge_ref.shape[0]
    taps = conv_ref.shape[0]
    normed[:lead] = unit_rows(edge_ref[...].astype(jnp.float32), gain)

    @pl.loop(0, count // step)
    def _(block):
        at = pl.multiple_of(block * step, step)
        rows = rows_ref[pl.ds(at, step), :].astype(jnp.float32)
        normed[pl.ds(lead + at, step), :] = unit_rows(rows, gain)

    @pl.loop(0, count // step)
    def _(block):
        at = pl.multiple_of(block * step, step)
        window = normed[pl.ds(at, step + lead), :]
        here = window[lead:]
        total = conv_ref[0:1] * here
        for tap in range(1, taps):
            total = total + conv_ref[tap : tap + 1] * window[lead - tap : lead - tap + step]
        gated[pl.ds(at, step), :] = (total * jax.nn.sigmoid(here)).astype(jnp.bfloat16)

    rows = gated[...]
    for weight_ref, out_ref, factor in (
        (query_ref, queries_ref, scale),
        (key_ref, keys_ref, scale),
        (value_ref, values_ref, None),
    ):
        product = jnp.dot(rows, weight_ref[...], preferred_element_type=jnp.float32)
        if factor is not None:
            product = product * factor
        out_ref[...] = product.astype(jnp.bfloat16)


def project(rows, edge, mix_gain, conv_weight, query_weight, key_weight, value_weight, scale):
    count, width = rows.shape
    step = 32
    return kernel_call(
        functools.partial(project_body, step, scale),
        "project",
        tuple(like(count, w.shape[1], jnp.bfloat16) for w in (query_weight, key_weight, value_weight)),
        rows,
        edge,
        mix_gain[None],
        conv_weight,
        query_weight,
        key_weight,
        value_weight,
        scratch=(
            pltpu.VMEM((count + edge.shape[0], width), jnp.float32),
            pltpu.VMEM((count, width), jnp.bfloat16),
        ),
    )


def attend_body(
    feat_in,
    value_len,
    count_ref,
    rate_ref,
    queries_ref,
    keys_ref,
    values_ref,
    numer_ref,
    denom_ref,
    state_ref,
    norm_ref,
    turned,
    total,
    norms,
):
    heads, count = rate_ref.shape
    columns = values_ref.shape[1]
    lane = lax.broadcasted_iota(jnp.int32, (count, count), 1)
    row = lax.broadcasted_iota(jnp.int32, (count, count), 0)
    valid = (lane[:1] < count_ref[0]).astype(jnp.float32)
    rate = jnp.where(valid > 0, rate_ref[...], 0.0)
    upto = (row <= lane).astype(jnp.float32)
    across = jnp.dot(
        rate, upto, precision=lax.Precision.HIGHEST, preferred_element_type=jnp.float32
    )
    down = across.T
    closing = across[:, count - 1 : count]
    fading = jnp.exp(closing - across) * valid
    causal = row >= lane
    keys = keys_ref[...]
    turned[...] = keys.astype(jnp.float32).T
    owner = lax.broadcasted_iota(jnp.int32, queries_ref.shape, 1)
    spare = lax.broadcasted_iota(jnp.int32, (8, count), 0) == 0
    head_lane = lax.broadcasted_iota(jnp.int32, (count, 128), 1)
    numer_ref[...] = jnp.zeros(numer_ref.shape, jnp.float32)
    total[...] = jnp.zeros(total.shape, jnp.float32)
    norms[...] = jnp.zeros(norms.shape, jnp.float32)
    norm_total = jnp.zeros((total.shape[0], 128), jnp.float32)
    denominators = jnp.zeros((count, 128), jnp.float32)
    for h in range(heads):
        low = min(h * value_len // 128 * 128, max(columns - 256, 0))
        high = min(low + 256, columns)
        mine = lax.broadcasted_iota(jnp.int32, (count, high - low), 1) + low
        mine = (mine >= h * value_len) & (mine < (h + 1) * value_len)
        values = jnp.where(mine, values_ref[:, low:high].astype(jnp.float32), 0.0)
        values = values.astype(jnp.bfloat16)
        asks = (owner >= h * feat_in) & (owner < (h + 1) * feat_in)
        queries = jnp.where(asks, queries_ref[...].astype(jnp.float32), 0.0)
        scores = lax.dot_general(
            queries.astype(jnp.bfloat16), keys, NT, preferred_element_type=jnp.float32
        )
        gap = down[:, h : h + 1] - across[h : h + 1]
        weights = jnp.where(causal, jnp.exp(jnp.minimum(gap, 0.0)) * valid, 0.0)
        weights = weights * (1.0 + scores + 0.5 * scores * scores)
        numer_ref[:, low:high] += jnp.dot(
            weights.astype(jnp.bfloat16), values, preferred_element_type=jnp.float32
        )
        sums = jnp.sum(weights, axis=1, keepdims=True)
        denominators = jnp.where(head_lane == h, sums, denominators)
        own = turned[h * feat_in : (h + 1) * feat_in]
        fade = fading[h : h + 1]
        faded = own * fade
        scaled = faded * 0.5**0.5
        parts = [own[i : i + 1] * scaled for i in range(feat_in)]
        parts += [faded, jnp.where(spare, fade, 0.0)]
        feats = jnp.concatenate(parts, axis=0).astype(jnp.bfloat16)
        total[:, low:high] += jnp.dot(feats, values, preferred_element_type=jnp.float32)
        mark = (head_lane == h).astype(jnp.bfloat16)
        norm_total = norm_total + jnp.dot(feats, mark, preferred_element_type=jnp.float32)
    denom_ref[...] = denominators[:, :heads]
    pairs = feat_in * feat_in
    state_ref[0] = total[pairs + feat_in : pairs + feat_in + 1, :]
    for f in range(feat_in):
        state_ref[1 + f] = total[pairs + f : pairs + f + 1, :]

    @pl.loop(0, pairs // 8)
    def _(block):
        for k in range(8):
            f = block * 8 + k
            state_ref[1 + feat_in + f] = total[pl.ds(f, 1), :]

    norms[0:1, :] = norm_total[pairs + feat_in : pairs + feat_in + 1]
    norms[1 : 1 + feat_in, :] = norm_total[pairs : pairs + feat_in]
    norms[1 + feat_in : 1 + feat_in + pairs, :] = norm_total[:pairs]
    norm_ref[...] = norms[...].T[:heads, : 1 + feat_in + pairs]


def attend(valid_count, rate, queries, keys, values, feat_in, value_len):
    heads, count = rate.shape
    columns = values.shape[1]
    feat_len = 1 + feat_in + feat_in * feat_in
    padded = feat_in * feat_in + feat_in + 8
    return kernel_call(
        functools.partial(attend_body, feat_in, value_len),
        "attend",
        (
            like(count, columns, jnp.float32),
            like(count, heads, jnp.float32),
            jax.ShapeDtypeStruct((feat_len, 1, columns), jnp.float32),
            like(heads, feat_len, jnp.float32),
        ),
        valid_count,
        rate,
        queries,
        keys,
        values,
        specs=[pl.BlockSpec(memory_space=pltpu.SMEM)] + vmem(4),
        scratch=(
            pltpu.VMEM((queries.shape[1], count), jnp.float32),
            pltpu.VMEM((padded, columns), jnp.float32),
            pltpu.VMEM(((feat_len + 127) // 128 * 128, 128), jnp.float32),
        ),
    )


def mix_body(
    value_len, step, numer_ref, denom_ref, rows_ref, out_ref, gain_ref, mixed_ref, mlp_ref, sums
):
    count, columns = numer_ref.shape
    heads = denom_ref.shape[1]
    column = lax.broadcasted_iota(jnp.int32, (1, columns), 1)
    inverse = 1.0 / denom_ref[...]
    spread = jnp.zeros((count, columns), jnp.float32)
    for h in range(heads):
        here = (column >= h * value_len) & (column < (h + 1) * value_len)
        spread = jnp.where(here, inverse[:, h : h + 1], spread)
    attended = (numer_ref[...] * spread).astype(jnp.bfloat16)
    sums[...] = jnp.dot(attended, out_ref[...], preferred_element_type=jnp.float32)
    gain = gain_ref[...]

    @pl.loop(0, count // step)
    def _(block):
        at = pl.ds(pl.multiple_of(block * step, step), step)
        mixed = (rows_ref[at, :].astype(jnp.float32) + sums[at, :]).astype(jnp.bfloat16)
        mixed_ref[at, :] = mixed
        mlp_ref[at, :] = unit_rows(mixed.astype(jnp.float32), gain).astype(jnp.bfloat16)


def mix(numer, denom, rows, out_weight, mlp_gain, value_len):
    count, width = rows.shape
    shape = like(count, width, jnp.bfloat16)
    return kernel_call(
        functools.partial(mix_body, value_len, 32),
        "mix",
        (shape, shape),
        numer,
        denom,
        rows,
        out_weight,
        mlp_gain[None],
        scratch=(pltpu.VMEM((count, width), jnp.float32),),
    )


def swiglu_terms(rows, gate_rows, up_rows, down_rows):
    gate_act = lax.dot_general(rows, gate_rows, NT, preferred_element_type=jnp.float32)
    up_act = lax.dot_general(rows, up_rows, NT, preferred_element_type=jnp.float32)
    hidden_units = (gate_act * jax.nn.sigmoid(gate_act) * up_act).astype(jnp.bfloat16)
    return jnp.dot(hidden_units, down_rows, preferred_element_type=jnp.float32)


def on_grid(run):
    return all(low % 16 == 0 and high % 16 == 0 for _, low, high in run)


def read_units(refs, units):
    parts = []
    for k in range(3):
        rows = [refs[run[k][0]][run[k][1] : run[k][2]] for run in units if on_grid(run)]
        rest = [
            refs[run[k][0]][...].astype(jnp.float32)[run[k][1] : run[k][2]]
            for run in units
            if not on_grid(run)
        ]
        if rest:
            rows.append(jnp.concatenate(rest, axis=0).astype(jnp.bfloat16))
        parts.append(jnp.concatenate(rows, axis=0))
    return parts


def accumulate_body(units, n_weights, n_rows, n_acc, residual, *refs):
    weights = refs[:n_weights]
    rows = refs[n_weights : n_weights + n_rows]
    acc = refs[n_weights + n_rows : n_weights + n_rows + n_acc]
    parts = read_units(weights, units)
    for k, rows_ref in enumerate(rows):
        out_ref = refs[len(refs) - n_rows + k]
        terms = swiglu_terms(rows_ref[...], *parts)
        if n_acc:
            terms = terms + acc[k][...]
        if residual:
            terms = terms + refs[n_weights + n_rows + n_acc][...].astype(jnp.float32)
        out_ref[...] = terms.astype(out_ref.dtype)


def accumulate(rows, weights, units, acc, dtype, name, residual=None):
    shapes = tuple(like(*array.shape, dtype) for array in rows)
    start = len(weights) + len(rows)
    aliases = {start + k: k for k in range(len(acc))} if dtype == jnp.float32 else {}
    extra = () if residual is None else (residual,)
    body = functools.partial(
        accumulate_body, tuple(units), len(weights), len(rows), len(acc), bool(extra)
    )
    return kernel_call(body, name, shapes, *weights, *rows, *acc, *extra, aliases=aliases)


def runs(which, low, size):
    return tuple((which, low + k * size, low + (k + 1) * size) for k in range(3))


def split_runs(first, second, main):
    (i, at), (j, then) = first, second
    held = 2 * main // 3
    rest = main - held
    return (
        ((i, at, at + held), (i, at + main, at + main + held), (j, then + rest, then + main)),
        ((i, at + held, at + main), (j, then, then + rest), (j, then + main, then + rest + main)),
    )


def collect_body(plans, *refs):
    outs = refs[len(refs) - len(plans) :]
    for out_ref, plan in zip(outs, plans):
        rows = [refs[i][...].astype(jnp.float32)[low:high] for i, low, high in plan]
        out_ref[...] = jnp.concatenate(rows, axis=0).astype(jnp.bfloat16)


def collect(arrays, plans, name):
    columns = arrays[0].shape[1]
    shapes = tuple(like(sum(h - l for _, l, h in plan), columns, jnp.bfloat16) for plan in plans)
    return kernel_call(functools.partial(collect_body, plans), name, shapes, *arrays)


def shard_body(main, gate_ref, up_ref, down_ref, shard_ref, main_ref, *rest):
    buffers, sems = rest[:3], rest[3]
    copies = [
        pltpu.make_async_copy(source, buffer, sems.at[k])
        for k, (source, buffer) in enumerate(zip((gate_ref, up_ref, down_ref), buffers))
    ]
    for copy in copies:
        copy.start()
    for copy in copies:
        copy.wait()
    arrays = [buffer[...].astype(jnp.float32) for buffer in buffers]
    tops = [array[:main] for array in arrays]
    ends = [array[main:] for array in arrays]
    shard_ref[...] = jnp.concatenate(tops + ends, axis=0).astype(jnp.bfloat16)
    main_ref[...] = jnp.concatenate(tops, axis=0).astype(jnp.bfloat16)


def final_body(step, count_ref, kept_ref, given_ref, out_ref, done, sems):
    copies = []
    for block in range(kept_ref.shape[0] // step):
        first = block * step
        at = pl.ds(first, step)
        total = kept_ref[at, :] + given_ref[at, :].astype(jnp.float32)
        row = lax.broadcasted_iota(jnp.int32, total.shape, 0) + first
        done[at, :] = jnp.where(row < count_ref[0], total, 0.0).astype(done.dtype)
        copies.append(pltpu.make_async_copy(done.at[at, :], out_ref.at[at, :], sems.at[block]))
        copies[-1].start()
    for copy in copies:
        copy.wait()


def local(
    hidden_in,
    lengths,
    log_decay,
    mix_gain,
    conv_weight,
    query_weight,
    key_weight,
    value_weight,
    out_weight,
    mlp_gain,
    gate_weight,
    up_weight,
    down_weight,
):
    local_len = hidden_in.shape[1]
    rows_in = hidden_in[0]
    decays = log_decay[0]
    head_count = log_decay.shape[2]
    value_len = value_weight.shape[1] // head_count
    feat_in = query_weight.shape[1] // head_count
    feature_scale = feat_in ** (-0.25)
    valid_count = lengths - lax.axis_index("seq") * local_len
    spans = lax.axis_size("seq")
    units, model = gate_weight.shape[1], gate_weight.shape[0]
    edge = units // 7
    main = units - edge
    wide = 3 * main
    full = 3 * units
    narrow = full - wide
    cut = main + 2 * main // 3

    shard, shard_main = kernel_call(
        functools.partial(shard_body, main),
        "shard",
        (like(full, model, jnp.bfloat16), like(wide, model, jnp.bfloat16)),
        gate_weight.T,
        up_weight.T,
        down_weight.T,
        specs=[pl.BlockSpec(memory_space=pl.ANY)] * 3,
        scratch=[pltpu.VMEM((units, model), jnp.bfloat16)] * 3 + [pltpu.SemaphoreType.DMA((3,))],
        mib=56,
    )
    near, far, deep = slot((flip_near, shard), (flip_far, shard), (next_plane, shard_main))

    lead = 16
    if spans > 1:
        edge_in = from_behind(rows_in[local_len - lead :], "seq", 1)
    else:
        edge_in = jnp.zeros((lead, model), jnp.bfloat16)
    queries, key_rows, values = project(
        rows_in, edge_in, mix_gain, conv_weight, query_weight, key_weight, value_weight, feature_scale
    )
    near, far, deep, queries, key_rows, values = together(
        near, far, deep, queries, key_rows, values
    )

    sends = collect(
        (shard, near, far, deep),
        (
            ((3, 0, wide), (2, 0, cut)),
            ((3, 0, wide), (1, cut, full)),
            ((3, 0, wide), (0, wide, full), (1, wide, full), (2, wide, full)),
        ),
        "collect_second",
    )
    near1, far1, deep1 = slot(*zip((flip_near, flip_far, next_plane), sends))

    numerator, denominator, end_state, end_norm = attend(
        valid_count, log_decay[0].T, queries, key_rows, values, feat_in, value_len
    )
    if spans > 1:
        positions = jnp.arange(local_len, dtype=jnp.int32)
        numerator, denominator, end_state, end_norm = carry_in(
            (positions < valid_count).astype(jnp.float32),
            decays,
            queries,
            numerator,
            denominator,
            end_state[:, 0],
            end_norm.T,
        )
    else:
        end_norm = end_norm.T
    mixed_rows, mlp_in = mix(numerator, denominator, rows_in, out_weight, mlp_gain, value_len)
    near1, far1, deep1, mixed_rows, mlp_in, end_state, end_norm = together(
        near1, far1, deep1, mixed_rows, mlp_in, end_state, end_norm
    )

    middle = local_len // 2
    *sends, top, end = collect(
        (near1, far1, deep1, mlp_in),
        (
            ((2, 0, wide), (1, 0, cut)),
            ((2, 0, wide), (0, cut, wide)),
            ((2, 0, wide + 3 * narrow), (1, wide + wide - cut, wide + full - cut)),
            ((3, 0, middle),),
            ((3, middle, local_len),),
        ),
        "collect_third",
    )
    near2, far2, deep2 = slot(*zip((flip_near, flip_far, next_plane), sends))
    (other_in,) = collect(
        (flip_core(top), flip_core(end)),
        (((0, 0, middle), (1, 0, local_len - middle)),),
        "collect_rows",
    )
    rows = (mlp_in, other_in)
    acc = accumulate(
        rows,
        (shard, near, far, deep, near1, far1, deep1),
        [runs(i, 0, main) for i in range(7)] + list(split_runs((4, wide), (5, wide), main)),
        (),
        jnp.float32,
        "accumulate_second",
    )
    near2, far2, deep2, *acc = together(near2, far2, deep2, *acc)

    two = 2 * main
    sends = collect(
        (near2, far2, deep2),
        (
            ((2, main, wide),),
            ((2, 0, main), (2, two, wide)),
            ((2, wide, wide + 4 * narrow), (1, 2 * wide - cut - main, 2 * wide - cut)),
            ((2, 0, main), (1, 0, main)),
            ((2, main, two), (0, main, two)),
        ),
        "collect_fourth",
    )
    sends = together(*sends)
    near3, far3, deep3 = flip_near(sends[0]), flip_far(sends[1]), next_plane(sends[2])
    near3_more, far3_more = flip_near(sends[3]), flip_far(sends[4])
    acc = accumulate(
        rows,
        (shard, near, far, far1, deep1, near2, far2, deep2),
        [runs(i, 0, main) for i in (5, 6, 7)]
        + list(split_runs((5, wide), (6, wide), main))
        + [runs(i, wide, edge) for i in (0, 1, 2)]
        + [runs(3, wide + wide - cut, edge)]
        + [runs(4, wide + k * narrow, edge) for k in range(3)]
        + [runs(7, wide + k * narrow, edge) for k in range(4)],
        tuple(acc),
        jnp.float32,
        "accumulate_third",
    )
    near3, far3, deep3, *acc = together(near3, far3, deep3, *acc)

    sends = collect(
        (near3, far3, deep3),
        (
            ((1, 0, main),),
            ((0, 0, main),),
            ((2, 3 * narrow, 4 * narrow + main),),
        ),
        "collect_fifth",
    )
    near4, far4, deep4 = slot(*zip((flip_near, flip_far, next_plane), sends))
    line = 4 * narrow
    weights = (near3, near3_more, far3, far3_more, deep3, near4, far4, deep4)
    last = [
        ((1, 0, main), (0, 0, main), (0, main, two)),
        ((2, 0, main), (3, 0, main), (2, main, two)),
        ((1, main, two), (3, main, two), (4, line, line + main)),
        ((5, 0, main), (6, 0, main), (7, narrow, narrow + main)),
    ]
    last += [runs(4, k * narrow, edge) for k in range(4)] + [runs(7, 0, edge)]
    (given,) = accumulate(rows[1:], weights, last, acc[1:], jnp.bfloat16, "finish_other")
    (kept,) = accumulate(
        rows[:1], weights, last, acc[:1], jnp.float32, "finish_own", residual=mixed_rows
    )
    result = pl.pallas_call(
        functools.partial(final_body, 64),
        out_shape=like(local_len, model, jnp.bfloat16),
        in_specs=[pl.BlockSpec(memory_space=pltpu.SMEM)] + vmem(2),
        out_specs=pl.BlockSpec(memory_space=pl.ANY),
        scratch_shapes=[
            pltpu.VMEM((local_len, model), jnp.bfloat16),
            pltpu.SemaphoreType.DMA((local_len // 64,)),
        ],
        compiler_params=pltpu.CompilerParams(vmem_limit_bytes=24 * 1024 * 1024),
        name="final",
    )(valid_count, kept, flip_core(given))
    return (
        result[None],
        end_state.reshape((1, 1) + end_state.shape[:1] + end_state.shape[-1:]),
        end_norm[None, None],
    )


def solution(mesh):
    return jax.shard_map(
        local,
        mesh=mesh,
        in_specs=(
            P("req", "seq", None),
            P("req"),
            P("req", "seq", None),
            P(),
            P(),
            P(),
            P(),
            P(),
            P(),
            P(),
            P(None, "req"),
            P(None, "req"),
            P(None, "req"),
        ),
        out_specs=(P("req", "seq", None), P("req", "seq", None, None), P("req", "seq", None, None)),
        check_vma=False,
    )
```

```python
import functools

import jax
import jax.numpy as jnp
from jax import lax
from jax.experimental import pallas as pl
from jax.experimental.pallas import tpu as pltpu
from jax.sharding import PartitionSpec as P


def from_behind(array, axis, by):
    count = lax.axis_size(axis)
    pairs = [(i, i + by) for i in range(count) if 0 <= i + by < count]
    return lax.ppermute(array, axis, pairs)


def entering(array, axis, combine, identity):
    count, here = (lax.axis_size(axis), lax.axis_index(axis))
    everything = jax.tree.map(
        lambda part, kind: lax.all_gather(part.astype(kind), axis),
        array,
        (jnp.bfloat16, jnp.bfloat16, jnp.bfloat16),
    )
    start = jax.tree.map(
        lambda part, zero: jnp.broadcast_to(jnp.asarray(zero, part.dtype), part.shape),
        array,
        identity,
    )

    def hop(k, before):
        reached = k < here
        new = combine(
            before, jax.tree.map(lambda part, own: part[k].astype(own.dtype), everything, array)
        )
        return jax.tree.map(lambda a, b: jnp.where(reached, a, b), new, before)

    return lax.fori_loop(0, count, hop, start)


def features(vectors):
    constant = jnp.ones(vectors.shape[:-1] + (1,), jnp.float32)
    width = vectors.shape[-1]
    squares = (vectors[..., :, None] * vectors[..., None, :]).reshape(
        vectors.shape[:-1] + (width * width,)
    )
    return jnp.concatenate([constant, vectors, squares * 0.5**0.5], axis=-1)


def carry_in(valid_mask, decays, queries, numerator, denominator, flat_memory, key_sum):
    local_len = numerator.shape[0]
    feat_len, head_count = key_sum.shape
    value_len = flat_memory.shape[1] // head_count
    feat_in = queries.shape[1] // head_count
    decay_rate = jnp.where(valid_mask[:, None] > 0, decays, 0.0)
    span_decay = jnp.sum(decay_rate, axis=0)

    def merge_states(earlier, later):
        factor = jnp.exp(later[0])
        return (
            earlier[0] + later[0],
            earlier[1] * jnp.repeat(factor, value_len)[None, :] + later[1],
            earlier[2] * factor[None, :] + later[2],
        )

    neutral = (jnp.zeros_like(span_decay), jnp.zeros_like(flat_memory), jnp.zeros_like(key_sum))
    carried = entering((span_decay, flat_memory, key_sum), "seq", merge_states, neutral)
    prior_memory = carried[1]
    prior_keys = carried[2]
    highest = lax.Precision.HIGHEST
    growth = jnp.exp(jnp.cumsum(decay_rate, axis=0))
    query_feat = features(queries.astype(jnp.float32).reshape(local_len, head_count, feat_in))
    added = jnp.einsum(
        "thf,fhv->thv",
        query_feat,
        prior_memory.reshape(feat_len, head_count, value_len),
        precision=highest,
    )
    numerator = numerator + (added * growth[:, :, None]).reshape(local_len, -1)
    denominator = (
        denominator + jnp.einsum("thf,fh->th", query_feat, prior_keys, precision=highest) * growth
    )
    span_factor = jnp.exp(span_decay)
    end_state = prior_memory * jnp.repeat(span_factor, value_len)[None, :] + flat_memory
    end_norm = prior_keys * span_factor[None, :] + key_sum
    return numerator, denominator, end_state, end_norm


def permute(array, target):
    count = lax.axis_size("req")
    return lax.ppermute(array, "req", [(i, target(i)) for i in range(count)])


def flip_core(array):
    return permute(array, lambda i: i ^ 1)


def flip_near(array):
    return permute(array, lambda i: i ^ 2)


def flip_far(array):
    return permute(array, lambda i: i ^ 4)


def next_plane(array):
    return permute(array, lambda i: i ^ (8 if i // 8 in (1, 2) else 16))


def together(*arrays):
    return lax.optimization_barrier(arrays)


def slot(*sends):
    operands = together(*[array for _, array in sends])
    return together(*[send(array) for (send, _), array in zip(sends, operands)])


def vmem(count):
    return [pl.BlockSpec(memory_space=pltpu.VMEM)] * count


def kernel_call(body, name, out_shape, *operands, scratch=(), aliases=None, specs=None, mib=24):
    many = isinstance(out_shape, tuple)
    return pl.pallas_call(
        body,
        out_shape=out_shape,
        in_specs=specs or vmem(len(operands)),
        out_specs=tuple(vmem(len(out_shape))) if many else vmem(1)[0],
        scratch_shapes=list(scratch),
        input_output_aliases=aliases or {},
        compiler_params=pltpu.CompilerParams(vmem_limit_bytes=mib * 1024 * 1024),
        cost_estimate=pl.CostEstimate(flops=1000, bytes_accessed=1000, transcendentals=0),
        name=name,
    )(*operands)


def like(rows, columns, dtype):
    return jax.ShapeDtypeStruct((rows, columns), dtype)


NT = (((1,), (1,)), ((), ()))


def unit_rows(rows, gain):
    factor = lax.rsqrt(jnp.mean(rows * rows, axis=-1, keepdims=True) + 1e-05)
    return (rows * factor * gain).astype(jnp.bfloat16).astype(jnp.float32)


def project_body(
    step,
    scale,
    rows_ref,
    edge_ref,
    gain_ref,
    conv_ref,
    query_ref,
    key_ref,
    value_ref,
    queries_ref,
    keys_ref,
    values_ref,
    normed,
    gated,
):
    gain = gain_ref[...]
    count = rows_ref.shape[0]
    lead = edge_ref.shape[0]
    taps = conv_ref.shape[0]
    normed[:lead] = unit_rows(edge_ref[...].astype(jnp.float32), gain)

    @pl.loop(0, count // step)
    def _(block):
        at = pl.multiple_of(block * step, step)
        rows = rows_ref[pl.ds(at, step), :].astype(jnp.float32)
        normed[pl.ds(lead + at, step), :] = unit_rows(rows, gain)

    @pl.loop(0, count // step)
    def _(block):
        at = pl.multiple_of(block * step, step)
        window = normed[pl.ds(at, step + lead), :]
        here = window[lead:]
        total = conv_ref[0:1] * here
        for tap in range(1, taps):
            total = total + conv_ref[tap : tap + 1] * window[lead - tap : lead - tap + step]
        gated[pl.ds(at, step), :] = (total * jax.nn.sigmoid(here)).astype(jnp.bfloat16)

    rows = gated[...]
    for weight_ref, out_ref, factor in (
        (query_ref, queries_ref, scale),
        (key_ref, keys_ref, scale),
        (value_ref, values_ref, None),
    ):
        product = jnp.dot(rows, weight_ref[...], preferred_element_type=jnp.float32)
        if factor is not None:
            product = product * factor
        out_ref[...] = product.astype(jnp.bfloat16)


def project(rows, edge, mix_gain, conv_weight, query_weight, key_weight, value_weight, scale):
    count, width = rows.shape
    step = 32
    return kernel_call(
        functools.partial(project_body, step, scale),
        "project",
        tuple(like(count, w.shape[1], jnp.bfloat16) for w in (query_weight, key_weight, value_weight)),
        rows,
        edge,
        mix_gain[None],
        conv_weight,
        query_weight,
        key_weight,
        value_weight,
        scratch=(
            pltpu.VMEM((count + edge.shape[0], width), jnp.float32),
            pltpu.VMEM((count, width), jnp.bfloat16),
        ),
    )


def attend_body(
    feat_in,
    value_len,
    count_ref,
    rate_ref,
    queries_ref,
    keys_ref,
    values_ref,
    numer_ref,
    denom_ref,
    state_ref,
    norm_ref,
    turned,
    total,
    norms,
):
    heads, count = rate_ref.shape
    columns = values_ref.shape[1]
    lane = lax.broadcasted_iota(jnp.int32, (count, count), 1)
    row = lax.broadcasted_iota(jnp.int32, (count, count), 0)
    valid = (lane[:1] < count_ref[0]).astype(jnp.float32)
    rate = jnp.where(valid > 0, rate_ref[...], 0.0)
    upto = (row <= lane).astype(jnp.float32)
    across = jnp.dot(
        rate, upto, precision=lax.Precision.HIGHEST, preferred_element_type=jnp.float32
    )
    down = across.T
    closing = across[:, count - 1 : count]
    fading = jnp.exp(closing - across) * valid
    causal = row >= lane
    keys = keys_ref[...]
    turned[...] = keys.astype(jnp.float32).T
    owner = lax.broadcasted_iota(jnp.int32, queries_ref.shape, 1)
    spare = lax.broadcasted_iota(jnp.int32, (8, count), 0) == 0
    head_lane = lax.broadcasted_iota(jnp.int32, (count, 128), 1)
    numer_ref[...] = jnp.zeros(numer_ref.shape, jnp.float32)
    total[...] = jnp.zeros(total.shape, jnp.float32)
    norms[...] = jnp.zeros(norms.shape, jnp.float32)
    norm_total = jnp.zeros((total.shape[0], 128), jnp.float32)
    denominators = jnp.zeros((count, 128), jnp.float32)
    for h in range(heads):
        low = min(h * value_len // 128 * 128, max(columns - 256, 0))
        high = min(low + 256, columns)
        mine = lax.broadcasted_iota(jnp.int32, (count, high - low), 1) + low
        mine = (mine >= h * value_len) & (mine < (h + 1) * value_len)
        values = jnp.where(mine, values_ref[:, low:high].astype(jnp.float32), 0.0)
        values = values.astype(jnp.bfloat16)
        asks = (owner >= h * feat_in) & (owner < (h + 1) * feat_in)
        queries = jnp.where(asks, queries_ref[...].astype(jnp.float32), 0.0)
        scores = lax.dot_general(
            queries.astype(jnp.bfloat16), keys, NT, preferred_element_type=jnp.float32
        )
        gap = down[:, h : h + 1] - across[h : h + 1]
        weights = jnp.where(causal, jnp.exp(jnp.minimum(gap, 0.0)) * valid, 0.0)
        weights = weights * (1.0 + scores + 0.5 * scores * scores)
        numer_ref[:, low:high] += jnp.dot(
            weights.astype(jnp.bfloat16), values, preferred_element_type=jnp.float32
        )
        sums = jnp.sum(weights, axis=1, keepdims=True)
        denominators = jnp.where(head_lane == h, sums, denominators)
        own = turned[h * feat_in : (h + 1) * feat_in]
        fade = fading[h : h + 1]
        faded = own * fade
        scaled = faded * 0.5**0.5
        parts = [own[i : i + 1] * scaled for i in range(feat_in)]
        parts += [faded, jnp.where(spare, fade, 0.0)]
        feats = jnp.concatenate(parts, axis=0).astype(jnp.bfloat16)
        total[:, low:high] += jnp.dot(feats, values, preferred_element_type=jnp.float32)
        mark = (head_lane == h).astype(jnp.bfloat16)
        norm_total = norm_total + jnp.dot(feats, mark, preferred_element_type=jnp.float32)
    denom_ref[...] = denominators[:, :heads]
    pairs = feat_in * feat_in
    state_ref[0] = total[pairs + feat_in : pairs + feat_in + 1, :]
    for f in range(feat_in):
        state_ref[1 + f] = total[pairs + f : pairs + f + 1, :]

    @pl.loop(0, pairs // 8)
    def _(block):
        for k in range(8):
            f = block * 8 + k
            state_ref[1 + feat_in + f] = total[pl.ds(f, 1), :]

    norms[0:1, :] = norm_total[pairs + feat_in : pairs + feat_in + 1]
    norms[1 : 1 + feat_in, :] = norm_total[pairs : pairs + feat_in]
    norms[1 + feat_in : 1 + feat_in + pairs, :] = norm_total[:pairs]
    norm_ref[...] = norms[...].T[:heads, : 1 + feat_in + pairs]


def attend(valid_count, rate, queries, keys, values, feat_in, value_len):
    heads, count = rate.shape
    columns = values.shape[1]
    feat_len = 1 + feat_in + feat_in * feat_in
    padded = feat_in * feat_in + feat_in + 8
    return kernel_call(
        functools.partial(attend_body, feat_in, value_len),
        "attend",
        (
            like(count, columns, jnp.float32),
            like(count, heads, jnp.float32),
            jax.ShapeDtypeStruct((feat_len, 1, columns), jnp.float32),
            like(heads, feat_len, jnp.float32),
        ),
        valid_count,
        rate,
        queries,
        keys,
        values,
        specs=[pl.BlockSpec(memory_space=pltpu.SMEM)] + vmem(4),
        scratch=(
            pltpu.VMEM((queries.shape[1], count), jnp.float32),
            pltpu.VMEM((padded, columns), jnp.float32),
            pltpu.VMEM(((feat_len + 127) // 128 * 128, 128), jnp.float32),
        ),
    )


def mix_body(
    value_len, step, numer_ref, denom_ref, rows_ref, out_ref, gain_ref, mixed_ref, mlp_ref, sums
):
    count, columns = numer_ref.shape
    heads = denom_ref.shape[1]
    column = lax.broadcasted_iota(jnp.int32, (1, columns), 1)
    inverse = 1.0 / denom_ref[...]
    spread = jnp.zeros((count, columns), jnp.float32)
    for h in range(heads):
        here = (column >= h * value_len) & (column < (h + 1) * value_len)
        spread = jnp.where(here, inverse[:, h : h + 1], spread)
    attended = (numer_ref[...] * spread).astype(jnp.bfloat16)
    sums[...] = jnp.dot(attended, out_ref[...], preferred_element_type=jnp.float32)
    gain = gain_ref[...]

    @pl.loop(0, count // step)
    def _(block):
        at = pl.ds(pl.multiple_of(block * step, step), step)
        mixed = (rows_ref[at, :].astype(jnp.float32) + sums[at, :]).astype(jnp.bfloat16)
        mixed_ref[at, :] = mixed
        mlp_ref[at, :] = unit_rows(mixed.astype(jnp.float32), gain).astype(jnp.bfloat16)


def mix(numer, denom, rows, out_weight, mlp_gain, value_len):
    count, width = rows.shape
    shape = like(count, width, jnp.bfloat16)
    return kernel_call(
        functools.partial(mix_body, value_len, 32),
        "mix",
        (shape, shape),
        numer,
        denom,
        rows,
        out_weight,
        mlp_gain[None],
        scratch=(pltpu.VMEM((count, width), jnp.float32),),
    )


def swiglu_terms(rows, gate_rows, up_rows, down_rows):
    gate_act = lax.dot_general(rows, gate_rows, NT, preferred_element_type=jnp.float32)
    up_act = lax.dot_general(rows, up_rows, NT, preferred_element_type=jnp.float32)
    hidden_units = (gate_act * jax.nn.sigmoid(gate_act) * up_act).astype(jnp.bfloat16)
    return jnp.dot(hidden_units, down_rows, preferred_element_type=jnp.float32)


def on_grid(run):
    return all(low % 16 == 0 and high % 16 == 0 for _, low, high in run)


def read_units(refs, units):
    parts = []
    for k in range(3):
        rows = [refs[run[k][0]][run[k][1] : run[k][2]] for run in units if on_grid(run)]
        rest = [
            refs[run[k][0]][...].astype(jnp.float32)[run[k][1] : run[k][2]]
            for run in units
            if not on_grid(run)
        ]
        if rest:
            rows.append(jnp.concatenate(rest, axis=0).astype(jnp.bfloat16))
        parts.append(jnp.concatenate(rows, axis=0))
    return parts


def accumulate_body(units, n_weights, n_rows, n_acc, residual, *refs):
    weights = refs[:n_weights]
    rows = refs[n_weights : n_weights + n_rows]
    acc = refs[n_weights + n_rows : n_weights + n_rows + n_acc]
    parts = read_units(weights, units)
    for k, rows_ref in enumerate(rows):
        out_ref = refs[len(refs) - n_rows + k]
        terms = swiglu_terms(rows_ref[...], *parts)
        if n_acc:
            terms = terms + acc[k][...]
        if residual:
            terms = terms + refs[n_weights + n_rows + n_acc][...].astype(jnp.float32)
        out_ref[...] = terms.astype(out_ref.dtype)


def accumulate(rows, weights, units, acc, dtype, name, residual=None):
    shapes = tuple(like(*array.shape, dtype) for array in rows)
    start = len(weights) + len(rows)
    aliases = {start + k: k for k in range(len(acc))} if dtype == jnp.float32 else {}
    extra = () if residual is None else (residual,)
    body = functools.partial(
        accumulate_body, tuple(units), len(weights), len(rows), len(acc), bool(extra)
    )
    return kernel_call(body, name, shapes, *weights, *rows, *acc, *extra, aliases=aliases)


def runs(which, low, size):
    return tuple((which, low + k * size, low + (k + 1) * size) for k in range(3))


def split_runs(first, second, main):
    (i, at), (j, then) = first, second
    held = 2 * main // 3
    rest = main - held
    return (
        ((i, at, at + held), (i, at + main, at + main + held), (j, then + rest, then + main)),
        ((i, at + held, at + main), (j, then, then + rest), (j, then + main, then + rest + main)),
    )


def collect_body(plans, *refs):
    outs = refs[len(refs) - len(plans) :]
    for out_ref, plan in zip(outs, plans):
        rows = [refs[i][...].astype(jnp.float32)[low:high] for i, low, high in plan]
        out_ref[...] = jnp.concatenate(rows, axis=0).astype(jnp.bfloat16)


def collect(arrays, plans, name):
    columns = arrays[0].shape[1]
    shapes = tuple(like(sum(h - l for _, l, h in plan), columns, jnp.bfloat16) for plan in plans)
    return kernel_call(functools.partial(collect_body, plans), name, shapes, *arrays)


def shard_body(main, gate_ref, up_ref, down_ref, shard_ref, main_ref, *rest):
    buffers, sems = rest[:3], rest[3]
    copies = [
        pltpu.make_async_copy(source, buffer, sems.at[k])
        for k, (source, buffer) in enumerate(zip((gate_ref, up_ref, down_ref), buffers))
    ]
    for copy in copies:
        copy.start()
    for copy in copies:
        copy.wait()
    arrays = [buffer[...].astype(jnp.float32) for buffer in buffers]
    tops = [array[:main] for array in arrays]
    ends = [array[main:] for array in arrays]
    shard_ref[...] = jnp.concatenate(tops + ends, axis=0).astype(jnp.bfloat16)
    main_ref[...] = jnp.concatenate(tops, axis=0).astype(jnp.bfloat16)


def final_body(step, count_ref, kept_ref, given_ref, out_ref, done, sems):
    copies = []
    for block in range(kept_ref.shape[0] // step):
        first = block * step
        at = pl.ds(first, step)
        total = kept_ref[at, :] + given_ref[at, :].astype(jnp.float32)
        row = lax.broadcasted_iota(jnp.int32, total.shape, 0) + first
        done[at, :] = jnp.where(row < count_ref[0], total, 0.0).astype(done.dtype)
        copies.append(pltpu.make_async_copy(done.at[at, :], out_ref.at[at, :], sems.at[block]))
        copies[-1].start()
    for copy in copies:
        copy.wait()


def local(
    hidden_in,
    lengths,
    log_decay,
    mix_gain,
    conv_weight,
    query_weight,
    key_weight,
    value_weight,
    out_weight,
    mlp_gain,
    gate_weight,
    up_weight,
    down_weight,
):
    local_len = hidden_in.shape[1]
    rows_in = hidden_in[0]
    decays = log_decay[0]
    head_count = log_decay.shape[2]
    value_len = value_weight.shape[1] // head_count
    feat_in = query_weight.shape[1] // head_count
    feature_scale = feat_in ** (-0.25)
    valid_count = lengths - lax.axis_index("seq") * local_len
    spans = lax.axis_size("seq")
    units, model = gate_weight.shape[1], gate_weight.shape[0]
    edge = units // 7
    main = units - edge
    wide = 3 * main
    full = 3 * units
    narrow = full - wide
    cut = main + 2 * main // 3

    shard, shard_main = kernel_call(
        functools.partial(shard_body, main),
        "shard",
        (like(full, model, jnp.bfloat16), like(wide, model, jnp.bfloat16)),
        gate_weight.T,
        up_weight.T,
        down_weight.T,
        specs=[pl.BlockSpec(memory_space=pl.ANY)] * 3,
        scratch=[pltpu.VMEM((units, model), jnp.bfloat16)] * 3 + [pltpu.SemaphoreType.DMA((3,))],
        mib=56,
    )
    near, far, deep = slot((flip_near, shard), (flip_far, shard), (next_plane, shard_main))

    lead = 16
    if spans > 1:
        edge_in = from_behind(rows_in[local_len - lead :], "seq", 1)
    else:
        edge_in = jnp.zeros((lead, model), jnp.bfloat16)
    queries, key_rows, values = project(
        rows_in, edge_in, mix_gain, conv_weight, query_weight, key_weight, value_weight, feature_scale
    )
    near, far, deep, queries, key_rows, values = together(
        near, far, deep, queries, key_rows, values
    )

    sends = collect(
        (shard, near, far, deep),
        (
            ((3, 0, wide), (2, 0, cut)),
            ((3, 0, wide), (1, cut, full)),
            ((3, 0, wide), (0, wide, full), (1, wide, full), (2, wide, full)),
        ),
        "collect_second",
    )
    near1, far1, deep1 = slot(*zip((flip_near, flip_far, next_plane), sends))

    numerator, denominator, end_state, end_norm = attend(
        valid_count, log_decay[0].T, queries, key_rows, values, feat_in, value_len
    )
    if spans > 1:
        positions = jnp.arange(local_len, dtype=jnp.int32)
        numerator, denominator, end_state, end_norm = carry_in(
            (positions < valid_count).astype(jnp.float32),
            decays,
            queries,
            numerator,
            denominator,
            end_state[:, 0],
            end_norm.T,
        )
    else:
        end_norm = end_norm.T
    mixed_rows, mlp_in = mix(numerator, denominator, rows_in, out_weight, mlp_gain, value_len)
    near1, far1, deep1, mixed_rows, mlp_in, end_state, end_norm = together(
        near1, far1, deep1, mixed_rows, mlp_in, end_state, end_norm
    )

    middle = local_len // 2
    *sends, top, end = collect(
        (near1, far1, deep1, mlp_in),
        (
            ((2, 0, wide), (1, 0, cut)),
            ((2, 0, wide), (0, cut, wide)),
            ((2, 0, wide + 3 * narrow), (1, wide + wide - cut, wide + full - cut)),
            ((3, 0, middle),),
            ((3, middle, local_len),),
        ),
        "collect_third",
    )
    near2, far2, deep2 = slot(*zip((flip_near, flip_far, next_plane), sends))
    (other_in,) = collect(
        (flip_core(top), flip_core(end)),
        (((0, 0, middle), (1, 0, local_len - middle)),),
        "collect_rows",
    )
    rows = (mlp_in, other_in)
    acc = accumulate(
        rows,
        (shard, near, far, deep, near1, far1, deep1),
        [runs(i, 0, main) for i in range(7)] + list(split_runs((4, wide), (5, wide), main)),
        (),
        jnp.float32,
        "accumulate_second",
    )
    near2, far2, deep2, *acc = together(near2, far2, deep2, *acc)

    two = 2 * main
    sends = collect(
        (near2, far2, deep2),
        (
            ((2, main, wide),),
            ((2, 0, main), (2, two, wide)),
            ((2, wide, wide + 4 * narrow), (1, 2 * wide - cut - main, 2 * wide - cut)),
            ((2, 0, main), (1, 0, main)),
            ((2, main, two), (0, main, two)),
        ),
        "collect_fourth",
    )
    sends = together(*sends)
    near3, far3, deep3 = flip_near(sends[0]), flip_far(sends[1]), next_plane(sends[2])
    near3_more, far3_more = flip_near(sends[3]), flip_far(sends[4])
    acc = accumulate(
        rows,
        (shard, near, far, far1, deep1, near2, far2, deep2),
        [runs(i, 0, main) for i in (5, 6, 7)]
        + list(split_runs((5, wide), (6, wide), main))
        + [runs(i, wide, edge) for i in (0, 1, 2)]
        + [runs(3, wide + wide - cut, edge)]
        + [runs(4, wide + k * narrow, edge) for k in range(3)]
        + [runs(7, wide + k * narrow, edge) for k in range(4)],
        tuple(acc),
        jnp.float32,
        "accumulate_third",
    )
    near3, far3, *acc = together(near3, far3, *acc)

    near4, far4 = flip_near(far3[:main]), flip_far(near3[:main])
    deep4 = next_plane(deep3[3 * narrow :])
    line = 4 * narrow
    weights = (near3, near3_more, far3, far3_more, deep3, near4, far4, deep4)
    last = [
        ((1, 0, main), (0, 0, main), (0, main, two)),
        ((2, 0, main), (3, 0, main), (2, main, two)),
        ((1, main, two), (3, main, two), (4, line, line + main)),
        ((5, 0, main), (6, 0, main), (7, narrow, narrow + main)),
    ]
    last += [runs(4, k * narrow, edge) for k in range(4)] + [runs(7, 0, edge)]
    (given,) = accumulate(rows[1:], weights, last, acc[1:], jnp.bfloat16, "finish_other")
    (kept,) = accumulate(
        rows[:1], weights, last, acc[:1], jnp.float32, "finish_own", residual=mixed_rows
    )
    result = pl.pallas_call(
        functools.partial(final_body, 64),
        out_shape=like(local_len, model, jnp.bfloat16),
        in_specs=[pl.BlockSpec(memory_space=pltpu.SMEM)] + vmem(2),
        out_specs=pl.BlockSpec(memory_space=pl.ANY),
        scratch_shapes=[
            pltpu.VMEM((local_len, model), jnp.bfloat16),
            pltpu.SemaphoreType.DMA((local_len // 64,)),
        ],
        compiler_params=pltpu.CompilerParams(vmem_limit_bytes=24 * 1024 * 1024),
        name="final",
    )(valid_count, kept, flip_core(given))
    return (
        result[None],
        end_state.reshape((1, 1) + end_state.shape[:1] + end_state.shape[-1:]),
        end_norm[None, None],
    )


def solution(mesh):
    return jax.shard_map(
        local,
        mesh=mesh,
        in_specs=(
            P("req", "seq", None),
            P("req"),
            P("req", "seq", None),
            P(),
            P(),
            P(),
            P(),
            P(),
            P(),
            P(),
            P(None, "req"),
            P(None, "req"),
            P(None, "req"),
        ),
        out_specs=(P("req", "seq", None), P("req", "seq", None, None), P("req", "seq", None, None)),
        check_vma=False,
    )
```
